32 devices in a mesh: expert: 8 (over z, x), tensor: 4 (over y, core).
Axes of the slice: x: 2, y: 2, z: 4, core: 2. Of those that a mesh axis runs over, the one named last changes fastest.
Arguments:
- inputs: bfloat16 [8192, 2048], P('expert'), may hold values from -6 to 6
- attn_gain: float32 [2048], replicated, may hold values from 0.25 to 1.75
- w_query: bfloat16 [2048, 2048], P(None, 'tensor'), may hold values from -1.5 to 1.5
- w_key: bfloat16 [2048, 2048], P(None, 'tensor'), may hold values from -1.5 to 1.5
- w_value: bfloat16 [2048, 2048], P(None, 'tensor'), may hold values from -0.125 to 0.125
- w_output: bfloat16 [2048, 2048], P('tensor'), may hold values from -2 to 2
- query_gain: float32 [2048], P('tensor'), may hold values from 0.25 to 1.75
- key_gain: float32 [2048], P('tensor'), may hold values from 0.25 to 1.75
- moe_gain: float32 [2048], replicated, may hold values from 0.25 to 1.75
- w_router: bfloat16 [2048, 64], replicated, may hold values from -0.0625 to 0.0625
- w_gate: bfloat16 [64, 2048, 1024], P('expert', None, 'tensor'), may hold values from -0.125 to 0.125
- w_up: bfloat16 [64, 2048, 1024], P('expert', None, 'tensor'), may hold values from -0.125 to 0.125
- w_down: bfloat16 [64, 1024, 2048], P('expert', 'tensor'), may hold values from -4 to 4
- routes: int32 [8192, 8], P('expert'), may hold values from 0 to 63, all different within a row; in each aligned block of 1024 rows (0 to 1023, 1024 to 2047, ...) at most 160 rows name the same one
- piece_start: int32 [8, 2], P('expert'), may hold values from 0 to 768, as said below
- piece_length: int32 [8, 2], P('expert'), may hold values from 128 to 256, as said below
- clip_threshold: float32 [16], P('tensor'), may hold values from 1.1313709 to 11.313708
- cotangent: float32 [8192, 2048], P('expert', 'tensor'), may hold values from -6 to 6
Outputs:
- out: float32 [8192, 2048], P('expert', 'tensor')
- grad_input: float32 [8192, 2048], P('expert', 'tensor')
- grad_attn_gain: float32 [2048], replicated
- grad_query: float32 [2048, 2048], P(None, 'tensor')
- grad_key: float32 [2048, 2048], P(None, 'tensor')
- grad_value: float32 [2048, 2048], P(None, 'tensor')
- grad_output: float32 [2048, 2048], P('tensor')
- grad_query_gain: float32 [2048], P('tensor')
- grad_key_gain: float32 [2048], P('tensor')
- grad_moe_gain: float32 [2048], P('tensor')
- grad_router: float32 [2048, 64], replicated
- grad_gate: float32 [64, 2048, 1024], P('expert', None, 'tensor')
- grad_up: float32 [64, 2048, 1024], P('expert', None, 'tensor')
- grad_down: float32 [64, 1024, 2048], P('expert', 'tensor')
- head_max: float32 [16], P('tensor')
- query_clipped: bfloat16 [2048, 2048], P(None, 'tensor')
- key_clipped: bfloat16 [2048, 2048], P(None, 'tensor')
The draws below stay inside these ranges and needn't reach their ends.
Inputs may be any that keep to these rules, and one draw needn't show every extreme that they name: `routes`: each row names 8 different experts; in each aligned block of 1024 rows (the rows of one device) no expert is named by more than 160 rows. `piece_start`: piece 0 of a sequence lies in its first half, piece 1 starts in its second half. `piece_length`: in each sequence one of the two pieces holds exactly 256 tokens.
All inputs are finite; a program needn't handle non-finite values.
Results may differ from the reference program's by a relative error of at most 0.03.
Values may be sent and summed in bfloat16 or wider, within the bound.
No kernel may reach another device: no remote copies, remote signals or barrier semaphores. Data moves between devices by JAX's collectives and lax.ppermute only.
A program may use at most 576 MiB of HBM per device.

```python
import math
import jax
import jax.numpy as jnp
import numpy as np
from jax import lax

D = 2048
H = 16
HD = 128
E = 64
TOP = 8
FF = 1024
LENGTH = 1024
PIECE = 256
TOK_DEV = 1024
SEQS = 8
TOKENS = 8192
CAP = 160
N_EXPERT = 8


def draw_piece_start(key, part):
    key = jax.random.fold_in(key, 11)
    first_key, second_key = jax.random.split(key)
    first = jax.random.randint(first_key, (SEQS, 1), 0, LENGTH // 2 - PIECE + 1, dtype=jnp.int32)
    second = jax.random.randint(second_key, (SEQS, 1), LENGTH // 2, LENGTH - PIECE + 1, dtype=jnp.int32)
    return jnp.concatenate([first, second], axis=1)


def draw_piece_length(key, part):
    key = jax.random.fold_in(key, 12)
    size_key, full_key = jax.random.split(key)
    sizes = jax.random.randint(size_key, (SEQS, 2), PIECE // 2, PIECE + 1, dtype=jnp.int32)
    full = jax.random.randint(full_key, (SEQS, 1), 0, 2, dtype=jnp.int32)
    return jnp.where(jnp.arange(2, dtype=jnp.int32)[None, :] == full, PIECE, sizes)


def levels(stream_key, extent, cuts, low, top_value):
    loudness = 1.0
    for axis_at, blocks in cuts:
        heights = jax.random.uniform(jax.random.fold_in(jax.random.fold_in(stream_key, 6), axis_at), (blocks,), jnp.float32, low / len(cuts), top_value / len(cuts))
        loudness = loudness * jnp.repeat(jnp.exp(heights), extent[axis_at] // blocks).reshape((-1,) + (1,) * (len(extent) - 1 - axis_at))
    return loudness


def deal_out(key, own, number, rows, count, top, reach, lean):
    sequence = jax.random.permutation(key, count)
    crowded, common = shares(count, rows * top, reach, lean, True), shares(count, rows * top, reach, lean, False)
    places = jnp.arange(count)

    def named(sizes, offset_by):
        used = int((sizes > 0).sum())
        fixed = max(1, used // 4)
        shifted = fixed + (places - fixed + offset_by * (used - fixed)) % max(1, count - fixed)
        return jnp.zeros((count,), jnp.int32).at[sequence[jnp.where(places < fixed, places, shifted)]].set(jnp.asarray(sizes, jnp.int32))

    sizes = jnp.where(number % 4 == 0, named(crowded, number // 4), named(common, number - number // 4 - 1))
    mixed = jax.random.permutation(jax.random.fold_in(own, 3), count)
    giver, receiver = mixed[0:count // 2 * 2:2], mixed[1:count // 2 * 2:2]
    margin = jnp.minimum(sizes[giver] - 1, reach - sizes[receiver]) // 2
    margin = jnp.where((giver == sequence[0]) | (receiver == sequence[0]) | (sizes[receiver] == 0), 0, jnp.maximum(margin, 0))
    shifted = jax.random.randint(jax.random.fold_in(own, 4), (count // 2,), 0, 1 << 20) % (margin + 1)
    sizes = sizes.at[giver].add(-shifted).at[receiver].add(shifted)
    items = jnp.searchsorted(jnp.cumsum(sizes), jnp.arange(rows * top), side="right").astype(jnp.int32)
    table = items.reshape(top, rows).T
    table = table[jax.random.permutation(jax.random.fold_in(own, 1), rows)]
    offset_by = jax.random.randint(jax.random.fold_in(own, 2), (rows, 1), 0, top)
    return jnp.take_along_axis(table, (jnp.arange(top)[None, :] + offset_by) % top, axis=1)


def shares(amount, total, most, lean, full):
    loads = [(1 << 20) // math.isqrt(rank ** lean) + 1 for rank in range(1, amount + 1)]
    largest = most if full else min(most, max(-(-total // amount), total * loads[0] // sum(loads)))
    least = 1 if total - largest >= amount - 1 else 0
    given, surplus = [largest] + [least] * (amount - 1), total - largest - least * (amount - 1)
    while surplus > 0:
        free = [i for i in range(1, amount) if given[i] < largest] or [i for i in range(1, amount) if given[i] < most]
        whole, left = sum([loads[i] for i in free]), surplus
        for i in free:
            extra = min(most - given[i], max(1, left * loads[i] // whole), surplus)
            given[i] = given[i] + extra
            surplus = surplus - extra
    return np.array(given)


def gaussian(own_key, extent, width, reach, shards=(), kind=jnp.bfloat16):
    level = levels(own_key, extent, shards, -0.22, 0.18) if shards else 1.0
    values = jax.random.normal(own_key, extent, jnp.float32) * width * level
    return jnp.minimum(jnp.maximum(values, -reach), reach).astype(kind)


def setup_inputs(seed: int = 0) -> dict:
    key_list = jax.random.split(jax.random.key(seed), 19)
    inputs = gaussian(key_list[0], (TOKENS, D), 1.0, 6.0, ((0, 8),))
    attn_gain = jnp.clip(1.0 + 0.15 * jax.random.normal(key_list[1], (D,), jnp.float32), 0.25, 1.75)
    w_query = gaussian(key_list[2], (D, H * HD), (max(D // 128, 1)) ** -0.5, 1.5, ((1, 4),))
    w_key = gaussian(key_list[3], (D, H * HD), (max(D // 128, 1)) ** -0.5, 1.5, ((1, 4),))
    w_value = gaussian(key_list[4], (D, H * HD), D ** -0.5, 0.125, ((1, 4),))
    w_output = gaussian(key_list[5], (H * HD, D), (max(D // 256, 1)) ** -0.5, 2.0, ((0, 4),))
    query_gain = jnp.clip(1.0 + 0.15 * jax.random.normal(key_list[6], (H * HD,), jnp.float32), 0.25, 1.75)
    key_gain = jnp.clip(1.0 + 0.15 * jax.random.normal(key_list[7], (H * HD,), jnp.float32), 0.25, 1.75)
    moe_gain = jnp.clip(1.0 + 0.15 * jax.random.normal(key_list[8], (D,), jnp.float32), 0.25, 1.75)
    w_router = gaussian(key_list[9], (D, E), (4 * D) ** -0.5, 0.0625)
    w_gate = gaussian(key_list[10], (E, D, FF), D ** -0.5, 0.125, ((0, 8), (2, 4)))
    w_up = gaussian(key_list[11], (E, D, FF), D ** -0.5, 0.125, ((0, 8), (2, 4)))
    w_down = gaussian(key_list[12], (E, FF, D), (max(FF // 512, 1)) ** -0.5, 4.0, ((0, 8), (1, 4)))
    routes_keys = jax.random.split(jax.random.fold_in(key_list[13], 1), TOKENS // TOK_DEV)
    routes_turns = jax.random.permutation(jax.random.fold_in(key_list[13], 3), TOKENS // TOK_DEV)
    routes = jax.vmap(lambda own, number: deal_out(jax.random.fold_in(key_list[13], 2), own, number, TOK_DEV, E, TOP, CAP, 1))(routes_keys, routes_turns).reshape((TOKENS, TOP))
    piece_start = draw_piece_start(jax.random.fold_in(key_list[18], 71), 0)
    piece_length = draw_piece_length(jax.random.fold_in(key_list[18], 71), 0)
    clip_threshold = jnp.clip(jnp.exp(math.log(11.313708) - 2.30258503 * jax.random.uniform(key_list[16], (H,), jnp.float32) ** levels(key_list[16], (H,), ((0, 4),), -0.2, 0.2)), 1.1313709, 11.313708)
    cotangent = gaussian(key_list[17], (TOKENS, D), 1.0, 6.0, ((0, 8), (1, 4)), jnp.float32)
    return {"inputs": inputs, "attn_gain": attn_gain, "w_query": w_query, "w_key": w_key, "w_value": w_value, "w_output": w_output, "query_gain": query_gain, "key_gain": key_gain, "moe_gain": moe_gain, "w_router": w_router, "w_gate": w_gate, "w_up": w_up, "w_down": w_down, "routes": routes, "piece_start": piece_start, "piece_length": piece_length, "clip_threshold": clip_threshold, "cotangent": cotangent}


@jax.custom_vjp
def low(v):
    return lax.optimization_barrier(v.astype(jnp.bfloat16)).astype(jnp.float32)

@jax.custom_vjp
def low_back(v):
    return v

def low_keep(v):
    return (low(v), None)

def low_pass(kept, grad):
    return (grad,)

def back_keep(v):
    return (v, None)

def back_low(kept, grad):
    return (low(grad),)
low.defvjp(low_keep, low_pass)
low_back.defvjp(back_keep, back_low)
HIGH = lax.Precision.HIGHEST

def matmul(left, right):
    return jnp.dot(left, right, precision=HIGH)

def rms_rows(values, gain):
    return values * lax.rsqrt(lax.optimization_barrier(jnp.mean(values * values, axis=-1, keepdims=True)) + 1e-05) * gain

def head_norm(raw, gain):
    parts = raw.reshape(raw.shape[0], H, HD)
    normed = parts * lax.rsqrt(lax.optimization_barrier(jnp.mean(parts * parts, axis=-1, keepdims=True)) + 1e-06)
    return normed.reshape(raw.shape[0], H * HD) * gain

def inside_pieces(start, length, positions):
    return (positions[None, :] >= start[:, None]) & (positions[None, :] < (start + length)[:, None])

def attend_sequence(args):
    queries, keys, values, start, length = args
    block = min(512, LENGTH)
    scale = 1.0 / math.sqrt(HD)
    key_pos = jnp.arange(LENGTH, dtype=jnp.int32)
    key_in = inside_pieces(start, length, key_pos)

    def one_block(index):
        first = index * block
        rows = lax.dynamic_slice_in_dim(queries, first, block, 0)
        query_pos = first + jnp.arange(block, dtype=jnp.int32)
        query_in = inside_pieces(start, length, query_pos)
        allowed = (key_pos[None, :] <= query_pos[:, None]) | jnp.any(query_in[:, :, None] & key_in[:, None, :], axis=0)
        scores = low_back(jnp.einsum('qhd,khd->hqk', rows, keys, precision=HIGH) * scale)
        masked = jnp.where(allowed[None], scores, -1e+30)
        top = lax.optimization_barrier(jnp.max(masked, axis=-1, keepdims=True))
        weights = jnp.exp(masked - top)
        probs = weights / lax.optimization_barrier(jnp.sum(weights, axis=-1, keepdims=True))
        result = jnp.einsum('hqk,khd->qhd', low(probs), values, precision=HIGH)
        return (result, lax.optimization_barrier(jnp.max(masked, axis=(1, 2))))
    results, tops = lax.map(jax.checkpoint(one_block), jnp.arange(LENGTH // block, dtype=jnp.int32))
    return (results.reshape(LENGTH, H, HD), lax.optimization_barrier(jnp.max(tops, axis=0)))

def reference(inputs, attn_gain, w_query, w_key, w_value, w_output, query_gain, key_gain, moe_gain, w_router, w_gate, w_up, w_down, routes, piece_start, piece_length, clip_threshold, cotangent):
    capacity = N_EXPERT * CAP
    token_ids = jnp.arange(TOKENS, dtype=jnp.int32)

    def expert_rows(expert):
        chosen = jnp.any(routes == expert, axis=1)
        order = jnp.argsort(jnp.where(chosen, token_ids, token_ids + TOKENS))[:capacity].astype(jnp.int32)
        return (order, chosen[order].astype(jnp.float32))
    expert_ids = jnp.arange(E, dtype=jnp.int32)
    orders, valid = lax.map(expert_rows, expert_ids)
    seqs = TOKENS // LENGTH
    shape4 = (seqs, LENGTH, H, HD)

    def forward(inputs, attn_gain, w_query, w_key, w_value, w_output, query_gain, key_gain, moe_gain, w_router, w_gate, w_up, w_down):
        normed_a = low(rms_rows(inputs, attn_gain))
        queries = low(head_norm(low_back(matmul(normed_a, w_query)), query_gain))
        keys = low(head_norm(low_back(matmul(normed_a, w_key)), key_gain))
        values = low(low_back(matmul(normed_a, w_value)))
        results, tops = lax.map(jax.checkpoint(attend_sequence), (queries.reshape(shape4), keys.reshape(shape4), values.reshape(shape4), piece_start, piece_length))
        attended = low(low_back(results.reshape(TOKENS, H * HD)))
        residual = inputs + low_back(matmul(attended, w_output))
        normed_m = low(rms_rows(residual, moe_gain))
        router = jax.nn.softmax(low_back(matmul(normed_m, w_router)), axis=-1)

        def expert_out(args):
            gate_w, up_w, down_w, order = args
            rows = normed_m[order]
            gate_pre = low_back(matmul(rows, gate_w))
            up_pre = low_back(matmul(rows, up_w))
            hidden = low(jax.nn.silu(gate_pre) * up_pre)
            return low(low_back(matmul(hidden, down_w)))
        outputs = lax.map(jax.checkpoint(expert_out), (w_gate, w_up, w_down, orders))
        weights = router[orders, expert_ids[:, None]] * valid
        mixture = jnp.zeros_like(residual).at[orders.reshape(-1)].add((weights[:, :, None] * outputs).reshape(-1, D))
        return (residual + mixture, lax.optimization_barrier(jnp.max(tops, axis=0)))
    floats = tuple((item.astype(jnp.float32) for item in (inputs, attn_gain, w_query, w_key, w_value, w_output, query_gain, key_gain, moe_gain, w_router, w_gate, w_up, w_down)))
    result, backward, head_max = jax.vjp(forward, *floats, has_aux=True)
    grads = backward(cotangent)
    factor = clip_threshold / jnp.maximum(head_max, clip_threshold)
    spread = jnp.repeat(jnp.sqrt(factor), HD)
    query_clipped = (floats[2] * spread[None, :]).astype(jnp.bfloat16)
    key_clipped = (floats[3] * spread[None, :]).astype(jnp.bfloat16)
    return (result, grads[0], grads[1], grads[2], grads[3], grads[4], grads[5], grads[6], grads[7], grads[8], grads[9], grads[10], grads[11], grads[12], head_max, query_clipped, key_clipped)
```

```python
from functools import partial
import math

import jax
import jax.numpy as jnp
from jax import lax
from jax.experimental import pallas as pl
from jax.experimental.pallas import tpu as pltpu
from jax.sharding import PartitionSpec as P

HD = 128
E = 64
TOP = 8
LENGTH = 1024
CAP = 160
NB = 2
BOTH = ("expert", "tensor")
F32 = jnp.float32
BF16 = jnp.bfloat16
VMEM = 60 * 1024 * 1024


def matmul(left, right):
    return jnp.dot(left, right, preferred_element_type=F32)


def matmul_nt(left, right):
    return lax.dot_general(left, right, (((1,), (1,)), ((), ())), preferred_element_type=F32)


def matmul_tn(left, right):
    return lax.dot_general(left, right, (((0,), (0,)), ((), ())), preferred_element_type=F32)


def flip(dz, dx, dy, dc):
    pairs = []
    for z in range(4):
        for x in range(2):
            for y in range(2):
                for c in range(2):
                    pairs.append(
                        (
                            ((z * 2 + x) * 2 + y) * 2 + c,
                            (((z ^ dz) * 2 + (x ^ dx)) * 2 + (y ^ dy)) * 2 + (c ^ dc),
                        )
                    )
    return pairs


def send(value, dz=0, dx=0, dy=0, dc=0):
    return lax.ppermute(value, BOTH, flip(dz, dx, dy, dc))


def is_cube():
    return lax.axis_size("expert") == 8 and lax.axis_size("tensor") == 4


def core_swap(value):
    if is_cube():
        return send(value, dc=1)
    count = lax.axis_size("tensor")
    return lax.ppermute(value, "tensor", [(i, i ^ 1) for i in range(count)])


def slot_blocks():
    owner, part = lax.axis_index("expert"), lax.axis_index("tensor")
    core = part % 2
    if is_cube():
        blocks = [[owner ^ (k * 2 + b) for b in range(NB)] for k in range(4)]
        mine = [part ^ (y * 2) for y in range(2)]
    else:
        blocks = [[k * NB + b for b in range(NB)] for k in range(lax.axis_size("expert") // NB)]
        mine = [y * 2 + core for y in range(lax.axis_size("tensor") // 2)]
    theirs = [m ^ 1 for m in mine]
    return [jnp.stack([jnp.asarray(v, jnp.int32) for v in b + mine + theirs]) for b in blocks]


def same_core():
    count = lax.axis_size("tensor")
    return [[y * 2 + c for y in range(count // 2)] for c in range(2)]


def gather_slots(own):
    if not is_cube():
        blocks = lax.all_gather(own, "expert")
        full = lax.all_gather(blocks, "tensor", axis_index_groups=same_core())
        return [
            [[full[y, k * NB + b] for y in range(full.shape[0])] for b in range(NB)]
            for k in range(full.shape[1] // NB)
        ]
    half = own.shape[0] // 2
    starts = [own] + [send(own, dz=k) for k in (1, 2, 3)]
    slots = []
    for block in starts:
        over_x = send(block, dx=1)
        over_y = send(block, dy=1)
        low = send(over_x[:half], dy=1)
        high = send(over_y[half:], dx=1)
        slots.append([[block, over_y], [over_x, jnp.concatenate([low, high], axis=0)]])
    return slots


def scatter_slot(parts):
    half = parts[0][0].shape[0] // 2
    low = send(parts[1][1][:half], dy=1)
    high = send(parts[1][1][half:], dx=1)

    def joined(first, second):
        return (first.astype(F32) + second.astype(F32)).astype(BF16)

    to_x = jnp.concatenate([joined(parts[1][0][:half], low), parts[1][0][half:]], axis=0)
    to_y = jnp.concatenate([parts[0][1][:half], joined(parts[0][1][half:], high)], axis=0)
    from_x = send(to_x, dx=1)
    from_y = send(to_y, dy=1)
    return parts[0][0].astype(F32) + from_x.astype(F32) + from_y.astype(F32)


def scatter_slots(slots):
    if not is_cube():
        full = jnp.stack(
            [jnp.stack([s[b][y] for s in slots for b in range(NB)]) for y in range(len(slots[0][0]))]
        )
        mine = lax.psum_scatter(full, "tensor", axis_index_groups=same_core(), scatter_dimension=0)
        return lax.psum_scatter(mine, "expert", scatter_dimension=0).astype(F32)
    total = None
    for k, parts in enumerate(slots):
        term = scatter_slot(parts)
        if k:
            term = send(term.astype(BF16), dz=k).astype(F32)
        total = term if total is None else total + term
    return total


def tensor_gather(own, over_y=None):
    if not is_cube():
        full = lax.all_gather(own, "tensor")
        return [full[i] for i in range(full.shape[0])]
    if over_y is None:
        over_y = send(own, dy=1)
    return [own, send(own, dc=1), over_y, send(over_y, dc=1)]


def tensor_order():
    part = lax.axis_index("tensor")
    count = lax.axis_size("tensor")
    if is_cube():
        return [part ^ i for i in range(count)]
    return [jnp.int32(i) for i in range(count)]


def one_hot(pos_row):
    rows = lax.broadcasted_iota(jnp.int32, (CAP, pos_row.shape[1]), 0)
    return rows == pos_row


def as_bf16(mask):
    return jnp.where(mask, 1.0, 0.0).astype(BF16)


def pick_kernel(group, slices, where_ref, *refs):
    pos_refs, x_refs = refs[:NB], refs[NB : NB + NB * slices]
    out_ref, hot_ref = refs[-2:]
    step = pl.program_id(0)
    for b in range(NB):
        for i in range(group):
            hot_ref[b, i * CAP : (i + 1) * CAP, :] = as_bf16(
                one_hot(pos_refs[b][0, pl.ds(step * group + i, 1), :])
            )
        for y in range(slices):
            out_ref[b, y] = matmul(hot_ref[b], x_refs[b * slices + y][...]).astype(BF16)


def pick_rows(where, pos, blocks):
    slices = len(blocks[0])
    tokens, width = blocks[0][0].shape
    held = pos.shape[1]
    group = 2
    flat = [a for b in blocks for a in b]

    def block_spec(b):
        return pl.BlockSpec((1, held, tokens), lambda i, where: (where[b], 0, 0))

    return pl.pallas_call(
        partial(pick_kernel, group, slices),
        grid_spec=pltpu.PrefetchScalarGridSpec(
            num_scalar_prefetch=1,
            grid=(held // group,),
            in_specs=[block_spec(b) for b in range(NB)]
            + [pl.BlockSpec((tokens, width), lambda i, where: (0, 0)) for _ in flat],
            out_specs=pl.BlockSpec(
                (NB, slices, group * CAP, width), lambda i, where: (0, 0, i, 0)
            ),
            scratch_shapes=[pltpu.VMEM((NB, group * CAP, tokens), BF16)],
        ),
        out_shape=jax.ShapeDtypeStruct((NB, slices, held * CAP, width), BF16),
        compiler_params=pltpu.CompilerParams(vmem_limit_bytes=VMEM),
        cost_estimate=pl.CostEstimate(
            flops=2 * NB * slices * held * CAP * tokens * width,
            bytes_accessed=2 * NB * slices * (held * CAP + tokens) * width,
            transcendentals=0,
        ),
        name="pick_rows",
    )(where, *([pos] * NB), *flat)


def expert_kernel(slices, where_ref, *refs):
    pos_refs, gate_refs = refs[:NB], refs[NB : 2 * NB]
    rows_mine, rows_theirs, cot_mine, cot_theirs, wg_ref, wu_ref, wd_ref = refs[2 * NB : 2 * NB + 7]
    scaled_ref, gate_grad_ref, up_grad_ref, prob_ref, keep_ref, give_ref = refs[2 * NB + 7 :]
    e = pl.program_id(0)
    width = rows_mine.shape[3]
    ff = wg_ref.shape[2]
    gate_pre = jnp.zeros((NB * CAP, ff), F32)
    up_pre = jnp.zeros((NB * CAP, ff), F32)
    grad_hidden = jnp.zeros((NB * CAP, ff), F32)

    def columns(j):
        return pl.ds(pl.multiple_of(where_ref[NB + j] * width, width), width)

    for j in range(2 * slices):
        x_ref, c_ref = (rows_mine, cot_mine) if j < slices else (rows_theirs, cot_theirs)
        x = x_ref[:, j % slices].reshape(NB * CAP, width)
        c = c_ref[:, j % slices].reshape(NB * CAP, width)
        gate_pre = gate_pre + matmul(x, wg_ref[0, columns(j), :])
        up_pre = up_pre + matmul(x, wu_ref[0, columns(j), :])
        grad_hidden = grad_hidden + matmul_nt(c, wd_ref[0, :, columns(j)])
    masks = [one_hot(pos_refs[b][0, pl.ds(e, 1), :]) for b in range(NB)]
    gates = jnp.concatenate(
        [
            jnp.sum(jnp.where(masks[b], gate_refs[b][0, pl.ds(e, 1), :], 0.0), axis=1, keepdims=True)
            for b in range(NB)
        ],
        axis=0,
    )
    sigma = jax.nn.sigmoid(gate_pre)
    swish = gate_pre * sigma
    hidden = (swish * up_pre).astype(BF16).astype(F32)
    prob = jnp.sum(hidden * grad_hidden, axis=1, keepdims=True)
    for b in range(NB):
        prob_ref[0, b : b + 1, :] = jnp.sum(
            jnp.where(masks[b], prob[b * CAP : (b + 1) * CAP], 0.0), axis=0, keepdims=True
        )
    grad_hidden = grad_hidden * gates
    scaled_ref[0] = (hidden * gates).astype(BF16)
    gate_grad = (grad_hidden * up_pre * (sigma * (1.0 + gate_pre * (1.0 - sigma)))).astype(BF16)
    up_grad = (grad_hidden * swish).astype(BF16)
    gate_grad_ref[0] = gate_grad
    up_grad_ref[0] = up_grad
    for j in range(2 * slices):
        to = keep_ref if j < slices else give_ref
        back = matmul_nt(gate_grad, wg_ref[0, columns(j), :]) + matmul_nt(
            up_grad, wu_ref[0, columns(j), :]
        )
        to[:, j % slices] = back.astype(BF16).reshape(NB, CAP, width)


def expert_slot(where, pos, gate, rows, cots, w_gate, w_up, w_down):
    held, depth, ff = w_gate.shape
    tokens = pos.shape[2]
    slices, width = rows[0].shape[1], rows[0].shape[3]

    def block_spec(b):
        return pl.BlockSpec((1, held, tokens), lambda e, where: (where[b], 0, 0))

    rows_spec = pl.BlockSpec((NB, slices, CAP, width), lambda e, where: (0, 0, e, 0))
    rows_shape = jax.ShapeDtypeStruct((NB, slices, held * CAP, width), BF16)
    in_spec = pl.BlockSpec((1, depth, ff), lambda e, where: (e, 0, 0))
    hidden_spec = pl.BlockSpec((1, NB * CAP, ff), lambda e, where: (e, 0, 0))
    hidden_shape = jax.ShapeDtypeStruct((held, NB * CAP, ff), BF16)
    return pl.pallas_call(
        partial(expert_kernel, slices),
        grid_spec=pltpu.PrefetchScalarGridSpec(
            num_scalar_prefetch=1,
            grid=(held,),
            in_specs=[block_spec(b) for b in range(NB)] * 2
            + [rows_spec] * 4
            + [in_spec, in_spec, pl.BlockSpec((1, ff, depth), lambda e, where: (e, 0, 0))],
            out_specs=[hidden_spec] * 3
            + [pl.BlockSpec((1, NB, tokens), lambda e, where: (e, 0, 0)), rows_spec, rows_spec],
        ),
        out_shape=[hidden_shape] * 3
        + [jax.ShapeDtypeStruct((held, NB, tokens), F32), rows_shape, rows_shape],
        compiler_params=pltpu.CompilerParams(vmem_limit_bytes=VMEM),
        cost_estimate=pl.CostEstimate(
            flops=10 * NB * held * CAP * depth * ff,
            bytes_accessed=6 * held * depth * ff + 6 * NB * held * CAP * depth,
            transcendentals=NB * held * CAP * ff,
        ),
        name="expert_slot",
    )(where, *([pos] * NB), *([gate] * NB), *rows, *cots, w_gate, w_up, w_down)


def down_kernel(slices, where_ref, scaled_ref, wd_ref, keep_ref, give_ref):
    width = keep_ref.shape[3]
    for j in range(2 * slices):
        to = keep_ref if j < slices else give_ref
        columns = pl.ds(pl.multiple_of(where_ref[NB + j] * width, width), width)
        rows = matmul(scaled_ref[0], wd_ref[0, :, columns])
        to[:, j % slices] = rows.astype(BF16).reshape(NB, CAP, width)


def down_slot(where, scaled, w_down, slices):
    held, ff, depth = w_down.shape
    width = depth // (2 * slices)
    rows_spec = pl.BlockSpec((NB, slices, CAP, width), lambda e, where: (0, 0, e, 0))
    rows_shape = jax.ShapeDtypeStruct((NB, slices, held * CAP, width), BF16)
    return pl.pallas_call(
        partial(down_kernel, slices),
        grid_spec=pltpu.PrefetchScalarGridSpec(
            num_scalar_prefetch=1,
            grid=(held,),
            in_specs=[
                pl.BlockSpec((1, NB * CAP, ff), lambda e, where: (e, 0, 0)),
                pl.BlockSpec((1, ff, depth), lambda e, where: (e, 0, 0)),
            ],
            out_specs=[rows_spec, rows_spec],
        ),
        out_shape=[rows_shape, rows_shape],
        compiler_params=pltpu.CompilerParams(vmem_limit_bytes=VMEM),
        cost_estimate=pl.CostEstimate(
            flops=2 * NB * held * CAP * depth * ff,
            bytes_accessed=2 * held * depth * ff + 2 * NB * held * CAP * depth,
            transcendentals=0,
        ),
        name="down_slot",
    )(where, scaled, w_down)


def place_kernel(slices, held, where_ref, *refs):
    at_refs, mine_ref, theirs_ref = refs[:NB], refs[NB], refs[NB + 1]
    out_refs, hot_ref = refs[NB + 2 : -1], refs[-1]
    b, y = pl.program_id(0), pl.program_id(1)
    tokens = hot_ref.shape[0]
    for block in range(NB):

        @pl.when((b == block) & (y == 0))
        def _():
            at = at_refs[block][0]
            for tile in range(held * CAP // 128):
                lanes = lax.broadcasted_iota(jnp.int32, (tokens, 128), 1) + tile * 128
                mask = None
                for e in range(tile * 128 // CAP, (tile * 128 + 127) // CAP + 1):
                    hit = at[:, e : e + 1] == lanes
                    mask = hit if mask is None else mask | hit
                hot_ref[:, tile * 128 : (tile + 1) * 128] = as_bf16(mask)

    rows = (mine_ref[0, 0].astype(F32) + theirs_ref[0, 0].astype(F32)).astype(BF16)
    placed = matmul(hot_ref[...], rows).astype(BF16)
    for block in range(NB):
        for part in range(slices):

            @pl.when((b == block) & (y == part))
            def _():
                out_refs[block * slices + part][...] = placed


def place_rows(where, at, mine, theirs):
    _, slices, count, width = mine.shape
    _, tokens, held = at.shape

    def block_spec(b):
        return pl.BlockSpec((1, tokens, held), lambda i, y, where: (where[b], 0, 0))

    rows_spec = pl.BlockSpec((1, 1, count, width), lambda i, y, where: (i, y, 0, 0))
    out = pl.pallas_call(
        partial(place_kernel, slices, held),
        grid_spec=pltpu.PrefetchScalarGridSpec(
            num_scalar_prefetch=1,
            grid=(NB, slices),
            in_specs=[block_spec(b) for b in range(NB)] + [rows_spec, rows_spec],
            out_specs=[pl.BlockSpec((tokens, width), lambda i, y, where: (0, 0))] * (NB * slices),
            scratch_shapes=[pltpu.VMEM((tokens, count), BF16)],
        ),
        out_shape=[jax.ShapeDtypeStruct((tokens, width), BF16)] * (NB * slices),
        compiler_params=pltpu.CompilerParams(vmem_limit_bytes=VMEM),
        cost_estimate=pl.CostEstimate(
            flops=2 * NB * slices * count * tokens * width,
            bytes_accessed=2 * NB * slices * (2 * count + tokens) * width,
            transcendentals=0,
        ),
        name="place_rows",
    )(where, *([at] * NB), mine, theirs)
    return [out[b * slices : (b + 1) * slices] for b in range(NB)]


def weight_kernel(slots, slices, where_ref, *refs):
    rows, cots, scaled, gate_grads, up_grads = (
        refs[: 2 * slots],
        refs[2 * slots : 4 * slots],
        refs[4 * slots : 5 * slots],
        refs[5 * slots : 6 * slots],
        refs[6 * slots : 7 * slots],
    )
    gate_ref, up_ref, down_ref = refs[7 * slots :]
    width = rows[0].shape[3]
    for j in range(2 * slices):
        columns = pl.ds(pl.multiple_of(where_ref[NB + j] * width, width), width)
        side = j // slices
        gate = up = down = None
        for k in range(slots):
            x = rows[2 * k + side][:, j % slices].reshape(NB * CAP, width)
            c = cots[2 * k + side][:, j % slices].reshape(NB * CAP, width)
            terms = (
                matmul_tn(x, gate_grads[k][0]),
                matmul_tn(x, up_grads[k][0]),
                matmul_tn(scaled[k][0], c),
            )
            if gate is None:
                gate, up, down = terms
            else:
                gate, up, down = gate + terms[0], up + terms[1], down + terms[2]
        gate_ref[0, columns, :] = gate
        up_ref[0, columns, :] = up
        down_ref[0, :, columns] = down


def weight_grads(where, rows, cots, scaled, gate_grads, up_grads, depth):
    slots = len(rows)
    held, _, ff = scaled[0].shape
    slices, width = rows[0][0].shape[1], rows[0][0].shape[3]
    rows_spec = pl.BlockSpec((NB, slices, CAP, width), lambda e, where: (0, 0, e, 0))
    hidden_spec = pl.BlockSpec((1, NB * CAP, ff), lambda e, where: (e, 0, 0))
    in_spec = pl.BlockSpec((1, depth, ff), lambda e, where: (e, 0, 0))
    return pl.pallas_call(
        partial(weight_kernel, slots, slices),
        grid_spec=pltpu.PrefetchScalarGridSpec(
            num_scalar_prefetch=1,
            grid=(held,),
            in_specs=[rows_spec] * (4 * slots) + [hidden_spec] * (3 * slots),
            out_specs=[in_spec, in_spec, pl.BlockSpec((1, ff, depth), lambda e, where: (e, 0, 0))],
        ),
        out_shape=[jax.ShapeDtypeStruct((held, depth, ff), F32)] * 2
        + [jax.ShapeDtypeStruct((held, ff, depth), F32)],
        compiler_params=pltpu.CompilerParams(vmem_limit_bytes=VMEM),
        cost_estimate=pl.CostEstimate(
            flops=6 * slots * NB * held * CAP * depth * ff,
            bytes_accessed=12 * held * depth * ff + 4 * slots * NB * held * CAP * depth,
            transcendentals=0,
        ),
        name="weight_grads",
    )(
        where,
        *[a for pair in rows for a in pair],
        *[a for pair in cots for a in pair],
        *scaled,
        *gate_grads,
        *up_grads,
    )


def inside_pieces(start, length, positions):
    return (positions[None, :] >= start[:, None]) & (positions[None, :] < (start + length)[:, None])


def allowed_block(start, length, first, rows):
    query_pos = first + jnp.arange(rows, dtype=jnp.int32)
    key_pos = jnp.arange(LENGTH, dtype=jnp.int32)
    query_in = inside_pieces(start, length, query_pos)
    key_in = inside_pieces(start, length, key_pos)
    return (key_pos[None, :] <= query_pos[:, None]) | jnp.any(
        query_in[:, :, None] & key_in[:, None, :], axis=0
    )


def head_stats(raw, heads):
    parts = raw.reshape(raw.shape[0], heads, HD)
    inverse = lax.rsqrt(jnp.mean(parts * parts, axis=-1, keepdims=True) + 1e-06)
    return (parts * inverse, inverse)


def head_backward(grad_heads, hat, inverse, gain):
    upstream = grad_heads * gain.reshape(hat.shape[1], HD)
    raw = inverse * (upstream - hat * jnp.mean(upstream * hat, axis=-1, keepdims=True))
    return (
        raw.reshape(hat.shape[0], -1).astype(jnp.bfloat16),
        jnp.sum(grad_heads * hat, axis=0).reshape(-1),
    )


def attend_forward(args, block, scale):
    queries, keys, values, start, length = args

    def one_block(index):
        first = index * block
        rows = lax.dynamic_slice_in_dim(queries, first, block, 0)
        scores = jnp.einsum("qhd,khd->hqk", rows, keys, preferred_element_type=jnp.float32) * scale
        masked = jnp.where(allowed_block(start, length, first, block)[None], scores, -1e30)
        top = jnp.max(masked, axis=-1, keepdims=True)
        weights = jnp.exp(masked - top)
        total = jnp.sum(weights, axis=-1, keepdims=True)
        probs = (weights / total).astype(jnp.bfloat16)
        result = jnp.einsum("hqk,khd->qhd", probs, values, preferred_element_type=jnp.float32)
        return (result, (top + jnp.log(total))[..., 0], jnp.max(masked, axis=(1, 2)))

    results, log_sums, tops = lax.map(one_block, jnp.arange(LENGTH // block, dtype=jnp.int32))
    return (results.reshape(LENGTH, queries.shape[1], HD), log_sums, jnp.max(tops, axis=0))


def attend_backward(args, block, scale):
    queries, keys, values, grads_o, log_sums, start, length = args

    def one_block(carry, index):
        key_acc, value_acc = carry
        first = index * block
        rows = lax.dynamic_slice_in_dim(queries, first, block, 0)
        grad_rows = lax.dynamic_slice_in_dim(grads_o, first, block, 0)
        scores = jnp.einsum("qhd,khd->hqk", rows, keys, preferred_element_type=jnp.float32) * scale
        masked = jnp.where(allowed_block(start, length, first, block)[None], scores, -1e30)
        probs = jnp.exp(masked - log_sums[index][:, :, None])
        grad_p = jnp.einsum("qhd,khd->hqk", grad_rows, values, preferred_element_type=jnp.float32)
        delta = jnp.sum(probs * grad_p, axis=-1, keepdims=True)
        grad_s = (probs * (grad_p - delta)).astype(jnp.bfloat16)
        query_part = (
            jnp.einsum("hqk,khd->qhd", grad_s, keys, preferred_element_type=jnp.float32) * scale
        )
        key_acc = (
            key_acc
            + jnp.einsum("hqk,qhd->khd", grad_s, rows, preferred_element_type=jnp.float32) * scale
        )
        value_acc = value_acc + jnp.einsum(
            "hqk,qhd->khd",
            probs.astype(jnp.bfloat16),
            grad_rows,
            preferred_element_type=jnp.float32,
        )
        return ((key_acc, value_acc), query_part)

    zeros = jnp.zeros(keys.shape, jnp.float32)
    (key_grad, value_grad), query_parts = lax.scan(
        one_block, (zeros, zeros), jnp.arange(LENGTH // block, dtype=jnp.int32)
    )
    return (query_parts.reshape(keys.shape), key_grad, value_grad)


def per_device(
    inputs,
    attn_gain,
    w_query,
    w_key,
    w_value,
    w_output,
    query_gain,
    key_gain,
    moe_gain,
    w_router,
    w_gate,
    w_up,
    w_down,
    routes,
    piece_start,
    piece_length,
    clip_threshold,
    cotangent,
):
    tokens_here, width = inputs.shape
    slice_width = cotangent.shape[1]
    part = lax.axis_index("tensor")
    owner = lax.axis_index("expert")
    column = part * slice_width
    heads_here = query_gain.shape[0] // HD
    experts_here = w_gate.shape[0]
    owners = lax.axis_size("expert")
    sequences = tokens_here // LENGTH
    block = min(512, LENGTH)
    scale = 1.0 / math.sqrt(HD)

    cot_own = cotangent.astype(BF16)
    cot_slots = gather_slots(cot_own)
    cot_pieces = tensor_gather(cot_own, cot_slots[0][0][1])
    output_pieces = jnp.concatenate(tensor_gather(w_output), axis=0)

    all_routes = lax.all_gather(routes, "expert")
    held_ids = owner * experts_here + jnp.arange(experts_here, dtype=jnp.int32)
    chosen = jnp.any(all_routes[:, None, :, :] == held_ids[None, :, None, None], axis=3)
    places = jnp.arange(tokens_here, dtype=jnp.int32)
    before = (places[:, None] < places[None, :]).astype(BF16)
    earlier = jnp.einsum(
        "set,tu->seu", chosen.astype(BF16), before, preferred_element_type=F32
    ).astype(jnp.int32)
    pos = jnp.where(chosen, earlier, -1)
    at = jnp.where(
        chosen, earlier + jnp.arange(experts_here, dtype=jnp.int32)[None, :, None] * CAP, -1
    ).transpose(0, 2, 1)
    where = slot_blocks()

    inputs_f = inputs.astype(F32)
    attn_inv = lax.rsqrt(jnp.mean(inputs_f * inputs_f, axis=-1, keepdims=True) + 1e-05)
    attn_hat = inputs_f * attn_inv
    normed_a = (attn_hat * attn_gain).astype(BF16)
    query_hat, query_inv = head_stats(matmul(normed_a, w_query), heads_here)
    key_hat, key_inv = head_stats(matmul(normed_a, w_key), heads_here)
    values = matmul(normed_a, w_value).astype(BF16)
    queries = (query_hat * query_gain.reshape(heads_here, HD)).astype(BF16)
    keys = (key_hat * key_gain.reshape(heads_here, HD)).astype(BF16)
    shape4 = (sequences, LENGTH, heads_here, HD)
    seq_query = queries.reshape(shape4)
    seq_key = keys.reshape(shape4)
    seq_value = values.reshape(shape4)
    results, log_sums, tops = lax.map(
        partial(attend_forward, block=block, scale=scale),
        (seq_query, seq_key, seq_value, piece_start, piece_length),
    )
    attended = results.reshape(tokens_here, heads_here * HD).astype(BF16)
    head_top = lax.pmax(jnp.max(tops, axis=0), "expert")
    attended_pieces = jnp.concatenate(tensor_gather(attended), axis=1)
    residual = inputs_f + matmul(attended_pieces, output_pieces)
    moe_inv = lax.rsqrt(jnp.mean(residual * residual, axis=-1, keepdims=True) + 1e-05)
    moe_hat = residual * moe_inv
    normed_m = (moe_hat * moe_gain).astype(BF16)

    normed_slots = gather_slots(lax.dynamic_slice_in_dim(normed_m, column, slice_width, 1))
    router = jax.nn.softmax(
        lax.dot_general(w_router, normed_m, (((0,), (1,)), ((), ())), preferred_element_type=F32),
        axis=0,
    )
    gate = lax.all_to_all(
        router.reshape(owners, experts_here, tokens_here),
        "expert",
        split_axis=0,
        concat_axis=0,
        tiled=True,
    )

    slots = len(where)
    slices = len(cot_slots[0][0])
    cots, rows, scaled, gate_grads, up_grads, probs, back = [], [], [], [], [], [], []
    for k in range(slots):
        mine = pick_rows(where[k], pos, cot_slots[k])
        cots.append((mine, core_swap(mine)))
    for k in range(slots):
        mine = pick_rows(where[k], pos, normed_slots[k])
        rows.append((mine, core_swap(mine)))
        kept, gate_grad, up_grad, prob, keep, give = expert_slot(
            where[k], pos, gate, rows[k], cots[k], w_gate, w_up, w_down
        )
        scaled.append(kept)
        gate_grads.append(gate_grad)
        up_grads.append(up_grad)
        probs.append(prob)
        back.append(place_rows(where[k], at, keep, core_swap(give)))
    expert_path = scatter_slots(back)

    prob_grads = jnp.stack([probs[k][:, b] for k in range(slots) for b in range(NB)])
    if is_cube():
        prob_grads = prob_grads[jnp.arange(owners, dtype=jnp.int32) ^ owner]
    prob_grads = lax.all_to_all(prob_grads, "expert", split_axis=0, concat_axis=0, tiled=True)
    prob_grads = lax.psum(prob_grads, "tensor").reshape(E, tokens_here)
    grad_logits = (
        router * (prob_grads - jnp.sum(router * prob_grads, axis=0, keepdims=True))
    ).astype(BF16)
    grad_router = lax.dot_general(
        normed_m, grad_logits, (((0,), (1,)), ((), ())), preferred_element_type=F32
    )
    router_slice = lax.dynamic_slice_in_dim(w_router, column, slice_width, 0)
    grad_normed = expert_path + lax.dot_general(
        grad_logits, router_slice, (((0,), (1,)), ((), ())), preferred_element_type=F32
    )
    moe_hat_slice = lax.dynamic_slice_in_dim(moe_hat, column, slice_width, 1)
    gain_slice = lax.dynamic_slice_in_dim(moe_gain, column, slice_width, 0)
    grad_moe_gain = jnp.sum(grad_normed * moe_hat_slice, axis=0)

    order = tensor_order()
    normed_pieces = tensor_gather(grad_normed.astype(BF16))
    hats = [lax.dynamic_slice_in_dim(moe_hat, o * slice_width, slice_width, 1) for o in order]
    gains = [lax.dynamic_slice_in_dim(moe_gain, o * slice_width, slice_width, 0) for o in order]
    ups = [p.astype(F32) * g for p, g in zip(normed_pieces, gains)]
    mean_dot = (
        sum(jnp.sum(u * h, axis=-1, keepdims=True) for u, h in zip(ups, hats)) / width
    )
    grad_residual = cotangent + moe_inv * (grad_normed * gain_slice - moe_hat_slice * mean_dot)
    grad_branch = jnp.zeros((tokens_here, width), BF16)
    for o, c, u, h in zip(order, cot_pieces, ups, hats):
        piece = (c.astype(F32) + moe_inv * (u - h * mean_dot)).astype(BF16)
        grad_branch = lax.dynamic_update_slice_in_dim(grad_branch, piece, o * slice_width, 1)

    placed = []
    for k in range(slots):
        keep, give = down_slot(where[k], scaled[k], w_down, slices)
        placed.append(place_rows(where[k], at, keep, core_swap(give)))
    mixture = scatter_slots(placed)
    out = lax.dynamic_slice_in_dim(residual, column, slice_width, 1) + mixture
    grad_gate, grad_up, grad_down = weight_grads(
        where[0], rows, cots, scaled, gate_grads, up_grads, width
    )

    grad_output = matmul_tn(attended, grad_branch)
    grad_attended = matmul_nt(grad_branch, w_output).astype(BF16)
    grad_q, grad_k, grad_v = lax.map(
        partial(attend_backward, block=block, scale=scale),
        (
            seq_query,
            seq_key,
            seq_value,
            grad_attended.reshape(shape4),
            log_sums,
            piece_start,
            piece_length,
        ),
    )
    heads_shape = (tokens_here, heads_here, HD)
    grad_query_raw, grad_query_gain = head_backward(
        grad_q.reshape(heads_shape), query_hat, query_inv, query_gain
    )
    grad_key_raw, grad_key_gain = head_backward(
        grad_k.reshape(heads_shape), key_hat, key_inv, key_gain
    )
    grad_value_raw = grad_v.reshape(tokens_here, heads_here * HD).astype(BF16)
    grad_query = matmul_tn(normed_a, grad_query_raw)
    grad_key = matmul_tn(normed_a, grad_key_raw)
    grad_value = matmul_tn(normed_a, grad_value_raw)
    grad_normed_a = matmul_nt(grad_query_raw, w_query)
    grad_normed_a = grad_normed_a + matmul_nt(grad_key_raw, w_key)
    grad_normed_a = grad_normed_a + matmul_nt(grad_value_raw, w_value)
    grad_normed_a = lax.psum(grad_normed_a.astype(BF16), "tensor").astype(F32)
    upstream = grad_normed_a * attn_gain
    grad_attn_gain = jnp.sum(grad_normed_a * attn_hat, axis=0)
    grad_input_full = attn_inv * (
        upstream - attn_hat * jnp.mean(upstream * attn_hat, axis=-1, keepdims=True)
    )
    grad_input = grad_residual + lax.dynamic_slice_in_dim(grad_input_full, column, slice_width, 1)
    totals = [
        lax.psum(g.astype(BF16), "expert").astype(F32)
        for g in (
            grad_query,
            grad_key,
            grad_value,
            grad_output,
            grad_query_gain,
            grad_key_gain,
            grad_attn_gain,
            grad_moe_gain,
            grad_router,
        )
    ]
    factor = clip_threshold / jnp.maximum(head_top, clip_threshold)
    spread = jnp.repeat(jnp.sqrt(factor), HD)
    query_clipped = (w_query.astype(F32) * spread[None, :]).astype(BF16)
    key_clipped = (w_key.astype(F32) * spread[None, :]).astype(BF16)
    return (
        out,
        grad_input,
        totals[6],
        totals[0],
        totals[1],
        totals[2],
        totals[3],
        totals[4],
        totals[5],
        totals[7],
        totals[8],
        grad_gate,
        grad_up,
        grad_down,
        head_top,
        query_clipped,
        key_clipped,
    )


def solution(mesh):
    return jax.shard_map(
        per_device,
        mesh=mesh,
        in_specs=(
            P("expert", None),
            P(),
            P(None, "tensor"),
            P(None, "tensor"),
            P(None, "tensor"),
            P("tensor", None),
            P("tensor"),
            P("tensor"),
            P(),
            P(),
            P("expert", None, "tensor"),
            P("expert", None, "tensor"),
            P("expert", "tensor", None),
            P("expert", None),
            P("expert", None),
            P("expert", None),
            P("tensor"),
            P("expert", "tensor"),
        ),
        out_specs=(
            P("expert", "tensor"),
            P("expert", "tensor"),
            P(),
            P(None, "tensor"),
            P(None, "tensor"),
            P(None, "tensor"),
            P("tensor", None),
            P("tensor"),
            P("tensor"),
            P("tensor"),
            P(),
            P("expert", None, "tensor"),
            P("expert", None, "tensor"),
            P("expert", "tensor", None),
            P("tensor"),
            P(None, "tensor"),
            P(None, "tensor"),
        ),
        check_vma=False,
    )
```

```python
from functools import partial
import math

import jax
import jax.numpy as jnp
from jax import lax
from jax.experimental import pallas as pl
from jax.experimental.pallas import tpu as pltpu
from jax.sharding import PartitionSpec as P

HD = 128
E = 64
TOP = 8
LENGTH = 1024
CAP = 160
NB = 2
BOTH = ("expert", "tensor")
F32 = jnp.float32
BF16 = jnp.bfloat16
VMEM = 60 * 1024 * 1024
DUE = {
    ("attended", 0): "cx0 cy0 cz1",
    ("branch", 0): "cz2 cx1",
    ("normed", 0): "cy1",
    ("cot", 1): "cx2 cz3 nx0 ny0 nz1",
    ("row", 0): "cy2 nz2",
    ("expert", 0): "nx1 ny1 cd2",
    ("row", 1): "nx2",
    ("place", 0): "cx3 nz3",
    ("expert", 1): "ny2",
    ("row", 2): "e00 nx3 cy3",
    ("place", 1): "e10",
    ("expert", 2): "ny3",
    ("row", 3): "e01",
    ("place", 2): "e11",
    ("expert", 3): "e02",
    ("place", 3): "e12",
}


def matmul(left, right):
    return jnp.dot(left, right, preferred_element_type=F32)


def matmul_nt(left, right):
    return lax.dot_general(left, right, (((1,), (1,)), ((), ())), preferred_element_type=F32)


def matmul_tn(left, right):
    return lax.dot_general(left, right, (((0,), (0,)), ((), ())), preferred_element_type=F32)


def after(value, *others):
    return lax.optimization_barrier((value, *others))[0]


def flip(dz, dx, dy, dc):
    pairs = []
    for z in range(4):
        for x in range(2):
            for y in range(2):
                for c in range(2):
                    pairs.append(
                        (
                            ((z * 2 + x) * 2 + y) * 2 + c,
                            (((z ^ dz) * 2 + (x ^ dx)) * 2 + (y ^ dy)) * 2 + (c ^ dc),
                        )
                    )
    return pairs


def send(value, dz=0, dx=0, dy=0, dc=0):
    return lax.ppermute(value, BOTH, flip(dz, dx, dy, dc))


def is_cube():
    return lax.axis_size("expert") == 8 and lax.axis_size("tensor") == 4


def core_swap(value):
    if is_cube():
        return send(value, dc=1)
    count = lax.axis_size("tensor")
    return lax.ppermute(value, "tensor", [(i, i ^ 1) for i in range(count)])


def slot_blocks():
    owner, part = lax.axis_index("expert"), lax.axis_index("tensor")
    core = part % 2
    if is_cube():
        blocks = [[owner ^ (k * 2 + b) for b in range(NB)] for k in range(4)]
        mine = [part ^ (y * 2) for y in range(2)]
    else:
        blocks = [[k * NB + b for b in range(NB)] for k in range(lax.axis_size("expert") // NB)]
        mine = [y * 2 + core for y in range(lax.axis_size("tensor") // 2)]
    theirs = [m ^ 1 for m in mine]
    return [jnp.stack([jnp.asarray(v, jnp.int32) for v in b + mine + theirs]) for b in blocks]


def same_core():
    count = lax.axis_size("tensor")
    return [[y * 2 + c for y in range(count // 2)] for c in range(2)]


def gather_slots(own):
    if not is_cube():
        blocks = lax.all_gather(own, "expert")
        full = lax.all_gather(blocks, "tensor", axis_index_groups=same_core())
        return [
            [[full[y, k * NB + b] for y in range(full.shape[0])] for b in range(NB)]
            for k in range(full.shape[1] // NB)
        ]
    slots = []
    for k in range(4):
        block = send(own, dz=k) if k else own
        over_x = send(block, dx=1)
        over_y = send(block, dy=1)
        far = send(over_x, dy=1) if k % 2 else send(over_y, dx=1)
        slots.append([[block, over_y], [over_x, far]])
    return slots


def added(*terms):
    return sum(t.astype(F32) for t in terms)


def scatter_plane(parts, odd):
    near, over_y, over_x, far = parts[0][0], parts[0][1], parts[1][0], parts[1][1]
    if odd:
        far = send(far, dy=1)
        from_y = send(over_y, dy=1)
        from_x = send(added(over_x, far).astype(BF16), dx=1)
        return added(near, from_x, from_y), (far, from_y), (from_x,)
    far = send(far, dx=1)
    from_x = send(over_x, dx=1)
    from_y = send(added(over_y, far).astype(BF16), dy=1)
    return added(near, from_x, from_y), (far, from_x), (from_y,)


def scatter_all(slots):
    full = jnp.stack(
        [jnp.stack([s[b][y] for s in slots for b in range(NB)]) for y in range(len(slots[0][0]))]
    )
    mine = lax.psum_scatter(full, "tensor", axis_index_groups=same_core(), scatter_dimension=0)
    return lax.psum_scatter(mine, "expert", scatter_dimension=0).astype(F32)


def scatter_pairs(pairs):
    if not is_cube():
        return scatter_all(
            [[[a[i] for a in b] for b in pair] for pair in pairs for i in range(pair[0][0].shape[0])]
        )
    low, high = (scatter_plane(p, k)[0] for k, p in enumerate(pairs))
    total = low + send(high.astype(BF16), dz=2).astype(F32)
    return total[0] + send(total[1].astype(BF16), dz=1).astype(F32)


def tensor_order():
    part = lax.axis_index("tensor")
    if is_cube():
        return [part ^ i for i in (0, 2, 1, 3)]
    return [jnp.int32(i) for i in range(lax.axis_size("tensor"))]


def tensor_gather(own):
    if not is_cube():
        full = lax.all_gather(own, "tensor")
        return [full[i] for i in range(full.shape[0])]
    over_y = send(own, dy=1)
    return [own, over_y, core_swap(own), core_swap(over_y)]


def tensor_scatter(product, pieces):
    if not is_cube():
        full = jnp.concatenate([product(p).astype(BF16) for p in pieces], axis=1)
        return lax.psum_scatter(full, "tensor", scatter_dimension=1, tiled=True).astype(F32)
    away_y = product(pieces[3]).astype(BF16)
    away = product(pieces[2]).astype(BF16)
    from_y, near = core_swap(away_y), core_swap(away)
    over_y = send(added(product(pieces[1]), from_y).astype(BF16), dy=1)
    return added(product(pieces[0]), near, over_y)


def tensor_sum(value):
    if not is_cube():
        return lax.psum(value, "tensor")
    value = value + core_swap(value)
    return value + send(value, dy=1)


def one_hot(pos_row):
    rows = lax.broadcasted_iota(jnp.int32, (CAP, pos_row.shape[1]), 0)
    return rows == pos_row


def as_bf16(mask):
    return jnp.where(mask, 1.0, 0.0).astype(BF16)


def pick_kernel(group, slices, where_ref, *refs):
    pos_refs, x_refs = refs[:NB], refs[NB : NB + NB * slices]
    out_ref, hot_ref = refs[-2:]
    step = pl.program_id(0)
    for b in range(NB):
        for i in range(group):
            hot_ref[b, i * CAP : (i + 1) * CAP, :] = as_bf16(
                one_hot(pos_refs[b][0, pl.ds(step * group + i, 1), :])
            )
        for y in range(slices):
            out_ref[b, y] = matmul(hot_ref[b], x_refs[b * slices + y][...]).astype(BF16)


def pick_rows(where, pos, blocks):
    slices = len(blocks[0])
    tokens, width = blocks[0][0].shape
    held = pos.shape[1]
    group = 2
    flat = [a for b in blocks for a in b]

    def block_spec(b):
        return pl.BlockSpec((1, held, tokens), lambda i, where: (where[b], 0, 0))

    return pl.pallas_call(
        partial(pick_kernel, group, slices),
        grid_spec=pltpu.PrefetchScalarGridSpec(
            num_scalar_prefetch=1,
            grid=(held // group,),
            in_specs=[block_spec(b) for b in range(NB)]
            + [pl.BlockSpec((tokens, width), lambda i, where: (0, 0)) for _ in flat],
            out_specs=pl.BlockSpec(
                (NB, slices, group * CAP, width), lambda i, where: (0, 0, i, 0)
            ),
            scratch_shapes=[pltpu.VMEM((NB, group * CAP, tokens), BF16)],
        ),
        out_shape=jax.ShapeDtypeStruct((NB, slices, held * CAP, width), BF16),
        compiler_params=pltpu.CompilerParams(vmem_limit_bytes=VMEM),
        cost_estimate=pl.CostEstimate(
            flops=2 * NB * slices * held * CAP * tokens * width,
            bytes_accessed=2 * NB * slices * (held * CAP + tokens) * width,
            transcendentals=0,
        ),
        name="pick_rows",
    )(where, *([pos] * NB), *flat)


def expert_kernel(slices, where_ref, *refs):
    pos_refs, gate_refs = refs[:NB], refs[NB : 2 * NB]
    rows_mine, rows_theirs, cot_mine, cot_theirs, wg_ref, wu_ref, wd_ref = refs[2 * NB : 2 * NB + 7]
    scaled_ref, gate_grad_ref, up_grad_ref, prob_ref, keep_ref, give_ref = refs[2 * NB + 7 :]
    e = pl.program_id(0)
    width = rows_mine.shape[3]
    ff = wg_ref.shape[2]
    gate_pre = jnp.zeros((NB * CAP, ff), F32)
    up_pre = jnp.zeros((NB * CAP, ff), F32)
    grad_hidden = jnp.zeros((NB * CAP, ff), F32)

    def columns(j):
        return pl.ds(pl.multiple_of(where_ref[NB + j] * width, width), width)

    for j in range(2 * slices):
        x_ref, c_ref = (rows_mine, cot_mine) if j < slices else (rows_theirs, cot_theirs)
        x = x_ref[:, j % slices].reshape(NB * CAP, width)
        c = c_ref[:, j % slices].reshape(NB * CAP, width)
        gate_pre = gate_pre + matmul(x, wg_ref[0, columns(j), :])
        up_pre = up_pre + matmul(x, wu_ref[0, columns(j), :])
        grad_hidden = grad_hidden + matmul_nt(c, wd_ref[0, :, columns(j)])
    masks = [one_hot(pos_refs[b][0, pl.ds(e, 1), :]) for b in range(NB)]
    gates = jnp.concatenate(
        [
            jnp.sum(jnp.where(masks[b], gate_refs[b][0, pl.ds(e, 1), :], 0.0), axis=1, keepdims=True)
            for b in range(NB)
        ],
        axis=0,
    )
    sigma = jax.nn.sigmoid(gate_pre)
    swish = gate_pre * sigma
    hidden = (swish * up_pre).astype(BF16).astype(F32)
    prob = jnp.sum(hidden * grad_hidden, axis=1, keepdims=True)
    for b in range(NB):
        prob_ref[0, b : b + 1, :] = jnp.sum(
            jnp.where(masks[b], prob[b * CAP : (b + 1) * CAP], 0.0), axis=0, keepdims=True
        )
    grad_hidden = grad_hidden * gates
    scaled_ref[0] = (hidden * gates).astype(BF16)
    gate_grad = (grad_hidden * up_pre * (sigma * (1.0 + gate_pre * (1.0 - sigma)))).astype(BF16)
    up_grad = (grad_hidden * swish).astype(BF16)
    gate_grad_ref[0] = gate_grad
    up_grad_ref[0] = up_grad
    for j in range(2 * slices):
        to = keep_ref if j < slices else give_ref
        back = matmul_nt(gate_grad, wg_ref[0, columns(j), :]) + matmul_nt(
            up_grad, wu_ref[0, columns(j), :]
        )
        to[:, j % slices] = back.astype(BF16).reshape(NB, CAP, width)


def expert_slot(where, pos, gate, rows, cots, w_gate, w_up, w_down):
    held, depth, ff = w_gate.shape
    tokens = pos.shape[2]
    slices, width = rows[0].shape[1], rows[0].shape[3]

    def block_spec(b):
        return pl.BlockSpec((1, held, tokens), lambda e, where: (where[b], 0, 0))

    rows_spec = pl.BlockSpec((NB, slices, CAP, width), lambda e, where: (0, 0, e, 0))
    rows_shape = jax.ShapeDtypeStruct((NB, slices, held * CAP, width), BF16)
    in_spec = pl.BlockSpec((1, depth, ff), lambda e, where: (e, 0, 0))
    hidden_spec = pl.BlockSpec((1, NB * CAP, ff), lambda e, where: (e, 0, 0))
    hidden_shape = jax.ShapeDtypeStruct((held, NB * CAP, ff), BF16)
    return pl.pallas_call(
        partial(expert_kernel, slices),
        grid_spec=pltpu.PrefetchScalarGridSpec(
            num_scalar_prefetch=1,
            grid=(held,),
            in_specs=[block_spec(b) for b in range(NB)] * 2
            + [rows_spec] * 4
            + [in_spec, in_spec, pl.BlockSpec((1, ff, depth), lambda e, where: (e, 0, 0))],
            out_specs=[hidden_spec] * 3
            + [pl.BlockSpec((1, NB, tokens), lambda e, where: (e, 0, 0)), rows_spec, rows_spec],
        ),
        out_shape=[hidden_shape] * 3
        + [jax.ShapeDtypeStruct((held, NB, tokens), F32), rows_shape, rows_shape],
        compiler_params=pltpu.CompilerParams(vmem_limit_bytes=VMEM),
        cost_estimate=pl.CostEstimate(
            flops=10 * NB * held * CAP * depth * ff,
            bytes_accessed=6 * held * depth * ff + 6 * NB * held * CAP * depth,
            transcendentals=NB * held * CAP * ff,
        ),
        name="expert_slot",
    )(where, *([pos] * NB), *([gate] * NB), *rows, *cots, w_gate, w_up, w_down)


def down_kernel(slices, slots, where_ref, *refs):
    scaled_refs, wd_ref, keep_ref, give_ref = refs[:slots], refs[slots], refs[-2], refs[-1]
    width = keep_ref.shape[3]
    for j in range(2 * slices):
        to = keep_ref if j < slices else give_ref
        columns = pl.ds(pl.multiple_of(where_ref[NB + j] * width, width), width)
        for k in range(slots):
            rows = matmul(scaled_refs[k][0], wd_ref[0, :, columns])
            to[k * NB : (k + 1) * NB, j % slices] = rows.astype(BF16).reshape(NB, CAP, width)


def down_slots(where, scaled, w_down, slices):
    held, ff, depth = w_down.shape
    width = depth // (2 * slices)
    slots = len(scaled)
    rows_spec = pl.BlockSpec((slots * NB, slices, CAP, width), lambda e, where: (0, 0, e, 0))
    rows_shape = jax.ShapeDtypeStruct((slots * NB, slices, held * CAP, width), BF16)
    return pl.pallas_call(
        partial(down_kernel, slices, slots),
        grid_spec=pltpu.PrefetchScalarGridSpec(
            num_scalar_prefetch=1,
            grid=(held,),
            in_specs=[pl.BlockSpec((1, NB * CAP, ff), lambda e, where: (e, 0, 0))] * slots
            + [pl.BlockSpec((1, ff, depth), lambda e, where: (e, 0, 0))],
            out_specs=[rows_spec, rows_spec],
        ),
        out_shape=[rows_shape, rows_shape],
        compiler_params=pltpu.CompilerParams(vmem_limit_bytes=VMEM),
        cost_estimate=pl.CostEstimate(
            flops=2 * slots * NB * held * CAP * depth * ff,
            bytes_accessed=2 * held * depth * ff + 2 * slots * NB * held * CAP * depth,
            transcendentals=0,
        ),
        name="down_slots",
    )(where, *scaled, w_down)


def place_kernel(slices, held, slots, where_ref, *refs):
    count = NB * slots
    at_refs, mine_ref, theirs_ref = refs[:count], refs[count], refs[count + 1]
    out_refs, hot_ref = refs[count + 2 : -1], refs[-1]
    b, y = pl.program_id(0), pl.program_id(1)
    tokens = hot_ref.shape[0]
    for block in range(count):

        @pl.when((b == block) & (y == 0))
        def _():
            at = at_refs[block][0]
            for tile in range(held * CAP // 128):
                lanes = lax.broadcasted_iota(jnp.int32, (tokens, 128), 1) + tile * 128
                mask = None
                for e in range(tile * 128 // CAP, (tile * 128 + 127) // CAP + 1):
                    hit = at[:, e : e + 1] == lanes
                    mask = hit if mask is None else mask | hit
                hot_ref[:, tile * 128 : (tile + 1) * 128] = as_bf16(mask)

    rows = (mine_ref[0, 0].astype(F32) + theirs_ref[0, 0].astype(F32)).astype(BF16)
    placed = matmul(hot_ref[...], rows).astype(BF16)
    for block in range(count):
        for part in range(slices):

            @pl.when((b == block) & (y == part))
            def _():
                out_refs[block % NB * slices + part][block // NB] = placed


def place_rows(wheres, at, mine, theirs):
    _, slices, count, width = mine.shape
    _, tokens, held = at.shape
    slots = len(wheres)
    blocks = jnp.concatenate([w[:NB] for w in wheres])

    def block_spec(b):
        return pl.BlockSpec((1, tokens, held), lambda i, y, where: (where[b], 0, 0))

    rows_spec = pl.BlockSpec((1, 1, count, width), lambda i, y, where: (i, y, 0, 0))
    out = pl.pallas_call(
        partial(place_kernel, slices, held, slots),
        grid_spec=pltpu.PrefetchScalarGridSpec(
            num_scalar_prefetch=1,
            grid=(NB * slots, slices),
            in_specs=[block_spec(b) for b in range(NB * slots)] + [rows_spec, rows_spec],
            out_specs=[pl.BlockSpec((slots, tokens, width), lambda i, y, where: (0, 0, 0))]
            * (NB * slices),
            scratch_shapes=[pltpu.VMEM((tokens, count), BF16)],
        ),
        out_shape=[jax.ShapeDtypeStruct((slots, tokens, width), BF16)] * (NB * slices),
        compiler_params=pltpu.CompilerParams(vmem_limit_bytes=VMEM),
        cost_estimate=pl.CostEstimate(
            flops=2 * NB * slots * slices * count * tokens * width,
            bytes_accessed=2 * NB * slots * slices * (2 * count + tokens) * width,
            transcendentals=0,
        ),
        name="place_rows",
    )(blocks, *([at] * (NB * slots)), mine, theirs)
    return [out[b * slices : (b + 1) * slices] for b in range(NB)]


def weight_kernel(slots, slices, where_ref, *refs):
    rows, gate_grads, up_grads = refs[: 2 * slots], refs[2 * slots : 3 * slots], refs[3 * slots : 4 * slots]
    gate_ref, up_ref = refs[4 * slots :]
    width = rows[0].shape[3]
    for j in range(2 * slices):
        columns = pl.ds(pl.multiple_of(where_ref[NB + j] * width, width), width)
        gate = up = None
        for k in range(slots):
            x = rows[2 * k + j // slices][:, j % slices].reshape(NB * CAP, width)
            terms = matmul_tn(x, gate_grads[k][0]), matmul_tn(x, up_grads[k][0])
            gate, up = terms if gate is None else (gate + terms[0], up + terms[1])
        gate_ref[0, columns, :] = gate
        up_ref[0, columns, :] = up


def weight_down_kernel(slots, slices, where_ref, *refs):
    cots, scaled, down_ref = refs[: 2 * slots], refs[2 * slots : 3 * slots], refs[3 * slots]
    width = cots[0].shape[3]
    for j in range(2 * slices):
        columns = pl.ds(pl.multiple_of(where_ref[NB + j] * width, width), width)
        down = None
        for k in range(slots):
            c = cots[2 * k + j // slices][:, j % slices].reshape(NB * CAP, width)
            term = matmul_tn(scaled[k][0], c)
            down = term if down is None else down + term
        down_ref[0, :, columns] = down


def weight_grads(kernel, where, rows, hiddens, outs, name):
    slots = len(rows)
    held, _, ff = hiddens[0].shape
    slices, width = rows[0][0].shape[1], rows[0][0].shape[3]
    depth = 2 * slices * width
    rows_spec = pl.BlockSpec((NB, slices, CAP, width), lambda e, where: (0, 0, e, 0))
    hidden_spec = pl.BlockSpec((1, NB * CAP, ff), lambda e, where: (e, 0, 0))
    return pl.pallas_call(
        partial(kernel, slots, slices),
        grid_spec=pltpu.PrefetchScalarGridSpec(
            num_scalar_prefetch=1,
            grid=(held,),
            in_specs=[rows_spec] * (2 * slots) + [hidden_spec] * len(hiddens),
            out_specs=[pl.BlockSpec((1, *o), lambda e, where: (e, 0, 0)) for o in outs],
        ),
        out_shape=[jax.ShapeDtypeStruct((held, *o), F32) for o in outs],
        compiler_params=pltpu.CompilerParams(vmem_limit_bytes=VMEM),
        cost_estimate=pl.CostEstimate(
            flops=2 * len(outs) * slots * NB * held * CAP * depth * ff,
            bytes_accessed=4 * len(outs) * held * depth * ff + 2 * slots * NB * held * CAP * depth,
            transcendentals=0,
        ),
        name=name,
    )(where, *[a for pair in rows for a in pair], *hiddens)


def project_kernel(x_ref, wq_ref, wk_ref, wv_ref, qg_ref, kg_ref, qr_ref, kr_ref, q_ref, k_ref, v_ref):
    x = x_ref[...]
    for w_ref, gain_ref, raw_ref, to_ref in ((wq_ref, qg_ref, qr_ref, q_ref), (wk_ref, kg_ref, kr_ref, k_ref)):
        raw = matmul(x, w_ref[...])
        raw_ref[...] = raw
        for h in range(raw.shape[1] // HD):
            part = raw[:, h * HD : (h + 1) * HD]
            inverse = lax.rsqrt(jnp.mean(part * part, axis=1, keepdims=True) + 1e-06)
            gain = gain_ref[:, h * HD : (h + 1) * HD]
            to_ref[:, h * HD : (h + 1) * HD] = (part * inverse * gain).astype(BF16)
    v_ref[...] = matmul(x, wv_ref[...]).astype(BF16)


def project(x, w_query, w_key, w_value, query_gain, key_gain):
    tokens, depth = x.shape
    columns = w_query.shape[1]
    step = min(256, columns)
    weight = pl.BlockSpec((depth, step), lambda i: (0, i))
    gain = pl.BlockSpec((1, step), lambda i: (0, i))
    out = pl.BlockSpec((tokens, step), lambda i: (0, i))
    return pl.pallas_call(
        project_kernel,
        grid=(columns // step,),
        in_specs=[pl.BlockSpec((tokens, depth), lambda i: (0, 0)), weight, weight, weight, gain, gain],
        out_specs=[out] * 5,
        out_shape=[jax.ShapeDtypeStruct((tokens, columns), t) for t in (F32, F32, BF16, BF16, BF16)],
        compiler_params=pltpu.CompilerParams(vmem_limit_bytes=VMEM),
        cost_estimate=pl.CostEstimate(
            flops=6 * tokens * depth * columns,
            bytes_accessed=2 * tokens * depth + 6 * depth * columns + 14 * tokens * columns,
            transcendentals=0,
        ),
        name="project",
    )(x, w_query, w_key, w_value, query_gain.reshape(1, -1), key_gain.reshape(1, -1))


def allowed_pairs(pieces_ref, base, first, rows, keys):
    query = first + lax.broadcasted_iota(jnp.int32, (rows, 1), 0)
    key = lax.broadcasted_iota(jnp.int32, (1, keys), 1)

    def piece_of(at, other):
        found = jnp.full(at.shape, other, jnp.int32)
        for j in range(2):
            start, length = pieces_ref[base + j], pieces_ref[base + 2 + j]
            found = jnp.where((at >= start) & (at < start + length), j, found)
        return found

    return (key <= query) | (piece_of(query, -1) == piece_of(key, -2))


def query_blocks():
    half = LENGTH // 2
    return ((0, half, half), (half, half, LENGTH))


def attend_kernel(scale, pieces_ref, q_ref, k_ref, v_ref, o_ref, log_ref, top_ref):
    base = pl.program_id(0) * 4
    best = None
    for first, rows, keys in query_blocks():
        allowed = allowed_pairs(pieces_ref, base, first, rows, keys)
        scores = matmul_nt(q_ref[first : first + rows, :], k_ref[:keys, :]) * scale
        masked = jnp.where(allowed, scores, -1e30)
        top = jnp.max(masked, axis=1, keepdims=True)
        weights = jnp.exp(masked - top)
        total = jnp.sum(weights, axis=1, keepdims=True)
        probs = (weights * (1.0 / total)).astype(BF16)
        o_ref[first : first + rows, :] = matmul(probs, v_ref[:keys, :]).astype(BF16)
        log_ref[0, first : first + rows, :] = top + jnp.log(total)
        most = jnp.max(top, axis=0, keepdims=True)
        best = most if best is None else jnp.maximum(best, most)
    top_ref[0] = jnp.broadcast_to(best, (8, HD))


def attend(pieces, queries, keys, values, scale):
    tokens, columns = queries.shape
    sequences, heads = tokens // LENGTH, columns // HD
    block = pl.BlockSpec((LENGTH, HD), lambda s, h, pieces: (s, h))
    return pl.pallas_call(
        partial(attend_kernel, scale),
        grid_spec=pltpu.PrefetchScalarGridSpec(
            num_scalar_prefetch=1,
            grid=(sequences, heads),
            in_specs=[block] * 3,
            out_specs=[
                block,
                pl.BlockSpec((1, LENGTH, 1), lambda s, h, pieces: (h, s, 0)),
                pl.BlockSpec((1, 8, HD), lambda s, h, pieces: (s * heads + h, 0, 0)),
            ],
        ),
        out_shape=[
            jax.ShapeDtypeStruct((tokens, columns), BF16),
            jax.ShapeDtypeStruct((heads, tokens, 1), F32),
            jax.ShapeDtypeStruct((sequences * heads, 8, HD), F32),
        ],
        compiler_params=pltpu.CompilerParams(vmem_limit_bytes=VMEM),
        cost_estimate=pl.CostEstimate(
            flops=4 * tokens * LENGTH * columns,
            bytes_accessed=8 * tokens * columns,
            transcendentals=tokens * heads * LENGTH,
        ),
        name="attend",
    )(pieces, queries, keys, values)


def attend_back_kernel(
    scale, pieces_ref, q_ref, k_ref, v_ref, g_ref, log_ref, qr_ref, kr_ref, qg_ref, kg_ref,
    gq_ref, gk_ref, gv_ref, gqg_ref, gkg_ref, dq_ref, dk_ref, dv_ref,
):
    base = pl.program_id(0) * 4
    blocks = query_blocks()
    for first, rows, keys in blocks[::-1]:
        allowed = allowed_pairs(pieces_ref, base, first, rows, keys)
        q, g = q_ref[first : first + rows, :], g_ref[first : first + rows, :]
        k, v = k_ref[:keys, :], v_ref[:keys, :]
        scores = matmul_nt(q, k) * scale
        probs = jnp.exp(jnp.where(allowed, scores, -1e30) - log_ref[0, first : first + rows, :])
        grad_p = matmul_nt(g, v)
        delta = jnp.sum(probs * grad_p, axis=1, keepdims=True)
        grad_s = (probs * (grad_p - delta)).astype(BF16)
        dq_ref[first : first + rows, :] = matmul(grad_s, k) * scale
        dk = matmul_tn(grad_s, q) * scale
        dv = matmul_tn(probs.astype(BF16), g)
        if keys == LENGTH:
            dk_ref[...] = dk
            dv_ref[...] = dv
        else:
            dk_ref[:keys, :] += dk
            dv_ref[:keys, :] += dv
    gv_ref[...] = dv_ref[...].astype(BF16)
    for raw_ref, gain_ref, grad_ref, to_ref, sum_ref in (
        (qr_ref, qg_ref, dq_ref, gq_ref, gqg_ref),
        (kr_ref, kg_ref, dk_ref, gk_ref, gkg_ref),
    ):
        raw, grad = raw_ref[...], grad_ref[...]
        inverse = lax.rsqrt(jnp.mean(raw * raw, axis=1, keepdims=True) + 1e-06)
        hat = raw * inverse
        up = grad * gain_ref[...]
        mean = jnp.mean(up * hat, axis=1, keepdims=True)
        to_ref[...] = (inverse * (up - hat * mean)).astype(BF16)
        sum_ref[0] = jnp.sum(grad * hat, axis=0, keepdims=True)


def attend_back(pieces, queries, keys, values, grads, logs, query_raw, key_raw, query_gain, key_gain, scale):
    tokens, columns = queries.shape
    sequences, heads = tokens // LENGTH, columns // HD
    block = pl.BlockSpec((LENGTH, HD), lambda s, h, pieces: (s, h))
    gain = pl.BlockSpec((1, HD), lambda s, h, pieces: (0, h))
    sums = pl.BlockSpec((1, 1, HD), lambda s, h, pieces: (s, 0, h))
    return pl.pallas_call(
        partial(attend_back_kernel, scale),
        grid_spec=pltpu.PrefetchScalarGridSpec(
            num_scalar_prefetch=1,
            grid=(sequences, heads),
            in_specs=[block] * 4
            + [pl.BlockSpec((1, LENGTH, 1), lambda s, h, pieces: (h, s, 0)), block, block, gain, gain],
            out_specs=[block, block, block, sums, sums],
            scratch_shapes=[pltpu.VMEM((LENGTH, HD), F32)] * 3,
        ),
        out_shape=[jax.ShapeDtypeStruct((tokens, columns), BF16)] * 3
        + [jax.ShapeDtypeStruct((sequences, 1, columns), F32)] * 2,
        compiler_params=pltpu.CompilerParams(vmem_limit_bytes=VMEM),
        cost_estimate=pl.CostEstimate(
            flops=10 * tokens * LENGTH * columns,
            bytes_accessed=22 * tokens * columns,
            transcendentals=tokens * heads * LENGTH,
        ),
        name="attend_back",
    )(
        pieces, queries, keys, values, grads, logs, query_raw, key_raw,
        query_gain.reshape(1, -1), key_gain.reshape(1, -1),
    )


def expert_steps(slots):
    steps = [("cot", 0), ("cot", 1), ("row", 0)]
    for k in range(slots):
        steps.append(("expert", k))
        if k + 2 < slots:
            steps.append(("cot", k + 2))
        if k + 1 < slots:
            steps.append(("row", k + 1))
        steps.append(("place", k))
    return steps


def transfers_due(kind, k, cots, rows, terms):
    if not is_cube():
        return []
    at = {"z": (0, 0), "y": (0, 1), "x": (1, 0), "d": (1, 1)}
    due = DUE.get((kind, k), "").split()
    found = []
    for name in due:
        if name[0] == "e":
            found.extend(terms[int(name[2])][int(name[1])])
        else:
            b, y = at[name[1]]
            found.append((cots if name[0] == "c" else rows)[int(name[2])][b][y])
    return found


def per_device(
    inputs,
    attn_gain,
    w_query,
    w_key,
    w_value,
    w_output,
    query_gain,
    key_gain,
    moe_gain,
    w_router,
    w_gate,
    w_up,
    w_down,
    routes,
    piece_start,
    piece_length,
    clip_threshold,
    cotangent,
):
    tokens_here, width = inputs.shape
    slice_width = cotangent.shape[1]
    owner = lax.axis_index("expert")
    column = lax.axis_index("tensor") * slice_width
    heads_here = query_gain.shape[0] // HD
    experts_here = w_gate.shape[0]
    owners = lax.axis_size("expert")
    sequences = tokens_here // LENGTH
    scale = 1.0 / math.sqrt(HD)
    where = slot_blocks()
    slots = len(where)
    slices = lax.axis_size("tensor") // 2

    def own_columns(value):
        return lax.dynamic_slice_in_dim(value, column, slice_width, value.ndim - 1)

    all_routes = lax.all_to_all(
        jnp.broadcast_to(routes.T[None], (owners, TOP, tokens_here)),
        "expert",
        split_axis=0,
        concat_axis=0,
        tiled=True,
    )
    cot_slots = gather_slots(cotangent.astype(BF16))

    held_ids = owner * experts_here + jnp.arange(experts_here, dtype=jnp.int32)
    chosen = jnp.any(all_routes[:, None] == held_ids[None, :, None, None], axis=2)
    places = jnp.arange(tokens_here, dtype=jnp.int32)
    before = (places[:, None] < places[None, :]).astype(BF16)
    earlier = jnp.einsum(
        "set,tu->seu", chosen.astype(BF16), before, preferred_element_type=F32
    ).astype(jnp.int32)
    pos = jnp.where(chosen, earlier, -1)
    at = jnp.where(
        chosen, earlier + jnp.arange(experts_here, dtype=jnp.int32)[None, :, None] * CAP, -1
    ).transpose(0, 2, 1)

    order = tensor_order()
    output_pieces = [lax.dynamic_slice_in_dim(w_output, o * slice_width, slice_width, 1) for o in order]
    inputs_f = inputs.astype(F32)
    attn_inv = lax.rsqrt(jnp.mean(inputs_f * inputs_f, axis=-1, keepdims=True) + 1e-05)
    normed_a = (inputs_f * attn_inv * attn_gain).astype(BF16)
    query_raw, key_raw, queries, keys, values = project(
        normed_a, w_query, w_key, w_value, query_gain, key_gain
    )
    pieces = jnp.concatenate([piece_start, piece_length], axis=1).reshape(-1)
    attended, logs, tops = attend(pieces, queries, keys, values, scale)
    head_top = lax.pmax(
        jnp.max(tops[:, 0, 0].reshape(sequences, heads_here), axis=0), "expert"
    )
    attended = after(attended, *transfers_due("attended", 0, cot_slots, None, None))
    branch = tensor_scatter(partial(matmul, attended), output_pieces)
    first_cot = pick_rows(after(where[0], attended), pos, cot_slots[0])
    branch = after(branch, first_cot, *transfers_due("branch", 0, cot_slots, None, None))
    residual = own_columns(inputs).astype(F32) + branch
    gain_slice = own_columns(moe_gain)
    router_slice = lax.dynamic_slice_in_dim(w_router, column, slice_width, 0)
    lifted = residual * gain_slice
    row_sums = tensor_sum(
        jnp.concatenate(
            [
                lax.dot_general(
                    router_slice,
                    lifted.astype(BF16),
                    (((0,), (1,)), ((), ())),
                    preferred_element_type=F32,
                ),
                jnp.sum(residual * residual, axis=1)[None],
            ],
            axis=0,
        )
    )
    moe_inv_row = lax.rsqrt(row_sums[E] / width + 1e-05)
    moe_inv = moe_inv_row[:, None]
    normed_m = (lifted * moe_inv).astype(BF16)
    normed_m = after(normed_m, *transfers_due("normed", 0, cot_slots, None, None))

    normed_slots = gather_slots(normed_m)
    router = jax.nn.softmax(row_sums[:E] * moe_inv_row[None], axis=0)
    gate = lax.all_to_all(
        router.reshape(owners, experts_here, tokens_here),
        "expert",
        split_axis=0,
        concat_axis=0,
        tiled=True,
    )

    cots, rows, scaled, gate_grads, up_grads, probs, back = [], [], [], [], [], [], []
    terms = []
    last = first_cot
    for kind, k in expert_steps(slots):
        due = [last] + transfers_due(kind, k, cot_slots, normed_slots, terms)
        now = after(where[k], *due)
        if kind == "cot":
            last = pick_rows(now, pos, cot_slots[k]) if k else first_cot
            cots.append((last, core_swap(last)))
        elif kind == "row":
            last = pick_rows(now, pos, normed_slots[k])
            rows.append((last, core_swap(last)))
        elif kind == "expert":
            kept, gate_grad, up_grad, prob, keep, give = expert_slot(
                now, pos, gate, rows[k], cots[k], w_gate, w_up, w_down
            )
            last = kept
            scaled.append(kept)
            gate_grads.append(gate_grad)
            up_grads.append(up_grad)
            probs.append(prob)
            back.append((keep, core_swap(give)))
        else:
            placed = place_rows([now], at, *back[k])
            last = placed[0][0]
            back[k] = [[a[0] for a in b] for b in placed]
            if is_cube():
                term, first, second = scatter_plane(back[k], k % 2)
                if k:
                    term = send(term.astype(BF16), dz=k).astype(F32)
                terms.append((term, first, second))
    expert_path = sum(t[0] for t in terms) if is_cube() else scatter_all(back)

    prob_grads = jnp.stack([probs[k][:, b] for k in range(slots) for b in range(NB)])
    if is_cube():
        prob_grads = prob_grads[jnp.arange(owners, dtype=jnp.int32) ^ owner]
    prob_grads = lax.all_to_all(prob_grads, "expert", split_axis=0, concat_axis=0, tiled=True)
    prob_grads = tensor_sum(prob_grads.reshape(E, tokens_here))
    grad_logits = (
        router * (prob_grads - jnp.sum(router * prob_grads, axis=0, keepdims=True))
    ).astype(BF16)
    grad_router = lax.dot_general(
        normed_m, grad_logits, (((0,), (1,)), ((), ())), preferred_element_type=F32
    )
    router_path = lax.dot_general(
        grad_logits, router_slice, (((0,), (1,)), ((), ())), preferred_element_type=F32
    )
    grad_normed = expert_path + router_path
    moe_hat = residual * moe_inv
    grad_moe_gain = jnp.sum(grad_normed * moe_hat, axis=0)
    upstream = grad_normed * gain_slice
    mean_dot = tensor_sum(jnp.sum(upstream * moe_hat, axis=-1).reshape(8, -1)).reshape(-1, 1) / width
    grad_residual = cotangent + moe_inv * (upstream - moe_hat * mean_dot)
    branch_pieces = tensor_gather(grad_residual.astype(BF16))
    grad_branch = jnp.concatenate(branch_pieces, axis=1)

    pairs = []
    for k in range(0, slots, 2):
        now = after(where[0], last)
        keep, give = down_slots(now, scaled[k : k + 2], w_down, slices)
        last = keep
        pairs.append((keep, core_swap(give)))
    for i, pair in enumerate(pairs):
        now = after(where[2 * i], branch_pieces[0]) if i else after(where[0], last)
        placed = place_rows([now, where[2 * i + 1]], at, *pair)
        last = placed[0][0]
        if is_cube():
            placed = [[after(a, branch_pieces[1]) for a in b] for b in placed]
        pairs[i] = placed
    mixture = scatter_pairs(pairs)
    out = residual + mixture
    grad_output = matmul_tn(attended, grad_branch)
    grad_attended = matmul_nt(grad_branch, jnp.concatenate(output_pieces, axis=1)).astype(BF16)
    grad_query_raw, grad_key_raw, grad_v, grad_query_gain, grad_key_gain = attend_back(
        pieces, queries, keys, values, grad_attended, logs, query_raw, key_raw, query_gain, key_gain, scale
    )
    grad_query = matmul_tn(normed_a, grad_query_raw)
    grad_key = matmul_tn(normed_a, grad_key_raw)
    grad_value = matmul_tn(normed_a, grad_v)
    grad_gate, grad_up = weight_grads(
        weight_kernel, after(where[0], grad_value), rows, gate_grads + up_grads, [w_gate.shape[1:]] * 2, "weight_grads"
    )
    (grad_down,) = weight_grads(
        weight_down_kernel, after(where[0], grad_gate), cots, scaled, [w_down.shape[1:]], "weight_down_grads"
    )
    grad_raw = jnp.concatenate([grad_query_raw, grad_key_raw, grad_v], axis=1)
    weights = jnp.concatenate([w_query, w_key, w_value], axis=1)
    weight_pieces = [lax.dynamic_slice_in_dim(weights, o * slice_width, slice_width, 0) for o in order]
    grad_normed_a = tensor_scatter(partial(matmul_nt, grad_raw), weight_pieces)
    attn_hat = own_columns(inputs).astype(F32) * attn_inv
    upstream = grad_normed_a * own_columns(attn_gain)
    grad_attn_gain = jnp.sum(grad_normed_a * attn_hat, axis=0)
    mean_dot = tensor_sum(jnp.sum(upstream * attn_hat, axis=-1).reshape(8, -1)).reshape(-1, 1) / width
    grad_input = grad_residual + attn_inv * (upstream - attn_hat * mean_dot)

    def total(*values):
        return [lax.psum(v.astype(BF16), "expert").astype(F32) for v in values]

    sum_output, sum_moe_gain, sum_router = total(grad_output, grad_moe_gain, grad_router)
    grad_query = after(grad_query, sum_output)
    sum_query, sum_key, sum_value, sum_query_gain, sum_key_gain, sum_attn_gain = total(
        grad_query,
        grad_key,
        grad_value,
        jnp.sum(grad_query_gain, axis=(0, 1)),
        jnp.sum(grad_key_gain, axis=(0, 1)),
        grad_attn_gain,
    )
    sum_attn_gain = lax.all_gather(sum_attn_gain, "tensor", tiled=True)
    sum_router = lax.all_gather(sum_router, "tensor", tiled=True)
    ordered = jnp.zeros_like(sum_output)
    for i, o in enumerate(order):
        ordered = lax.dynamic_update_slice_in_dim(
            ordered, sum_output[:, i * slice_width : (i + 1) * slice_width], o * slice_width, 1
        )
    factor = clip_threshold / jnp.maximum(head_top, clip_threshold)
    spread = jnp.repeat(jnp.sqrt(factor), HD)
    query_clipped = (w_query.astype(F32) * spread[None, :]).astype(BF16)
    key_clipped = (w_key.astype(F32) * spread[None, :]).astype(BF16)
    return (
        out,
        grad_input,
        sum_attn_gain,
        sum_query,
        sum_key,
        sum_value,
        ordered,
        sum_query_gain,
        sum_key_gain,
        sum_moe_gain,
        sum_router,
        grad_gate,
        grad_up,
        grad_down,
        head_top,
        query_clipped,
        key_clipped,
    )


def solution(mesh):
    return jax.shard_map(
        per_device,
        mesh=mesh,
        in_specs=(
            P("expert", None),
            P(),
            P(None, "tensor"),
            P(None, "tensor"),
            P(None, "tensor"),
            P("tensor", None),
            P("tensor"),
            P("tensor"),
            P(),
            P(),
            P("expert", None, "tensor"),
            P("expert", None, "tensor"),
            P("expert", "tensor", None),
            P("expert", None),
            P("expert", None),
            P("expert", None),
            P("tensor"),
            P("expert", "tensor"),
        ),
        out_specs=(
            P("expert", "tensor"),
            P("expert", "tensor"),
            P(),
            P(None, "tensor"),
            P(None, "tensor"),
            P(None, "tensor"),
            P("tensor", None),
            P("tensor"),
            P("tensor"),
            P("tensor"),
            P(),
            P("expert", None, "tensor"),
            P("expert", None, "tensor"),
            P("expert", "tensor", None),
            P("tensor"),
            P(None, "tensor"),
            P(None, "tensor"),
        ),
        check_vma=False,
    )
```

```python
from functools import partial
import math

import jax
import jax.numpy as jnp
from jax import lax
from jax.experimental import pallas as pl
from jax.experimental.pallas import tpu as pltpu
from jax.sharding import PartitionSpec as P

HD = 128
E = 64
TOP = 8
LENGTH = 1024
CAP = 160
NB = 2
BOTH = ("expert", "tensor")
F32 = jnp.float32
BF16 = jnp.bfloat16
VMEM = 60 * 1024 * 1024
ORDER = (0, 2, 3, 1)
ODD = (1, 2)
DUE = {
    "attend": ("cx0", "cy0"),
    "mmB": ("cz2",),
    "addB": ("cd0", "b0"),
    "cot0": ("b1",),
    "sums": ("by", "cz3"),
    "normed": ("cz1", "sc0"),
    "row0": ("cx1", "cy1", "nx0", "cx2", "ny0", "cy2", "nd0"),
    "cot2": ("cy3", "nz3", "cd2"),
    "exp0": ("nz2", "cx3", "sr0"),
    "row2": ("cd3", "sc2", "ny3", "nx2", "ny2", "sg0", "nd2"),
    "place0": ("nz1",),
    "cot3": ("cd1", "sr2", "nd3"),
    "exp2": ("nx3",),
    "row3": ("ny1", "sc3"),
    "place2": ("nx1", "sg2"),
    "cot1": ("sr3", "ed0", "ex0"),
    "row1": ("sc1", "nd1"),
    "place3": ("sg3",),
    "exp1": ("sr1",),
    "down0": ("ey2", "ed2", "ey0"),
    "place1": ("sg1",),
    "down1": ("ed3", "ex3"),
    "pd0": ("sd0", "ex2"),
    "pd1": ("sd1",),
    "weight": ("hs", "gd0", "gx0", "gd1"),
    "weight_down": ("gy0", "gy1", "gx1"),
}


def matmul(left, right):
    return jnp.dot(left, right, preferred_element_type=F32)


def matmul_nt(left, right):
    return lax.dot_general(left, right, (((1,), (1,)), ((), ())), preferred_element_type=F32)


def matmul_tn(left, right):
    return lax.dot_general(left, right, (((0,), (0,)), ((), ())), preferred_element_type=F32)


def after(value, *others):
    return lax.optimization_barrier((value, *others))[0]


def flip(dz, dx, dy, dc):
    pairs = []
    for z in range(4):
        for x in range(2):
            for y in range(2):
                for c in range(2):
                    pairs.append(
                        (
                            ((z * 2 + x) * 2 + y) * 2 + c,
                            (((z ^ dz) * 2 + (x ^ dx)) * 2 + (y ^ dy)) * 2 + (c ^ dc),
                        )
                    )
    return pairs


def send(value, dz=0, dx=0, dy=0, dc=0):
    return lax.ppermute(value, BOTH, flip(dz, dx, dy, dc))


def is_cube():
    return lax.axis_size("expert") == 8 and lax.axis_size("tensor") == 4


def core_swap(value):
    if is_cube():
        return send(value, dc=1)
    count = lax.axis_size("tensor")
    return lax.ppermute(value, "tensor", [(i, i ^ 1) for i in range(count)])


def slot_blocks():
    owner, part = lax.axis_index("expert"), lax.axis_index("tensor")
    core = part % 2
    found = []
    for k in range(lax.axis_size("expert") // NB):
        places = [k * NB + b for b in range(NB)]
        if is_cube():
            owners = [owner ^ p for p in places]
            mine = [part ^ (y * 2) for y in range(2)]
        else:
            owners = places
            mine = [y * 2 + core for y in range(lax.axis_size("tensor") // 2)]
        theirs = [m ^ 1 for m in mine]
        found.append(jnp.stack([jnp.asarray(v, jnp.int32) for v in places + owners + mine + theirs]))
    return found


def gather_routes(routes):
    if not is_cube():
        return lax.all_gather(routes, "expert")
    both = jnp.stack([routes, send(routes, dx=1)])
    both = jnp.concatenate([both, send(both, dz=1)])
    return jnp.concatenate([both, send(both, dz=2)])


def same_core():
    count = lax.axis_size("tensor")
    return [[y * 2 + c for y in range(count // 2)] for c in range(2)]


def gather_slots(own, tag, seen):
    if not is_cube():
        blocks = lax.all_gather(own, "expert")
        full = lax.all_gather(blocks, "tensor", axis_index_groups=same_core())
        return [
            [[full[y, k * NB + b] for y in range(full.shape[0])] for b in range(NB)]
            for k in range(full.shape[1] // NB)
        ]
    slots = []
    for k in range(4):
        block = send(own, dz=k) if k else own
        over_x = send(block, dx=1)
        over_y = send(block, dy=1)
        far = send(over_x, dy=1) if k in ODD else send(over_y, dx=1)
        for link, value in zip("zxyd", (block, over_x, over_y, far)):
            seen[tag + link + str(k)] = value
        slots.append([[block, over_y], [over_x, far]])
    return slots


def added(*terms):
    return sum(t.astype(F32) for t in terms)


def scatter_plane(parts, odd, hold=()):
    near, over_y, over_x, far = parts[0][0], parts[0][1], parts[1][0], parts[1][1]
    if odd:
        far = send(far, dy=1)
        from_y = send(over_y, dy=1)
        from_x = send(after(added(over_x, far).astype(BF16), *hold), dx=1)
    else:
        far = send(far, dx=1)
        from_x = send(over_x, dx=1)
        from_y = send(after(added(over_y, far).astype(BF16), *hold), dy=1)
    return added(near, from_x, from_y), {"d": far, "x": from_x, "y": from_y}


def scatter_all(slots):
    full = jnp.stack(
        [jnp.stack([s[b][y] for s in slots for b in range(NB)]) for y in range(len(slots[0][0]))]
    )
    mine = lax.psum_scatter(full, "tensor", axis_index_groups=same_core(), scatter_dimension=0)
    return lax.psum_scatter(mine, "expert", scatter_dimension=0).astype(F32)


def scatter_pairs(pairs, hold, seen):
    if not is_cube():
        return scatter_all(
            [[[a[i] for a in b] for b in pair] for pair in pairs for i in range(pair[0][0].shape[0])]
        )
    (low, low_sent), (high, high_sent) = (scatter_plane(p, k, hold) for k, p in enumerate(pairs))
    seen.update({"g" + link + "0": value for link, value in low_sent.items()})
    seen.update({"g" + link + "1": value for link, value in high_sent.items()})
    total = low + send(high.astype(BF16), dz=2).astype(F32)
    return total[0] + send(total[1].astype(BF16), dz=1).astype(F32)


def tensor_order():
    part = lax.axis_index("tensor")
    if is_cube():
        return [part ^ i for i in (0, 2, 1, 3)]
    return [jnp.int32(i) for i in range(lax.axis_size("tensor"))]


def tensor_gather(own):
    if not is_cube():
        full = lax.all_gather(own, "tensor")
        return [full[i] for i in range(full.shape[0])]
    over_y = send(own, dy=1)
    return [own, over_y, core_swap(own), core_swap(over_y)]


def tensor_scatter(product, pieces, tag, seen):
    if not is_cube():
        full = jnp.concatenate([product(p).astype(BF16) for p in pieces], axis=1)
        return lax.psum_scatter(full, "tensor", scatter_dimension=1, tiled=True).astype(F32)
    away_y = product(pieces[3]).astype(BF16)
    away = product(pieces[2]).astype(BF16)
    from_y, near = core_swap(away_y), core_swap(away)
    away = added(product(pieces[1]), from_y).astype(BF16)
    over_y = send(away, dy=1)
    seen.update({tag + "0": from_y, tag + "1": near, tag + "y": over_y, tag + "s": away})
    return added(product(pieces[0]), near, over_y)


def tensor_sum(value):
    if not is_cube():
        return lax.psum(value, "tensor")
    value = value + core_swap(value)
    return value + send(value, dy=1)


def expert_total(sums, tops):
    if not is_cube():
        return lax.psum(sums, "expert"), lax.pmax(tops, "expert")
    count = sums.shape[0]
    both = jnp.concatenate([sums, tops], axis=0)
    for step in ({"dx": 1}, {"dz": 1}, {"dz": 2}):
        other = send(both, **step)
        both = jnp.concatenate([both[:count] + other[:count], jnp.maximum(both[count:], other[count:])])
    return both[:count], both[count:]


def one_hot(pos_row):
    rows = lax.broadcasted_iota(jnp.int32, (CAP, pos_row.shape[1]), 0)
    return rows == pos_row


def as_bf16(mask):
    return jnp.where(mask, 1.0, 0.0).astype(BF16)


def pick_kernel(group, slices, where_ref, *refs):
    pos_refs, x_refs = refs[:NB], refs[NB : NB + NB * slices]
    out_ref, hot_ref = refs[-2:]
    step = pl.program_id(0)
    for b in range(NB):
        for i in range(group):
            hot_ref[b, i * CAP : (i + 1) * CAP, :] = as_bf16(
                one_hot(pos_refs[b][0, pl.ds(step * group + i, 1), :])
            )
        for y in range(slices):
            out_ref[b, y] = matmul(hot_ref[b], x_refs[b * slices + y][...]).astype(BF16)


def pick_rows(where, pos, blocks):
    slices = len(blocks[0])
    tokens, width = blocks[0][0].shape
    held = pos.shape[1]
    group = 2
    flat = [a for b in blocks for a in b]

    def block_spec(b):
        return pl.BlockSpec((1, held, tokens), lambda i, where: (where[b], 0, 0))

    return pl.pallas_call(
        partial(pick_kernel, group, slices),
        grid_spec=pltpu.PrefetchScalarGridSpec(
            num_scalar_prefetch=1,
            grid=(held // group,),
            in_specs=[block_spec(b) for b in range(NB)]
            + [pl.BlockSpec((tokens, width), lambda i, where: (0, 0)) for _ in flat],
            out_specs=pl.BlockSpec(
                (NB, slices, group * CAP, width), lambda i, where: (0, 0, i, 0)
            ),
            scratch_shapes=[pltpu.VMEM((NB, group * CAP, tokens), BF16)],
        ),
        out_shape=jax.ShapeDtypeStruct((NB, slices, held * CAP, width), BF16),
        compiler_params=pltpu.CompilerParams(vmem_limit_bytes=VMEM),
        cost_estimate=pl.CostEstimate(
            flops=2 * NB * slices * held * CAP * tokens * width,
            bytes_accessed=2 * NB * slices * (held * CAP + tokens) * width,
            transcendentals=0,
        ),
        name="pick_rows",
    )(where, *([pos] * NB), *flat)


def expert_kernel(slices, where_ref, *refs):
    pos_refs, gate_refs = refs[:NB], refs[NB : 2 * NB]
    rows_mine, rows_theirs, cot_mine, cot_theirs, wg_ref, wu_ref, wd_ref = refs[2 * NB : 2 * NB + 7]
    scaled_ref, gate_grad_ref, up_grad_ref, prob_ref, keep_ref, give_ref = refs[2 * NB + 7 :]
    e = pl.program_id(0)
    width = rows_mine.shape[3]
    ff = wg_ref.shape[2]
    gate_pre = jnp.zeros((NB * CAP, ff), F32)
    up_pre = jnp.zeros((NB * CAP, ff), F32)
    grad_hidden = jnp.zeros((NB * CAP, ff), F32)

    def columns(j):
        return pl.ds(pl.multiple_of(where_ref[2 * NB + j] * width, width), width)

    for j in range(2 * slices):
        x_ref, c_ref = (rows_mine, cot_mine) if j < slices else (rows_theirs, cot_theirs)
        x = x_ref[:, j % slices].reshape(NB * CAP, width)
        c = c_ref[:, j % slices].reshape(NB * CAP, width)
        gate_pre = gate_pre + matmul(x, wg_ref[0, columns(j), :])
        up_pre = up_pre + matmul(x, wu_ref[0, columns(j), :])
        grad_hidden = grad_hidden + matmul_nt(c, wd_ref[0, :, columns(j)])
    masks = [one_hot(pos_refs[b][0, pl.ds(e, 1), :]) for b in range(NB)]
    gates = jnp.concatenate(
        [
            jnp.sum(jnp.where(masks[b], gate_refs[b][0, pl.ds(e, 1), :], 0.0), axis=1, keepdims=True)
            for b in range(NB)
        ],
        axis=0,
    )
    sigma = jax.nn.sigmoid(gate_pre)
    swish = gate_pre * sigma
    hidden = (swish * up_pre).astype(BF16).astype(F32)
    prob = jnp.sum(hidden * grad_hidden, axis=1, keepdims=True)
    for b in range(NB):
        prob_ref[0, b : b + 1, :] = jnp.sum(
            jnp.where(masks[b], prob[b * CAP : (b + 1) * CAP], 0.0), axis=0, keepdims=True
        )
    grad_hidden = grad_hidden * gates
    scaled_ref[0] = (hidden * gates).astype(BF16)
    gate_grad = (grad_hidden * up_pre * (sigma * (1.0 + gate_pre * (1.0 - sigma)))).astype(BF16)
    up_grad = (grad_hidden * swish).astype(BF16)
    gate_grad_ref[0] = gate_grad
    up_grad_ref[0] = up_grad
    for j in range(2 * slices):
        to = keep_ref if j < slices else give_ref
        back = matmul_nt(gate_grad, wg_ref[0, columns(j), :]) + matmul_nt(
            up_grad, wu_ref[0, columns(j), :]
        )
        to[:, j % slices] = back.astype(BF16).reshape(NB, CAP, width)


def expert_slot(where, pos, gate, rows, cots, w_gate, w_up, w_down):
    held, depth, ff = w_gate.shape
    tokens = pos.shape[2]
    slices, width = rows[0].shape[1], rows[0].shape[3]

    def block_spec(b):
        return pl.BlockSpec((1, held, tokens), lambda e, where: (where[b], 0, 0))

    rows_spec = pl.BlockSpec((NB, slices, CAP, width), lambda e, where: (0, 0, e, 0))
    rows_shape = jax.ShapeDtypeStruct((NB, slices, held * CAP, width), BF16)
    in_spec = pl.BlockSpec((1, depth, ff), lambda e, where: (e, 0, 0))
    hidden_spec = pl.BlockSpec((1, NB * CAP, ff), lambda e, where: (e, 0, 0))
    hidden_shape = jax.ShapeDtypeStruct((held, NB * CAP, ff), BF16)
    return pl.pallas_call(
        partial(expert_kernel, slices),
        grid_spec=pltpu.PrefetchScalarGridSpec(
            num_scalar_prefetch=1,
            grid=(held,),
            in_specs=[block_spec(b) for b in range(2 * NB)]
            + [rows_spec] * 4
            + [in_spec, in_spec, pl.BlockSpec((1, ff, depth), lambda e, where: (e, 0, 0))],
            out_specs=[hidden_spec] * 3
            + [pl.BlockSpec((1, NB, tokens), lambda e, where: (e, 0, 0)), rows_spec, rows_spec],
        ),
        out_shape=[hidden_shape] * 3
        + [jax.ShapeDtypeStruct((held, NB, tokens), F32), rows_shape, rows_shape],
        compiler_params=pltpu.CompilerParams(vmem_limit_bytes=VMEM),
        cost_estimate=pl.CostEstimate(
            flops=10 * NB * held * CAP * depth * ff,
            bytes_accessed=6 * held * depth * ff + 6 * NB * held * CAP * depth,
            transcendentals=NB * held * CAP * ff,
        ),
        name="expert_slot",
    )(where, *([pos] * NB), *([gate] * NB), *rows, *cots, w_gate, w_up, w_down)


def down_kernel(slices, slots, where_ref, *refs):
    scaled_refs, wd_ref, keep_ref, give_ref = refs[:slots], refs[slots], refs[-2], refs[-1]
    width = keep_ref.shape[3]
    for j in range(2 * slices):
        to = keep_ref if j < slices else give_ref
        columns = pl.ds(pl.multiple_of(where_ref[2 * NB + j] * width, width), width)
        for k in range(slots):
            rows = matmul(scaled_refs[k][0], wd_ref[0, :, columns])
            to[k * NB : (k + 1) * NB, j % slices] = rows.astype(BF16).reshape(NB, CAP, width)


def down_slots(where, scaled, w_down, slices):
    held, ff, depth = w_down.shape
    width = depth // (2 * slices)
    slots = len(scaled)
    rows_spec = pl.BlockSpec((slots * NB, slices, CAP, width), lambda e, where: (0, 0, e, 0))
    rows_shape = jax.ShapeDtypeStruct((slots * NB, slices, held * CAP, width), BF16)
    return pl.pallas_call(
        partial(down_kernel, slices, slots),
        grid_spec=pltpu.PrefetchScalarGridSpec(
            num_scalar_prefetch=1,
            grid=(held,),
            in_specs=[pl.BlockSpec((1, NB * CAP, ff), lambda e, where: (e, 0, 0))] * slots
            + [pl.BlockSpec((1, ff, depth), lambda e, where: (e, 0, 0))],
            out_specs=[rows_spec, rows_spec],
        ),
        out_shape=[rows_shape, rows_shape],
        compiler_params=pltpu.CompilerParams(vmem_limit_bytes=VMEM),
        cost_estimate=pl.CostEstimate(
            flops=2 * slots * NB * held * CAP * depth * ff,
            bytes_accessed=2 * held * depth * ff + 2 * slots * NB * held * CAP * depth,
            transcendentals=0,
        ),
        name="down_slots",
    )(where, *scaled, w_down)


def place_kernel(slices, held, slots, where_ref, *refs):
    count = NB * slots
    at_refs, mine_ref, theirs_ref = refs[:count], refs[count], refs[count + 1]
    out_refs, hot_ref = refs[count + 2 : -1], refs[-1]
    b, y = pl.program_id(0), pl.program_id(1)
    tokens = hot_ref.shape[0]
    for block in range(count):

        @pl.when((b == block) & (y == 0))
        def _():
            at = at_refs[block][0]
            for tile in range(held * CAP // 128):
                lanes = lax.broadcasted_iota(jnp.int32, (tokens, 128), 1) + tile * 128
                mask = None
                for e in range(tile * 128 // CAP, (tile * 128 + 127) // CAP + 1):
                    hit = at[:, e : e + 1] == lanes
                    mask = hit if mask is None else mask | hit
                hot_ref[:, tile * 128 : (tile + 1) * 128] = as_bf16(mask)

    rows = (mine_ref[0, 0].astype(F32) + theirs_ref[0, 0].astype(F32)).astype(BF16)
    placed = matmul(hot_ref[...], rows).astype(BF16)
    for block in range(count):
        for part in range(slices):

            @pl.when((b == block) & (y == part))
            def _():
                out_refs[block % NB * slices + part][block // NB] = placed


def place_rows(wheres, at, mine, theirs):
    _, slices, count, width = mine.shape
    _, tokens, held = at.shape
    slots = len(wheres)
    blocks = jnp.concatenate([w[:NB] for w in wheres])

    def block_spec(b):
        return pl.BlockSpec((1, tokens, held), lambda i, y, where: (where[b], 0, 0))

    rows_spec = pl.BlockSpec((1, 1, count, width), lambda i, y, where: (i, y, 0, 0))
    out = pl.pallas_call(
        partial(place_kernel, slices, held, slots),
        grid_spec=pltpu.PrefetchScalarGridSpec(
            num_scalar_prefetch=1,
            grid=(NB * slots, slices),
            in_specs=[block_spec(b) for b in range(NB * slots)] + [rows_spec, rows_spec],
            out_specs=[pl.BlockSpec((slots, tokens, width), lambda i, y, where: (0, 0, 0))]
            * (NB * slices),
            scratch_shapes=[pltpu.VMEM((tokens, count), BF16)],
        ),
        out_shape=[jax.ShapeDtypeStruct((slots, tokens, width), BF16)] * (NB * slices),
        compiler_params=pltpu.CompilerParams(vmem_limit_bytes=VMEM),
        cost_estimate=pl.CostEstimate(
            flops=2 * NB * slots * slices * count * tokens * width,
            bytes_accessed=2 * NB * slots * slices * (2 * count + tokens) * width,
            transcendentals=0,
        ),
        name="place_rows",
    )(blocks, *([at] * (NB * slots)), mine, theirs)
    return [out[b * slices : (b + 1) * slices] for b in range(NB)]


def weight_kernel(slots, slices, where_ref, *refs):
    rows, gate_grads, up_grads = refs[: 2 * slots], refs[2 * slots : 3 * slots], refs[3 * slots : 4 * slots]
    gate_ref, up_ref = refs[4 * slots :]
    width = rows[0].shape[3]
    for j in range(2 * slices):
        columns = pl.ds(pl.multiple_of(where_ref[2 * NB + j] * width, width), width)
        gate = up = None
        for k in range(slots):
            x = rows[2 * k + j // slices][:, j % slices].reshape(NB * CAP, width)
            terms = matmul_tn(x, gate_grads[k][0]), matmul_tn(x, up_grads[k][0])
            gate, up = terms if gate is None else (gate + terms[0], up + terms[1])
        gate_ref[0, columns, :] = gate
        up_ref[0, columns, :] = up


def weight_down_kernel(slots, slices, where_ref, *refs):
    cots, scaled, down_ref = refs[: 2 * slots], refs[2 * slots : 3 * slots], refs[3 * slots]
    width = cots[0].shape[3]
    for j in range(2 * slices):
        columns = pl.ds(pl.multiple_of(where_ref[2 * NB + j] * width, width), width)
        down = None
        for k in range(slots):
            c = cots[2 * k + j // slices][:, j % slices].reshape(NB * CAP, width)
            term = matmul_tn(scaled[k][0], c)
            down = term if down is None else down + term
        down_ref[0, :, columns] = down


def weight_grads(kernel, where, rows, hiddens, outs, name):
    slots = len(rows)
    held, _, ff = hiddens[0].shape
    slices, width = rows[0][0].shape[1], rows[0][0].shape[3]
    depth = 2 * slices * width
    rows_spec = pl.BlockSpec((NB, slices, CAP, width), lambda e, where: (0, 0, e, 0))
    hidden_spec = pl.BlockSpec((1, NB * CAP, ff), lambda e, where: (e, 0, 0))
    return pl.pallas_call(
        partial(kernel, slots, slices),
        grid_spec=pltpu.PrefetchScalarGridSpec(
            num_scalar_prefetch=1,
            grid=(held,),
            in_specs=[rows_spec] * (2 * slots) + [hidden_spec] * len(hiddens),
            out_specs=[pl.BlockSpec((1, *o), lambda e, where: (e, 0, 0)) for o in outs],
        ),
        out_shape=[jax.ShapeDtypeStruct((held, *o), F32) for o in outs],
        compiler_params=pltpu.CompilerParams(vmem_limit_bytes=VMEM),
        cost_estimate=pl.CostEstimate(flops=10**6, bytes_accessed=10**6, transcendentals=0),
        name=name,
    )(where, *[a for pair in rows for a in pair], *hiddens)


def project_kernel(
    in_ref, ag_ref, wq_ref, wk_ref, wv_ref, qg_ref, kg_ref,
    x_ref, inv_ref, qr_ref, kr_ref, q_ref, k_ref, v_ref,
):
    @pl.when(pl.program_id(0) == 0)
    def _():
        for first in range(0, in_ref.shape[0], 256):
            rows = in_ref[first : first + 256, :].astype(F32)
            inverse = lax.rsqrt(jnp.mean(rows * rows, axis=1, keepdims=True) + 1e-05)
            inv_ref[first : first + 256, :] = inverse
            x_ref[first : first + 256, :] = (rows * inverse * ag_ref[...]).astype(BF16)

    x = x_ref[...]
    for w_ref, gain_ref, raw_ref, to_ref in ((wq_ref, qg_ref, qr_ref, q_ref), (wk_ref, kg_ref, kr_ref, k_ref)):
        raw = matmul(x, w_ref[...])
        raw_ref[...] = raw
        for h in range(raw.shape[1] // HD):
            part = raw[:, h * HD : (h + 1) * HD]
            inverse = lax.rsqrt(jnp.mean(part * part, axis=1, keepdims=True) + 1e-06)
            gain = gain_ref[:, h * HD : (h + 1) * HD]
            to_ref[:, h * HD : (h + 1) * HD] = (part * inverse * gain).astype(BF16)
    v_ref[...] = matmul(x, wv_ref[...]).astype(BF16)


def project(inputs, attn_gain, w_query, w_key, w_value, query_gain, key_gain):
    tokens, depth = inputs.shape
    columns = w_query.shape[1]
    step = min(256, columns)
    whole = pl.BlockSpec((tokens, depth), lambda i: (0, 0))
    weight = pl.BlockSpec((depth, step), lambda i: (0, i))
    gain = pl.BlockSpec((1, step), lambda i: (0, i))
    out = pl.BlockSpec((tokens, step), lambda i: (0, i))
    return pl.pallas_call(
        project_kernel,
        grid=(columns // step,),
        in_specs=[whole, pl.BlockSpec((1, depth), lambda i: (0, 0)), weight, weight, weight, gain, gain],
        out_specs=[whole, pl.BlockSpec((tokens, 1), lambda i: (0, 0))] + [out] * 5,
        out_shape=[
            jax.ShapeDtypeStruct((tokens, depth), BF16),
            jax.ShapeDtypeStruct((tokens, 1), F32),
        ]
        + [jax.ShapeDtypeStruct((tokens, columns), t) for t in (F32, F32, BF16, BF16, BF16)],
        compiler_params=pltpu.CompilerParams(vmem_limit_bytes=VMEM),
        cost_estimate=pl.CostEstimate(
            flops=6 * tokens * depth * columns,
            bytes_accessed=4 * tokens * depth + 6 * depth * columns + 14 * tokens * columns,
            transcendentals=0,
        ),
        name="project",
    )(
        inputs, attn_gain.reshape(1, -1), w_query, w_key, w_value,
        query_gain.reshape(1, -1), key_gain.reshape(1, -1),
    )


def allowed_pairs(pieces_ref, base, first, rows, keys):
    query = first + lax.broadcasted_iota(jnp.int32, (rows, 1), 0)
    key = lax.broadcasted_iota(jnp.int32, (1, keys), 1)

    def piece_of(at, other):
        found = jnp.full(at.shape, other, jnp.int32)
        for j in range(2):
            start, length = pieces_ref[base + j], pieces_ref[base + 2 + j]
            found = jnp.where((at >= start) & (at < start + length), j, found)
        return found

    return (key <= query) | (piece_of(query, -1) == piece_of(key, -2))


def query_blocks():
    half = LENGTH // 2
    return ((0, half, half), (half, half, LENGTH))


def attend_kernel(scale, pieces_ref, q_ref, k_ref, v_ref, o_ref, log_ref, top_ref):
    base = pl.program_id(0) * 4
    best = None
    for first, rows, keys in query_blocks():
        allowed = allowed_pairs(pieces_ref, base, first, rows, keys)
        scores = matmul_nt(q_ref[first : first + rows, :], k_ref[:keys, :]) * scale
        masked = jnp.where(allowed, scores, -1e30)
        top = jnp.max(masked, axis=1, keepdims=True)
        weights = jnp.exp(masked - top)
        total = jnp.sum(weights, axis=1, keepdims=True)
        probs = (weights * (1.0 / total)).astype(BF16)
        o_ref[first : first + rows, :] = matmul(probs, v_ref[:keys, :]).astype(BF16)
        log_ref[0, first : first + rows, :] = top + jnp.log(total)
        most = jnp.max(top, axis=0, keepdims=True)
        best = most if best is None else jnp.maximum(best, most)
    top_ref[0] = jnp.broadcast_to(best, (8, HD))


def attend(pieces, queries, keys, values, scale):
    tokens, columns = queries.shape
    sequences, heads = tokens // LENGTH, columns // HD
    block = pl.BlockSpec((LENGTH, HD), lambda s, h, pieces: (s, h))
    return pl.pallas_call(
        partial(attend_kernel, scale),
        grid_spec=pltpu.PrefetchScalarGridSpec(
            num_scalar_prefetch=1,
            grid=(sequences, heads),
            in_specs=[block] * 3,
            out_specs=[
                block,
                pl.BlockSpec((1, LENGTH, 1), lambda s, h, pieces: (h, s, 0)),
                pl.BlockSpec((1, 8, HD), lambda s, h, pieces: (s * heads + h, 0, 0)),
            ],
        ),
        out_shape=[
            jax.ShapeDtypeStruct((tokens, columns), BF16),
            jax.ShapeDtypeStruct((heads, tokens, 1), F32),
            jax.ShapeDtypeStruct((sequences * heads, 8, HD), F32),
        ],
        compiler_params=pltpu.CompilerParams(vmem_limit_bytes=VMEM),
        cost_estimate=pl.CostEstimate(
            flops=4 * tokens * LENGTH * columns,
            bytes_accessed=8 * tokens * columns,
            transcendentals=tokens * heads * LENGTH,
        ),
        name="attend",
    )(pieces, queries, keys, values)


def attend_back_kernel(
    scale, pieces_ref, q_ref, k_ref, v_ref, g_ref, log_ref, qr_ref, kr_ref, qg_ref, kg_ref,
    gq_ref, gk_ref, gv_ref, gqg_ref, gkg_ref, dq_ref, dk_ref, dv_ref,
):
    base = pl.program_id(0) * 4
    blocks = query_blocks()
    for first, rows, keys in blocks[::-1]:
        allowed = allowed_pairs(pieces_ref, base, first, rows, keys)
        q, g = q_ref[first : first + rows, :], g_ref[first : first + rows, :]
        k, v = k_ref[:keys, :], v_ref[:keys, :]
        scores = matmul_nt(q, k) * scale
        probs = jnp.exp(jnp.where(allowed, scores, -1e30) - log_ref[0, first : first + rows, :])
        grad_p = matmul_nt(g, v)
        delta = jnp.sum(probs * grad_p, axis=1, keepdims=True)
        grad_s = (probs * (grad_p - delta)).astype(BF16)
        dq_ref[first : first + rows, :] = matmul(grad_s, k) * scale
        dk = matmul_tn(grad_s, q) * scale
        dv = matmul_tn(probs.astype(BF16), g)
        if keys == LENGTH:
            dk_ref[...] = dk
            dv_ref[...] = dv
        else:
            dk_ref[:keys, :] += dk
            dv_ref[:keys, :] += dv
    gv_ref[...] = dv_ref[...].astype(BF16)
    for raw_ref, gain_ref, grad_ref, to_ref, sum_ref in (
        (qr_ref, qg_ref, dq_ref, gq_ref, gqg_ref),
        (kr_ref, kg_ref, dk_ref, gk_ref, gkg_ref),
    ):
        raw, grad = raw_ref[...], grad_ref[...]
        inverse = lax.rsqrt(jnp.mean(raw * raw, axis=1, keepdims=True) + 1e-06)
        hat = raw * inverse
        up = grad * gain_ref[...]
        mean = jnp.mean(up * hat, axis=1, keepdims=True)
        to_ref[...] = (inverse * (up - hat * mean)).astype(BF16)
        sum_ref[0] = jnp.sum(grad * hat, axis=0, keepdims=True)


def attend_back(pieces, queries, keys, values, grads, logs, query_raw, key_raw, query_gain, key_gain, scale):
    tokens, columns = queries.shape
    sequences, heads = tokens // LENGTH, columns // HD
    block = pl.BlockSpec((LENGTH, HD), lambda s, h, pieces: (s, h))
    gain = pl.BlockSpec((1, HD), lambda s, h, pieces: (0, h))
    sums = pl.BlockSpec((1, 1, HD), lambda s, h, pieces: (s, 0, h))
    return pl.pallas_call(
        partial(attend_back_kernel, scale),
        grid_spec=pltpu.PrefetchScalarGridSpec(
            num_scalar_prefetch=1,
            grid=(sequences, heads),
            in_specs=[block] * 4
            + [pl.BlockSpec((1, LENGTH, 1), lambda s, h, pieces: (h, s, 0)), block, block, gain, gain],
            out_specs=[block, block, block, sums, sums],
            scratch_shapes=[pltpu.VMEM((LENGTH, HD), F32)] * 3,
        ),
        out_shape=[jax.ShapeDtypeStruct((tokens, columns), BF16)] * 3
        + [jax.ShapeDtypeStruct((sequences, 1, columns), F32)] * 2,
        compiler_params=pltpu.CompilerParams(vmem_limit_bytes=VMEM),
        cost_estimate=pl.CostEstimate(
            flops=10 * tokens * LENGTH * columns,
            bytes_accessed=22 * tokens * columns,
            transcendentals=tokens * heads * LENGTH,
        ),
        name="attend_back",
    )(
        pieces, queries, keys, values, grads, logs, query_raw, key_raw,
        query_gain.reshape(1, -1), key_gain.reshape(1, -1),
    )


def expert_steps(slots):
    order = ORDER if is_cube() else range(slots)
    steps = [("row", order[0]), ("cot", order[1])]
    for i, k in enumerate(order):
        steps.append(("exp", k))
        if i + 1 < slots:
            steps.append(("row", order[i + 1]))
        else:
            steps.append(("down", 0))
        steps.append(("place", k))
        if i + 2 < slots:
            steps.append(("cot", order[i + 2]))
    return steps


def due(step, seen):
    return [seen[name] for name in DUE.get(step, ()) if name in seen]


def per_device(
    inputs,
    attn_gain,
    w_query,
    w_key,
    w_value,
    w_output,
    query_gain,
    key_gain,
    moe_gain,
    w_router,
    w_gate,
    w_up,
    w_down,
    routes,
    piece_start,
    piece_length,
    clip_threshold,
    cotangent,
):
    tokens_here, width = inputs.shape
    slice_width = cotangent.shape[1]
    owner = lax.axis_index("expert")
    column = lax.axis_index("tensor") * slice_width
    heads_here = query_gain.shape[0] // HD
    experts_here = w_gate.shape[0]
    owners = lax.axis_size("expert")
    sequences = tokens_here // LENGTH
    scale = 1.0 / math.sqrt(HD)
    where = slot_blocks()
    slots = len(where)
    slices = lax.axis_size("tensor") // 2

    def own_columns(value):
        return lax.dynamic_slice_in_dim(value, column, slice_width, value.ndim - 1)

    seen = {}
    all_routes = gather_routes(routes.T)
    cot_slots = gather_slots(cotangent.astype(BF16), "c", seen)
    order = tensor_order()
    first_slot = ORDER[0] if is_cube() else 0

    held_ids = owner * experts_here + jnp.arange(experts_here, dtype=jnp.int32)
    chosen = jnp.any(all_routes[:, None] == held_ids[None, :, None, None], axis=2)
    places = jnp.arange(tokens_here, dtype=jnp.int32)
    before = (places[:, None] < places[None, :]).astype(BF16)
    earlier = jnp.einsum(
        "set,tu->seu", chosen.astype(BF16), before, preferred_element_type=F32
    ).astype(jnp.int32)
    pos = jnp.where(chosen, earlier, -1)
    at = jnp.where(
        chosen, earlier + jnp.arange(experts_here, dtype=jnp.int32)[None, :, None] * CAP, -1
    ).transpose(0, 2, 1)

    output_pieces = [lax.dynamic_slice_in_dim(w_output, o * slice_width, slice_width, 1) for o in order]
    normed_a, attn_inv, query_raw, key_raw, queries, keys, values = project(
        inputs, attn_gain, w_query, w_key, w_value, query_gain, key_gain
    )
    pieces = jnp.concatenate([piece_start, piece_length], axis=1).reshape(-1)
    attended, logs, tops = attend(
        after(pieces, values, *due("attend", seen)), queries, keys, values, scale
    )
    head_top = jnp.max(tops[:, 0, 0].reshape(sequences, heads_here), axis=0)
    attended = after(attended, *due("mmB", seen))
    branch = tensor_scatter(partial(matmul, attended), output_pieces, "b", seen)
    first_cot = pick_rows(
        after(where[first_slot], attended, *due("addB", seen), *due("cot" + str(first_slot), seen)),
        pos,
        cot_slots[first_slot],
    )
    branch = after(branch, first_cot, *due("sums", seen))
    residual = own_columns(inputs).astype(F32) + branch
    gain_slice = own_columns(moe_gain)
    router_slice = lax.dynamic_slice_in_dim(w_router, column, slice_width, 0)
    lifted = residual * gain_slice
    row_sums = tensor_sum(
        jnp.concatenate(
            [
                lax.dot_general(
                    router_slice,
                    lifted.astype(BF16),
                    (((0,), (1,)), ((), ())),
                    preferred_element_type=F32,
                ),
                jnp.sum(residual * residual, axis=1)[None],
            ],
            axis=0,
        )
    )
    moe_inv_row = lax.rsqrt(row_sums[E] / width + 1e-05)
    moe_inv = moe_inv_row[:, None]
    normed_m = (lifted * moe_inv).astype(BF16)
    normed_m = after(normed_m, *due("normed", seen))

    normed_slots = gather_slots(normed_m, "n", seen)
    router = jax.nn.softmax(row_sums[:E] * moe_inv_row[None], axis=0)
    gate = lax.all_to_all(
        router.reshape(owners, experts_here, tokens_here),
        "expert",
        split_axis=0,
        concat_axis=0,
        tiled=True,
    )

    rows, cots, back, sums = [None] * slots, [None] * slots, [None] * slots, [None] * slots
    scaled, gate_grads, up_grads, probs = [None] * slots, [None] * slots, [None] * slots, [None] * slots
    last = first_cot
    cots[first_slot] = (first_cot, core_swap(first_cot))
    seen["sc" + str(first_slot)] = cots[first_slot][1]
    downs = {}

    def turn(name, k):
        return after(where[k], last, *due(name, seen))

    def lower(k):
        keep, give = down_slots(turn("down" + str(k), 0), scaled[2 * k : 2 * k + 2], w_down, slices)
        downs[k] = (keep, core_swap(give))
        seen["sd" + str(k)] = downs[k][1]
        return keep

    for kind, k in expert_steps(slots):
        now = turn(kind + str(k), k)
        if kind == "cot":
            last = pick_rows(now, pos, cot_slots[k])
            cots[k] = (last, core_swap(last))
            seen["sc" + str(k)] = cots[k][1]
        elif kind == "row":
            last = pick_rows(now, pos, normed_slots[k])
            rows[k] = (last, core_swap(last))
            seen["sr" + str(k)] = rows[k][1]
        elif kind == "exp":
            scaled[k], gate_grads[k], up_grads[k], probs[k], keep, give = expert_slot(
                now, pos, gate, rows[k], cots[k], w_gate, w_up, w_down
            )
            last = scaled[k]
            back[k] = (keep, core_swap(give))
            seen["sg" + str(k)] = back[k][1]
        elif kind == "down":
            last = lower(k)
        else:
            placed = place_rows([now], at, *back[k])
            last = placed[0][0]
            back[k] = [[a[0] for a in b] for b in placed]
            if is_cube():
                sums[k], sent = scatter_plane(back[k], k in ODD)
                if k:
                    sent["z"] = send(sums[k].astype(BF16), dz=k)
                    sums[k] = sent["z"].astype(F32)
                seen.update({"e" + link + str(k): value for link, value in sent.items()})
    for k in range(1, slots // 2):
        last = lower(k)
    pairs = []
    for k in range(slots // 2):
        now = turn("pd" + str(k), 2 * k)
        placed = place_rows([now, where[2 * k + 1]], at, *downs[k])
        last = placed[0][0]
        pairs.append(placed)
    if is_cube():
        expert_path = sum(after(s, last) for s in sums)
    else:
        expert_path = scatter_all(back)

    prob_grads = jnp.stack([probs[k][:, b] for k in range(slots) for b in range(NB)])
    if is_cube():
        prob_grads = prob_grads[jnp.arange(owners, dtype=jnp.int32) ^ owner]
    prob_grads = lax.all_to_all(prob_grads, "expert", split_axis=0, concat_axis=0, tiled=True)
    prob_grads = tensor_sum(prob_grads.reshape(E, tokens_here))
    grad_logits = (
        router * (prob_grads - jnp.sum(router * prob_grads, axis=0, keepdims=True))
    ).astype(BF16)
    grad_router = lax.dot_general(
        normed_m, grad_logits, (((0,), (1,)), ((), ())), preferred_element_type=F32
    )
    router_path = lax.dot_general(
        grad_logits, router_slice, (((0,), (1,)), ((), ())), preferred_element_type=F32
    )
    grad_normed = expert_path + router_path
    moe_hat = residual * moe_inv
    grad_moe_gain = jnp.sum(grad_normed * moe_hat, axis=0)
    upstream = grad_normed * gain_slice
    mean_dot = tensor_sum(jnp.sum(upstream * moe_hat, axis=-1).reshape(8, -1)).reshape(-1, 1) / width
    grad_residual = cotangent + moe_inv * (upstream - moe_hat * mean_dot)
    branch_pieces = tensor_gather(grad_residual.astype(BF16))
    grad_branch = jnp.concatenate(branch_pieces, axis=1)

    if is_cube():
        ends = [seen["e" + link + str(ORDER[i])] for i in (-2, -1) for link in "xyd"]
        pairs[0] = [[after(a, *ends) for a in b] for b in pairs[0]]
        pairs[1] = [[after(a, branch_pieces[1]) for a in b] for b in pairs[1]]
    mixture = scatter_pairs(pairs, branch_pieces[1:2], seen)
    out = residual + mixture

    grad_output = matmul_tn(attended, grad_branch).astype(BF16)
    grad_attended = matmul_nt(grad_branch, jnp.concatenate(output_pieces, axis=1)).astype(BF16)
    grad_attended = after(grad_attended, grad_output)
    grad_query_raw, grad_key_raw, grad_v, grad_query_gain, grad_key_gain = attend_back(
        pieces, queries, keys, values, grad_attended, logs, query_raw, key_raw, query_gain, key_gain, scale
    )
    grad_raw = jnp.concatenate([grad_query_raw, grad_key_raw, grad_v], axis=1)
    grad_three = matmul_tn(normed_a, grad_raw).astype(BF16)
    sum_output = lax.psum(grad_output, "expert").astype(F32)
    sum_three = lax.psum_scatter(grad_three, "expert", scatter_dimension=0, tiled=True)
    grad_raw = after(grad_raw, grad_three)
    weights = jnp.concatenate([w_query, w_key, w_value], axis=1)
    weight_pieces = [lax.dynamic_slice_in_dim(weights, o * slice_width, slice_width, 0) for o in order]
    grad_normed_a = tensor_scatter(partial(matmul_nt, grad_raw), weight_pieces, "h", seen)
    now = after(where[0], sum_output, *due("weight", seen))
    grad_gate, grad_up = weight_grads(
        weight_kernel, now, rows, gate_grads + up_grads, [w_gate.shape[1:]] * 2, "weight_grads"
    )
    (grad_down,) = weight_grads(
        weight_down_kernel, after(now, grad_gate, sum_three, *due("weight_down", seen)), cots, scaled, [w_down.shape[1:]], "weight_down_grads"
    )
    sum_three = lax.all_gather(sum_three, "expert", tiled=True)
    sum_query, sum_key, sum_value = jnp.split(sum_three.astype(F32), 3, axis=1)
    grad_normed_a = after(grad_normed_a, grad_gate)
    attn_hat = own_columns(inputs).astype(F32) * attn_inv
    upstream = grad_normed_a * own_columns(attn_gain)
    grad_attn_gain = jnp.sum(grad_normed_a * attn_hat, axis=0)
    mean_dot = tensor_sum(jnp.sum(upstream * attn_hat, axis=-1).reshape(8, -1)).reshape(-1, 1) / width
    grad_input = grad_residual + attn_inv * (upstream - attn_hat * mean_dot)

    small = jnp.concatenate(
        [
            grad_router.T,
            jnp.stack(
                [
                    grad_attn_gain,
                    grad_moe_gain,
                    jnp.sum(grad_query_gain, axis=(0, 1)),
                    jnp.sum(grad_key_gain, axis=(0, 1)),
                ]
            ),
        ],
        axis=0,
    )
    top_row = jnp.pad(head_top, (0, slice_width - heads_here), constant_values=-3e38)
    small, top_row = expert_total(small, top_row[None])
    head_top = top_row[0, :heads_here]
    sum_moe_gain, sum_query_gain, sum_key_gain = small[E + 1], small[E + 2], small[E + 3]
    every = lax.all_gather(small[: E + 1], "tensor")
    sum_router = every[:, :E].transpose(0, 2, 1).reshape(width, E)
    sum_attn_gain = every[:, E].reshape(width)
    ordered = jnp.zeros_like(sum_output)
    for i, o in enumerate(order):
        ordered = lax.dynamic_update_slice_in_dim(
            ordered, sum_output[:, i * slice_width : (i + 1) * slice_width], o * slice_width, 1
        )
    factor = clip_threshold / jnp.maximum(head_top, clip_threshold)
    spread = jnp.repeat(jnp.sqrt(factor), HD)
    query_clipped = (w_query.astype(F32) * spread[None, :]).astype(BF16)
    key_clipped = (w_key.astype(F32) * spread[None, :]).astype(BF16)
    return (
        out,
        grad_input,
        sum_attn_gain,
        sum_query,
        sum_key,
        sum_value,
        ordered,
        sum_query_gain,
        sum_key_gain,
        sum_moe_gain,
        sum_router,
        grad_gate,
        grad_up,
        grad_down,
        head_top,
        query_clipped,
        key_clipped,
    )


def solution(mesh):
    return jax.shard_map(
        per_device,
        mesh=mesh,
        in_specs=(
            P("expert", None),
            P(),
            P(None, "tensor"),
            P(None, "tensor"),
            P(None, "tensor"),
            P("tensor", None),
            P("tensor"),
            P("tensor"),
            P(),
            P(),
            P("expert", None, "tensor"),
            P("expert", None, "tensor"),
            P("expert", "tensor", None),
            P("expert", None),
            P("expert", None),
            P("expert", None),
            P("tensor"),
            P("expert", "tensor"),
        ),
        out_specs=(
            P("expert", "tensor"),
            P("expert", "tensor"),
            P(),
            P(None, "tensor"),
            P(None, "tensor"),
            P(None, "tensor"),
            P("tensor", None),
            P("tensor"),
            P("tensor"),
            P("tensor"),
            P(),
            P("expert", None, "tensor"),
            P("expert", None, "tensor"),
            P("expert", "tensor", None),
            P("tensor"),
            P(None, "tensor"),
            P(None, "tensor"),
        ),
        check_vma=False,
    )
```

```python
from functools import partial
import math

import jax
import jax.numpy as jnp
from jax import lax
from jax.experimental import pallas as pl
from jax.experimental.pallas import tpu as pltpu
from jax.sharding import PartitionSpec as P

HD = 128
E = 64
TOP = 8
LENGTH = 1024
CAP = 160
NB = 2
BOTH = ("expert", "tensor")
F32 = jnp.float32
BF16 = jnp.bfloat16
VMEM = 60 * 1024 * 1024
WEIGHT = 16
ORDER = (0, 2, 3, 1)
ODD = (1, 2)
DUE = {
    "attended": ("cx0", "cy0"),
    "normed": ("cz2", "cd0", "cx2"),
    "row0": ("cz3", "cy2"),
    "cot2": ("nz2",),
    "exp0": ("cx3",),
    "row2": ("sc2", "cy3"),
    "cot3": ("sg0",),
    "place0": ("sr2",),
    "exp2": ("sc3",),
    "cot1": ("sg2",),
    "place2": ("sr3", "ed0"),
    "exp3": ("sc1",),
    "place3": ("ex0", "ey0", "ed2"),
    "down1": ("ex2", "ey2", "ed3"),
    "pd0": ("ed1", "sd0"),
    "weight": ("ex3", "ey3", "ex1", "ey1"),
    "weight_down": ("hs", "gd0", "gd1"),
}


def cost(flops, bytes_accessed, transcendentals):
    return pl.CostEstimate(
        flops=flops * WEIGHT, bytes_accessed=bytes_accessed * WEIGHT, transcendentals=transcendentals * WEIGHT
    )


def matmul(left, right):
    return jnp.dot(left, right, preferred_element_type=F32)


def matmul_nt(left, right):
    return lax.dot_general(left, right, (((1,), (1,)), ((), ())), preferred_element_type=F32)


def matmul_tn(left, right):
    return lax.dot_general(left, right, (((0,), (0,)), ((), ())), preferred_element_type=F32)


def after(value, *others):
    return lax.optimization_barrier((value, *others))[0]


def flip(dz, dx, dy, dc):
    pairs = []
    for z in range(4):
        for x in range(2):
            for y in range(2):
                for c in range(2):
                    pairs.append(
                        (
                            ((z * 2 + x) * 2 + y) * 2 + c,
                            (((z ^ dz) * 2 + (x ^ dx)) * 2 + (y ^ dy)) * 2 + (c ^ dc),
                        )
                    )
    return pairs


def send(value, dz=0, dx=0, dy=0, dc=0):
    return lax.ppermute(value, BOTH, flip(dz, dx, dy, dc))


def is_cube():
    return lax.axis_size("expert") == 8 and lax.axis_size("tensor") == 4


def core_swap(value):
    if is_cube():
        return send(value, dc=1)
    count = lax.axis_size("tensor")
    return lax.ppermute(value, "tensor", [(i, i ^ 1) for i in range(count)])


def slot_blocks():
    owner, part = lax.axis_index("expert"), lax.axis_index("tensor")
    core = part % 2
    found = []
    for k in range(lax.axis_size("expert") // NB):
        places = [k * NB + b for b in range(NB)]
        if is_cube():
            owners = [owner ^ p for p in places]
            mine = [part ^ (y * 2) for y in range(2)]
        else:
            owners = places
            mine = [y * 2 + core for y in range(lax.axis_size("tensor") // 2)]
        theirs = [m ^ 1 for m in mine]
        rows = [m // 2 for m in mine]
        found.append(
            jnp.stack([jnp.asarray(v, jnp.int32) for v in places + owners + mine + theirs + rows])
        )
    return found


def gather_routes(routes):
    if not is_cube():
        return lax.all_gather(routes, "expert")
    both = jnp.stack([routes, send(routes, dx=1)])
    both = jnp.concatenate([both, send(both, dz=1)])
    return jnp.concatenate([both, send(both, dz=2)])


def same_core():
    count = lax.axis_size("tensor")
    return [[y * 2 + c for y in range(count // 2)] for c in range(2)]


def gather_all(own):
    owners, parts = lax.axis_size("expert"), lax.axis_size("tensor")
    groups = [[e * parts + t for e in range(owners) for t in range(c, parts, 2)] for c in range(2)]
    full = lax.all_gather(own, BOTH, axis_index_groups=groups)
    return full.reshape(owners, parts // 2, *own.shape)


def gather_slots(own, tag, seen):
    if not is_cube():
        return [gather_all(own)] * (lax.axis_size("expert") // NB)
    slots = []
    for k in range(4):
        block = send(own, dz=k) if k else own
        over_x = send(block, dx=1)
        over_y = send(block, dy=1)
        far = send(over_x, dy=1) if k in ODD else send(over_y, dx=1)
        for link, value in zip("zxyd", (block, over_x, over_y, far)):
            seen[tag + link + str(k)] = value
        slots.append([[block, over_y], [over_x, far]])
    return slots


def added(*terms):
    return sum(t.astype(F32) for t in terms)


def scatter_plane(parts, odd):
    near, over_y, over_x, far = parts[0][0], parts[0][1], parts[1][0], parts[1][1]
    if odd:
        far = send(far, dy=1)
        over_x, over_y = added(over_x, far).astype(BF16), after(over_y, far)
    else:
        far = send(far, dx=1)
        over_x, over_y = after(over_x, far), added(over_y, far).astype(BF16)
    from_x, from_y = send(over_x, dx=1), send(over_y, dy=1)
    return added(near, from_x, from_y), {"d": far, "x": from_x, "y": from_y}


def scatter_all(slots):
    full = jnp.stack(
        [jnp.stack([s[b][y] for s in slots for b in range(NB)]) for y in range(len(slots[0][0]))]
    )
    mine = lax.psum_scatter(full, "tensor", axis_index_groups=same_core(), scatter_dimension=0)
    return lax.psum_scatter(mine, "expert", scatter_dimension=0).astype(F32)


def scatter_pairs(pairs, seen):
    if not is_cube():
        return scatter_all(
            [[[a[i] for a in b] for b in pair] for pair in pairs for i in range(pair[0][0].shape[0])]
        )
    (low, low_sent), (high, high_sent) = (scatter_plane(p, True) for p in pairs)
    seen.update({"g" + link + "0": value for link, value in low_sent.items()})
    seen.update({"g" + link + "1": value for link, value in high_sent.items()})
    total = low + send(high.astype(BF16), dz=2).astype(F32)
    return total[0] + send(total[1].astype(BF16), dz=1).astype(F32)


def tensor_order():
    part = lax.axis_index("tensor")
    if is_cube():
        return [part ^ i for i in (0, 2, 1, 3)]
    return [jnp.int32(i) for i in range(lax.axis_size("tensor"))]


def tensor_gather(own):
    if not is_cube():
        full = lax.all_gather(own, "tensor")
        return [full[i] for i in range(full.shape[0])]
    over_y = send(own, dy=1)
    return [own, over_y, core_swap(own), core_swap(over_y)]


def tensor_scatter(product, pieces, tag, seen):
    if not is_cube():
        full = jnp.concatenate([product(p).astype(BF16) for p in pieces], axis=1)
        return lax.psum_scatter(full, "tensor", scatter_dimension=1, tiled=True).astype(F32)
    away_y = product(pieces[3]).astype(BF16)
    away = product(pieces[2]).astype(BF16)
    from_y, near = core_swap(away_y), core_swap(away)
    away = added(product(pieces[1]), from_y).astype(BF16)
    over_y = send(away, dy=1)
    seen.update({tag + "0": from_y, tag + "1": near, tag + "y": over_y, tag + "s": away})
    return added(product(pieces[0]), near, over_y)


def tensor_sum(value):
    if not is_cube():
        return lax.psum(value, "tensor")
    value = value + core_swap(value)
    return value + send(value, dy=1)


def expert_total(sums, tops):
    if not is_cube():
        return lax.psum(sums, "expert"), lax.pmax(tops, "expert")
    count = sums.shape[0]
    both = jnp.concatenate([sums, tops], axis=0)
    for step in ({"dx": 1}, {"dz": 1}, {"dz": 2}):
        other = send(both, **step)
        both = jnp.concatenate([both[:count] + other[:count], jnp.maximum(both[count:], other[count:])])
    return both[:count], both[count:]


def one_hot(pos_row):
    rows = lax.broadcasted_iota(jnp.int32, (CAP, pos_row.shape[1]), 0)
    return rows == pos_row


def as_bf16(mask):
    return jnp.where(mask, 1.0, 0.0).astype(BF16)


def pick_kernel(group, slices, where_ref, *refs):
    pos_refs, x_refs = refs[:NB], refs[NB : NB + NB * slices]
    out_ref, hot_ref = refs[-2:]
    step = pl.program_id(0)
    for b in range(NB):
        for i in range(group):
            hot_ref[b, i * CAP : (i + 1) * CAP, :] = as_bf16(
                one_hot(pos_refs[b][0, pl.ds(step * group + i, 1), :])
            )
        for y in range(slices):
            out_ref[b, y] = matmul(hot_ref[b], x_refs[b * slices + y][...]).astype(BF16)


def pick_rows(where, pos, blocks):
    held = pos.shape[1]
    group = 2
    if isinstance(blocks, list):
        slices = len(blocks[0])
        flat = [a for b in blocks for a in b]
        tokens, width = flat[0].shape
        specs = [pl.BlockSpec((tokens, width), lambda i, where: (0, 0)) for _ in flat]
    else:
        slices, tokens, width = blocks.shape[1:]
        flat = [blocks] * (NB * slices)

        def part_spec(b, y):
            return pl.BlockSpec(
                (None, None, tokens, width),
                lambda i, where: (where[NB + b], where[2 * NB + 2 * slices + y], 0, 0),
            )

        specs = [part_spec(b, y) for b in range(NB) for y in range(slices)]

    def block_spec(b):
        return pl.BlockSpec((1, held, tokens), lambda i, where: (where[b], 0, 0))

    return pl.pallas_call(
        partial(pick_kernel, group, slices),
        grid_spec=pltpu.PrefetchScalarGridSpec(
            num_scalar_prefetch=1,
            grid=(held // group,),
            in_specs=[block_spec(b) for b in range(NB)]
            + specs,
            out_specs=pl.BlockSpec(
                (NB, slices, group * CAP, width), lambda i, where: (0, 0, i, 0)
            ),
            scratch_shapes=[pltpu.VMEM((NB, group * CAP, tokens), BF16)],
        ),
        out_shape=jax.ShapeDtypeStruct((NB, slices, held * CAP, width), BF16),
        compiler_params=pltpu.CompilerParams(vmem_limit_bytes=VMEM),
        cost_estimate=cost(
            flops=2 * NB * slices * held * CAP * tokens * width,
            bytes_accessed=2 * NB * slices * (held * CAP + tokens) * width,
            transcendentals=0,
        ),
        name="pick_rows",
    )(where, *([pos] * NB), *flat)


def expert_kernel(slices, where_ref, *refs):
    pos_refs, gate_refs = refs[:NB], refs[NB : 2 * NB]
    rows_mine, rows_theirs, cot_mine, cot_theirs, wg_ref, wu_ref, wd_ref = refs[2 * NB : 2 * NB + 7]
    scaled_ref, gate_grad_ref, up_grad_ref, prob_ref, keep_ref, give_ref = refs[2 * NB + 7 :]
    e = pl.program_id(0)
    width = rows_mine.shape[3]
    ff = wg_ref.shape[2]
    gate_pre = jnp.zeros((NB * CAP, ff), F32)
    up_pre = jnp.zeros((NB * CAP, ff), F32)
    grad_hidden = jnp.zeros((NB * CAP, ff), F32)

    def columns(j):
        return pl.ds(pl.multiple_of(where_ref[2 * NB + j] * width, width), width)

    for j in range(2 * slices):
        x_ref, c_ref = (rows_mine, cot_mine) if j < slices else (rows_theirs, cot_theirs)
        x = x_ref[:, j % slices].reshape(NB * CAP, width)
        c = c_ref[:, j % slices].reshape(NB * CAP, width)
        gate_pre = gate_pre + matmul(x, wg_ref[0, columns(j), :])
        up_pre = up_pre + matmul(x, wu_ref[0, columns(j), :])
        grad_hidden = grad_hidden + matmul_nt(c, wd_ref[0, :, columns(j)])
    masks = [one_hot(pos_refs[b][0, pl.ds(e, 1), :]) for b in range(NB)]
    gates = jnp.concatenate(
        [
            jnp.sum(jnp.where(masks[b], gate_refs[b][0, pl.ds(e, 1), :], 0.0), axis=1, keepdims=True)
            for b in range(NB)
        ],
        axis=0,
    )
    sigma = jax.nn.sigmoid(gate_pre)
    swish = gate_pre * sigma
    hidden = (swish * up_pre).astype(BF16).astype(F32)
    prob = jnp.sum(hidden * grad_hidden, axis=1, keepdims=True)
    for b in range(NB):
        prob_ref[0, b : b + 1, :] = jnp.sum(
            jnp.where(masks[b], prob[b * CAP : (b + 1) * CAP], 0.0), axis=0, keepdims=True
        )
    grad_hidden = grad_hidden * gates
    scaled_ref[0] = (hidden * gates).astype(BF16)
    gate_grad = (grad_hidden * up_pre * (sigma * (1.0 + gate_pre * (1.0 - sigma)))).astype(BF16)
    up_grad = (grad_hidden * swish).astype(BF16)
    gate_grad_ref[0] = gate_grad
    up_grad_ref[0] = up_grad
    for j in range(2 * slices):
        to = keep_ref if j < slices else give_ref
        back = matmul_nt(gate_grad, wg_ref[0, columns(j), :]) + matmul_nt(
            up_grad, wu_ref[0, columns(j), :]
        )
        to[:, j % slices] = back.astype(BF16).reshape(NB, CAP, width)


def expert_slot(where, pos, gate, rows, cots, w_gate, w_up, w_down):
    held, depth, ff = w_gate.shape
    tokens = pos.shape[2]
    slices, width = rows[0].shape[1], rows[0].shape[3]

    def block_spec(b):
        return pl.BlockSpec((1, held, tokens), lambda e, where: (where[b], 0, 0))

    rows_spec = pl.BlockSpec((NB, slices, CAP, width), lambda e, where: (0, 0, e, 0))
    rows_shape = jax.ShapeDtypeStruct((NB, slices, held * CAP, width), BF16)
    in_spec = pl.BlockSpec((1, depth, ff), lambda e, where: (e, 0, 0))
    hidden_spec = pl.BlockSpec((1, NB * CAP, ff), lambda e, where: (e, 0, 0))
    hidden_shape = jax.ShapeDtypeStruct((held, NB * CAP, ff), BF16)
    return pl.pallas_call(
        partial(expert_kernel, slices),
        grid_spec=pltpu.PrefetchScalarGridSpec(
            num_scalar_prefetch=1,
            grid=(held,),
            in_specs=[block_spec(b) for b in range(2 * NB)]
            + [rows_spec] * 4
            + [in_spec, in_spec, pl.BlockSpec((1, ff, depth), lambda e, where: (e, 0, 0))],
            out_specs=[hidden_spec] * 3
            + [pl.BlockSpec((1, NB, tokens), lambda e, where: (e, 0, 0)), rows_spec, rows_spec],
        ),
        out_shape=[hidden_shape] * 3
        + [jax.ShapeDtypeStruct((held, NB, tokens), F32), rows_shape, rows_shape],
        compiler_params=pltpu.CompilerParams(vmem_limit_bytes=VMEM),
        cost_estimate=cost(
            flops=10 * NB * held * CAP * depth * ff,
            bytes_accessed=6 * held * depth * ff + 6 * NB * held * CAP * depth,
            transcendentals=NB * held * CAP * ff,
        ),
        name="expert_slot",
    )(where, *([pos] * NB), *([gate] * NB), *rows, *cots, w_gate, w_up, w_down)


def down_kernel(slices, slots, where_ref, *refs):
    scaled_refs, wd_ref, keep_ref, give_ref = refs[:slots], refs[slots], refs[-2], refs[-1]
    width = keep_ref.shape[3]
    for j in range(2 * slices):
        to = keep_ref if j < slices else give_ref
        columns = pl.ds(pl.multiple_of(where_ref[2 * NB + j] * width, width), width)
        for k in range(slots):
            rows = matmul(scaled_refs[k][0], wd_ref[0, :, columns])
            to[k * NB : (k + 1) * NB, j % slices] = rows.astype(BF16).reshape(NB, CAP, width)


def down_slots(where, scaled, w_down, slices):
    held, ff, depth = w_down.shape
    width = depth // (2 * slices)
    slots = len(scaled)
    rows_spec = pl.BlockSpec((slots * NB, slices, CAP, width), lambda e, where: (0, 0, e, 0))
    rows_shape = jax.ShapeDtypeStruct((slots * NB, slices, held * CAP, width), BF16)
    return pl.pallas_call(
        partial(down_kernel, slices, slots),
        grid_spec=pltpu.PrefetchScalarGridSpec(
            num_scalar_prefetch=1,
            grid=(held,),
            in_specs=[pl.BlockSpec((1, NB * CAP, ff), lambda e, where: (e, 0, 0))] * slots
            + [pl.BlockSpec((1, ff, depth), lambda e, where: (e, 0, 0))],
            out_specs=[rows_spec, rows_spec],
        ),
        out_shape=[rows_shape, rows_shape],
        compiler_params=pltpu.CompilerParams(vmem_limit_bytes=VMEM),
        cost_estimate=cost(
            flops=2 * slots * NB * held * CAP * depth * ff,
            bytes_accessed=2 * held * depth * ff + 2 * slots * NB * held * CAP * depth,
            transcendentals=0,
        ),
        name="down_slots",
    )(where, *scaled, w_down)


def place_kernel(slices, held, slots, where_ref, *refs):
    count = NB * slots
    at_refs, mine_ref, theirs_ref = refs[:count], refs[count], refs[count + 1]
    out_refs, hot_ref = refs[count + 2 : -1], refs[-1]
    b, y = pl.program_id(0), pl.program_id(1)
    tokens = hot_ref.shape[0]
    for block in range(count):

        @pl.when((b == block) & (y == 0))
        def _():
            at = at_refs[block][0]
            for tile in range(held * CAP // 128):
                lanes = lax.broadcasted_iota(jnp.int32, (tokens, 128), 1) + tile * 128
                mask = None
                for e in range(tile * 128 // CAP, (tile * 128 + 127) // CAP + 1):
                    hit = at[:, e : e + 1] == lanes
                    mask = hit if mask is None else mask | hit
                hot_ref[:, tile * 128 : (tile + 1) * 128] = as_bf16(mask)

    rows = (mine_ref[0, 0].astype(F32) + theirs_ref[0, 0].astype(F32)).astype(BF16)
    placed = matmul(hot_ref[...], rows).astype(BF16)
    for block in range(count):
        for part in range(slices):

            @pl.when((b == block) & (y == part))
            def _():
                out_refs[block % NB * slices + part][block // NB] = placed


def place_rows(wheres, at, mine, theirs):
    _, slices, count, width = mine.shape
    _, tokens, held = at.shape
    slots = len(wheres)
    blocks = jnp.concatenate([w[:NB] for w in wheres])

    def block_spec(b):
        return pl.BlockSpec((1, tokens, held), lambda i, y, where: (where[b], 0, 0))

    rows_spec = pl.BlockSpec((1, 1, count, width), lambda i, y, where: (i, y, 0, 0))
    out = pl.pallas_call(
        partial(place_kernel, slices, held, slots),
        grid_spec=pltpu.PrefetchScalarGridSpec(
            num_scalar_prefetch=1,
            grid=(NB * slots, slices),
            in_specs=[block_spec(b) for b in range(NB * slots)] + [rows_spec, rows_spec],
            out_specs=[pl.BlockSpec((slots, tokens, width), lambda i, y, where: (0, 0, 0))]
            * (NB * slices),
            scratch_shapes=[pltpu.VMEM((tokens, count), BF16)],
        ),
        out_shape=[jax.ShapeDtypeStruct((slots, tokens, width), BF16)] * (NB * slices),
        compiler_params=pltpu.CompilerParams(vmem_limit_bytes=VMEM),
        cost_estimate=cost(
            flops=2 * NB * slots * slices * count * tokens * width,
            bytes_accessed=2 * NB * slots * slices * (2 * count + tokens) * width,
            transcendentals=0,
        ),
        name="place_rows",
    )(blocks, *([at] * (NB * slots)), mine, theirs)
    return [out[b * slices : (b + 1) * slices] for b in range(NB)]


def weight_kernel(slots, slices, where_ref, *refs):
    rows, gate_grads, up_grads = refs[: 2 * slots], refs[2 * slots : 3 * slots], refs[3 * slots : 4 * slots]
    gate_ref, up_ref = refs[4 * slots :]
    width = rows[0].shape[3]
    for j in range(2 * slices):
        columns = pl.ds(pl.multiple_of(where_ref[2 * NB + j] * width, width), width)
        gate = up = None
        for k in range(slots):
            x = rows[2 * k + j // slices][:, j % slices].reshape(NB * CAP, width)
            terms = matmul_tn(x, gate_grads[k][0]), matmul_tn(x, up_grads[k][0])
            gate, up = terms if gate is None else (gate + terms[0], up + terms[1])
        gate_ref[0, columns, :] = gate
        up_ref[0, columns, :] = up


def weight_down_kernel(slots, slices, where_ref, *refs):
    cots, scaled, down_ref = refs[: 2 * slots], refs[2 * slots : 3 * slots], refs[3 * slots]
    width = cots[0].shape[3]
    for j in range(2 * slices):
        columns = pl.ds(pl.multiple_of(where_ref[2 * NB + j] * width, width), width)
        down = None
        for k in range(slots):
            c = cots[2 * k + j // slices][:, j % slices].reshape(NB * CAP, width)
            term = matmul_tn(scaled[k][0], c)
            down = term if down is None else down + term
        down_ref[0, :, columns] = down


def weight_grads(kernel, where, rows, hiddens, outs, name):
    slots = len(rows)
    held, _, ff = hiddens[0].shape
    slices, width = rows[0][0].shape[1], rows[0][0].shape[3]
    depth = 2 * slices * width
    rows_spec = pl.BlockSpec((NB, slices, CAP, width), lambda e, where: (0, 0, e, 0))
    hidden_spec = pl.BlockSpec((1, NB * CAP, ff), lambda e, where: (e, 0, 0))
    return pl.pallas_call(
        partial(kernel, slots, slices),
        grid_spec=pltpu.PrefetchScalarGridSpec(
            num_scalar_prefetch=1,
            grid=(held,),
            in_specs=[rows_spec] * (2 * slots) + [hidden_spec] * len(hiddens),
            out_specs=[pl.BlockSpec((1, *o), lambda e, where: (e, 0, 0)) for o in outs],
        ),
        out_shape=[jax.ShapeDtypeStruct((held, *o), F32) for o in outs],
        compiler_params=pltpu.CompilerParams(vmem_limit_bytes=VMEM),
        cost_estimate=cost(flops=10**10, bytes_accessed=10**6, transcendentals=0),
        name=name,
    )(where, *[a for pair in rows for a in pair], *hiddens)


def project_kernel(
    in_ref, ag_ref, wq_ref, wk_ref, wv_ref, qg_ref, kg_ref,
    x_ref, inv_ref, qr_ref, kr_ref, q_ref, k_ref, v_ref,
):
    @pl.when(pl.program_id(0) == 0)
    def _():
        for first in range(0, in_ref.shape[0], 256):
            rows = in_ref[first : first + 256, :].astype(F32)
            inverse = lax.rsqrt(jnp.mean(rows * rows, axis=1, keepdims=True) + 1e-05)
            inv_ref[first : first + 256, :] = inverse
            x_ref[first : first + 256, :] = (rows * inverse * ag_ref[...]).astype(BF16)

    x = x_ref[...]
    for w_ref, gain_ref, raw_ref, to_ref in ((wq_ref, qg_ref, qr_ref, q_ref), (wk_ref, kg_ref, kr_ref, k_ref)):
        raw = matmul(x, w_ref[...])
        raw_ref[...] = raw
        for h in range(raw.shape[1] // HD):
            part = raw[:, h * HD : (h + 1) * HD]
            inverse = lax.rsqrt(jnp.mean(part * part, axis=1, keepdims=True) + 1e-06)
            gain = gain_ref[:, h * HD : (h + 1) * HD]
            to_ref[:, h * HD : (h + 1) * HD] = (part * inverse * gain).astype(BF16)
    v_ref[...] = matmul(x, wv_ref[...]).astype(BF16)


def project(inputs, attn_gain, w_query, w_key, w_value, query_gain, key_gain):
    tokens, depth = inputs.shape
    columns = w_query.shape[1]
    step = min(256, columns)
    whole = pl.BlockSpec((tokens, depth), lambda i: (0, 0))
    weight = pl.BlockSpec((depth, step), lambda i: (0, i))
    gain = pl.BlockSpec((1, step), lambda i: (0, i))
    out = pl.BlockSpec((tokens, step), lambda i: (0, i))
    return pl.pallas_call(
        project_kernel,
        grid=(columns // step,),
        in_specs=[whole, pl.BlockSpec((1, depth), lambda i: (0, 0)), weight, weight, weight, gain, gain],
        out_specs=[whole, pl.BlockSpec((tokens, 1), lambda i: (0, 0))] + [out] * 5,
        out_shape=[
            jax.ShapeDtypeStruct((tokens, depth), BF16),
            jax.ShapeDtypeStruct((tokens, 1), F32),
        ]
        + [jax.ShapeDtypeStruct((tokens, columns), t) for t in (F32, F32, BF16, BF16, BF16)],
        compiler_params=pltpu.CompilerParams(vmem_limit_bytes=VMEM),
        cost_estimate=cost(
            flops=6 * tokens * depth * columns,
            bytes_accessed=4 * tokens * depth + 6 * depth * columns + 14 * tokens * columns,
            transcendentals=0,
        ),
        name="project",
    )(
        inputs, attn_gain.reshape(1, -1), w_query, w_key, w_value,
        query_gain.reshape(1, -1), key_gain.reshape(1, -1),
    )


def allowed_pairs(pieces_ref, base, first, rows, keys):
    query = first + lax.broadcasted_iota(jnp.int32, (rows, 1), 0)
    key = lax.broadcasted_iota(jnp.int32, (1, keys), 1)

    def piece_of(at, other):
        found = jnp.full(at.shape, other, jnp.int32)
        for j in range(2):
            start, length = pieces_ref[base + j], pieces_ref[base + 2 + j]
            found = jnp.where((at >= start) & (at < start + length), j, found)
        return found

    return (key <= query) | (piece_of(query, -1) == piece_of(key, -2))


def query_blocks():
    half = LENGTH // 2
    return ((0, half, half), (half, half, LENGTH))


def attend_kernel(scale, pieces_ref, q_ref, k_ref, v_ref, o_ref, log_ref, top_ref):
    base = pl.program_id(0) * 4
    best = None
    for first, rows, keys in query_blocks():
        allowed = allowed_pairs(pieces_ref, base, first, rows, keys)
        scores = matmul_nt(q_ref[first : first + rows, :], k_ref[:keys, :]) * scale
        masked = jnp.where(allowed, scores, -1e30)
        top = jnp.max(masked, axis=1, keepdims=True)
        weights = jnp.exp(masked - top)
        total = jnp.sum(weights, axis=1, keepdims=True)
        probs = (weights * (1.0 / total)).astype(BF16)
        o_ref[first : first + rows, :] = matmul(probs, v_ref[:keys, :]).astype(BF16)
        log_ref[0, first : first + rows, :] = top + jnp.log(total)
        most = jnp.max(top, axis=0, keepdims=True)
        best = most if best is None else jnp.maximum(best, most)
    top_ref[0] = jnp.broadcast_to(best, (8, HD))


def attend(pieces, queries, keys, values, scale):
    tokens, columns = queries.shape
    sequences, heads = tokens // LENGTH, columns // HD
    block = pl.BlockSpec((LENGTH, HD), lambda s, h, pieces: (s, h))
    return pl.pallas_call(
        partial(attend_kernel, scale),
        grid_spec=pltpu.PrefetchScalarGridSpec(
            num_scalar_prefetch=1,
            grid=(sequences, heads),
            in_specs=[block] * 3,
            out_specs=[
                block,
                pl.BlockSpec((1, LENGTH, 1), lambda s, h, pieces: (h, s, 0)),
                pl.BlockSpec((1, 8, HD), lambda s, h, pieces: (s * heads + h, 0, 0)),
            ],
        ),
        out_shape=[
            jax.ShapeDtypeStruct((tokens, columns), BF16),
            jax.ShapeDtypeStruct((heads, tokens, 1), F32),
            jax.ShapeDtypeStruct((sequences * heads, 8, HD), F32),
        ],
        compiler_params=pltpu.CompilerParams(vmem_limit_bytes=VMEM),
        cost_estimate=cost(
            flops=4 * tokens * LENGTH * columns,
            bytes_accessed=8 * tokens * columns,
            transcendentals=tokens * heads * LENGTH,
        ),
        name="attend",
    )(pieces, queries, keys, values)


def attend_back_kernel(
    scale, pieces_ref, q_ref, k_ref, v_ref, g_ref, log_ref, qr_ref, kr_ref, qg_ref, kg_ref,
    gq_ref, gk_ref, gv_ref, gqg_ref, gkg_ref, dq_ref, dk_ref, dv_ref,
):
    base = pl.program_id(0) * 4
    blocks = query_blocks()
    for first, rows, keys in blocks[::-1]:
        allowed = allowed_pairs(pieces_ref, base, first, rows, keys)
        q, g = q_ref[first : first + rows, :], g_ref[first : first + rows, :]
        k, v = k_ref[:keys, :], v_ref[:keys, :]
        scores = matmul_nt(q, k) * scale
        probs = jnp.exp(jnp.where(allowed, scores, -1e30) - log_ref[0, first : first + rows, :])
        grad_p = matmul_nt(g, v)
        delta = jnp.sum(probs * grad_p, axis=1, keepdims=True)
        grad_s = (probs * (grad_p - delta)).astype(BF16)
        dq_ref[first : first + rows, :] = matmul(grad_s, k) * scale
        dk = matmul_tn(grad_s, q) * scale
        dv = matmul_tn(probs.astype(BF16), g)
        if keys == LENGTH:
            dk_ref[...] = dk
            dv_ref[...] = dv
        else:
            dk_ref[:keys, :] += dk
            dv_ref[:keys, :] += dv
    gv_ref[...] = dv_ref[...].astype(BF16)
    for raw_ref, gain_ref, grad_ref, to_ref, sum_ref in (
        (qr_ref, qg_ref, dq_ref, gq_ref, gqg_ref),
        (kr_ref, kg_ref, dk_ref, gk_ref, gkg_ref),
    ):
        raw, grad = raw_ref[...], grad_ref[...]
        inverse = lax.rsqrt(jnp.mean(raw * raw, axis=1, keepdims=True) + 1e-06)
        hat = raw * inverse
        up = grad * gain_ref[...]
        mean = jnp.mean(up * hat, axis=1, keepdims=True)
        to_ref[...] = (inverse * (up - hat * mean)).astype(BF16)
        sum_ref[0] = jnp.sum(grad * hat, axis=0, keepdims=True)


def attend_back(pieces, queries, keys, values, grads, logs, query_raw, key_raw, query_gain, key_gain, scale):
    tokens, columns = queries.shape
    sequences, heads = tokens // LENGTH, columns // HD
    block = pl.BlockSpec((LENGTH, HD), lambda s, h, pieces: (s, h))
    gain = pl.BlockSpec((1, HD), lambda s, h, pieces: (0, h))
    sums = pl.BlockSpec((1, 1, HD), lambda s, h, pieces: (s, 0, h))
    return pl.pallas_call(
        partial(attend_back_kernel, scale),
        grid_spec=pltpu.PrefetchScalarGridSpec(
            num_scalar_prefetch=1,
            grid=(sequences, heads),
            in_specs=[block] * 4
            + [pl.BlockSpec((1, LENGTH, 1), lambda s, h, pieces: (h, s, 0)), block, block, gain, gain],
            out_specs=[block, block, block, sums, sums],
            scratch_shapes=[pltpu.VMEM((LENGTH, HD), F32)] * 3,
        ),
        out_shape=[jax.ShapeDtypeStruct((tokens, columns), BF16)] * 3
        + [jax.ShapeDtypeStruct((sequences, 1, columns), F32)] * 2,
        compiler_params=pltpu.CompilerParams(vmem_limit_bytes=VMEM),
        cost_estimate=cost(
            flops=10 * tokens * LENGTH * columns,
            bytes_accessed=22 * tokens * columns,
            transcendentals=tokens * heads * LENGTH,
        ),
        name="attend_back",
    )(
        pieces, queries, keys, values, grads, logs, query_raw, key_raw,
        query_gain.reshape(1, -1), key_gain.reshape(1, -1),
    )


def expert_steps(slots):
    order = list(ORDER) if is_cube() else list(range(slots))
    steps = [("cot", order[0]), ("row", order[0]), ("cot", order[1]), ("exp", order[0])]
    for i, k in enumerate(order):
        if i + 1 < slots:
            steps.append(("row", order[i + 1]))
        else:
            steps.append(("down", 0))
        if i + 2 < slots:
            steps.append(("cot", order[i + 2]))
        steps.append(("place", k))
        if i + 1 < slots:
            steps.append(("exp", order[i + 1]))
    return steps


def due(step, seen):
    return [seen[name] for name in DUE.get(step, ()) if name in seen]


def per_device(
    inputs,
    attn_gain,
    w_query,
    w_key,
    w_value,
    w_output,
    query_gain,
    key_gain,
    moe_gain,
    w_router,
    w_gate,
    w_up,
    w_down,
    routes,
    piece_start,
    piece_length,
    clip_threshold,
    cotangent,
):
    tokens_here, width = inputs.shape
    slice_width = cotangent.shape[1]
    owner = lax.axis_index("expert")
    column = lax.axis_index("tensor") * slice_width
    heads_here = query_gain.shape[0] // HD
    experts_here = w_gate.shape[0]
    owners = lax.axis_size("expert")
    sequences = tokens_here // LENGTH
    scale = 1.0 / math.sqrt(HD)
    where = slot_blocks()
    slots = len(where)
    slices = lax.axis_size("tensor") // 2

    def own_columns(value):
        return lax.dynamic_slice_in_dim(value, column, slice_width, value.ndim - 1)

    seen = {}
    all_routes = gather_routes(routes.T)
    cot_slots = gather_slots(cotangent.astype(BF16), "c", seen)
    order = tensor_order()

    held_ids = owner * experts_here + jnp.arange(experts_here, dtype=jnp.int32)
    chosen = jnp.any(all_routes[:, None] == held_ids[None, :, None, None], axis=2)
    places = jnp.arange(tokens_here, dtype=jnp.int32)
    before = (places[:, None] < places[None, :]).astype(BF16)
    earlier = jnp.einsum(
        "set,tu->seu", chosen.astype(BF16), before, preferred_element_type=F32
    ).astype(jnp.int32)
    pos = jnp.where(chosen, earlier, -1)
    at = jnp.where(
        chosen, earlier + jnp.arange(experts_here, dtype=jnp.int32)[None, :, None] * CAP, -1
    ).transpose(0, 2, 1)

    output_pieces = [lax.dynamic_slice_in_dim(w_output, o * slice_width, slice_width, 1) for o in order]
    normed_a, attn_inv, query_raw, key_raw, queries, keys, values = project(
        inputs, attn_gain, w_query, w_key, w_value, query_gain, key_gain
    )
    pieces = jnp.concatenate([piece_start, piece_length], axis=1).reshape(-1)
    attended, logs, tops = attend(
        after(pieces, values, all_routes), queries, keys, values, scale
    )
    head_top = jnp.max(tops[:, 0, 0].reshape(sequences, heads_here), axis=0)
    attended = after(attended, *due("attended", seen))
    branch = tensor_scatter(partial(matmul, attended), output_pieces, "b", seen)
    residual = own_columns(inputs).astype(F32) + branch
    gain_slice = own_columns(moe_gain)
    router_slice = lax.dynamic_slice_in_dim(w_router, column, slice_width, 0)
    lifted = residual * gain_slice
    row_sums = tensor_sum(
        jnp.concatenate(
            [
                lax.dot_general(
                    router_slice,
                    lifted.astype(BF16),
                    (((0,), (1,)), ((), ())),
                    preferred_element_type=F32,
                ),
                jnp.sum(residual * residual, axis=1)[None],
            ],
            axis=0,
        )
    )
    moe_inv_row = lax.rsqrt(row_sums[E] / width + 1e-05)
    moe_inv = moe_inv_row[:, None]
    normed_m = (lifted * moe_inv).astype(BF16)
    normed_m = after(normed_m, *due("normed", seen))

    normed_slots = gather_slots(normed_m, "n", seen)
    router = jax.nn.softmax(row_sums[:E] * moe_inv_row[None], axis=0)
    gate = lax.all_to_all(
        router.reshape(owners, experts_here, tokens_here),
        "expert",
        split_axis=0,
        concat_axis=0,
        tiled=True,
    )

    rows, cots, back, sums = [None] * slots, [None] * slots, [None] * slots, [None] * slots
    scaled, gate_grads, up_grads, probs = [None] * slots, [None] * slots, [None] * slots, [None] * slots
    last = normed_m
    downs = {}

    def turn(name, k):
        return after(where[k], last, *due(name, seen))

    def lower(k):
        keep, give = down_slots(turn("down" + str(k), 0), scaled[2 * k : 2 * k + 2], w_down, slices)
        downs[k] = (keep, core_swap(give))
        seen["sd" + str(k)] = downs[k][1]
        return keep

    for kind, k in expert_steps(slots):
        now = turn(kind + str(k), k)
        if kind == "cot":
            last = pick_rows(now, pos, cot_slots[k])
            cots[k] = (last, core_swap(last))
            seen["sc" + str(k)] = cots[k][1]
        elif kind == "row":
            last = pick_rows(now, pos, normed_slots[k])
            rows[k] = (last, core_swap(last))
            seen["sr" + str(k)] = rows[k][1]
        elif kind == "exp":
            scaled[k], gate_grads[k], up_grads[k], probs[k], keep, give = expert_slot(
                now, pos, gate, rows[k], cots[k], w_gate, w_up, w_down
            )
            last = scaled[k]
            back[k] = (keep, core_swap(give))
            seen["sg" + str(k)] = back[k][1]
        elif kind == "down":
            last = lower(k)
        else:
            placed = place_rows([now], at, *back[k])
            last = placed[0][0]
            back[k] = [[a[0] for a in b] for b in placed]
            if is_cube():
                sums[k], sent = scatter_plane(back[k], k in ODD)
                if k:
                    sums[k] = sent["z"] = send(sums[k].astype(BF16), dz=k)
                seen.update({"e" + link + str(k): value for link, value in sent.items()})
    for k in range(1, slots // 2):
        last = lower(k)
    pairs = [place_rows([turn("pd0", 0), where[1]], at, *downs[0])]
    last = pairs[0][0][0]
    grad_gate, grad_up = weight_grads(
        weight_kernel,
        turn("weight", 0),
        rows,
        gate_grads + up_grads,
        [w_gate.shape[1:]] * 2,
        "weight_grads",
    )
    if is_cube():
        expert_path = added(*[after(s, grad_gate) for s in sums])
    else:
        expert_path = scatter_all(back)

    prob_grads = jnp.stack([probs[k][:, b] for k in range(slots) for b in range(NB)])
    if is_cube():
        prob_grads = prob_grads[jnp.arange(owners, dtype=jnp.int32) ^ owner]
    prob_grads = lax.all_to_all(prob_grads, "expert", split_axis=0, concat_axis=0, tiled=True)
    prob_grads = tensor_sum(prob_grads.reshape(E, tokens_here))
    grad_logits = (
        router * (prob_grads - jnp.sum(router * prob_grads, axis=0, keepdims=True))
    ).astype(BF16)
    grad_router = lax.dot_general(
        normed_m, grad_logits, (((0,), (1,)), ((), ())), preferred_element_type=F32
    )
    router_path = lax.dot_general(
        grad_logits, router_slice, (((0,), (1,)), ((), ())), preferred_element_type=F32
    )
    grad_normed = expert_path + router_path
    moe_hat = residual * moe_inv
    grad_moe_gain = jnp.sum(grad_normed * moe_hat, axis=0)
    upstream = grad_normed * gain_slice
    mean_dot = tensor_sum(jnp.sum(upstream * moe_hat, axis=-1).reshape(8, -1)).reshape(-1, 1) / width
    grad_residual = cotangent + moe_inv * (upstream - moe_hat * mean_dot)
    branch_pieces = tensor_gather(grad_residual.astype(BF16))
    grad_branch = jnp.concatenate(branch_pieces, axis=1)

    for k in range(1, slots // 2):
        now = after(where[2 * k], branch_pieces[0])
        pairs.append(place_rows([now, where[2 * k + 1]], at, *downs[k]))
    last = pairs[-1][0][0]
    if is_cube():
        pairs = [[[after(a, branch_pieces[1]) for a in b] for b in pair] for pair in pairs]
    mixture = scatter_pairs(pairs, seen)
    out = residual + mixture

    grad_output = matmul_tn(attended, grad_branch).astype(BF16)
    grad_attended = matmul_nt(grad_branch, jnp.concatenate(output_pieces, axis=1)).astype(BF16)
    grad_attended = after(grad_attended, grad_output, last)
    grad_query_raw, grad_key_raw, grad_v, grad_query_gain, grad_key_gain = attend_back(
        pieces, queries, keys, values, grad_attended, logs, query_raw, key_raw, query_gain, key_gain, scale
    )
    grad_raw = jnp.concatenate([grad_query_raw, grad_key_raw, grad_v], axis=1)
    grad_three = matmul_tn(normed_a, grad_raw).astype(BF16)
    sum_output = lax.psum(grad_output, "expert").astype(F32)
    sum_three = lax.psum_scatter(grad_three, "expert", scatter_dimension=0, tiled=True)
    grad_raw = after(grad_raw, grad_three)
    weights = jnp.concatenate([w_query, w_key, w_value], axis=1)
    weight_pieces = [lax.dynamic_slice_in_dim(weights, o * slice_width, slice_width, 0) for o in order]
    grad_normed_a = tensor_scatter(partial(matmul_nt, grad_raw), weight_pieces, "h", seen)
    now = after(where[0], *due("weight_down", seen))
    (grad_down,) = weight_grads(
        weight_down_kernel, now, cots, scaled, [w_down.shape[1:]], "weight_down_grads"
    )
    sum_three = lax.all_gather(sum_three, "expert", tiled=True)
    sum_query, sum_key, sum_value = jnp.split(sum_three.astype(F32), 3, axis=1)
    grad_normed_a = after(grad_normed_a, grad_down)
    attn_hat = own_columns(inputs).astype(F32) * attn_inv
    upstream = grad_normed_a * own_columns(attn_gain)
    grad_attn_gain = jnp.sum(grad_normed_a * attn_hat, axis=0)
    mean_dot = tensor_sum(jnp.sum(upstream * attn_hat, axis=-1).reshape(8, -1)).reshape(-1, 1) / width
    grad_input = grad_residual + attn_inv * (upstream - attn_hat * mean_dot)

    small = jnp.concatenate(
        [
            grad_router.T,
            jnp.stack(
                [
                    grad_attn_gain,
                    grad_moe_gain,
                    jnp.sum(grad_query_gain, axis=(0, 1)),
                    jnp.sum(grad_key_gain, axis=(0, 1)),
                ]
            ),
        ],
        axis=0,
    )
    top_row = jnp.pad(head_top, (0, slice_width - heads_here), constant_values=-3e38)
    small, top_row = expert_total(small, top_row[None])
    head_top = top_row[0, :heads_here]
    sum_moe_gain, sum_query_gain, sum_key_gain = small[E + 1], small[E + 2], small[E + 3]
    every = lax.all_gather(small[: E + 1], "tensor")
    sum_router = every[:, :E].transpose(0, 2, 1).reshape(width, E)
    sum_attn_gain = every[:, E].reshape(width)
    ordered = jnp.zeros_like(sum_output)
    for i, o in enumerate(order):
        ordered = lax.dynamic_update_slice_in_dim(
            ordered, sum_output[:, i * slice_width : (i + 1) * slice_width], o * slice_width, 1
        )
    factor = clip_threshold / jnp.maximum(head_top, clip_threshold)
    spread = jnp.repeat(jnp.sqrt(factor), HD)
    query_clipped = (w_query.astype(F32) * spread[None, :]).astype(BF16)
    key_clipped = (w_key.astype(F32) * spread[None, :]).astype(BF16)
    return (
        out,
        grad_input,
        sum_attn_gain,
        sum_query,
        sum_key,
        sum_value,
        ordered,
        sum_query_gain,
        sum_key_gain,
        sum_moe_gain,
        sum_router,
        grad_gate,
        grad_up,
        grad_down,
        head_top,
        query_clipped,
        key_clipped,
    )


def solution(mesh):
    return jax.shard_map(
        per_device,
        mesh=mesh,
        in_specs=(
            P("expert", None),
            P(),
            P(None, "tensor"),
            P(None, "tensor"),
            P(None, "tensor"),
            P("tensor", None),
            P("tensor"),
            P("tensor"),
            P(),
            P(),
            P("expert", None, "tensor"),
            P("expert", None, "tensor"),
            P("expert", "tensor", None),
            P("expert", None),
            P("expert", None),
            P("expert", None),
            P("tensor"),
            P("expert", "tensor"),
        ),
        out_specs=(
            P("expert", "tensor"),
            P("expert", "tensor"),
            P(),
            P(None, "tensor"),
            P(None, "tensor"),
            P(None, "tensor"),
            P("tensor", None),
            P("tensor"),
            P("tensor"),
            P("tensor"),
            P(),
            P("expert", None, "tensor"),
            P("expert", None, "tensor"),
            P("expert", "tensor", None),
            P("tensor"),
            P(None, "tensor"),
            P(None, "tensor"),
        ),
        check_vma=False,
    )
```

```python
from functools import partial
import math

import jax
import jax.numpy as jnp
from jax import lax
from jax.experimental import pallas as pl
from jax.experimental.pallas import tpu as pltpu
from jax.sharding import PartitionSpec as P

HD = 128
E = 64
TOP = 8
LENGTH = 1024
CAP = 160
NB = 2
BOTH = ("expert", "tensor")
F32 = jnp.float32
BF16 = jnp.bfloat16
VMEM = 60 * 1024 * 1024
WEIGHT = 16
ORDER = (0, 2, 3, 1)
ODD = (1, 2)
DUE = {
    "attended": ("cx0", "cy0", "cz2"),
    "normed": ("cd0",),
    "row0": ("cx2", "cz3", "cy2"),
    "exp0": ("cx3",),
    "row2": ("sc2", "cy3"),
    "cot3": ("sg0",),
    "place0": ("sr2",),
    "exp2": ("sc3",),
    "cot1": ("sg2",),
    "place2": ("sr3", "ed0"),
    "exp3": ("sc1",),
    "place3": ("ex0", "ey0", "ed2"),
    "down1": ("ex2", "ey2", "ed3"),
    "pd0": ("ed1", "sd0"),
    "weight": ("ex3", "ey3", "ex1", "ey1"),
    "normed_grad": ("gd0",),
    "weight_down": ("hs", "gd1"),
}


def cost(flops, bytes_accessed, transcendentals):
    return pl.CostEstimate(
        flops=flops * WEIGHT, bytes_accessed=bytes_accessed * WEIGHT, transcendentals=transcendentals * WEIGHT
    )


def matmul(left, right):
    return jnp.dot(left, right, preferred_element_type=F32)


def matmul_nt(left, right):
    return lax.dot_general(left, right, (((1,), (1,)), ((), ())), preferred_element_type=F32)


def matmul_tn(left, right):
    return lax.dot_general(left, right, (((0,), (0,)), ((), ())), preferred_element_type=F32)


def after(value, *others):
    return lax.optimization_barrier((value, *others))[0]


def flip(dz, dx, dy, dc):
    pairs = []
    for z in range(4):
        for x in range(2):
            for y in range(2):
                for c in range(2):
                    pairs.append(
                        (
                            ((z * 2 + x) * 2 + y) * 2 + c,
                            (((z ^ dz) * 2 + (x ^ dx)) * 2 + (y ^ dy)) * 2 + (c ^ dc),
                        )
                    )
    return pairs


def send(value, dz=0, dx=0, dy=0, dc=0):
    return lax.ppermute(value, BOTH, flip(dz, dx, dy, dc))


def is_cube():
    return lax.axis_size("expert") == 8 and lax.axis_size("tensor") == 4


def core_swap(value):
    if is_cube():
        return send(value, dc=1)
    count = lax.axis_size("tensor")
    return lax.ppermute(value, "tensor", [(i, i ^ 1) for i in range(count)])


def slot_blocks():
    owner, part = lax.axis_index("expert"), lax.axis_index("tensor")
    core = part % 2
    found = []
    for k in range(lax.axis_size("expert") // NB):
        places = [k * NB + b for b in range(NB)]
        if is_cube():
            owners = [owner ^ p for p in places]
            mine = [part ^ (y * 2) for y in range(2)]
        else:
            owners = places
            mine = [y * 2 + core for y in range(lax.axis_size("tensor") // 2)]
        theirs = [m ^ 1 for m in mine]
        rows = [m // 2 for m in mine]
        found.append(
            jnp.stack([jnp.asarray(v, jnp.int32) for v in places + owners + mine + theirs + rows])
        )
    return found


def gather_routes(routes):
    if not is_cube():
        return lax.all_gather(routes, "expert")
    both = jnp.stack([routes, send(routes, dx=1)])
    both = jnp.concatenate([both, send(both, dz=1)])
    return jnp.concatenate([both, send(both, dz=2)])


def same_core():
    count = lax.axis_size("tensor")
    return [[y * 2 + c for y in range(count // 2)] for c in range(2)]


def gather_all(own):
    owners, parts = lax.axis_size("expert"), lax.axis_size("tensor")
    groups = [[e * parts + t for e in range(owners) for t in range(c, parts, 2)] for c in range(2)]
    full = lax.all_gather(own, BOTH, axis_index_groups=groups)
    return full.reshape(owners, parts // 2, *own.shape)


def gather_slots(own, tag, seen):
    if not is_cube():
        return [gather_all(own)] * (lax.axis_size("expert") // NB)
    slots = []
    for k in range(4):
        block = send(own, dz=k) if k else own
        over_x = send(block, dx=1)
        over_y = send(block, dy=1)
        far = send(over_x, dy=1) if k in ODD else send(over_y, dx=1)
        for link, value in zip("zxyd", (block, over_x, over_y, far)):
            seen[tag + link + str(k)] = value
        slots.append([[block, over_y], [over_x, far]])
    return slots


def added(*terms):
    return sum(t.astype(F32) for t in terms)


def scatter_plane(parts, odd):
    near, over_y, over_x, far = parts[0][0], parts[0][1], parts[1][0], parts[1][1]
    if odd:
        far = send(far, dy=1)
        over_x, over_y = added(over_x, far).astype(BF16), after(over_y, far)
    else:
        far = send(far, dx=1)
        over_x, over_y = after(over_x, far), added(over_y, far).astype(BF16)
    from_x, from_y = send(over_x, dx=1), send(over_y, dy=1)
    return added(near, from_x, from_y), {"d": far, "x": from_x, "y": from_y}


def scatter_all(slots):
    full = jnp.stack(
        [jnp.stack([s[b][y] for s in slots for b in range(NB)]) for y in range(len(slots[0][0]))]
    )
    mine = lax.psum_scatter(full, "tensor", axis_index_groups=same_core(), scatter_dimension=0)
    return lax.psum_scatter(mine, "expert", scatter_dimension=0).astype(F32)


def scatter_pairs(pairs, seen):
    if not is_cube():
        return scatter_all(
            [[[a[i] for a in b] for b in pair] for pair in pairs for i in range(pair[0][0].shape[0])]
        )
    (low, low_sent), (high, high_sent) = (scatter_plane(p, True) for p in pairs)
    seen.update({"g" + link + "0": value for link, value in low_sent.items()})
    seen.update({"g" + link + "1": value for link, value in high_sent.items()})
    total = low + send(high.astype(BF16), dz=2).astype(F32)
    return total[0] + send(total[1].astype(BF16), dz=1).astype(F32)


def tensor_order():
    part = lax.axis_index("tensor")
    if is_cube():
        return [part ^ i for i in (0, 2, 1, 3)]
    return [jnp.int32(i) for i in range(lax.axis_size("tensor"))]


def order_spots():
    if not is_cube():
        return lambda s: s
    part = lax.axis_index("tensor")
    return lambda s: (part ^ s) % 2 * 2 + (part ^ s) // 2


def tensor_gather(own):
    if not is_cube():
        full = lax.all_gather(own, "tensor")
        return [full[i] for i in range(full.shape[0])]
    over_y = send(own, dy=1)
    return [own, over_y, core_swap(own), core_swap(over_y)]


def tensor_scatter(product, pieces, tag, seen):
    if not is_cube():
        full = jnp.concatenate([product(p).astype(BF16) for p in pieces], axis=1)
        return lax.psum_scatter(full, "tensor", scatter_dimension=1, tiled=True).astype(F32)
    away_y = product(pieces[3]).astype(BF16)
    away = product(pieces[2]).astype(BF16)
    from_y, near = core_swap(away_y), core_swap(away)
    away = added(product(pieces[1]), from_y).astype(BF16)
    over_y = send(away, dy=1)
    seen.update({tag + "0": from_y, tag + "1": near, tag + "y": over_y, tag + "s": away})
    return added(product(pieces[0]), near, over_y)


def tensor_sum(value):
    if not is_cube():
        return lax.psum(value, "tensor")
    value = value + core_swap(value)
    return value + send(value, dy=1)


def row_blocks():
    if not is_cube():
        return [jnp.int32(i) for i in range(8)]
    owner = lax.axis_index("expert")
    return [owner ^ (b | first << 1 | second << 2) for b in (0, 1) for first in (0, 1) for second in (0, 1)]


def expert_sum(value):
    half = value.shape[0] // 2
    if not is_cube():
        value = lax.psum(value, "expert")
        return value[:half], value[half:]
    for step in ({"dx": 1}, {"dz": 1}, {"dz": 2}):
        half = value.shape[0] // 2
        value = added(value[:half], send(value[half:], **step)).astype(BF16)
    for step in ({"dz": 2}, {"dz": 1}):
        value = jnp.concatenate([value, send(value, **step)], axis=0)
    return value, send(value, dx=1)


def expert_total(sums, tops):
    if not is_cube():
        return lax.psum(sums, "expert"), lax.pmax(tops, "expert")
    count = sums.shape[0]
    both = jnp.concatenate([sums, tops], axis=0)
    for step in ({"dx": 1}, {"dz": 1}, {"dz": 2}):
        other = send(both, **step)
        both = jnp.concatenate([both[:count] + other[:count], jnp.maximum(both[count:], other[count:])])
    return both[:count], both[count:]


def one_hot(pos_row):
    rows = lax.broadcasted_iota(jnp.int32, (CAP, pos_row.shape[1]), 0)
    return rows == pos_row


def as_bf16(mask):
    return jnp.where(mask, 1.0, 0.0).astype(BF16)


def pick_kernel(group, slices, where_ref, *refs):
    pos_refs, x_refs = refs[:NB], refs[NB : NB + NB * slices]
    out_ref, hot_ref = refs[-2:]
    step = pl.program_id(0)
    for b in range(NB):
        for i in range(group):
            hot_ref[b, i * CAP : (i + 1) * CAP, :] = as_bf16(
                one_hot(pos_refs[b][0, pl.ds(step * group + i, 1), :])
            )
        for y in range(slices):
            out_ref[b, y] = matmul(hot_ref[b], x_refs[b * slices + y][...]).astype(BF16)


def pick_rows(where, pos, blocks):
    held = pos.shape[1]
    group = 2
    if isinstance(blocks, list):
        slices = len(blocks[0])
        flat = [a for b in blocks for a in b]
        tokens, width = flat[0].shape
        specs = [pl.BlockSpec((tokens, width), lambda i, where: (0, 0)) for _ in flat]
    else:
        slices, tokens, width = blocks.shape[1:]
        flat = [blocks] * (NB * slices)

        def part_spec(b, y):
            return pl.BlockSpec(
                (None, None, tokens, width),
                lambda i, where: (where[NB + b], where[2 * NB + 2 * slices + y], 0, 0),
            )

        specs = [part_spec(b, y) for b in range(NB) for y in range(slices)]

    def block_spec(b):
        return pl.BlockSpec((1, held, tokens), lambda i, where: (where[b], 0, 0))

    return pl.pallas_call(
        partial(pick_kernel, group, slices),
        grid_spec=pltpu.PrefetchScalarGridSpec(
            num_scalar_prefetch=1,
            grid=(held // group,),
            in_specs=[block_spec(b) for b in range(NB)]
            + specs,
            out_specs=pl.BlockSpec(
                (NB, slices, group * CAP, width), lambda i, where: (0, 0, i, 0)
            ),
            scratch_shapes=[pltpu.VMEM((NB, group * CAP, tokens), BF16)],
        ),
        out_shape=jax.ShapeDtypeStruct((NB, slices, held * CAP, width), BF16),
        compiler_params=pltpu.CompilerParams(vmem_limit_bytes=VMEM),
        cost_estimate=cost(
            flops=2 * NB * slices * held * CAP * tokens * width,
            bytes_accessed=2 * NB * slices * (held * CAP + tokens) * width,
            transcendentals=0,
        ),
        name="pick_rows",
    )(where, *([pos] * NB), *flat)


def expert_kernel(slices, where_ref, *refs):
    pos_refs, gate_refs = refs[:NB], refs[NB : 2 * NB]
    rows_mine, rows_theirs, cot_mine, cot_theirs, wg_ref, wu_ref, wd_ref = refs[2 * NB : 2 * NB + 7]
    scaled_ref, gate_grad_ref, up_grad_ref, prob_ref, keep_ref, give_ref = refs[2 * NB + 7 :]
    e = pl.program_id(0)
    width = rows_mine.shape[3]
    ff = wg_ref.shape[2]
    gate_pre = jnp.zeros((NB * CAP, ff), F32)
    up_pre = jnp.zeros((NB * CAP, ff), F32)
    grad_hidden = jnp.zeros((NB * CAP, ff), F32)

    def columns(j):
        return pl.ds(pl.multiple_of(where_ref[2 * NB + j] * width, width), width)

    for j in range(2 * slices):
        x_ref, c_ref = (rows_mine, cot_mine) if j < slices else (rows_theirs, cot_theirs)
        x = x_ref[:, j % slices].reshape(NB * CAP, width)
        c = c_ref[:, j % slices].reshape(NB * CAP, width)
        gate_pre = gate_pre + matmul(x, wg_ref[0, columns(j), :])
        up_pre = up_pre + matmul(x, wu_ref[0, columns(j), :])
        grad_hidden = grad_hidden + matmul_nt(c, wd_ref[0, :, columns(j)])
    masks = [one_hot(pos_refs[b][0, pl.ds(e, 1), :]) for b in range(NB)]
    gates = jnp.concatenate(
        [
            jnp.sum(jnp.where(masks[b], gate_refs[b][0, pl.ds(e, 1), :], 0.0), axis=1, keepdims=True)
            for b in range(NB)
        ],
        axis=0,
    )
    sigma = jax.nn.sigmoid(gate_pre)
    swish = gate_pre * sigma
    hidden = (swish * up_pre).astype(BF16).astype(F32)
    prob = jnp.sum(hidden * grad_hidden, axis=1, keepdims=True)
    for b in range(NB):
        prob_ref[0, b : b + 1, :] = jnp.sum(
            jnp.where(masks[b], prob[b * CAP : (b + 1) * CAP], 0.0), axis=0, keepdims=True
        )
    grad_hidden = grad_hidden * gates
    scaled_ref[0] = (hidden * gates).astype(BF16)
    gate_grad = (grad_hidden * up_pre * (sigma * (1.0 + gate_pre * (1.0 - sigma)))).astype(BF16)
    up_grad = (grad_hidden * swish).astype(BF16)
    gate_grad_ref[0] = gate_grad
    up_grad_ref[0] = up_grad
    for j in range(2 * slices):
        to = keep_ref if j < slices else give_ref
        back = matmul_nt(gate_grad, wg_ref[0, columns(j), :]) + matmul_nt(
            up_grad, wu_ref[0, columns(j), :]
        )
        to[:, j % slices] = back.astype(BF16).reshape(NB, CAP, width)


def expert_slot(where, pos, gate, rows, cots, w_gate, w_up, w_down):
    held, depth, ff = w_gate.shape
    tokens = pos.shape[2]
    slices, width = rows[0].shape[1], rows[0].shape[3]

    def block_spec(b):
        return pl.BlockSpec((1, held, tokens), lambda e, where: (where[b], 0, 0))

    rows_spec = pl.BlockSpec((NB, slices, CAP, width), lambda e, where: (0, 0, e, 0))
    rows_shape = jax.ShapeDtypeStruct((NB, slices, held * CAP, width), BF16)
    in_spec = pl.BlockSpec((1, depth, ff), lambda e, where: (e, 0, 0))
    hidden_spec = pl.BlockSpec((1, NB * CAP, ff), lambda e, where: (e, 0, 0))
    hidden_shape = jax.ShapeDtypeStruct((held, NB * CAP, ff), BF16)
    return pl.pallas_call(
        partial(expert_kernel, slices),
        grid_spec=pltpu.PrefetchScalarGridSpec(
            num_scalar_prefetch=1,
            grid=(held,),
            in_specs=[block_spec(b) for b in range(2 * NB)]
            + [rows_spec] * 4
            + [in_spec, in_spec, pl.BlockSpec((1, ff, depth), lambda e, where: (e, 0, 0))],
            out_specs=[hidden_spec] * 3
            + [pl.BlockSpec((1, NB, tokens), lambda e, where: (e, 0, 0)), rows_spec, rows_spec],
        ),
        out_shape=[hidden_shape] * 3
        + [jax.ShapeDtypeStruct((held, NB, tokens), F32), rows_shape, rows_shape],
        compiler_params=pltpu.CompilerParams(vmem_limit_bytes=VMEM),
        cost_estimate=cost(
            flops=10 * NB * held * CAP * depth * ff,
            bytes_accessed=6 * held * depth * ff + 6 * NB * held * CAP * depth,
            transcendentals=NB * held * CAP * ff,
        ),
        name="expert_slot",
    )(where, *([pos] * NB), *([gate] * NB), *rows, *cots, w_gate, w_up, w_down)


def down_kernel(slices, slots, where_ref, *refs):
    scaled_refs, wd_ref, keep_ref, give_ref = refs[:slots], refs[slots], refs[-2], refs[-1]
    width = keep_ref.shape[3]
    for j in range(2 * slices):
        to = keep_ref if j < slices else give_ref
        columns = pl.ds(pl.multiple_of(where_ref[2 * NB + j] * width, width), width)
        for k in range(slots):
            rows = matmul(scaled_refs[k][0], wd_ref[0, :, columns])
            to[k * NB : (k + 1) * NB, j % slices] = rows.astype(BF16).reshape(NB, CAP, width)


def down_slots(where, scaled, w_down, slices):
    held, ff, depth = w_down.shape
    width = depth // (2 * slices)
    slots = len(scaled)
    rows_spec = pl.BlockSpec((slots * NB, slices, CAP, width), lambda e, where: (0, 0, e, 0))
    rows_shape = jax.ShapeDtypeStruct((slots * NB, slices, held * CAP, width), BF16)
    return pl.pallas_call(
        partial(down_kernel, slices, slots),
        grid_spec=pltpu.PrefetchScalarGridSpec(
            num_scalar_prefetch=1,
            grid=(held,),
            in_specs=[pl.BlockSpec((1, NB * CAP, ff), lambda e, where: (e, 0, 0))] * slots
            + [pl.BlockSpec((1, ff, depth), lambda e, where: (e, 0, 0))],
            out_specs=[rows_spec, rows_spec],
        ),
        out_shape=[rows_shape, rows_shape],
        compiler_params=pltpu.CompilerParams(vmem_limit_bytes=VMEM),
        cost_estimate=cost(
            flops=2 * slots * NB * held * CAP * depth * ff,
            bytes_accessed=2 * held * depth * ff + 2 * slots * NB * held * CAP * depth,
            transcendentals=0,
        ),
        name="down_slots",
    )(where, *scaled, w_down)


def place_kernel(slices, held, slots, where_ref, *refs):
    count = NB * slots
    at_refs, mine_ref, theirs_ref = refs[:count], refs[count], refs[count + 1]
    out_refs, hot_ref = refs[count + 2 : -1], refs[-1]
    b, y = pl.program_id(0), pl.program_id(1)
    tokens = hot_ref.shape[0]
    for block in range(count):

        @pl.when((b == block) & (y == 0))
        def _():
            at = at_refs[block][0]
            for tile in range(held * CAP // 128):
                lanes = lax.broadcasted_iota(jnp.int32, (tokens, 128), 1) + tile * 128
                mask = None
                for e in range(tile * 128 // CAP, (tile * 128 + 127) // CAP + 1):
                    hit = at[:, e : e + 1] == lanes
                    mask = hit if mask is None else mask | hit
                hot_ref[:, tile * 128 : (tile + 1) * 128] = as_bf16(mask)

    rows = (mine_ref[0, 0].astype(F32) + theirs_ref[0, 0].astype(F32)).astype(BF16)
    placed = matmul(hot_ref[...], rows).astype(BF16)
    for block in range(count):
        for part in range(slices):

            @pl.when((b == block) & (y == part))
            def _():
                out_refs[block % NB * slices + part][block // NB] = placed


def place_rows(wheres, at, mine, theirs):
    _, slices, count, width = mine.shape
    _, tokens, held = at.shape
    slots = len(wheres)
    blocks = jnp.concatenate([w[:NB] for w in wheres])

    def block_spec(b):
        return pl.BlockSpec((1, tokens, held), lambda i, y, where: (where[b], 0, 0))

    rows_spec = pl.BlockSpec((1, 1, count, width), lambda i, y, where: (i, y, 0, 0))
    out = pl.pallas_call(
        partial(place_kernel, slices, held, slots),
        grid_spec=pltpu.PrefetchScalarGridSpec(
            num_scalar_prefetch=1,
            grid=(NB * slots, slices),
            in_specs=[block_spec(b) for b in range(NB * slots)] + [rows_spec, rows_spec],
            out_specs=[pl.BlockSpec((slots, tokens, width), lambda i, y, where: (0, 0, 0))]
            * (NB * slices),
            scratch_shapes=[pltpu.VMEM((tokens, count), BF16)],
        ),
        out_shape=[jax.ShapeDtypeStruct((slots, tokens, width), BF16)] * (NB * slices),
        compiler_params=pltpu.CompilerParams(vmem_limit_bytes=VMEM),
        cost_estimate=cost(
            flops=2 * NB * slots * slices * count * tokens * width,
            bytes_accessed=2 * NB * slots * slices * (2 * count + tokens) * width,
            transcendentals=0,
        ),
        name="place_rows",
    )(blocks, *([at] * (NB * slots)), mine, theirs)
    return [out[b * slices : (b + 1) * slices] for b in range(NB)]


def weight_kernel(slots, slices, where_ref, *refs):
    rows, gate_grads, up_grads = refs[: 2 * slots], refs[2 * slots : 3 * slots], refs[3 * slots : 4 * slots]
    gate_ref, up_ref = refs[4 * slots :]
    width = rows[0].shape[3]
    for j in range(2 * slices):
        columns = pl.ds(pl.multiple_of(where_ref[2 * NB + j] * width, width), width)
        gate = up = None
        for k in range(slots):
            x = rows[2 * k + j // slices][:, j % slices].reshape(NB * CAP, width)
            terms = matmul_tn(x, gate_grads[k][0]), matmul_tn(x, up_grads[k][0])
            gate, up = terms if gate is None else (gate + terms[0], up + terms[1])
        gate_ref[0, columns, :] = gate
        up_ref[0, columns, :] = up


def weight_down_kernel(slots, slices, where_ref, *refs):
    cots, scaled, down_ref = refs[: 2 * slots], refs[2 * slots : 3 * slots], refs[3 * slots]
    width = cots[0].shape[3]
    for j in range(2 * slices):
        columns = pl.ds(pl.multiple_of(where_ref[2 * NB + j] * width, width), width)
        down = None
        for k in range(slots):
            c = cots[2 * k + j // slices][:, j % slices].reshape(NB * CAP, width)
            term = matmul_tn(scaled[k][0], c)
            down = term if down is None else down + term
        down_ref[0, :, columns] = down


def weight_grads(kernel, where, rows, hiddens, outs, name):
    slots = len(rows)
    held, _, ff = hiddens[0].shape
    slices, width = rows[0][0].shape[1], rows[0][0].shape[3]
    depth = 2 * slices * width
    rows_spec = pl.BlockSpec((NB, slices, CAP, width), lambda e, where: (0, 0, e, 0))
    hidden_spec = pl.BlockSpec((1, NB * CAP, ff), lambda e, where: (e, 0, 0))
    return pl.pallas_call(
        partial(kernel, slots, slices),
        grid_spec=pltpu.PrefetchScalarGridSpec(
            num_scalar_prefetch=1,
            grid=(held,),
            in_specs=[rows_spec] * (2 * slots) + [hidden_spec] * len(hiddens),
            out_specs=[pl.BlockSpec((1, *o), lambda e, where: (e, 0, 0)) for o in outs],
        ),
        out_shape=[jax.ShapeDtypeStruct((held, *o), F32) for o in outs],
        compiler_params=pltpu.CompilerParams(vmem_limit_bytes=VMEM),
        cost_estimate=cost(flops=10**10, bytes_accessed=10**6, transcendentals=0),
        name=name,
    )(where, *[a for pair in rows for a in pair], *hiddens)


def settle_kernel(where_ref, *refs):
    halves, (output_ref, value_ref, query_ref, key_ref) = refs[:6], refs[6:]

    def settle(output, value, both):
        output_ref[...] = output[...].astype(F32).T
        value_ref[...] = value[...].astype(F32)
        width = query_ref.shape[1]
        query_ref[...] = both[:, :width].astype(F32)
        key_ref[...] = both[:, width:].astype(F32)

    @pl.when(pl.program_id(0) < 4)
    def _():
        settle(*halves[0::2])

    @pl.when(pl.program_id(0) >= 4)
    def _():
        settle(*halves[1::2])


def settle_rows(where, output, value, both):
    rows = 2 * value[0].shape[0]
    step = rows // 8
    width = value[0].shape[1]
    near = lambda n: pl.BlockSpec((step, n), lambda i, where: (jnp.minimum(i, 3), 0))
    far = lambda n: pl.BlockSpec((step, n), lambda i, where: (jnp.maximum(i, 4) - 4, 0))
    placed = pl.BlockSpec((step, width), lambda i, where: (where[i], 0))
    return pl.pallas_call(
        settle_kernel,
        grid_spec=pltpu.PrefetchScalarGridSpec(
            num_scalar_prefetch=1,
            grid=(8,),
            in_specs=[s(n) for n in (width, width, 2 * width) for s in (near, far)],
            out_specs=[pl.BlockSpec((width, step), lambda i, where: (0, where[i]))] + [placed] * 3,
        ),
        out_shape=[jax.ShapeDtypeStruct((width, rows), F32)]
        + [jax.ShapeDtypeStruct((rows, width), F32)] * 3,
        compiler_params=pltpu.CompilerParams(vmem_limit_bytes=VMEM),
        cost_estimate=cost(flops=0, bytes_accessed=24 * rows * width, transcendentals=0),
        name="settle_rows",
    )(where, *output, *value, *both)


def project_kernel(
    in_ref, ag_ref, wq_ref, wk_ref, wv_ref, qg_ref, kg_ref,
    x_ref, inv_ref, qr_ref, kr_ref, q_ref, k_ref, v_ref,
):
    @pl.when(pl.program_id(0) == 0)
    def _():
        for first in range(0, in_ref.shape[0], 256):
            rows = in_ref[first : first + 256, :].astype(F32)
            inverse = lax.rsqrt(jnp.mean(rows * rows, axis=1, keepdims=True) + 1e-05)
            inv_ref[first : first + 256, :] = inverse
            x_ref[first : first + 256, :] = (rows * inverse * ag_ref[...]).astype(BF16)

    x = x_ref[...]
    for w_ref, gain_ref, raw_ref, to_ref in ((wq_ref, qg_ref, qr_ref, q_ref), (wk_ref, kg_ref, kr_ref, k_ref)):
        raw = matmul(x, w_ref[...])
        raw_ref[...] = raw
        for h in range(raw.shape[1] // HD):
            part = raw[:, h * HD : (h + 1) * HD]
            inverse = lax.rsqrt(jnp.mean(part * part, axis=1, keepdims=True) + 1e-06)
            gain = gain_ref[:, h * HD : (h + 1) * HD]
            to_ref[:, h * HD : (h + 1) * HD] = (part * inverse * gain).astype(BF16)
    v_ref[...] = matmul(x, wv_ref[...]).astype(BF16)


def project(inputs, attn_gain, w_query, w_key, w_value, query_gain, key_gain):
    tokens, depth = inputs.shape
    columns = w_query.shape[1]
    step = min(256, columns)
    whole = pl.BlockSpec((tokens, depth), lambda i: (0, 0))
    weight = pl.BlockSpec((depth, step), lambda i: (0, i))
    gain = pl.BlockSpec((1, step), lambda i: (0, i))
    out = pl.BlockSpec((tokens, step), lambda i: (0, i))
    return pl.pallas_call(
        project_kernel,
        grid=(columns // step,),
        in_specs=[whole, pl.BlockSpec((1, depth), lambda i: (0, 0)), weight, weight, weight, gain, gain],
        out_specs=[whole, pl.BlockSpec((tokens, 1), lambda i: (0, 0))] + [out] * 5,
        out_shape=[
            jax.ShapeDtypeStruct((tokens, depth), BF16),
            jax.ShapeDtypeStruct((tokens, 1), F32),
        ]
        + [jax.ShapeDtypeStruct((tokens, columns), t) for t in (F32, F32, BF16, BF16, BF16)],
        compiler_params=pltpu.CompilerParams(vmem_limit_bytes=VMEM),
        cost_estimate=cost(
            flops=6 * tokens * depth * columns,
            bytes_accessed=4 * tokens * depth + 6 * depth * columns + 14 * tokens * columns,
            transcendentals=0,
        ),
        name="project",
    )(
        inputs, attn_gain.reshape(1, -1), w_query, w_key, w_value,
        query_gain.reshape(1, -1), key_gain.reshape(1, -1),
    )


def allowed_pairs(pieces_ref, base, first, rows, keys):
    query = first + lax.broadcasted_iota(jnp.int32, (rows, 1), 0)
    key = lax.broadcasted_iota(jnp.int32, (1, keys), 1)

    def piece_of(at, other):
        found = jnp.full(at.shape, other, jnp.int32)
        for j in range(2):
            start, length = pieces_ref[base + j], pieces_ref[base + 2 + j]
            found = jnp.where((at >= start) & (at < start + length), j, found)
        return found

    return (key <= query) | (piece_of(query, -1) == piece_of(key, -2))


def query_blocks():
    half = LENGTH // 2
    return ((0, half, half), (half, half, LENGTH))


def attend_kernel(scale, pieces_ref, q_ref, k_ref, v_ref, o_ref, log_ref, top_ref):
    base = pl.program_id(0) * 4
    best = None
    for first, rows, keys in query_blocks():
        allowed = allowed_pairs(pieces_ref, base, first, rows, keys)
        scores = matmul_nt(q_ref[first : first + rows, :], k_ref[:keys, :]) * scale
        masked = jnp.where(allowed, scores, -1e30)
        top = jnp.max(masked, axis=1, keepdims=True)
        weights = jnp.exp(masked - top)
        total = jnp.sum(weights, axis=1, keepdims=True)
        probs = (weights * (1.0 / total)).astype(BF16)
        o_ref[first : first + rows, :] = matmul(probs, v_ref[:keys, :]).astype(BF16)
        log_ref[0, first : first + rows, :] = top + jnp.log(total)
        most = jnp.max(top, axis=0, keepdims=True)
        best = most if best is None else jnp.maximum(best, most)
    top_ref[0] = jnp.broadcast_to(best, (8, HD))


def attend(pieces, queries, keys, values, scale):
    tokens, columns = queries.shape
    sequences, heads = tokens // LENGTH, columns // HD
    block = pl.BlockSpec((LENGTH, HD), lambda s, h, pieces: (s, h))
    return pl.pallas_call(
        partial(attend_kernel, scale),
        grid_spec=pltpu.PrefetchScalarGridSpec(
            num_scalar_prefetch=1,
            grid=(sequences, heads),
            in_specs=[block] * 3,
            out_specs=[
                block,
                pl.BlockSpec((1, LENGTH, 1), lambda s, h, pieces: (h, s, 0)),
                pl.BlockSpec((1, 8, HD), lambda s, h, pieces: (s * heads + h, 0, 0)),
            ],
        ),
        out_shape=[
            jax.ShapeDtypeStruct((tokens, columns), BF16),
            jax.ShapeDtypeStruct((heads, tokens, 1), F32),
            jax.ShapeDtypeStruct((sequences * heads, 8, HD), F32),
        ],
        compiler_params=pltpu.CompilerParams(vmem_limit_bytes=VMEM),
        cost_estimate=cost(
            flops=4 * tokens * LENGTH * columns,
            bytes_accessed=8 * tokens * columns,
            transcendentals=tokens * heads * LENGTH,
        ),
        name="attend",
    )(pieces, queries, keys, values)


def attend_back_kernel(
    scale, pieces_ref, q_ref, k_ref, v_ref, g_ref, log_ref, qr_ref, kr_ref, qg_ref, kg_ref,
    gq_ref, gk_ref, gv_ref, gqg_ref, gkg_ref, dq_ref, dk_ref, dv_ref,
):
    base = pl.program_id(0) * 4
    blocks = query_blocks()
    for first, rows, keys in blocks[::-1]:
        allowed = allowed_pairs(pieces_ref, base, first, rows, keys)
        q, g = q_ref[first : first + rows, :], g_ref[first : first + rows, :]
        k, v = k_ref[:keys, :], v_ref[:keys, :]
        scores = matmul_nt(q, k) * scale
        probs = jnp.exp(jnp.where(allowed, scores, -1e30) - log_ref[0, first : first + rows, :])
        grad_p = matmul_nt(g, v)
        delta = jnp.sum(probs * grad_p, axis=1, keepdims=True)
        grad_s = (probs * (grad_p - delta)).astype(BF16)
        dq_ref[first : first + rows, :] = matmul(grad_s, k) * scale
        dk = matmul_tn(grad_s, q) * scale
        dv = matmul_tn(probs.astype(BF16), g)
        if keys == LENGTH:
            dk_ref[...] = dk
            dv_ref[...] = dv
        else:
            dk_ref[:keys, :] += dk
            dv_ref[:keys, :] += dv
    gv_ref[...] = dv_ref[...].astype(BF16)
    for raw_ref, gain_ref, grad_ref, to_ref, sum_ref in (
        (qr_ref, qg_ref, dq_ref, gq_ref, gqg_ref),
        (kr_ref, kg_ref, dk_ref, gk_ref, gkg_ref),
    ):
        raw, grad = raw_ref[...], grad_ref[...]
        inverse = lax.rsqrt(jnp.mean(raw * raw, axis=1, keepdims=True) + 1e-06)
        hat = raw * inverse
        up = grad * gain_ref[...]
        mean = jnp.mean(up * hat, axis=1, keepdims=True)
        to_ref[...] = (inverse * (up - hat * mean)).astype(BF16)
        sum_ref[0] = jnp.sum(grad * hat, axis=0, keepdims=True)


def attend_back(pieces, queries, keys, values, grads, logs, query_raw, key_raw, query_gain, key_gain, scale):
    tokens, columns = queries.shape
    sequences, heads = tokens // LENGTH, columns // HD
    block = pl.BlockSpec((LENGTH, HD), lambda s, h, pieces: (s, h))
    gain = pl.BlockSpec((1, HD), lambda s, h, pieces: (0, h))
    sums = pl.BlockSpec((1, 1, HD), lambda s, h, pieces: (s, 0, h))
    return pl.pallas_call(
        partial(attend_back_kernel, scale),
        grid_spec=pltpu.PrefetchScalarGridSpec(
            num_scalar_prefetch=1,
            grid=(sequences, heads),
            in_specs=[block] * 4
            + [pl.BlockSpec((1, LENGTH, 1), lambda s, h, pieces: (h, s, 0)), block, block, gain, gain],
            out_specs=[block, block, block, sums, sums],
            scratch_shapes=[pltpu.VMEM((LENGTH, HD), F32)] * 3,
        ),
        out_shape=[jax.ShapeDtypeStruct((tokens, columns), BF16)] * 3
        + [jax.ShapeDtypeStruct((sequences, 1, columns), F32)] * 2,
        compiler_params=pltpu.CompilerParams(vmem_limit_bytes=VMEM),
        cost_estimate=cost(
            flops=10 * tokens * LENGTH * columns,
            bytes_accessed=22 * tokens * columns,
            transcendentals=tokens * heads * LENGTH,
        ),
        name="attend_back",
    )(
        pieces, queries, keys, values, grads, logs, query_raw, key_raw,
        query_gain.reshape(1, -1), key_gain.reshape(1, -1),
    )


def expert_steps(slots):
    order = list(ORDER) if is_cube() else list(range(slots))
    steps = [("cot", order[0]), ("row", order[0]), ("cot", order[1]), ("exp", order[0])]
    for i, k in enumerate(order):
        if i + 1 < slots:
            steps.append(("row", order[i + 1]))
        else:
            steps.append(("down", 0))
        if i + 2 < slots:
            steps.append(("cot", order[i + 2]))
        steps.append(("place", k))
        if i + 1 < slots:
            steps.append(("exp", order[i + 1]))
    return steps


def due(step, seen):
    return [seen[name] for name in DUE.get(step, ()) if name in seen]


def per_device(
    inputs,
    attn_gain,
    w_query,
    w_key,
    w_value,
    w_output,
    query_gain,
    key_gain,
    moe_gain,
    w_router,
    w_gate,
    w_up,
    w_down,
    routes,
    piece_start,
    piece_length,
    clip_threshold,
    cotangent,
):
    tokens_here, width = inputs.shape
    slice_width = cotangent.shape[1]
    owner = lax.axis_index("expert")
    column = lax.axis_index("tensor") * slice_width
    heads_here = query_gain.shape[0] // HD
    experts_here = w_gate.shape[0]
    owners = lax.axis_size("expert")
    sequences = tokens_here // LENGTH
    scale = 1.0 / math.sqrt(HD)
    where = slot_blocks()
    slots = len(where)
    slices = lax.axis_size("tensor") // 2

    def own_columns(value):
        return lax.dynamic_slice_in_dim(value, column, slice_width, value.ndim - 1)

    seen = {}
    all_routes = gather_routes(routes.T)
    cot_slots = gather_slots(cotangent.astype(BF16), "c", seen)
    order = tensor_order()

    held_ids = owner * experts_here + jnp.arange(experts_here, dtype=jnp.int32)
    chosen = jnp.any(all_routes[:, None] == held_ids[None, :, None, None], axis=2)
    places = jnp.arange(tokens_here, dtype=jnp.int32)
    before = (places[:, None] < places[None, :]).astype(BF16)
    earlier = jnp.einsum(
        "set,tu->seu", chosen.astype(BF16), before, preferred_element_type=F32
    ).astype(jnp.int32)
    pos = jnp.where(chosen, earlier, -1)
    at = jnp.where(
        chosen, earlier + jnp.arange(experts_here, dtype=jnp.int32)[None, :, None] * CAP, -1
    ).transpose(0, 2, 1)

    output_pieces = [lax.dynamic_slice_in_dim(w_output, o * slice_width, slice_width, 1) for o in order]
    normed_a, attn_inv, query_raw, key_raw, queries, keys, values = project(
        inputs, attn_gain, w_query, w_key, w_value, query_gain, key_gain
    )
    blocks = row_blocks()
    normed_rows = jnp.concatenate(
        [lax.dynamic_slice_in_dim(normed_a, r * (width // 8), width // 8, 1) for r in blocks], axis=1
    )
    pieces = jnp.concatenate([piece_start, piece_length], axis=1).reshape(-1)
    attended, logs, tops = attend(
        after(pieces, values, all_routes), queries, keys, values, scale
    )
    head_top = jnp.max(tops[:, 0, 0].reshape(sequences, heads_here), axis=0)
    attended = after(attended, *due("attended", seen))
    branch = tensor_scatter(partial(matmul, attended), output_pieces, "b", seen)
    residual = own_columns(inputs).astype(F32) + branch
    gain_slice = own_columns(moe_gain)
    router_slice = lax.dynamic_slice_in_dim(w_router, column, slice_width, 0)
    lifted = residual * gain_slice
    row_sums = tensor_sum(
        jnp.concatenate(
            [
                lax.dot_general(
                    router_slice,
                    lifted.astype(BF16),
                    (((0,), (1,)), ((), ())),
                    preferred_element_type=F32,
                ),
                jnp.sum(residual * residual, axis=1)[None],
            ],
            axis=0,
        )
    )
    moe_inv_row = lax.rsqrt(row_sums[E] / width + 1e-05)
    moe_inv = moe_inv_row[:, None]
    normed_m = (lifted * moe_inv).astype(BF16)
    normed_m = after(normed_m, *due("normed", seen))

    normed_slots = gather_slots(normed_m, "n", seen)
    router = jax.nn.softmax(row_sums[:E] * moe_inv_row[None], axis=0)
    gate = lax.all_to_all(
        router.reshape(owners, experts_here, tokens_here),
        "expert",
        split_axis=0,
        concat_axis=0,
        tiled=True,
    )

    rows, cots, back, sums = [None] * slots, [None] * slots, [None] * slots, [None] * slots
    scaled, gate_grads, up_grads, probs = [None] * slots, [None] * slots, [None] * slots, [None] * slots
    last = normed_m
    downs = {}

    def turn(name, k):
        return after(where[k], last, *due(name, seen))

    def lower(k):
        keep, give = down_slots(turn("down" + str(k), 0), scaled[2 * k : 2 * k + 2], w_down, slices)
        downs[k] = (keep, core_swap(give))
        seen["sd" + str(k)] = downs[k][1]
        return keep

    for kind, k in expert_steps(slots):
        now = turn(kind + str(k), k)
        if kind == "cot":
            last = pick_rows(now, pos, cot_slots[k])
            cots[k] = (last, core_swap(last))
            seen["sc" + str(k)] = cots[k][1]
        elif kind == "row":
            last = pick_rows(now, pos, normed_slots[k])
            rows[k] = (last, core_swap(last))
            seen["sr" + str(k)] = rows[k][1]
        elif kind == "exp":
            scaled[k], gate_grads[k], up_grads[k], probs[k], keep, give = expert_slot(
                now, pos, gate, rows[k], cots[k], w_gate, w_up, w_down
            )
            last = scaled[k]
            back[k] = (keep, core_swap(give))
            seen["sg" + str(k)] = back[k][1]
        elif kind == "down":
            last = lower(k)
        else:
            placed = place_rows([now], at, *back[k])
            last = placed[0][0]
            back[k] = [[a[0] for a in b] for b in placed]
            if is_cube():
                sums[k], sent = scatter_plane(back[k], k in ODD)
                if k:
                    sums[k] = sent["z"] = send(sums[k].astype(BF16), dz=k)
                seen.update({"e" + link + str(k): value for link, value in sent.items()})
    for k in range(1, slots // 2):
        last = lower(k)
    pairs = [place_rows([turn("pd0", 0), where[1]], at, *downs[0])]
    last = pairs[0][0][0]
    grad_gate, grad_up = weight_grads(
        weight_kernel,
        turn("weight", 0),
        rows,
        gate_grads + up_grads,
        [w_gate.shape[1:]] * 2,
        "weight_grads",
    )
    if is_cube():
        expert_path = added(*[after(s, grad_gate) for s in sums])
    else:
        expert_path = scatter_all(back)

    prob_grads = jnp.stack([probs[k][:, b] for k in range(slots) for b in range(NB)])
    if is_cube():
        prob_grads = prob_grads[jnp.arange(owners, dtype=jnp.int32) ^ owner]
    prob_grads = lax.all_to_all(prob_grads, "expert", split_axis=0, concat_axis=0, tiled=True)
    prob_grads = tensor_sum(prob_grads.reshape(E, tokens_here))
    grad_logits = (
        router * (prob_grads - jnp.sum(router * prob_grads, axis=0, keepdims=True))
    ).astype(BF16)
    grad_router = lax.dot_general(
        normed_m, grad_logits, (((0,), (1,)), ((), ())), preferred_element_type=F32
    )
    router_path = lax.dot_general(
        grad_logits, router_slice, (((0,), (1,)), ((), ())), preferred_element_type=F32
    )
    grad_normed = expert_path + router_path
    moe_hat = residual * moe_inv
    grad_moe_gain = jnp.sum(grad_normed * moe_hat, axis=0)
    upstream = grad_normed * gain_slice
    mean_dot = tensor_sum(jnp.sum(upstream * moe_hat, axis=-1).reshape(8, -1)).reshape(-1, 1) / width
    grad_residual = cotangent + moe_inv * (upstream - moe_hat * mean_dot)
    branch_pieces = tensor_gather(grad_residual.astype(BF16))
    grad_branch = jnp.concatenate(branch_pieces, axis=1)

    for k in range(1, slots // 2):
        now = after(where[2 * k], branch_pieces[0])
        pairs.append(place_rows([now, where[2 * k + 1]], at, *downs[k]))
    last = pairs[-1][0][0]
    if is_cube():
        pairs = [[[after(a, branch_pieces[1]) for a in b] for b in pair] for pair in pairs]
    mixture = scatter_pairs(pairs, seen)
    out = residual + mixture

    grad_output = matmul_tn(grad_branch, attended).astype(BF16)
    spots = order_spots()
    eighth = width // 8
    wide = slice_width // eighth
    grad_output = jnp.concatenate(
        [
            lax.dynamic_slice_in_dim(
                grad_output, (spots(r // wide) * wide + r % wide) * eighth, eighth, 0
            )
            for r in blocks
        ],
        axis=0,
    )
    sum_output = expert_sum(grad_output)
    grad_attended = matmul_nt(grad_branch, jnp.concatenate(output_pieces, axis=1)).astype(BF16)
    grad_attended = after(grad_attended, grad_output, last)
    grad_query_raw, grad_key_raw, grad_v, grad_query_gain, grad_key_gain = attend_back(
        pieces, queries, keys, values, grad_attended, logs, query_raw, key_raw, query_gain, key_gain, scale
    )
    sum_value = expert_sum(matmul_tn(normed_rows, grad_v).astype(BF16))
    grad_raw = jnp.concatenate([grad_query_raw, grad_key_raw, grad_v], axis=1)
    grad_both = matmul_tn(normed_rows, grad_raw[:, : 2 * slice_width]).astype(BF16)
    sum_both = expert_sum(grad_both)
    grad_raw = after(grad_raw, grad_both, *due("normed_grad", seen))
    weights = jnp.concatenate([w_query, w_key, w_value], axis=1)
    weight_pieces = [lax.dynamic_slice_in_dim(weights, o * slice_width, slice_width, 0) for o in order]
    grad_normed_a = tensor_scatter(partial(matmul_nt, grad_raw), weight_pieces, "h", seen)
    now = after(where[0], *due("weight_down", seen))
    (grad_down,) = weight_grads(
        weight_down_kernel, now, cots, scaled, [w_down.shape[1:]], "weight_down_grads"
    )
    grad_normed_a = after(grad_normed_a, grad_down)
    attn_hat = own_columns(inputs).astype(F32) * attn_inv
    upstream = grad_normed_a * own_columns(attn_gain)
    grad_attn_gain = jnp.sum(grad_normed_a * attn_hat, axis=0)
    mean_dot = tensor_sum(jnp.sum(upstream * attn_hat, axis=-1).reshape(8, -1)).reshape(-1, 1) / width
    grad_input = grad_residual + attn_inv * (upstream - attn_hat * mean_dot)

    small = jnp.concatenate(
        [
            grad_router.T,
            jnp.stack(
                [
                    grad_attn_gain,
                    grad_moe_gain,
                    jnp.sum(grad_query_gain, axis=(0, 1)),
                    jnp.sum(grad_key_gain, axis=(0, 1)),
                ]
            ),
        ],
        axis=0,
    )
    top_row = jnp.pad(head_top, (0, slice_width - heads_here), constant_values=-3e38)
    small, top_row = expert_total(small, top_row[None])
    head_top = top_row[0, :heads_here]
    sum_moe_gain, sum_query_gain, sum_key_gain = small[E + 1], small[E + 2], small[E + 3]
    every = lax.all_gather(small[: E + 1], "tensor")
    sum_router = every[:, :E].transpose(0, 2, 1).reshape(width, E)
    sum_attn_gain = every[:, E].reshape(width)
    sum_output, sum_value, sum_query, sum_key = settle_rows(
        jnp.stack(blocks), sum_output, sum_value, sum_both
    )
    factor = clip_threshold / jnp.maximum(head_top, clip_threshold)
    spread = jnp.repeat(jnp.sqrt(factor), HD)
    query_clipped = (w_query.astype(F32) * spread[None, :]).astype(BF16)
    key_clipped = (w_key.astype(F32) * spread[None, :]).astype(BF16)
    return (
        out,
        grad_input,
        sum_attn_gain,
        sum_query,
        sum_key,
        sum_value,
        sum_output,
        sum_query_gain,
        sum_key_gain,
        sum_moe_gain,
        sum_router,
        grad_gate,
        grad_up,
        grad_down,
        head_top,
        query_clipped,
        key_clipped,
    )


def solution(mesh):
    return jax.shard_map(
        per_device,
        mesh=mesh,
        in_specs=(
            P("expert", None),
            P(),
            P(None, "tensor"),
            P(None, "tensor"),
            P(None, "tensor"),
            P("tensor", None),
            P("tensor"),
            P("tensor"),
            P(),
            P(),
            P("expert", None, "tensor"),
            P("expert", None, "tensor"),
            P("expert", "tensor", None),
            P("expert", None),
            P("expert", None),
            P("expert", None),
            P("tensor"),
            P("expert", "tensor"),
        ),
        out_specs=(
            P("expert", "tensor"),
            P("expert", "tensor"),
            P(),
            P(None, "tensor"),
            P(None, "tensor"),
            P(None, "tensor"),
            P("tensor", None),
            P("tensor"),
            P("tensor"),
            P("tensor"),
            P(),
            P("expert", None, "tensor"),
            P("expert", None, "tensor"),
            P("expert", "tensor", None),
            P("tensor"),
            P(None, "tensor"),
            P(None, "tensor"),
        ),
        check_vma=False,
    )
```

```python
from functools import partial
import math

import jax
import jax.numpy as jnp
from jax import lax
from jax.experimental import pallas as pl
from jax.experimental.pallas import tpu as pltpu
from jax.sharding import PartitionSpec as P

HD = 128
E = 64
TOP = 8
LENGTH = 1024
CAP = 160
NB = 2
BOTH = ("expert", "tensor")
F32 = jnp.float32
BF16 = jnp.bfloat16
VMEM = 60 * 1024 * 1024
WEIGHT = 16
ORDER = (0, 2, 3, 1)
ODD = (1, 2)
DUE = {
    "attended": ("cx0", "cy0"),
    "normed": ("cz2", "cd0"),
    "row0": ("cx2", "cz3", "cy2"),
    "exp0": ("cx3",),
    "row2": ("sc2", "cy3"),
    "cot3": ("sg0",),
    "place0": ("sr2",),
    "exp2": ("sc3",),
    "cot1": ("sg2",),
    "place2": ("sr3", "ed0"),
    "exp3": ("sc1",),
    "place3": ("ex0", "ey0", "ed2"),
    "down1": ("ex2", "ey2", "ed3"),
    "pd0": ("ed1", "sd0"),
    "weight": ("ex3", "ey3", "ex1", "ey1"),
    "back": ("gd0",),
    "normed_grad": ("gx0", "gy0", "gd1"),
    "weight_down": ("gx1", "gy1"),
}


def cost(flops, bytes_accessed, transcendentals):
    return pl.CostEstimate(
        flops=flops * WEIGHT, bytes_accessed=bytes_accessed * WEIGHT, transcendentals=transcendentals * WEIGHT
    )


def matmul(left, right):
    return jnp.dot(left, right, preferred_element_type=F32)


def matmul_nt(left, right):
    return lax.dot_general(left, right, (((1,), (1,)), ((), ())), preferred_element_type=F32)


def matmul_tn(left, right):
    return lax.dot_general(left, right, (((0,), (0,)), ((), ())), preferred_element_type=F32)


def after(value, *others):
    return lax.optimization_barrier((value, *others))[0]


def flip(dz, dx, dy, dc):
    pairs = []
    for z in range(4):
        for x in range(2):
            for y in range(2):
                for c in range(2):
                    pairs.append(
                        (
                            ((z * 2 + x) * 2 + y) * 2 + c,
                            (((z ^ dz) * 2 + (x ^ dx)) * 2 + (y ^ dy)) * 2 + (c ^ dc),
                        )
                    )
    return pairs


def send(value, dz=0, dx=0, dy=0, dc=0):
    return lax.ppermute(value, BOTH, flip(dz, dx, dy, dc))


def is_cube():
    return lax.axis_size("expert") == 8 and lax.axis_size("tensor") == 4


def core_swap(value):
    if is_cube():
        return send(value, dc=1)
    count = lax.axis_size("tensor")
    return lax.ppermute(value, "tensor", [(i, i ^ 1) for i in range(count)])


def slot_blocks():
    owner, part = lax.axis_index("expert"), lax.axis_index("tensor")
    core = part % 2
    found = []
    for k in range(lax.axis_size("expert") // NB):
        places = [k * NB + b for b in range(NB)]
        if is_cube():
            owners = [owner ^ p for p in places]
            mine = [part ^ (y * 2) for y in range(2)]
        else:
            owners = places
            mine = [y * 2 + core for y in range(lax.axis_size("tensor") // 2)]
        theirs = [m ^ 1 for m in mine]
        rows = [m // 2 for m in mine]
        found.append(
            jnp.stack([jnp.asarray(v, jnp.int32) for v in places + owners + mine + theirs + rows])
        )
    return found


def gather_routes(routes):
    if not is_cube():
        return lax.all_gather(routes, "expert")
    both = jnp.stack([routes, send(routes, dx=1)])
    both = jnp.concatenate([both, send(both, dz=1)])
    return jnp.concatenate([both, send(both, dz=2)])


def same_core():
    count = lax.axis_size("tensor")
    return [[y * 2 + c for y in range(count // 2)] for c in range(2)]


def gather_all(own):
    owners, parts = lax.axis_size("expert"), lax.axis_size("tensor")
    groups = [[e * parts + t for e in range(owners) for t in range(c, parts, 2)] for c in range(2)]
    full = lax.all_gather(own, BOTH, axis_index_groups=groups)
    return full.reshape(owners, parts // 2, *own.shape)


def gather_slots(own, tag, seen, first=()):
    if not is_cube():
        return [gather_all(own)] * (lax.axis_size("expert") // NB)
    slots = []
    far_own = after(own, *first) if first else own
    for k in range(4):
        block = send(far_own, dz=k) if k else own
        over_x = send(block, dx=1)
        over_y = send(block, dy=1)
        far = send(over_x, dy=1) if k in ODD else send(over_y, dx=1)
        for link, value in zip("zxyd", (block, over_x, over_y, far)):
            seen[tag + link + str(k)] = value
        slots.append([[block, over_y], [over_x, far]])
    return slots


def added(*terms):
    return sum(t.astype(F32) for t in terms)


def scatter_plane(parts, odd, hold=()):
    near, over_y, over_x, far = parts[0][0], parts[0][1], parts[1][0], parts[1][1]
    if odd:
        far = send(far, dy=1)
        over_x, over_y = added(over_x, far).astype(BF16), after(over_y, far)
    else:
        far = send(far, dx=1)
        over_x, over_y = after(over_x, far), added(over_y, far).astype(BF16)
    if hold:
        over_x, over_y = after(over_x, *hold), after(over_y, *hold)
    from_x, from_y = send(over_x, dx=1), send(over_y, dy=1)
    return added(near, from_x, from_y), {"d": far, "x": from_x, "y": from_y}


def scatter_all(slots):
    full = jnp.stack(
        [jnp.stack([s[b][y] for s in slots for b in range(NB)]) for y in range(len(slots[0][0]))]
    )
    mine = lax.psum_scatter(full, "tensor", axis_index_groups=same_core(), scatter_dimension=0)
    return lax.psum_scatter(mine, "expert", scatter_dimension=0).astype(F32)


def scatter_planes(pairs, hold, seen):
    if not is_cube():
        return pairs
    planes = []
    for i, pair in enumerate(pairs):
        plane, sent = scatter_plane(pair, True, hold)
        planes.append(plane)
        seen.update({"g" + link + str(i): value for link, value in sent.items()})
    return planes


def scatter_ends(planes, hold):
    if not is_cube():
        return scatter_all(
            [[[a[i] for a in b] for b in pair] for pair in planes for i in range(pair[0][0].shape[0])]
        )
    low, high = planes
    total = low + send(after(high.astype(BF16), hold), dz=2).astype(F32)
    return total[0] + send(total[1].astype(BF16), dz=1).astype(F32)


def tensor_order():
    part = lax.axis_index("tensor")
    if is_cube():
        return [part ^ i for i in (0, 2, 1, 3)]
    return [jnp.int32(i) for i in range(lax.axis_size("tensor"))]


def order_spots():
    if not is_cube():
        return lambda s: s
    part = lax.axis_index("tensor")
    return lambda s: (part ^ s) % 2 * 2 + (part ^ s) // 2


def tensor_gather(own):
    if not is_cube():
        full = lax.all_gather(own, "tensor")
        return [full[i] for i in range(full.shape[0])]
    over_y = send(own, dy=1)
    return [own, over_y, core_swap(own), core_swap(over_y)]


def tensor_scatter(product, pieces, tag, seen, beside=()):
    if not is_cube():
        full = jnp.concatenate([product(p).astype(BF16) for p in pieces], axis=1)
        return lax.psum_scatter(full, "tensor", scatter_dimension=1, tiled=True).astype(F32)
    away_y = product(pieces[3]).astype(BF16)
    away = product(pieces[2]).astype(BF16)
    from_y, near = core_swap(away_y), core_swap(away)
    away = added(product(pieces[1]), from_y).astype(BF16)
    over_y = after(send(away, dy=1), *beside) if beside else send(away, dy=1)
    seen.update({tag + "0": from_y, tag + "1": near, tag + "y": over_y, tag + "s": away})
    return added(product(pieces[0]), near, over_y)


def tensor_sum(value):
    if not is_cube():
        return lax.psum(value, "tensor")
    value = value + core_swap(value)
    return value + send(value, dy=1)


def row_blocks():
    if not is_cube():
        return [jnp.int32(i) for i in range(8)]
    owner = lax.axis_index("expert")
    return [owner ^ (b | first << 1 | second << 2) for b in (0, 1) for first in (0, 1) for second in (0, 1)]


def expert_sum(value):
    half = value.shape[0] // 2
    if not is_cube():
        value = lax.psum(value, "expert")
        return value[:half], value[half:]
    for step in ({"dx": 1}, {"dz": 1}, {"dz": 2}):
        half = value.shape[0] // 2
        value = added(value[:half], send(value[half:], **step)).astype(BF16)
    for step in ({"dz": 2}, {"dz": 1}):
        value = jnp.concatenate([value, send(value, **step)], axis=0)
    return value, send(value, dx=1)


def expert_total(sums, tops):
    if not is_cube():
        return lax.psum(sums, "expert"), lax.pmax(tops, "expert")
    count = sums.shape[0]
    both = jnp.concatenate([sums, tops], axis=0)
    for step in ({"dx": 1}, {"dz": 1}, {"dz": 2}):
        other = send(both, **step)
        both = jnp.concatenate([both[:count] + other[:count], jnp.maximum(both[count:], other[count:])])
    return both[:count], both[count:]


def one_hot(pos_row):
    rows = lax.broadcasted_iota(jnp.int32, (CAP, pos_row.shape[1]), 0)
    return rows == pos_row


def as_bf16(mask):
    return jnp.where(mask, 1.0, 0.0).astype(BF16)


def pick_kernel(group, slices, where_ref, *refs):
    pos_refs, x_refs = refs[:NB], refs[NB : NB + NB * slices]
    out_ref, hot_ref = refs[-2:]
    step = pl.program_id(0)
    for b in range(NB):
        for i in range(group):
            hot_ref[b, i * CAP : (i + 1) * CAP, :] = as_bf16(
                one_hot(pos_refs[b][0, pl.ds(step * group + i, 1), :])
            )
        for y in range(slices):
            out_ref[b, y] = matmul(hot_ref[b], x_refs[b * slices + y][...]).astype(BF16)


def pick_rows(where, pos, blocks):
    held = pos.shape[1]
    group = 2
    if isinstance(blocks, list):
        slices = len(blocks[0])
        flat = [a for b in blocks for a in b]
        tokens, width = flat[0].shape
        specs = [pl.BlockSpec((tokens, width), lambda i, where: (0, 0)) for _ in flat]
    else:
        slices, tokens, width = blocks.shape[1:]
        flat = [blocks] * (NB * slices)

        def part_spec(b, y):
            return pl.BlockSpec(
                (None, None, tokens, width),
                lambda i, where: (where[NB + b], where[2 * NB + 2 * slices + y], 0, 0),
            )

        specs = [part_spec(b, y) for b in range(NB) for y in range(slices)]

    def block_spec(b):
        return pl.BlockSpec((1, held, tokens), lambda i, where: (where[b], 0, 0))

    return pl.pallas_call(
        partial(pick_kernel, group, slices),
        grid_spec=pltpu.PrefetchScalarGridSpec(
            num_scalar_prefetch=1,
            grid=(held // group,),
            in_specs=[block_spec(b) for b in range(NB)]
            + specs,
            out_specs=pl.BlockSpec(
                (NB, slices, group * CAP, width), lambda i, where: (0, 0, i, 0)
            ),
            scratch_shapes=[pltpu.VMEM((NB, group * CAP, tokens), BF16)],
        ),
        out_shape=jax.ShapeDtypeStruct((NB, slices, held * CAP, width), BF16),
        compiler_params=pltpu.CompilerParams(vmem_limit_bytes=VMEM),
        cost_estimate=cost(
            flops=2 * NB * slices * held * CAP * tokens * width,
            bytes_accessed=2 * NB * slices * (held * CAP + tokens) * width,
            transcendentals=0,
        ),
        name="pick_rows",
    )(where, *([pos] * NB), *flat)


def expert_kernel(slices, where_ref, *refs):
    pos_refs, gate_refs = refs[:NB], refs[NB : 2 * NB]
    rows_mine, rows_theirs, cot_mine, cot_theirs, wg_ref, wu_ref, wd_ref = refs[2 * NB : 2 * NB + 7]
    scaled_ref, gate_grad_ref, up_grad_ref, prob_ref, keep_ref, give_ref = refs[2 * NB + 7 :]
    e = pl.program_id(0)
    width = rows_mine.shape[3]
    ff = wg_ref.shape[2]
    gate_pre = jnp.zeros((NB * CAP, ff), F32)
    up_pre = jnp.zeros((NB * CAP, ff), F32)
    grad_hidden = jnp.zeros((NB * CAP, ff), F32)

    def columns(j):
        return pl.ds(pl.multiple_of(where_ref[2 * NB + j] * width, width), width)

    for j in range(2 * slices):
        x_ref, c_ref = (rows_mine, cot_mine) if j < slices else (rows_theirs, cot_theirs)
        x = x_ref[:, j % slices].reshape(NB * CAP, width)
        c = c_ref[:, j % slices].reshape(NB * CAP, width)
        gate_pre = gate_pre + matmul(x, wg_ref[0, columns(j), :])
        up_pre = up_pre + matmul(x, wu_ref[0, columns(j), :])
        grad_hidden = grad_hidden + matmul_nt(c, wd_ref[0, :, columns(j)])
    masks = [one_hot(pos_refs[b][0, pl.ds(e, 1), :]) for b in range(NB)]
    gates = jnp.concatenate(
        [
            jnp.sum(jnp.where(masks[b], gate_refs[b][0, pl.ds(e, 1), :], 0.0), axis=1, keepdims=True)
            for b in range(NB)
        ],
        axis=0,
    )
    sigma = jax.nn.sigmoid(gate_pre)
    swish = gate_pre * sigma
    hidden = (swish * up_pre).astype(BF16).astype(F32)
    prob = jnp.sum(hidden * grad_hidden, axis=1, keepdims=True)
    for b in range(NB):
        prob_ref[0, b : b + 1, :] = jnp.sum(
            jnp.where(masks[b], prob[b * CAP : (b + 1) * CAP], 0.0), axis=0, keepdims=True
        )
    grad_hidden = grad_hidden * gates
    scaled_ref[0] = (hidden * gates).astype(BF16)
    gate_grad = (grad_hidden * up_pre * (sigma * (1.0 + gate_pre * (1.0 - sigma)))).astype(BF16)
    up_grad = (grad_hidden * swish).astype(BF16)
    gate_grad_ref[0] = gate_grad
    up_grad_ref[0] = up_grad
    for j in range(2 * slices):
        to = keep_ref if j < slices else give_ref
        back = matmul_nt(gate_grad, wg_ref[0, columns(j), :]) + matmul_nt(
            up_grad, wu_ref[0, columns(j), :]
        )
        to[:, j % slices] = back.astype(BF16).reshape(NB, CAP, width)


def expert_slot(where, pos, gate, rows, cots, w_gate, w_up, w_down):
    held, depth, ff = w_gate.shape
    tokens = pos.shape[2]
    slices, width = rows[0].shape[1], rows[0].shape[3]

    def block_spec(b):
        return pl.BlockSpec((1, held, tokens), lambda e, where: (where[b], 0, 0))

    rows_spec = pl.BlockSpec((NB, slices, CAP, width), lambda e, where: (0, 0, e, 0))
    rows_shape = jax.ShapeDtypeStruct((NB, slices, held * CAP, width), BF16)
    in_spec = pl.BlockSpec((1, depth, ff), lambda e, where: (e, 0, 0))
    hidden_spec = pl.BlockSpec((1, NB * CAP, ff), lambda e, where: (e, 0, 0))
    hidden_shape = jax.ShapeDtypeStruct((held, NB * CAP, ff), BF16)
    return pl.pallas_call(
        partial(expert_kernel, slices),
        grid_spec=pltpu.PrefetchScalarGridSpec(
            num_scalar_prefetch=1,
            grid=(held,),
            in_specs=[block_spec(b) for b in range(2 * NB)]
            + [rows_spec] * 4
            + [in_spec, in_spec, pl.BlockSpec((1, ff, depth), lambda e, where: (e, 0, 0))],
            out_specs=[hidden_spec] * 3
            + [pl.BlockSpec((1, NB, tokens), lambda e, where: (e, 0, 0)), rows_spec, rows_spec],
        ),
        out_shape=[hidden_shape] * 3
        + [jax.ShapeDtypeStruct((held, NB, tokens), F32), rows_shape, rows_shape],
        compiler_params=pltpu.CompilerParams(vmem_limit_bytes=VMEM),
        cost_estimate=cost(
            flops=10 * NB * held * CAP * depth * ff,
            bytes_accessed=6 * held * depth * ff + 6 * NB * held * CAP * depth,
            transcendentals=NB * held * CAP * ff,
        ),
        name="expert_slot",
    )(where, *([pos] * NB), *([gate] * NB), *rows, *cots, w_gate, w_up, w_down)


def down_kernel(slices, slots, where_ref, *refs):
    scaled_refs, wd_ref, keep_ref, give_ref = refs[:slots], refs[slots], refs[-2], refs[-1]
    width = keep_ref.shape[3]
    for j in range(2 * slices):
        to = keep_ref if j < slices else give_ref
        columns = pl.ds(pl.multiple_of(where_ref[2 * NB + j] * width, width), width)
        for k in range(slots):
            rows = matmul(scaled_refs[k][0], wd_ref[0, :, columns])
            to[k * NB : (k + 1) * NB, j % slices] = rows.astype(BF16).reshape(NB, CAP, width)


def down_slots(where, scaled, w_down, slices):
    held, ff, depth = w_down.shape
    width = depth // (2 * slices)
    slots = len(scaled)
    rows_spec = pl.BlockSpec((slots * NB, slices, CAP, width), lambda e, where: (0, 0, e, 0))
    rows_shape = jax.ShapeDtypeStruct((slots * NB, slices, held * CAP, width), BF16)
    return pl.pallas_call(
        partial(down_kernel, slices, slots),
        grid_spec=pltpu.PrefetchScalarGridSpec(
            num_scalar_prefetch=1,
            grid=(held,),
            in_specs=[pl.BlockSpec((1, NB * CAP, ff), lambda e, where: (e, 0, 0))] * slots
            + [pl.BlockSpec((1, ff, depth), lambda e, where: (e, 0, 0))],
            out_specs=[rows_spec, rows_spec],
        ),
        out_shape=[rows_shape, rows_shape],
        compiler_params=pltpu.CompilerParams(vmem_limit_bytes=VMEM),
        cost_estimate=cost(
            flops=2 * slots * NB * held * CAP * depth * ff,
            bytes_accessed=2 * held * depth * ff + 2 * slots * NB * held * CAP * depth,
            transcendentals=0,
        ),
        name="down_slots",
    )(where, *scaled, w_down)


def place_kernel(slices, held, slots, where_ref, *refs):
    count = NB * slots
    at_refs, mine_ref, theirs_ref = refs[:count], refs[count], refs[count + 1]
    out_refs, hot_ref = refs[count + 2 : -1], refs[-1]
    b, y = pl.program_id(0), pl.program_id(1)
    tokens = hot_ref.shape[0]
    for block in range(count):

        @pl.when((b == block) & (y == 0))
        def _():
            at = at_refs[block][0]
            for tile in range(held * CAP // 128):
                lanes = lax.broadcasted_iota(jnp.int32, (tokens, 128), 1) + tile * 128
                mask = None
                for e in range(tile * 128 // CAP, (tile * 128 + 127) // CAP + 1):
                    hit = at[:, e : e + 1] == lanes
                    mask = hit if mask is None else mask | hit
                hot_ref[:, tile * 128 : (tile + 1) * 128] = as_bf16(mask)

    rows = (mine_ref[0, 0].astype(F32) + theirs_ref[0, 0].astype(F32)).astype(BF16)
    placed = matmul(hot_ref[...], rows).astype(BF16)
    for block in range(count):
        for part in range(slices):

            @pl.when((b == block) & (y == part))
            def _():
                out_refs[block % NB * slices + part][block // NB] = placed


def place_rows(wheres, at, mine, theirs):
    _, slices, count, width = mine.shape
    _, tokens, held = at.shape
    slots = len(wheres)
    blocks = jnp.concatenate([w[:NB] for w in wheres])

    def block_spec(b):
        return pl.BlockSpec((1, tokens, held), lambda i, y, where: (where[b], 0, 0))

    rows_spec = pl.BlockSpec((1, 1, count, width), lambda i, y, where: (i, y, 0, 0))
    out = pl.pallas_call(
        partial(place_kernel, slices, held, slots),
        grid_spec=pltpu.PrefetchScalarGridSpec(
            num_scalar_prefetch=1,
            grid=(NB * slots, slices),
            in_specs=[block_spec(b) for b in range(NB * slots)] + [rows_spec, rows_spec],
            out_specs=[pl.BlockSpec((slots, tokens, width), lambda i, y, where: (0, 0, 0))]
            * (NB * slices),
            scratch_shapes=[pltpu.VMEM((tokens, count), BF16)],
        ),
        out_shape=[jax.ShapeDtypeStruct((slots, tokens, width), BF16)] * (NB * slices),
        compiler_params=pltpu.CompilerParams(vmem_limit_bytes=VMEM),
        cost_estimate=cost(
            flops=2 * NB * slots * slices * count * tokens * width,
            bytes_accessed=2 * NB * slots * slices * (2 * count + tokens) * width,
            transcendentals=0,
        ),
        name="place_rows",
    )(blocks, *([at] * (NB * slots)), mine, theirs)
    return [out[b * slices : (b + 1) * slices] for b in range(NB)]


def weight_kernel(slots, slices, where_ref, *refs):
    rows, gate_grads, up_grads = refs[: 2 * slots], refs[2 * slots : 3 * slots], refs[3 * slots : 4 * slots]
    gate_ref, up_ref = refs[4 * slots :]
    width = rows[0].shape[3]
    for j in range(2 * slices):
        columns = pl.ds(pl.multiple_of(where_ref[2 * NB + j] * width, width), width)
        gate = up = None
        for k in range(slots):
            x = rows[2 * k + j // slices][:, j % slices].reshape(NB * CAP, width)
            terms = matmul_tn(x, gate_grads[k][0]), matmul_tn(x, up_grads[k][0])
            gate, up = terms if gate is None else (gate + terms[0], up + terms[1])
        gate_ref[0, columns, :] = gate
        up_ref[0, columns, :] = up


def weight_down_kernel(slots, slices, where_ref, *refs):
    cots, scaled, down_ref = refs[: 2 * slots], refs[2 * slots : 3 * slots], refs[3 * slots]
    width = cots[0].shape[3]
    for j in range(2 * slices):
        columns = pl.ds(pl.multiple_of(where_ref[2 * NB + j] * width, width), width)
        down = None
        for k in range(slots):
            c = cots[2 * k + j // slices][:, j % slices].reshape(NB * CAP, width)
            term = matmul_tn(scaled[k][0], c)
            down = term if down is None else down + term
        down_ref[0, :, columns] = down


def weight_grads(kernel, where, rows, hiddens, outs, name):
    slots = len(rows)
    held, _, ff = hiddens[0].shape
    slices, width = rows[0][0].shape[1], rows[0][0].shape[3]
    depth = 2 * slices * width
    rows_spec = pl.BlockSpec((NB, slices, CAP, width), lambda e, where: (0, 0, e, 0))
    hidden_spec = pl.BlockSpec((1, NB * CAP, ff), lambda e, where: (e, 0, 0))
    return pl.pallas_call(
        partial(kernel, slots, slices),
        grid_spec=pltpu.PrefetchScalarGridSpec(
            num_scalar_prefetch=1,
            grid=(held,),
            in_specs=[rows_spec] * (2 * slots) + [hidden_spec] * len(hiddens),
            out_specs=[pl.BlockSpec((1, *o), lambda e, where: (e, 0, 0)) for o in outs],
        ),
        out_shape=[jax.ShapeDtypeStruct((held, *o), F32) for o in outs],
        compiler_params=pltpu.CompilerParams(vmem_limit_bytes=VMEM),
        cost_estimate=cost(flops=10**10, bytes_accessed=10**6, transcendentals=0),
        name=name,
    )(where, *[a for pair in rows for a in pair], *hiddens)


def settle_kernel(where_ref, *refs):
    halves, (output_ref, value_ref, query_ref, key_ref) = refs[:6], refs[6:]

    def settle(output, value, both):
        output_ref[...] = output[...].astype(F32).T
        value_ref[...] = value[...].astype(F32)
        width = query_ref.shape[1]
        query_ref[...] = both[:, :width].astype(F32)
        key_ref[...] = both[:, width:].astype(F32)

    @pl.when(pl.program_id(0) < 4)
    def _():
        settle(*halves[0::2])

    @pl.when(pl.program_id(0) >= 4)
    def _():
        settle(*halves[1::2])


def settle_rows(where, output, value, both):
    rows = 2 * value[0].shape[0]
    step = rows // 8
    width = value[0].shape[1]
    near = lambda n: pl.BlockSpec((step, n), lambda i, where: (jnp.minimum(i, 3), 0))
    far = lambda n: pl.BlockSpec((step, n), lambda i, where: (jnp.maximum(i, 4) - 4, 0))
    placed = pl.BlockSpec((step, width), lambda i, where: (where[i], 0))
    return pl.pallas_call(
        settle_kernel,
        grid_spec=pltpu.PrefetchScalarGridSpec(
            num_scalar_prefetch=1,
            grid=(8,),
            in_specs=[s(n) for n in (width, width, 2 * width) for s in (near, far)],
            out_specs=[pl.BlockSpec((width, step), lambda i, where: (0, where[i]))] + [placed] * 3,
        ),
        out_shape=[jax.ShapeDtypeStruct((width, rows), F32)]
        + [jax.ShapeDtypeStruct((rows, width), F32)] * 3,
        compiler_params=pltpu.CompilerParams(vmem_limit_bytes=VMEM),
        cost_estimate=cost(flops=0, bytes_accessed=24 * rows * width, transcendentals=0),
        name="settle_rows",
    )(where, *output, *value, *both)


def project_kernel(
    in_ref, ag_ref, wq_ref, wk_ref, wv_ref, qg_ref, kg_ref,
    x_ref, inv_ref, qr_ref, kr_ref, q_ref, k_ref, v_ref,
):
    @pl.when(pl.program_id(0) == 0)
    def _():
        for first in range(0, in_ref.shape[0], 256):
            rows = in_ref[first : first + 256, :].astype(F32)
            inverse = lax.rsqrt(jnp.mean(rows * rows, axis=1, keepdims=True) + 1e-05)
            inv_ref[first : first + 256, :] = inverse
            x_ref[first : first + 256, :] = (rows * inverse * ag_ref[...]).astype(BF16)

    x = x_ref[...]
    for w_ref, gain_ref, raw_ref, to_ref in ((wq_ref, qg_ref, qr_ref, q_ref), (wk_ref, kg_ref, kr_ref, k_ref)):
        raw = matmul(x, w_ref[...])
        raw_ref[...] = raw
        for h in range(raw.shape[1] // HD):
            part = raw[:, h * HD : (h + 1) * HD]
            inverse = lax.rsqrt(jnp.mean(part * part, axis=1, keepdims=True) + 1e-06)
            gain = gain_ref[:, h * HD : (h + 1) * HD]
            to_ref[:, h * HD : (h + 1) * HD] = (part * inverse * gain).astype(BF16)
    v_ref[...] = matmul(x, wv_ref[...]).astype(BF16)


def project(inputs, attn_gain, w_query, w_key, w_value, query_gain, key_gain):
    tokens, depth = inputs.shape
    columns = w_query.shape[1]
    step = min(256, columns)
    whole = pl.BlockSpec((tokens, depth), lambda i: (0, 0))
    weight = pl.BlockSpec((depth, step), lambda i: (0, i))
    gain = pl.BlockSpec((1, step), lambda i: (0, i))
    out = pl.BlockSpec((tokens, step), lambda i: (0, i))
    return pl.pallas_call(
        project_kernel,
        grid=(columns // step,),
        in_specs=[whole, pl.BlockSpec((1, depth), lambda i: (0, 0)), weight, weight, weight, gain, gain],
        out_specs=[whole, pl.BlockSpec((tokens, 1), lambda i: (0, 0))] + [out] * 5,
        out_shape=[
            jax.ShapeDtypeStruct((tokens, depth), BF16),
            jax.ShapeDtypeStruct((tokens, 1), F32),
        ]
        + [jax.ShapeDtypeStruct((tokens, columns), t) for t in (F32, F32, BF16, BF16, BF16)],
        compiler_params=pltpu.CompilerParams(vmem_limit_bytes=VMEM),
        cost_estimate=cost(
            flops=6 * tokens * depth * columns,
            bytes_accessed=4 * tokens * depth + 6 * depth * columns + 14 * tokens * columns,
            transcendentals=0,
        ),
        name="project",
    )(
        inputs, attn_gain.reshape(1, -1), w_query, w_key, w_value,
        query_gain.reshape(1, -1), key_gain.reshape(1, -1),
    )


def allowed_pairs(pieces_ref, base, first, rows, keys):
    query = first + lax.broadcasted_iota(jnp.int32, (rows, 1), 0)
    key = lax.broadcasted_iota(jnp.int32, (1, keys), 1)

    def piece_of(at, other):
        found = jnp.full(at.shape, other, jnp.int32)
        for j in range(2):
            start, length = pieces_ref[base + j], pieces_ref[base + 2 + j]
            found = jnp.where((at >= start) & (at < start + length), j, found)
        return found

    return (key <= query) | (piece_of(query, -1) == piece_of(key, -2))


def query_blocks():
    half = LENGTH // 2
    return ((0, half, half), (half, half, LENGTH))


def attend_kernel(scale, pieces_ref, q_ref, k_ref, v_ref, o_ref, log_ref, top_ref):
    base = pl.program_id(0) * 4
    best = None
    for first, rows, keys in query_blocks():
        allowed = allowed_pairs(pieces_ref, base, first, rows, keys)
        scores = matmul_nt(q_ref[first : first + rows, :], k_ref[:keys, :]) * scale
        masked = jnp.where(allowed, scores, -1e30)
        top = jnp.max(masked, axis=1, keepdims=True)
        weights = jnp.exp(masked - top)
        total = jnp.sum(weights, axis=1, keepdims=True)
        probs = (weights * (1.0 / total)).astype(BF16)
        o_ref[first : first + rows, :] = matmul(probs, v_ref[:keys, :]).astype(BF16)
        log_ref[0, first : first + rows, :] = top + jnp.log(total)
        most = jnp.max(top, axis=0, keepdims=True)
        best = most if best is None else jnp.maximum(best, most)
    top_ref[0] = jnp.broadcast_to(best, (8, HD))


def attend(pieces, queries, keys, values, scale):
    tokens, columns = queries.shape
    sequences, heads = tokens // LENGTH, columns // HD
    block = pl.BlockSpec((LENGTH, HD), lambda s, h, pieces: (s, h))
    return pl.pallas_call(
        partial(attend_kernel, scale),
        grid_spec=pltpu.PrefetchScalarGridSpec(
            num_scalar_prefetch=1,
            grid=(sequences, heads),
            in_specs=[block] * 3,
            out_specs=[
                block,
                pl.BlockSpec((1, LENGTH, 1), lambda s, h, pieces: (h, s, 0)),
                pl.BlockSpec((1, 8, HD), lambda s, h, pieces: (s * heads + h, 0, 0)),
            ],
        ),
        out_shape=[
            jax.ShapeDtypeStruct((tokens, columns), BF16),
            jax.ShapeDtypeStruct((heads, tokens, 1), F32),
            jax.ShapeDtypeStruct((sequences * heads, 8, HD), F32),
        ],
        compiler_params=pltpu.CompilerParams(vmem_limit_bytes=VMEM),
        cost_estimate=cost(
            flops=4 * tokens * LENGTH * columns,
            bytes_accessed=8 * tokens * columns,
            transcendentals=tokens * heads * LENGTH,
        ),
        name="attend",
    )(pieces, queries, keys, values)


def attend_back_kernel(
    scale, pieces_ref, q_ref, k_ref, v_ref, g_ref, log_ref, qr_ref, kr_ref, qg_ref, kg_ref,
    gq_ref, gk_ref, gv_ref, gqg_ref, gkg_ref, dq_ref, dk_ref, dv_ref,
):
    base = pl.program_id(0) * 4
    blocks = query_blocks()
    for first, rows, keys in blocks[::-1]:
        allowed = allowed_pairs(pieces_ref, base, first, rows, keys)
        q, g = q_ref[first : first + rows, :], g_ref[first : first + rows, :]
        k, v = k_ref[:keys, :], v_ref[:keys, :]
        scores = matmul_nt(q, k) * scale
        probs = jnp.exp(jnp.where(allowed, scores, -1e30) - log_ref[0, first : first + rows, :])
        grad_p = matmul_nt(g, v)
        delta = jnp.sum(probs * grad_p, axis=1, keepdims=True)
        grad_s = (probs * (grad_p - delta)).astype(BF16)
        dq_ref[first : first + rows, :] = matmul(grad_s, k) * scale
        dk = matmul_tn(grad_s, q) * scale
        dv = matmul_tn(probs.astype(BF16), g)
        if keys == LENGTH:
            dk_ref[...] = dk
            dv_ref[...] = dv
        else:
            dk_ref[:keys, :] += dk
            dv_ref[:keys, :] += dv
    gv_ref[...] = dv_ref[...].astype(BF16)
    for raw_ref, gain_ref, grad_ref, to_ref, sum_ref in (
        (qr_ref, qg_ref, dq_ref, gq_ref, gqg_ref),
        (kr_ref, kg_ref, dk_ref, gk_ref, gkg_ref),
    ):
        raw, grad = raw_ref[...], grad_ref[...]
        inverse = lax.rsqrt(jnp.mean(raw * raw, axis=1, keepdims=True) + 1e-06)
        hat = raw * inverse
        up = grad * gain_ref[...]
        mean = jnp.mean(up * hat, axis=1, keepdims=True)
        to_ref[...] = (inverse * (up - hat * mean)).astype(BF16)
        sum_ref[0] = jnp.sum(grad * hat, axis=0, keepdims=True)


def attend_back(pieces, queries, keys, values, grads, logs, query_raw, key_raw, query_gain, key_gain, scale):
    tokens, columns = queries.shape
    sequences, heads = tokens // LENGTH, columns // HD
    block = pl.BlockSpec((LENGTH, HD), lambda s, h, pieces: (s, h))
    gain = pl.BlockSpec((1, HD), lambda s, h, pieces: (0, h))
    sums = pl.BlockSpec((1, 1, HD), lambda s, h, pieces: (s, 0, h))
    return pl.pallas_call(
        partial(attend_back_kernel, scale),
        grid_spec=pltpu.PrefetchScalarGridSpec(
            num_scalar_prefetch=1,
            grid=(sequences, heads),
            in_specs=[block] * 4
            + [pl.BlockSpec((1, LENGTH, 1), lambda s, h, pieces: (h, s, 0)), block, block, gain, gain],
            out_specs=[block, block, block, sums, sums],
            scratch_shapes=[pltpu.VMEM((LENGTH, HD), F32)] * 3,
        ),
        out_shape=[jax.ShapeDtypeStruct((tokens, columns), BF16)] * 3
        + [jax.ShapeDtypeStruct((sequences, 1, columns), F32)] * 2,
        compiler_params=pltpu.CompilerParams(vmem_limit_bytes=VMEM),
        cost_estimate=cost(
            flops=10 * tokens * LENGTH * columns,
            bytes_accessed=22 * tokens * columns,
            transcendentals=tokens * heads * LENGTH,
        ),
        name="attend_back",
    )(
        pieces, queries, keys, values, grads, logs, query_raw, key_raw,
        query_gain.reshape(1, -1), key_gain.reshape(1, -1),
    )


def expert_steps(slots):
    order = list(ORDER) if is_cube() else list(range(slots))
    steps = [("cot", order[0]), ("row", order[0]), ("cot", order[1]), ("exp", order[0])]
    for i, k in enumerate(order):
        if i + 1 < slots:
            steps.append(("row", order[i + 1]))
        else:
            steps.append(("down", 0))
        if i + 2 < slots:
            steps.append(("cot", order[i + 2]))
        steps.append(("place", k))
        if i + 1 < slots:
            steps.append(("exp", order[i + 1]))
    return steps


def due(step, seen):
    return [seen[name] for name in DUE.get(step, ()) if name in seen]


def per_device(
    inputs,
    attn_gain,
    w_query,
    w_key,
    w_value,
    w_output,
    query_gain,
    key_gain,
    moe_gain,
    w_router,
    w_gate,
    w_up,
    w_down,
    routes,
    piece_start,
    piece_length,
    clip_threshold,
    cotangent,
):
    tokens_here, width = inputs.shape
    slice_width = cotangent.shape[1]
    owner = lax.axis_index("expert")
    column = lax.axis_index("tensor") * slice_width
    heads_here = query_gain.shape[0] // HD
    experts_here = w_gate.shape[0]
    owners = lax.axis_size("expert")
    sequences = tokens_here // LENGTH
    scale = 1.0 / math.sqrt(HD)
    where = slot_blocks()
    slots = len(where)
    slices = lax.axis_size("tensor") // 2

    def own_columns(value):
        return lax.dynamic_slice_in_dim(value, column, slice_width, value.ndim - 1)

    seen = {}
    all_routes = gather_routes(routes.T)
    cot_slots = gather_slots(cotangent.astype(BF16), "c", seen, [all_routes])
    order = tensor_order()

    held_ids = owner * experts_here + jnp.arange(experts_here, dtype=jnp.int32)
    chosen = jnp.any(all_routes[:, None] == held_ids[None, :, None, None], axis=2)
    places = jnp.arange(tokens_here, dtype=jnp.int32)
    before = (places[:, None] < places[None, :]).astype(BF16)
    earlier = jnp.einsum(
        "set,tu->seu", chosen.astype(BF16), before, preferred_element_type=F32
    ).astype(jnp.int32)
    pos = jnp.where(chosen, earlier, -1)
    at = jnp.where(
        chosen, earlier + jnp.arange(experts_here, dtype=jnp.int32)[None, :, None] * CAP, -1
    ).transpose(0, 2, 1)

    output_pieces = [lax.dynamic_slice_in_dim(w_output, o * slice_width, slice_width, 1) for o in order]
    normed_a, attn_inv, query_raw, key_raw, queries, keys, values = project(
        inputs, attn_gain, w_query, w_key, w_value, query_gain, key_gain
    )
    blocks = row_blocks()
    normed_rows = jnp.concatenate(
        [lax.dynamic_slice_in_dim(normed_a, r * (width // 8), width // 8, 1) for r in blocks], axis=1
    )
    pieces = jnp.concatenate([piece_start, piece_length], axis=1).reshape(-1)
    attended, logs, tops = attend(
        after(pieces, values, all_routes), queries, keys, values, scale
    )
    head_top = jnp.max(tops[:, 0, 0].reshape(sequences, heads_here), axis=0)
    attended = after(attended, *due("attended", seen))
    branch = tensor_scatter(partial(matmul, attended), output_pieces, "b", seen, [pos, at])
    residual = own_columns(inputs).astype(F32) + branch
    gain_slice = own_columns(moe_gain)
    router_slice = lax.dynamic_slice_in_dim(w_router, column, slice_width, 0)
    lifted = residual * gain_slice
    row_sums = tensor_sum(
        jnp.concatenate(
            [
                lax.dot_general(
                    router_slice,
                    lifted.astype(BF16),
                    (((0,), (1,)), ((), ())),
                    preferred_element_type=F32,
                ),
                jnp.sum(residual * residual, axis=1)[None],
            ],
            axis=0,
        )
    )
    moe_inv_row = lax.rsqrt(row_sums[E] / width + 1e-05)
    moe_inv = moe_inv_row[:, None]
    normed_m = (lifted * moe_inv).astype(BF16)
    normed_m = after(normed_m, *due("normed", seen))

    normed_slots = gather_slots(normed_m, "n", seen)
    router = jax.nn.softmax(row_sums[:E] * moe_inv_row[None], axis=0)
    gate = lax.all_to_all(
        router.reshape(owners, experts_here, tokens_here),
        "expert",
        split_axis=0,
        concat_axis=0,
        tiled=True,
    )

    rows, cots, back, sums = [None] * slots, [None] * slots, [None] * slots, [None] * slots
    scaled, gate_grads, up_grads, probs = [None] * slots, [None] * slots, [None] * slots, [None] * slots
    last = normed_m
    downs = {}

    def turn(name, k):
        return after(where[k], last, *due(name, seen))

    def lower(k):
        keep, give = down_slots(turn("down" + str(k), 0), scaled[2 * k : 2 * k + 2], w_down, slices)
        downs[k] = (keep, core_swap(give))
        seen["sd" + str(k)] = downs[k][1]
        return keep

    for kind, k in expert_steps(slots):
        now = turn(kind + str(k), k)
        if kind == "cot":
            last = pick_rows(now, pos, cot_slots[k])
            cots[k] = (last, core_swap(last))
            seen["sc" + str(k)] = cots[k][1]
        elif kind == "row":
            last = pick_rows(now, pos, normed_slots[k])
            rows[k] = (last, core_swap(last))
            seen["sr" + str(k)] = rows[k][1]
        elif kind == "exp":
            scaled[k], gate_grads[k], up_grads[k], probs[k], keep, give = expert_slot(
                now, pos, gate, rows[k], cots[k], w_gate, w_up, w_down
            )
            last = scaled[k]
            back[k] = (keep, core_swap(give))
            seen["sg" + str(k)] = back[k][1]
        elif kind == "down":
            last = lower(k)
        else:
            placed = place_rows([now], at, *back[k])
            last = placed[0][0]
            back[k] = [[a[0] for a in b] for b in placed]
            if is_cube():
                sums[k], sent = scatter_plane(back[k], k in ODD)
                if k:
                    sums[k] = sent["z"] = send(sums[k].astype(BF16), dz=k)
                seen.update({"e" + link + str(k): value for link, value in sent.items()})
    for k in range(1, slots // 2):
        last = lower(k)
    pairs = [place_rows([turn("pd0", 0), where[1]], at, *downs[0])]
    last = pairs[0][0][0]
    grad_gate, grad_up = weight_grads(
        weight_kernel,
        turn("weight", 0),
        rows,
        gate_grads + up_grads,
        [w_gate.shape[1:]] * 2,
        "weight_grads",
    )
    if is_cube():
        expert_path = added(*[after(s, grad_gate) for s in sums])
    else:
        expert_path = scatter_all(back)

    prob_grads = jnp.stack([probs[k][:, b] for k in range(slots) for b in range(NB)])
    if is_cube():
        prob_grads = prob_grads[jnp.arange(owners, dtype=jnp.int32) ^ owner]
    prob_grads = lax.all_to_all(prob_grads, "expert", split_axis=0, concat_axis=0, tiled=True)
    prob_grads = tensor_sum(prob_grads.reshape(E, tokens_here))
    grad_logits = (
        router * (prob_grads - jnp.sum(router * prob_grads, axis=0, keepdims=True))
    ).astype(BF16)
    grad_router = lax.dot_general(
        normed_m, grad_logits, (((0,), (1,)), ((), ())), preferred_element_type=F32
    )
    router_path = lax.dot_general(
        grad_logits, router_slice, (((0,), (1,)), ((), ())), preferred_element_type=F32
    )
    grad_normed = expert_path + router_path
    moe_hat = residual * moe_inv
    grad_moe_gain = jnp.sum(grad_normed * moe_hat, axis=0)
    upstream = grad_normed * gain_slice
    mean_dot = tensor_sum(jnp.sum(upstream * moe_hat, axis=-1).reshape(8, -1)).reshape(-1, 1) / width
    grad_residual = cotangent + moe_inv * (upstream - moe_hat * mean_dot)
    branch_pieces = tensor_gather(grad_residual.astype(BF16))

    for k in range(1, slots // 2):
        now = after(where[2 * k], branch_pieces[0])
        pairs.append(place_rows([now, where[2 * k + 1]], at, *downs[k]))
    last = pairs[-1][0][0]
    if is_cube():
        pairs[1] = [[after(a, branch_pieces[1]) for a in b] for b in pairs[1]]
    planes = scatter_planes(pairs, branch_pieces[1:2], seen)
    branch_pieces = [after(p, last) for p in branch_pieces]
    grad_branch = jnp.concatenate(branch_pieces, axis=1)

    grad_output = matmul_tn(grad_branch, attended).astype(BF16)
    spots = order_spots()
    eighth = width // 8
    wide = slice_width // eighth
    grad_output = jnp.concatenate(
        [
            lax.dynamic_slice_in_dim(
                grad_output, (spots(r // wide) * wide + r % wide) * eighth, eighth, 0
            )
            for r in blocks
        ],
        axis=0,
    )
    sum_output = expert_sum(grad_output)
    grad_attended = matmul_nt(grad_branch, jnp.concatenate(output_pieces, axis=1)).astype(BF16)
    grad_attended = after(grad_attended, grad_output, last)
    grad_query_raw, grad_key_raw, grad_v, grad_query_gain, grad_key_gain = attend_back(
        after(pieces, *due("back", seen)),
        queries,
        keys,
        values,
        grad_attended,
        logs,
        query_raw,
        key_raw,
        query_gain,
        key_gain,
        scale,
    )
    sum_value = expert_sum(matmul_tn(normed_rows, grad_v).astype(BF16))
    grad_raw = jnp.concatenate([grad_query_raw, grad_key_raw, grad_v], axis=1)
    grad_both = matmul_tn(normed_rows, grad_raw[:, : 2 * slice_width]).astype(BF16)
    sum_both = expert_sum(grad_both)
    grad_raw = after(grad_raw, grad_both, *due("normed_grad", seen))
    weights = jnp.concatenate([w_query, w_key, w_value], axis=1)
    weight_pieces = [lax.dynamic_slice_in_dim(weights, o * slice_width, slice_width, 0) for o in order]
    grad_normed_a = tensor_scatter(partial(matmul_nt, grad_raw), weight_pieces, "h", seen)
    attn_hat = own_columns(inputs).astype(F32) * attn_inv
    upstream = grad_normed_a * own_columns(attn_gain)
    grad_attn_gain = jnp.sum(grad_normed_a * attn_hat, axis=0)
    mean_dot = tensor_sum(jnp.sum(upstream * attn_hat, axis=-1).reshape(8, -1)).reshape(-1, 1) / width
    grad_input = grad_residual + attn_inv * (upstream - attn_hat * mean_dot)

    small = jnp.concatenate(
        [
            grad_router.T,
            jnp.stack(
                [
                    grad_attn_gain,
                    grad_moe_gain,
                    jnp.sum(grad_query_gain, axis=(0, 1)),
                    jnp.sum(grad_key_gain, axis=(0, 1)),
                ]
            ),
        ],
        axis=0,
    )
    top_row = jnp.pad(head_top, (0, slice_width - heads_here), constant_values=-3e38)
    small, top_row = expert_total(small, top_row[None])
    head_top = top_row[0, :heads_here]
    if is_cube():
        seen["small"] = small
    (grad_down,) = weight_grads(
        weight_down_kernel,
        after(where[0], small, *due("weight_down", seen)),
        cots,
        scaled,
        [w_down.shape[1:]],
        "weight_down_grads",
    )
    mixture = scatter_ends(planes, small)
    out = residual + mixture
    sum_moe_gain, sum_query_gain, sum_key_gain = small[E + 1], small[E + 2], small[E + 3]
    every = lax.all_gather(small[: E + 1], "tensor")
    sum_router = every[:, :E].transpose(0, 2, 1).reshape(width, E)
    sum_attn_gain = every[:, E].reshape(width)
    sum_output, sum_value, sum_query, sum_key = settle_rows(
        jnp.stack(blocks), sum_output, sum_value, sum_both
    )
    factor = clip_threshold / jnp.maximum(head_top, clip_threshold)
    spread = jnp.repeat(jnp.sqrt(factor), HD)
    query_clipped = (w_query.astype(F32) * spread[None, :]).astype(BF16)
    key_clipped = (w_key.astype(F32) * spread[None, :]).astype(BF16)
    return (
        out,
        grad_input,
        sum_attn_gain,
        sum_query,
        sum_key,
        sum_value,
        sum_output,
        sum_query_gain,
        sum_key_gain,
        sum_moe_gain,
        sum_router,
        grad_gate,
        grad_up,
        grad_down,
        head_top,
        query_clipped,
        key_clipped,
    )


def solution(mesh):
    return jax.shard_map(
        per_device,
        mesh=mesh,
        in_specs=(
            P("expert", None),
            P(),
            P(None, "tensor"),
            P(None, "tensor"),
            P(None, "tensor"),
            P("tensor", None),
            P("tensor"),
            P("tensor"),
            P(),
            P(),
            P("expert", None, "tensor"),
            P("expert", None, "tensor"),
            P("expert", "tensor", None),
            P("expert", None),
            P("expert", None),
            P("expert", None),
            P("tensor"),
            P("expert", "tensor"),
        ),
        out_specs=(
            P("expert", "tensor"),
            P("expert", "tensor"),
            P(),
            P(None, "tensor"),
            P(None, "tensor"),
            P(None, "tensor"),
            P("tensor", None),
            P("tensor"),
            P("tensor"),
            P("tensor"),
            P(),
            P("expert", None, "tensor"),
            P("expert", None, "tensor"),
            P("expert", "tensor", None),
            P("tensor"),
            P(None, "tensor"),
            P(None, "tensor"),
        ),
        check_vma=False,
    )
```

```python
from functools import partial
import math

import jax
import jax.numpy as jnp
from jax import lax
from jax.experimental import pallas as pl
from jax.experimental.pallas import tpu as pltpu
from jax.sharding import PartitionSpec as P

HD = 128
E = 64
TOP = 8
LENGTH = 1024
CAP = 160
NB = 2
BOTH = ("expert", "tensor")
F32 = jnp.float32
BF16 = jnp.bfloat16
VMEM = 60 * 1024 * 1024
WEIGHT = 16
ORDER = (0, 2, 3, 1)
ODD = (1, 2)
DUE = {
    "attended": ("cx0", "cy0"),
    "normed": ("cd0",),
    "row0": ("cx2", "cy2", "nz2"),
    "cot2": ("cz3",),
    "row2": ("sc2",),
    "cot3": ("sg0",),
    "place0": ("sr2",),
    "exp2": ("sc3",),
    "cot1": ("sg2",),
    "place2": ("sr3", "ed0"),
    "exp3": ("sc1",),
    "place3": ("ex0", "ey0", "ed2"),
    "down1": ("sg1",),
    "place1": ("ed3", "ex2", "ey2"),
    "pd0": ("sd0",),
    "pd1": ("sd1", "ed1", "ex3", "ey3"),
    "weight": ("ex1", "ey1"),
    "residual_grad": ("gd0",),
    "back": ("gd1",),
    "normed_grad": ("gx0", "gy0"),
    "weight_down": ("hs",),
}


def cost(flops, bytes_accessed, transcendentals):
    return pl.CostEstimate(
        flops=flops * WEIGHT, bytes_accessed=bytes_accessed * WEIGHT, transcendentals=transcendentals * WEIGHT
    )


def matmul(left, right):
    return jnp.dot(left, right, preferred_element_type=F32)


def matmul_nt(left, right):
    return lax.dot_general(left, right, (((1,), (1,)), ((), ())), preferred_element_type=F32)


def matmul_tn(left, right):
    return lax.dot_general(left, right, (((0,), (0,)), ((), ())), preferred_element_type=F32)


def after(value, *others):
    return lax.optimization_barrier((value, *others))[0]


def flip(dz, dx, dy, dc):
    pairs = []
    for z in range(4):
        for x in range(2):
            for y in range(2):
                for c in range(2):
                    pairs.append(
                        (
                            ((z * 2 + x) * 2 + y) * 2 + c,
                            (((z ^ dz) * 2 + (x ^ dx)) * 2 + (y ^ dy)) * 2 + (c ^ dc),
                        )
                    )
    return pairs


def send(value, dz=0, dx=0, dy=0, dc=0):
    return lax.ppermute(value, BOTH, flip(dz, dx, dy, dc))


def is_cube():
    return lax.axis_size("expert") == 8 and lax.axis_size("tensor") == 4


def core_swap(value):
    if is_cube():
        return send(value, dc=1)
    count = lax.axis_size("tensor")
    return lax.ppermute(value, "tensor", [(i, i ^ 1) for i in range(count)])


def slot_blocks():
    owner, part = lax.axis_index("expert"), lax.axis_index("tensor")
    core = part % 2
    found = []
    for k in range(lax.axis_size("expert") // NB):
        places = [k * NB + b for b in range(NB)]
        if is_cube():
            owners = [owner ^ p for p in places]
            mine = [part ^ (y * 2) for y in range(2)]
        else:
            owners = places
            mine = [y * 2 + core for y in range(lax.axis_size("tensor") // 2)]
        theirs = [m ^ 1 for m in mine]
        rows = [m // 2 for m in mine]
        found.append(
            jnp.stack([jnp.asarray(v, jnp.int32) for v in places + owners + mine + theirs + rows])
        )
    return found


def gather_routes(routes):
    if not is_cube():
        return lax.all_gather(routes, "expert")
    both = jnp.stack([routes, send(routes, dx=1)])
    both = jnp.concatenate([both, send(both, dz=1)])
    return jnp.concatenate([both, send(both, dz=2)])


def same_core():
    count = lax.axis_size("tensor")
    return [[y * 2 + c for y in range(count // 2)] for c in range(2)]


def gather_all(own):
    owners, parts = lax.axis_size("expert"), lax.axis_size("tensor")
    groups = [[e * parts + t for e in range(owners) for t in range(c, parts, 2)] for c in range(2)]
    full = lax.all_gather(own, BOTH, axis_index_groups=groups)
    return full.reshape(owners, parts // 2, *own.shape)


def gather_slots(own, tag, seen, first=()):
    if not is_cube():
        return [gather_all(own)] * (lax.axis_size("expert") // NB)
    slots = []
    far_own = after(own, *first) if first else own
    for k in range(4):
        block = send(far_own, dz=k) if k else own
        over_x = send(block, dx=1)
        over_y = send(block, dy=1)
        far = send(over_x, dy=1) if k in ODD else send(over_y, dx=1)
        for link, value in zip("zxyd", (block, over_x, over_y, far)):
            seen[tag + link + str(k)] = value
        slots.append([[block, over_y], [over_x, far]])
    return slots


def added(*terms):
    return sum(t.astype(F32) for t in terms)


def scatter_corner(parts, odd):
    return send(parts[1][1], dy=1) if odd else send(parts[1][1], dx=1)


def scatter_plane(parts, far, odd, hold=()):
    near, over_y, over_x = parts[0][0], parts[0][1], parts[1][0]
    if odd:
        over_x, over_y = added(over_x, far).astype(BF16), after(over_y, far)
    else:
        over_x, over_y = after(over_x, far), added(over_y, far).astype(BF16)
    if hold:
        over_x, over_y = after(over_x, *hold), after(over_y, *hold)
    from_x, from_y = send(over_x, dx=1), send(over_y, dy=1)
    return added(near, from_x, from_y), {"d": far, "x": from_x, "y": from_y}


def scatter_all(slots):
    full = jnp.stack(
        [jnp.stack([s[b][y] for s in slots for b in range(NB)]) for y in range(len(slots[0][0]))]
    )
    mine = lax.psum_scatter(full, "tensor", axis_index_groups=same_core(), scatter_dimension=0)
    return lax.psum_scatter(mine, "expert", scatter_dimension=0).astype(F32)


def scatter_corners(pairs, seen):
    if not is_cube():
        return []
    far = [scatter_corner(pair, False) for pair in pairs]
    seen.update({"gd" + str(i): value for i, value in enumerate(far)})
    return far


def scatter_planes(pairs, far, hold, seen):
    if not is_cube():
        return pairs
    planes = []
    for i, pair in enumerate(pairs):
        plane, sent = scatter_plane(pair, far[i], False, hold)
        planes.append(plane)
        seen.update({"g" + link + str(i): value for link, value in sent.items()})
    return planes


def scatter_ends(planes, hold):
    if not is_cube():
        return scatter_all(
            [[[a[i] for a in b] for b in pair] for pair in planes for i in range(pair[0][0].shape[0])]
        )
    low, high = planes
    total = low + send(after(high.astype(BF16), hold), dz=2).astype(F32)
    return total[0] + send(total[1].astype(BF16), dz=1).astype(F32)


def tensor_order():
    part = lax.axis_index("tensor")
    if is_cube():
        return [part ^ i for i in (0, 2, 1, 3)]
    return [jnp.int32(i) for i in range(lax.axis_size("tensor"))]


def order_spots():
    if not is_cube():
        return lambda s: s
    part = lax.axis_index("tensor")
    return lambda s: (part ^ s) % 2 * 2 + (part ^ s) // 2


def tensor_gather(own):
    if not is_cube():
        full = lax.all_gather(own, "tensor")
        return [full[i] for i in range(full.shape[0])]
    over_y = send(own, dy=1)
    return [own, over_y, core_swap(own), core_swap(over_y)]


def tensor_scatter(product, pieces, tag, seen, beside=()):
    if not is_cube():
        full = jnp.concatenate([product(p).astype(BF16) for p in pieces], axis=1)
        return lax.psum_scatter(full, "tensor", scatter_dimension=1, tiled=True).astype(F32)
    away_y = product(pieces[3]).astype(BF16)
    away = product(pieces[2]).astype(BF16)
    from_y, near = core_swap(away_y), core_swap(away)
    away = added(product(pieces[1]), from_y).astype(BF16)
    over_y = after(send(away, dy=1), *beside) if beside else send(away, dy=1)
    seen.update({tag + "0": from_y, tag + "1": near, tag + "y": over_y, tag + "s": away})
    return added(product(pieces[0]), near, over_y)


def tensor_sum(value):
    if not is_cube():
        return lax.psum(value, "tensor")
    value = value + core_swap(value)
    return value + send(value, dy=1)


def row_blocks():
    if not is_cube():
        return [jnp.int32(i) for i in range(8)]
    owner = lax.axis_index("expert")
    return [owner ^ (b | first << 1 | second << 2) for b in (0, 1) for first in (0, 1) for second in (0, 1)]


def expert_sum(value):
    half = value.shape[0] // 2
    if not is_cube():
        value = lax.psum(value, "expert")
        return value[:half], value[half:]
    for step in ({"dx": 1}, {"dz": 1}, {"dz": 2}):
        half = value.shape[0] // 2
        value = added(value[:half], send(value[half:], **step)).astype(BF16)
    for step in ({"dz": 2}, {"dz": 1}):
        value = jnp.concatenate([value, send(value, **step)], axis=0)
    return value, send(value, dx=1)


def expert_total(sums, tops):
    if not is_cube():
        return lax.psum(sums, "expert"), lax.pmax(tops, "expert")
    count = sums.shape[0]
    both = jnp.concatenate([sums, tops], axis=0)
    for step in ({"dx": 1}, {"dz": 1}, {"dz": 2}):
        other = send(both, **step)
        both = jnp.concatenate([both[:count] + other[:count], jnp.maximum(both[count:], other[count:])])
    return both[:count], both[count:]


def one_hot(pos_row):
    rows = lax.broadcasted_iota(jnp.int32, (CAP, pos_row.shape[1]), 0)
    return rows == pos_row


def as_bf16(mask):
    return jnp.where(mask, 1.0, 0.0).astype(BF16)


def pick_kernel(group, slices, where_ref, *refs):
    pos_refs, x_refs = refs[:NB], refs[NB : NB + NB * slices]
    out_ref, hot_ref = refs[-2:]
    step = pl.program_id(0)
    for b in range(NB):
        for i in range(group):
            hot_ref[b, i * CAP : (i + 1) * CAP, :] = as_bf16(
                one_hot(pos_refs[b][0, pl.ds(step * group + i, 1), :])
            )
        for y in range(slices):
            out_ref[b, y] = matmul(hot_ref[b], x_refs[b * slices + y][...]).astype(BF16)


def pick_rows(where, pos, blocks):
    held = pos.shape[1]
    group = 2
    if isinstance(blocks, list):
        slices = len(blocks[0])
        flat = [a for b in blocks for a in b]
        tokens, width = flat[0].shape
        specs = [pl.BlockSpec((tokens, width), lambda i, where: (0, 0)) for _ in flat]
    else:
        slices, tokens, width = blocks.shape[1:]
        flat = [blocks] * (NB * slices)

        def part_spec(b, y):
            return pl.BlockSpec(
                (None, None, tokens, width),
                lambda i, where: (where[NB + b], where[2 * NB + 2 * slices + y], 0, 0),
            )

        specs = [part_spec(b, y) for b in range(NB) for y in range(slices)]

    def block_spec(b):
        return pl.BlockSpec((1, held, tokens), lambda i, where: (where[b], 0, 0))

    return pl.pallas_call(
        partial(pick_kernel, group, slices),
        grid_spec=pltpu.PrefetchScalarGridSpec(
            num_scalar_prefetch=1,
            grid=(held // group,),
            in_specs=[block_spec(b) for b in range(NB)]
            + specs,
            out_specs=pl.BlockSpec(
                (NB, slices, group * CAP, width), lambda i, where: (0, 0, i, 0)
            ),
            scratch_shapes=[pltpu.VMEM((NB, group * CAP, tokens), BF16)],
        ),
        out_shape=jax.ShapeDtypeStruct((NB, slices, held * CAP, width), BF16),
        compiler_params=pltpu.CompilerParams(vmem_limit_bytes=VMEM),
        cost_estimate=cost(
            flops=2 * NB * slices * held * CAP * tokens * width,
            bytes_accessed=2 * NB * slices * (held * CAP + tokens) * width,
            transcendentals=0,
        ),
        name="pick_rows",
    )(where, *([pos] * NB), *flat)


def expert_kernel(slices, where_ref, *refs):
    pos_refs, gate_refs = refs[:NB], refs[NB : 2 * NB]
    rows_mine, rows_theirs, cot_mine, cot_theirs, wg_ref, wu_ref, wd_ref = refs[2 * NB : 2 * NB + 7]
    scaled_ref, gate_grad_ref, up_grad_ref, prob_ref, keep_ref, give_ref = refs[2 * NB + 7 :]
    e = pl.program_id(0)
    width = rows_mine.shape[3]
    ff = wg_ref.shape[2]
    gate_pre = jnp.zeros((NB * CAP, ff), F32)
    up_pre = jnp.zeros((NB * CAP, ff), F32)
    grad_hidden = jnp.zeros((NB * CAP, ff), F32)

    def columns(j):
        return pl.ds(pl.multiple_of(where_ref[2 * NB + j] * width, width), width)

    for j in range(2 * slices):
        x_ref, c_ref = (rows_mine, cot_mine) if j < slices else (rows_theirs, cot_theirs)
        x = x_ref[:, j % slices].reshape(NB * CAP, width)
        c = c_ref[:, j % slices].reshape(NB * CAP, width)
        gate_pre = gate_pre + matmul(x, wg_ref[0, columns(j), :])
        up_pre = up_pre + matmul(x, wu_ref[0, columns(j), :])
        grad_hidden = grad_hidden + matmul_nt(c, wd_ref[0, :, columns(j)])
    masks = [one_hot(pos_refs[b][0, pl.ds(e, 1), :]) for b in range(NB)]
    gates = jnp.concatenate(
        [
            jnp.sum(jnp.where(masks[b], gate_refs[b][0, pl.ds(e, 1), :], 0.0), axis=1, keepdims=True)
            for b in range(NB)
        ],
        axis=0,
    )
    sigma = jax.nn.sigmoid(gate_pre)
    swish = gate_pre * sigma
    hidden = (swish * up_pre).astype(BF16).astype(F32)
    prob = jnp.sum(hidden * grad_hidden, axis=1, keepdims=True)
    for b in range(NB):
        prob_ref[0, b : b + 1, :] = jnp.sum(
            jnp.where(masks[b], prob[b * CAP : (b + 1) * CAP], 0.0), axis=0, keepdims=True
        )
    grad_hidden = grad_hidden * gates
    scaled_ref[0] = (hidden * gates).astype(BF16)
    gate_grad = (grad_hidden * up_pre * (sigma * (1.0 + gate_pre * (1.0 - sigma)))).astype(BF16)
    up_grad = (grad_hidden * swish).astype(BF16)
    gate_grad_ref[0] = gate_grad
    up_grad_ref[0] = up_grad
    for j in range(2 * slices):
        to = keep_ref if j < slices else give_ref
        back = matmul_nt(gate_grad, wg_ref[0, columns(j), :]) + matmul_nt(
            up_grad, wu_ref[0, columns(j), :]
        )
        to[:, j % slices] = back.astype(BF16).reshape(NB, CAP, width)


def expert_slot(where, pos, gate, rows, cots, w_gate, w_up, w_down):
    held, depth, ff = w_gate.shape
    tokens = pos.shape[2]
    slices, width = rows[0].shape[1], rows[0].shape[3]

    def block_spec(b):
        return pl.BlockSpec((1, held, tokens), lambda e, where: (where[b], 0, 0))

    rows_spec = pl.BlockSpec((NB, slices, CAP, width), lambda e, where: (0, 0, e, 0))
    rows_shape = jax.ShapeDtypeStruct((NB, slices, held * CAP, width), BF16)
    in_spec = pl.BlockSpec((1, depth, ff), lambda e, where: (e, 0, 0))
    hidden_spec = pl.BlockSpec((1, NB * CAP, ff), lambda e, where: (e, 0, 0))
    hidden_shape = jax.ShapeDtypeStruct((held, NB * CAP, ff), BF16)
    return pl.pallas_call(
        partial(expert_kernel, slices),
        grid_spec=pltpu.PrefetchScalarGridSpec(
            num_scalar_prefetch=1,
            grid=(held,),
            in_specs=[block_spec(b) for b in range(2 * NB)]
            + [rows_spec] * 4
            + [in_spec, in_spec, pl.BlockSpec((1, ff, depth), lambda e, where: (e, 0, 0))],
            out_specs=[hidden_spec] * 3
            + [pl.BlockSpec((1, NB, tokens), lambda e, where: (e, 0, 0)), rows_spec, rows_spec],
        ),
        out_shape=[hidden_shape] * 3
        + [jax.ShapeDtypeStruct((held, NB, tokens), F32), rows_shape, rows_shape],
        compiler_params=pltpu.CompilerParams(vmem_limit_bytes=VMEM),
        cost_estimate=cost(
            flops=10 * NB * held * CAP * depth * ff,
            bytes_accessed=6 * held * depth * ff + 6 * NB * held * CAP * depth,
            transcendentals=NB * held * CAP * ff,
        ),
        name="expert_slot",
    )(where, *([pos] * NB), *([gate] * NB), *rows, *cots, w_gate, w_up, w_down)


def down_kernel(slices, slots, where_ref, *refs):
    scaled_refs, wd_ref, keep_ref, give_ref = refs[:slots], refs[slots], refs[-2], refs[-1]
    width = keep_ref.shape[3]
    for j in range(2 * slices):
        to = keep_ref if j < slices else give_ref
        columns = pl.ds(pl.multiple_of(where_ref[2 * NB + j] * width, width), width)
        for k in range(slots):
            rows = matmul(scaled_refs[k][0], wd_ref[0, :, columns])
            to[k * NB : (k + 1) * NB, j % slices] = rows.astype(BF16).reshape(NB, CAP, width)


def down_slots(where, scaled, w_down, slices):
    held, ff, depth = w_down.shape
    width = depth // (2 * slices)
    slots = len(scaled)
    rows_spec = pl.BlockSpec((slots * NB, slices, CAP, width), lambda e, where: (0, 0, e, 0))
    rows_shape = jax.ShapeDtypeStruct((slots * NB, slices, held * CAP, width), BF16)
    return pl.pallas_call(
        partial(down_kernel, slices, slots),
        grid_spec=pltpu.PrefetchScalarGridSpec(
            num_scalar_prefetch=1,
            grid=(held,),
            in_specs=[pl.BlockSpec((1, NB * CAP, ff), lambda e, where: (e, 0, 0))] * slots
            + [pl.BlockSpec((1, ff, depth), lambda e, where: (e, 0, 0))],
            out_specs=[rows_spec, rows_spec],
        ),
        out_shape=[rows_shape, rows_shape],
        compiler_params=pltpu.CompilerParams(vmem_limit_bytes=VMEM),
        cost_estimate=cost(
            flops=2 * slots * NB * held * CAP * depth * ff,
            bytes_accessed=2 * held * depth * ff + 2 * slots * NB * held * CAP * depth,
            transcendentals=0,
        ),
        name="down_slots",
    )(where, *scaled, w_down)


def place_kernel(slices, held, slots, where_ref, *refs):
    count = NB * slots
    at_refs, mine_ref, theirs_ref = refs[:count], refs[count], refs[count + 1]
    out_refs, hot_ref = refs[count + 2 : -1], refs[-1]
    b, y = pl.program_id(0), pl.program_id(1)
    tokens = hot_ref.shape[0]
    for block in range(count):

        @pl.when((b == block) & (y == 0))
        def _():
            at = at_refs[block][0]
            for tile in range(held * CAP // 128):
                lanes = lax.broadcasted_iota(jnp.int32, (tokens, 128), 1) + tile * 128
                mask = None
                for e in range(tile * 128 // CAP, (tile * 128 + 127) // CAP + 1):
                    hit = at[:, e : e + 1] == lanes
                    mask = hit if mask is None else mask | hit
                hot_ref[:, tile * 128 : (tile + 1) * 128] = as_bf16(mask)

    rows = (mine_ref[0, 0].astype(F32) + theirs_ref[0, 0].astype(F32)).astype(BF16)
    placed = matmul(hot_ref[...], rows).astype(BF16)
    for block in range(count):
        for part in range(slices):

            @pl.when((b == block) & (y == part))
            def _():
                out_refs[block % NB * slices + part][block // NB] = placed


def place_rows(wheres, at, mine, theirs):
    _, slices, count, width = mine.shape
    _, tokens, held = at.shape
    slots = len(wheres)
    blocks = jnp.concatenate([w[:NB] for w in wheres])

    def block_spec(b):
        return pl.BlockSpec((1, tokens, held), lambda i, y, where: (where[b], 0, 0))

    rows_spec = pl.BlockSpec((1, 1, count, width), lambda i, y, where: (i, y, 0, 0))
    out = pl.pallas_call(
        partial(place_kernel, slices, held, slots),
        grid_spec=pltpu.PrefetchScalarGridSpec(
            num_scalar_prefetch=1,
            grid=(NB * slots, slices),
            in_specs=[block_spec(b) for b in range(NB * slots)] + [rows_spec, rows_spec],
            out_specs=[pl.BlockSpec((slots, tokens, width), lambda i, y, where: (0, 0, 0))]
            * (NB * slices),
            scratch_shapes=[pltpu.VMEM((tokens, count), BF16)],
        ),
        out_shape=[jax.ShapeDtypeStruct((slots, tokens, width), BF16)] * (NB * slices),
        compiler_params=pltpu.CompilerParams(vmem_limit_bytes=VMEM),
        cost_estimate=cost(
            flops=2 * NB * slots * slices * count * tokens * width,
            bytes_accessed=2 * NB * slots * slices * (2 * count + tokens) * width,
            transcendentals=0,
        ),
        name="place_rows",
    )(blocks, *([at] * (NB * slots)), mine, theirs)
    return [out[b * slices : (b + 1) * slices] for b in range(NB)]


def weight_kernel(slots, slices, where_ref, *refs):
    rows, gate_grads, up_grads = refs[: 2 * slots], refs[2 * slots : 3 * slots], refs[3 * slots : 4 * slots]
    gate_ref, up_ref = refs[4 * slots :]
    width = rows[0].shape[3]
    for j in range(2 * slices):
        columns = pl.ds(pl.multiple_of(where_ref[2 * NB + j] * width, width), width)
        gate = up = None
        for k in range(slots):
            x = rows[2 * k + j // slices][:, j % slices].reshape(NB * CAP, width)
            terms = matmul_tn(x, gate_grads[k][0]), matmul_tn(x, up_grads[k][0])
            gate, up = terms if gate is None else (gate + terms[0], up + terms[1])
        gate_ref[0, columns, :] = gate
        up_ref[0, columns, :] = up


def weight_down_kernel(slots, slices, where_ref, *refs):
    cots, scaled, down_ref = refs[: 2 * slots], refs[2 * slots : 3 * slots], refs[3 * slots]
    width = cots[0].shape[3]
    for j in range(2 * slices):
        columns = pl.ds(pl.multiple_of(where_ref[2 * NB + j] * width, width), width)
        down = None
        for k in range(slots):
            c = cots[2 * k + j // slices][:, j % slices].reshape(NB * CAP, width)
            term = matmul_tn(scaled[k][0], c)
            down = term if down is None else down + term
        down_ref[0, :, columns] = down


def weight_grads(kernel, where, rows, hiddens, outs, name):
    slots = len(rows)
    held, _, ff = hiddens[0].shape
    slices, width = rows[0][0].shape[1], rows[0][0].shape[3]
    depth = 2 * slices * width
    rows_spec = pl.BlockSpec((NB, slices, CAP, width), lambda e, where: (0, 0, e, 0))
    hidden_spec = pl.BlockSpec((1, NB * CAP, ff), lambda e, where: (e, 0, 0))
    return pl.pallas_call(
        partial(kernel, slots, slices),
        grid_spec=pltpu.PrefetchScalarGridSpec(
            num_scalar_prefetch=1,
            grid=(held,),
            in_specs=[rows_spec] * (2 * slots) + [hidden_spec] * len(hiddens),
            out_specs=[pl.BlockSpec((1, *o), lambda e, where: (e, 0, 0)) for o in outs],
        ),
        out_shape=[jax.ShapeDtypeStruct((held, *o), F32) for o in outs],
        compiler_params=pltpu.CompilerParams(vmem_limit_bytes=VMEM),
        cost_estimate=cost(flops=10**10, bytes_accessed=10**6, transcendentals=0),
        name=name,
    )(where, *[a for pair in rows for a in pair], *hiddens)


def settle_kernel(where_ref, *refs):
    halves, (output_ref, value_ref, query_ref, key_ref) = refs[:6], refs[6:]

    def settle(output, value, both):
        output_ref[...] = output[...].astype(F32).T
        value_ref[...] = value[...].astype(F32)
        width = query_ref.shape[1]
        query_ref[...] = both[:, :width].astype(F32)
        key_ref[...] = both[:, width:].astype(F32)

    @pl.when(pl.program_id(0) < 4)
    def _():
        settle(*halves[0::2])

    @pl.when(pl.program_id(0) >= 4)
    def _():
        settle(*halves[1::2])


def settle_rows(where, output, value, both):
    rows = 2 * value[0].shape[0]
    step = rows // 8
    width = value[0].shape[1]
    near = lambda n: pl.BlockSpec((step, n), lambda i, where: (jnp.minimum(i, 3), 0))
    far = lambda n: pl.BlockSpec((step, n), lambda i, where: (jnp.maximum(i, 4) - 4, 0))
    placed = pl.BlockSpec((step, width), lambda i, where: (where[i], 0))
    return pl.pallas_call(
        settle_kernel,
        grid_spec=pltpu.PrefetchScalarGridSpec(
            num_scalar_prefetch=1,
            grid=(8,),
            in_specs=[s(n) for n in (width, width, 2 * width) for s in (near, far)],
            out_specs=[pl.BlockSpec((width, step), lambda i, where: (0, where[i]))] + [placed] * 3,
        ),
        out_shape=[jax.ShapeDtypeStruct((width, rows), F32)]
        + [jax.ShapeDtypeStruct((rows, width), F32)] * 3,
        compiler_params=pltpu.CompilerParams(vmem_limit_bytes=VMEM),
        cost_estimate=cost(flops=0, bytes_accessed=24 * rows * width, transcendentals=0),
        name="settle_rows",
    )(where, *output, *value, *both)


def project_kernel(
    in_ref, ag_ref, wq_ref, wk_ref, wv_ref, qg_ref, kg_ref,
    x_ref, inv_ref, qr_ref, kr_ref, q_ref, k_ref, v_ref,
):
    @pl.when(pl.program_id(0) == 0)
    def _():
        for first in range(0, in_ref.shape[0], 256):
            rows = in_ref[first : first + 256, :].astype(F32)
            inverse = lax.rsqrt(jnp.mean(rows * rows, axis=1, keepdims=True) + 1e-05)
            inv_ref[first : first + 256, :] = inverse
            x_ref[first : first + 256, :] = (rows * inverse * ag_ref[...]).astype(BF16)

    x = x_ref[...]
    for w_ref, gain_ref, raw_ref, to_ref in ((wq_ref, qg_ref, qr_ref, q_ref), (wk_ref, kg_ref, kr_ref, k_ref)):
        raw = matmul(x, w_ref[...])
        raw_ref[...] = raw
        for h in range(raw.shape[1] // HD):
            part = raw[:, h * HD : (h + 1) * HD]
            inverse = lax.rsqrt(jnp.mean(part * part, axis=1, keepdims=True) + 1e-06)
            gain = gain_ref[:, h * HD : (h + 1) * HD]
            to_ref[:, h * HD : (h + 1) * HD] = (part * inverse * gain).astype(BF16)
    v_ref[...] = matmul(x, wv_ref[...]).astype(BF16)


def project(inputs, attn_gain, w_query, w_key, w_value, query_gain, key_gain):
    tokens, depth = inputs.shape
    columns = w_query.shape[1]
    step = min(256, columns)
    whole = pl.BlockSpec((tokens, depth), lambda i: (0, 0))
    weight = pl.BlockSpec((depth, step), lambda i: (0, i))
    gain = pl.BlockSpec((1, step), lambda i: (0, i))
    out = pl.BlockSpec((tokens, step), lambda i: (0, i))
    return pl.pallas_call(
        project_kernel,
        grid=(columns // step,),
        in_specs=[whole, pl.BlockSpec((1, depth), lambda i: (0, 0)), weight, weight, weight, gain, gain],
        out_specs=[whole, pl.BlockSpec((tokens, 1), lambda i: (0, 0))] + [out] * 5,
        out_shape=[
            jax.ShapeDtypeStruct((tokens, depth), BF16),
            jax.ShapeDtypeStruct((tokens, 1), F32),
        ]
        + [jax.ShapeDtypeStruct((tokens, columns), t) for t in (F32, F32, BF16, BF16, BF16)],
        compiler_params=pltpu.CompilerParams(vmem_limit_bytes=VMEM),
        cost_estimate=cost(
            flops=6 * tokens * depth * columns,
            bytes_accessed=4 * tokens * depth + 6 * depth * columns + 14 * tokens * columns,
            transcendentals=0,
        ),
        name="project",
    )(
        inputs, attn_gain.reshape(1, -1), w_query, w_key, w_value,
        query_gain.reshape(1, -1), key_gain.reshape(1, -1),
    )


def allowed_pairs(pieces_ref, base, first, rows, keys):
    query = first + lax.broadcasted_iota(jnp.int32, (rows, 1), 0)
    key = lax.broadcasted_iota(jnp.int32, (1, keys), 1)

    def piece_of(at, other):
        found = jnp.full(at.shape, other, jnp.int32)
        for j in range(2):
            start, length = pieces_ref[base + j], pieces_ref[base + 2 + j]
            found = jnp.where((at >= start) & (at < start + length), j, found)
        return found

    return (key <= query) | (piece_of(query, -1) == piece_of(key, -2))


def query_blocks():
    half = LENGTH // 2
    return ((0, half, half), (half, half, LENGTH))


def attend_kernel(scale, pieces_ref, q_ref, k_ref, v_ref, o_ref, log_ref, top_ref):
    base = pl.program_id(0) * 4
    best = None
    for first, rows, keys in query_blocks():
        allowed = allowed_pairs(pieces_ref, base, first, rows, keys)
        scores = matmul_nt(q_ref[first : first + rows, :], k_ref[:keys, :]) * scale
        masked = jnp.where(allowed, scores, -1e30)
        top = jnp.max(masked, axis=1, keepdims=True)
        weights = jnp.exp(masked - top)
        total = jnp.sum(weights, axis=1, keepdims=True)
        probs = (weights * (1.0 / total)).astype(BF16)
        o_ref[first : first + rows, :] = matmul(probs, v_ref[:keys, :]).astype(BF16)
        log_ref[0, first : first + rows, :] = top + jnp.log(total)
        most = jnp.max(top, axis=0, keepdims=True)
        best = most if best is None else jnp.maximum(best, most)
    top_ref[0] = jnp.broadcast_to(best, (8, HD))


def attend(pieces, queries, keys, values, scale):
    tokens, columns = queries.shape
    sequences, heads = tokens // LENGTH, columns // HD
    block = pl.BlockSpec((LENGTH, HD), lambda s, h, pieces: (s, h))
    return pl.pallas_call(
        partial(attend_kernel, scale),
        grid_spec=pltpu.PrefetchScalarGridSpec(
            num_scalar_prefetch=1,
            grid=(sequences, heads),
            in_specs=[block] * 3,
            out_specs=[
                block,
                pl.BlockSpec((1, LENGTH, 1), lambda s, h, pieces: (h, s, 0)),
                pl.BlockSpec((1, 8, HD), lambda s, h, pieces: (s * heads + h, 0, 0)),
            ],
        ),
        out_shape=[
            jax.ShapeDtypeStruct((tokens, columns), BF16),
            jax.ShapeDtypeStruct((heads, tokens, 1), F32),
            jax.ShapeDtypeStruct((sequences * heads, 8, HD), F32),
        ],
        compiler_params=pltpu.CompilerParams(vmem_limit_bytes=VMEM),
        cost_estimate=cost(
            flops=4 * tokens * LENGTH * columns,
            bytes_accessed=8 * tokens * columns,
            transcendentals=tokens * heads * LENGTH,
        ),
        name="attend",
    )(pieces, queries, keys, values)


def attend_back_kernel(
    scale, pieces_ref, q_ref, k_ref, v_ref, g_ref, log_ref, qr_ref, kr_ref, qg_ref, kg_ref,
    gq_ref, gk_ref, gv_ref, gqg_ref, gkg_ref, dq_ref, dk_ref, dv_ref,
):
    base = pl.program_id(0) * 4
    blocks = query_blocks()
    for first, rows, keys in blocks[::-1]:
        allowed = allowed_pairs(pieces_ref, base, first, rows, keys)
        q, g = q_ref[first : first + rows, :], g_ref[first : first + rows, :]
        k, v = k_ref[:keys, :], v_ref[:keys, :]
        scores = matmul_nt(q, k) * scale
        probs = jnp.exp(jnp.where(allowed, scores, -1e30) - log_ref[0, first : first + rows, :])
        grad_p = matmul_nt(g, v)
        delta = jnp.sum(probs * grad_p, axis=1, keepdims=True)
        grad_s = (probs * (grad_p - delta)).astype(BF16)
        dq_ref[first : first + rows, :] = matmul(grad_s, k) * scale
        dk = matmul_tn(grad_s, q) * scale
        dv = matmul_tn(probs.astype(BF16), g)
        if keys == LENGTH:
            dk_ref[...] = dk
            dv_ref[...] = dv
        else:
            dk_ref[:keys, :] += dk
            dv_ref[:keys, :] += dv
    gv_ref[...] = dv_ref[...].astype(BF16)
    for raw_ref, gain_ref, grad_ref, to_ref, sum_ref in (
        (qr_ref, qg_ref, dq_ref, gq_ref, gqg_ref),
        (kr_ref, kg_ref, dk_ref, gk_ref, gkg_ref),
    ):
        raw, grad = raw_ref[...], grad_ref[...]
        inverse = lax.rsqrt(jnp.mean(raw * raw, axis=1, keepdims=True) + 1e-06)
        hat = raw * inverse
        up = grad * gain_ref[...]
        mean = jnp.mean(up * hat, axis=1, keepdims=True)
        to_ref[...] = (inverse * (up - hat * mean)).astype(BF16)
        sum_ref[0] = jnp.sum(grad * hat, axis=0, keepdims=True)


def attend_back(pieces, queries, keys, values, grads, logs, query_raw, key_raw, query_gain, key_gain, scale):
    tokens, columns = queries.shape
    sequences, heads = tokens // LENGTH, columns // HD
    block = pl.BlockSpec((LENGTH, HD), lambda s, h, pieces: (s, h))
    gain = pl.BlockSpec((1, HD), lambda s, h, pieces: (0, h))
    sums = pl.BlockSpec((1, 1, HD), lambda s, h, pieces: (s, 0, h))
    return pl.pallas_call(
        partial(attend_back_kernel, scale),
        grid_spec=pltpu.PrefetchScalarGridSpec(
            num_scalar_prefetch=1,
            grid=(sequences, heads),
            in_specs=[block] * 4
            + [pl.BlockSpec((1, LENGTH, 1), lambda s, h, pieces: (h, s, 0)), block, block, gain, gain],
            out_specs=[block, block, block, sums, sums],
            scratch_shapes=[pltpu.VMEM((LENGTH, HD), F32)] * 3,
        ),
        out_shape=[jax.ShapeDtypeStruct((tokens, columns), BF16)] * 3
        + [jax.ShapeDtypeStruct((sequences, 1, columns), F32)] * 2,
        compiler_params=pltpu.CompilerParams(vmem_limit_bytes=VMEM),
        cost_estimate=cost(
            flops=10 * tokens * LENGTH * columns,
            bytes_accessed=22 * tokens * columns,
            transcendentals=tokens * heads * LENGTH,
        ),
        name="attend_back",
    )(
        pieces, queries, keys, values, grads, logs, query_raw, key_raw,
        query_gain.reshape(1, -1), key_gain.reshape(1, -1),
    )


def expert_steps(slots):
    order = list(ORDER) if is_cube() else list(range(slots))
    steps = [("cot", order[0]), ("row", order[0]), ("cot", order[1]), ("exp", order[0])]
    for i, k in enumerate(order):
        if i + 1 < slots:
            steps.append(("row", order[i + 1]))
        else:
            steps += [("down", j) for j in range(slots // 2)]
        if i + 2 < slots:
            steps.append(("cot", order[i + 2]))
        steps.append(("place", k))
        if i + 1 < slots:
            steps.append(("exp", order[i + 1]))
    return steps


def due(step, seen):
    return [seen[name] for name in DUE.get(step, ()) if name in seen]


def per_device(
    inputs,
    attn_gain,
    w_query,
    w_key,
    w_value,
    w_output,
    query_gain,
    key_gain,
    moe_gain,
    w_router,
    w_gate,
    w_up,
    w_down,
    routes,
    piece_start,
    piece_length,
    clip_threshold,
    cotangent,
):
    tokens_here, width = inputs.shape
    slice_width = cotangent.shape[1]
    owner = lax.axis_index("expert")
    column = lax.axis_index("tensor") * slice_width
    heads_here = query_gain.shape[0] // HD
    experts_here = w_gate.shape[0]
    owners = lax.axis_size("expert")
    sequences = tokens_here // LENGTH
    scale = 1.0 / math.sqrt(HD)
    where = slot_blocks()
    slots = len(where)
    slices = lax.axis_size("tensor") // 2

    def own_columns(value):
        return lax.dynamic_slice_in_dim(value, column, slice_width, value.ndim - 1)

    seen = {}
    all_routes = gather_routes(routes.T)
    cot_slots = gather_slots(cotangent.astype(BF16), "c", seen, [all_routes])
    order = tensor_order()

    held_ids = owner * experts_here + jnp.arange(experts_here, dtype=jnp.int32)
    chosen = jnp.any(all_routes[:, None] == held_ids[None, :, None, None], axis=2)
    places = jnp.arange(tokens_here, dtype=jnp.int32)
    before = (places[:, None] < places[None, :]).astype(BF16)
    earlier = jnp.einsum(
        "set,tu->seu", chosen.astype(BF16), before, preferred_element_type=F32
    ).astype(jnp.int32)
    pos = jnp.where(chosen, earlier, -1)
    at = jnp.where(
        chosen, earlier + jnp.arange(experts_here, dtype=jnp.int32)[None, :, None] * CAP, -1
    ).transpose(0, 2, 1)

    output_pieces = [lax.dynamic_slice_in_dim(w_output, o * slice_width, slice_width, 1) for o in order]
    normed_a, attn_inv, query_raw, key_raw, queries, keys, values = project(
        inputs, attn_gain, w_query, w_key, w_value, query_gain, key_gain
    )
    blocks = row_blocks()
    normed_rows = jnp.concatenate(
        [lax.dynamic_slice_in_dim(normed_a, r * (width // 8), width // 8, 1) for r in blocks], axis=1
    )
    pieces = jnp.concatenate([piece_start, piece_length], axis=1).reshape(-1)
    attended, logs, tops = attend(
        after(pieces, values, all_routes), queries, keys, values, scale
    )
    head_top = jnp.max(tops[:, 0, 0].reshape(sequences, heads_here), axis=0)
    attended = after(attended, *due("attended", seen))
    branch = tensor_scatter(partial(matmul, attended), output_pieces, "b", seen, [pos, at])
    residual = own_columns(inputs).astype(F32) + branch
    gain_slice = own_columns(moe_gain)
    router_slice = lax.dynamic_slice_in_dim(w_router, column, slice_width, 0)
    lifted = residual * gain_slice
    row_sums = tensor_sum(
        jnp.concatenate(
            [
                lax.dot_general(
                    router_slice,
                    lifted.astype(BF16),
                    (((0,), (1,)), ((), ())),
                    preferred_element_type=F32,
                ),
                jnp.sum(residual * residual, axis=1)[None],
            ],
            axis=0,
        )
    )
    moe_inv_row = lax.rsqrt(row_sums[E] / width + 1e-05)
    moe_inv = moe_inv_row[:, None]
    normed_m = (lifted * moe_inv).astype(BF16)
    normed_m = after(normed_m, *due("normed", seen))

    normed_slots = gather_slots(normed_m, "n", seen)
    router = jax.nn.softmax(row_sums[:E] * moe_inv_row[None], axis=0)
    gate = lax.all_to_all(
        router.reshape(owners, experts_here, tokens_here),
        "expert",
        split_axis=0,
        concat_axis=0,
        tiled=True,
    )

    rows, cots, back, sums = [None] * slots, [None] * slots, [None] * slots, [None] * slots
    scaled, gate_grads, up_grads, probs = [None] * slots, [None] * slots, [None] * slots, [None] * slots
    last = normed_m
    downs = {}

    def turn(name, k):
        return after(where[k], last, *due(name, seen))

    def lower(k):
        keep, give = down_slots(turn("down" + str(k), 0), scaled[2 * k : 2 * k + 2], w_down, slices)
        downs[k] = (keep, core_swap(give))
        seen["sd" + str(k)] = downs[k][1]
        return keep

    for kind, k in expert_steps(slots):
        now = turn(kind + str(k), k)
        if kind == "cot":
            last = pick_rows(now, pos, cot_slots[k])
            cots[k] = (last, core_swap(last))
            seen["sc" + str(k)] = cots[k][1]
        elif kind == "row":
            last = pick_rows(now, pos, normed_slots[k])
            rows[k] = (last, core_swap(last))
            seen["sr" + str(k)] = rows[k][1]
        elif kind == "exp":
            scaled[k], gate_grads[k], up_grads[k], probs[k], keep, give = expert_slot(
                now, pos, gate, rows[k], cots[k], w_gate, w_up, w_down
            )
            last = scaled[k]
            back[k] = (keep, core_swap(give))
            seen["sg" + str(k)] = back[k][1]
        elif kind == "down":
            last = lower(k)
        else:
            placed = place_rows([now], at, *back[k])
            last = placed[0][0]
            back[k] = [[a[0] for a in b] for b in placed]
            if is_cube():
                odd = k in ODD
                sums[k], sent = scatter_plane(back[k], scatter_corner(back[k], odd), odd)
                if k:
                    sums[k] = sent["z"] = send(sums[k].astype(BF16), dz=k)
                seen.update({"e" + link + str(k): value for link, value in sent.items()})
    pairs = []
    for k in range(slots // 2):
        pairs.append(place_rows([turn("pd" + str(k), 2 * k), where[2 * k + 1]], at, *downs[k]))
        last = pairs[k][0][0]
    far = scatter_corners(pairs, seen)
    grad_gate, grad_up = weight_grads(
        weight_kernel,
        turn("weight", 0),
        rows,
        gate_grads + up_grads,
        [w_gate.shape[1:]] * 2,
        "weight_grads",
    )
    if is_cube():
        expert_path = added(*[after(s, grad_gate) for s in sums])
    else:
        expert_path = scatter_all(back)

    prob_grads = jnp.stack([probs[k][:, b] for k in range(slots) for b in range(NB)])
    if is_cube():
        prob_grads = prob_grads[jnp.arange(owners, dtype=jnp.int32) ^ owner]
    prob_grads = lax.all_to_all(prob_grads, "expert", split_axis=0, concat_axis=0, tiled=True)
    prob_grads = tensor_sum(prob_grads.reshape(E, tokens_here))
    grad_logits = (
        router * (prob_grads - jnp.sum(router * prob_grads, axis=0, keepdims=True))
    ).astype(BF16)
    grad_router = lax.dot_general(
        normed_m, grad_logits, (((0,), (1,)), ((), ())), preferred_element_type=F32
    )
    router_path = lax.dot_general(
        grad_logits, router_slice, (((0,), (1,)), ((), ())), preferred_element_type=F32
    )
    grad_normed = expert_path + router_path
    moe_hat = residual * moe_inv
    grad_moe_gain = jnp.sum(grad_normed * moe_hat, axis=0)
    upstream = grad_normed * gain_slice
    mean_dot = tensor_sum(jnp.sum(upstream * moe_hat, axis=-1).reshape(8, -1)).reshape(-1, 1) / width
    grad_residual = cotangent + moe_inv * (upstream - moe_hat * mean_dot)
    branch_pieces = tensor_gather(after(grad_residual.astype(BF16), *due("residual_grad", seen)))

    planes = scatter_planes(pairs, far, branch_pieces[1:2], seen)
    grad_branch = jnp.concatenate(branch_pieces, axis=1)

    grad_output = matmul_tn(grad_branch, attended).astype(BF16)
    spots = order_spots()
    eighth = width // 8
    wide = slice_width // eighth
    grad_output = jnp.concatenate(
        [
            lax.dynamic_slice_in_dim(
                grad_output, (spots(r // wide) * wide + r % wide) * eighth, eighth, 0
            )
            for r in blocks
        ],
        axis=0,
    )
    sum_output = expert_sum(grad_output)
    grad_attended = matmul_nt(grad_branch, jnp.concatenate(output_pieces, axis=1)).astype(BF16)
    grad_attended = after(grad_attended, grad_output)
    grad_query_raw, grad_key_raw, grad_v, grad_query_gain, grad_key_gain = attend_back(
        after(pieces, *due("back", seen)),
        queries,
        keys,
        values,
        grad_attended,
        logs,
        query_raw,
        key_raw,
        query_gain,
        key_gain,
        scale,
    )
    sum_value = expert_sum(matmul_tn(normed_rows, grad_v).astype(BF16))
    grad_raw = jnp.concatenate([grad_query_raw, grad_key_raw, grad_v], axis=1)
    grad_both = matmul_tn(normed_rows, grad_raw[:, : 2 * slice_width]).astype(BF16)
    sum_both = expert_sum(grad_both)
    grad_raw = after(grad_raw, grad_both, *due("normed_grad", seen))
    weights = jnp.concatenate([w_query, w_key, w_value], axis=1)
    weight_pieces = [lax.dynamic_slice_in_dim(weights, o * slice_width, slice_width, 0) for o in order]
    grad_normed_a = tensor_scatter(partial(matmul_nt, grad_raw), weight_pieces, "h", seen)
    (grad_down,) = weight_grads(
        weight_down_kernel,
        after(where[0], *due("weight_down", seen)),
        cots,
        scaled,
        [w_down.shape[1:]],
        "weight_down_grads",
    )
    attn_hat = own_columns(inputs).astype(F32) * attn_inv
    upstream = grad_normed_a * own_columns(attn_gain)
    grad_attn_gain = jnp.sum(grad_normed_a * attn_hat, axis=0)
    mean_dot = tensor_sum(jnp.sum(upstream * attn_hat, axis=-1).reshape(8, -1)).reshape(-1, 1) / width
    grad_input = grad_residual + attn_inv * (upstream - attn_hat * mean_dot)

    small = jnp.concatenate(
        [
            grad_router.T,
            jnp.stack(
                [
                    grad_attn_gain,
                    grad_moe_gain,
                    jnp.sum(grad_query_gain, axis=(0, 1)),
                    jnp.sum(grad_key_gain, axis=(0, 1)),
                ]
            ),
        ],
        axis=0,
    )
    top_row = jnp.pad(head_top, (0, slice_width - heads_here), constant_values=-3e38)
    small, top_row = expert_total(small, top_row[None])
    head_top = top_row[0, :heads_here]
    mixture = scatter_ends(planes, small)
    out = residual + mixture
    sum_moe_gain, sum_query_gain, sum_key_gain = small[E + 1], small[E + 2], small[E + 3]
    every = lax.all_gather(small[: E + 1], "tensor")
    sum_router = every[:, :E].transpose(0, 2, 1).reshape(width, E)
    sum_attn_gain = every[:, E].reshape(width)
    sum_output, sum_value, sum_query, sum_key = settle_rows(
        jnp.stack(blocks), sum_output, sum_value, sum_both
    )
    factor = clip_threshold / jnp.maximum(head_top, clip_threshold)
    spread = jnp.repeat(jnp.sqrt(factor), HD)
    query_clipped = (w_query.astype(F32) * spread[None, :]).astype(BF16)
    key_clipped = (w_key.astype(F32) * spread[None, :]).astype(BF16)
    return (
        out,
        grad_input,
        sum_attn_gain,
        sum_query,
        sum_key,
        sum_value,
        sum_output,
        sum_query_gain,
        sum_key_gain,
        sum_moe_gain,
        sum_router,
        grad_gate,
        grad_up,
        grad_down,
        head_top,
        query_clipped,
        key_clipped,
    )


def solution(mesh):
    return jax.shard_map(
        per_device,
        mesh=mesh,
        in_specs=(
            P("expert", None),
            P(),
            P(None, "tensor"),
            P(None, "tensor"),
            P(None, "tensor"),
            P("tensor", None),
            P("tensor"),
            P("tensor"),
            P(),
            P(),
            P("expert", None, "tensor"),
            P("expert", None, "tensor"),
            P("expert", "tensor", None),
            P("expert", None),
            P("expert", None),
            P("expert", None),
            P("tensor"),
            P("expert", "tensor"),
        ),
        out_specs=(
            P("expert", "tensor"),
            P("expert", "tensor"),
            P(),
            P(None, "tensor"),
            P(None, "tensor"),
            P(None, "tensor"),
            P("tensor", None),
            P("tensor"),
            P("tensor"),
            P("tensor"),
            P(),
            P("expert", None, "tensor"),
            P("expert", None, "tensor"),
            P("expert", "tensor", None),
            P("tensor"),
            P(None, "tensor"),
            P(None, "tensor"),
        ),
        check_vma=False,
    )
```

```python
from functools import partial
import math

import jax
import jax.numpy as jnp
from jax import lax
from jax.experimental import pallas as pl
from jax.experimental.pallas import tpu as pltpu
from jax.sharding import PartitionSpec as P

HD = 128
E = 64
TOP = 8
LENGTH = 1024
CAP = 160
NB = 2
BOTH = ("expert", "tensor")
F32 = jnp.float32
BF16 = jnp.bfloat16
VMEM = 60 * 1024 * 1024
WEIGHT = 16
ORDER = (0, 2, 3, 1)
ODD = (1, 2)
DUE = {
    "attended": ("cx0", "cy0"),
    "normed": ("cz2", "cd0"),
    "row0": ("cx2", "cz3", "cy2"),
    "exp0": ("cx3",),
    "row2": ("sc2", "cy3"),
    "cot3": ("sg0",),
    "place0": ("sr2",),
    "exp2": ("sc3",),
    "cot1": ("sg2",),
    "place2": ("sr3", "ed0"),
    "exp3": ("sc1",),
    "place3": ("ex0", "ey0", "ed2"),
    "down1": ("ex2", "ey2", "ed3"),
    "pd0": ("ed1", "sd0"),
    "weight": ("ex3", "ey3", "ex1", "ey1"),
    "residual_grad": ("gd0", "gd1"),
    "back": ("gx0",),
    "normed_grad": ("gx1", "gy0"),
    "ends": ("qk2",),
}


def cost(flops, bytes_accessed, transcendentals):
    return pl.CostEstimate(
        flops=flops * WEIGHT, bytes_accessed=bytes_accessed * WEIGHT, transcendentals=transcendentals * WEIGHT
    )


def matmul(left, right):
    return jnp.dot(left, right, preferred_element_type=F32)


def matmul_nt(left, right):
    return lax.dot_general(left, right, (((1,), (1,)), ((), ())), preferred_element_type=F32)


def matmul_tn(left, right):
    return lax.dot_general(left, right, (((0,), (0,)), ((), ())), preferred_element_type=F32)


def after(value, *others):
    return lax.optimization_barrier((value, *others))[0]


def flip(dz, dx, dy, dc):
    pairs = []
    for z in range(4):
        for x in range(2):
            for y in range(2):
                for c in range(2):
                    pairs.append(
                        (
                            ((z * 2 + x) * 2 + y) * 2 + c,
                            (((z ^ dz) * 2 + (x ^ dx)) * 2 + (y ^ dy)) * 2 + (c ^ dc),
                        )
                    )
    return pairs


def send(value, dz=0, dx=0, dy=0, dc=0):
    return lax.ppermute(value, BOTH, flip(dz, dx, dy, dc))


def is_cube():
    return lax.axis_size("expert") == 8 and lax.axis_size("tensor") == 4


def core_swap(value):
    if is_cube():
        return send(value, dc=1)
    count = lax.axis_size("tensor")
    return lax.ppermute(value, "tensor", [(i, i ^ 1) for i in range(count)])


def slot_blocks():
    owner, part = lax.axis_index("expert"), lax.axis_index("tensor")
    core = part % 2
    found = []
    for k in range(lax.axis_size("expert") // NB):
        places = [k * NB + b for b in range(NB)]
        if is_cube():
            owners = [owner ^ p for p in places]
            mine = [part ^ (y * 2) for y in range(2)]
        else:
            owners = places
            mine = [y * 2 + core for y in range(lax.axis_size("tensor") // 2)]
        theirs = [m ^ 1 for m in mine]
        rows = [m // 2 for m in mine]
        found.append(
            jnp.stack([jnp.asarray(v, jnp.int32) for v in places + owners + mine + theirs + rows])
        )
    return found


def gather_routes(routes):
    if not is_cube():
        return lax.all_gather(routes, "expert")
    both = jnp.stack([routes, send(routes, dx=1)])
    both = jnp.concatenate([both, send(both, dz=1)])
    return jnp.concatenate([both, send(both, dz=2)])


def same_core():
    count = lax.axis_size("tensor")
    return [[y * 2 + c for y in range(count // 2)] for c in range(2)]


def gather_all(own):
    owners, parts = lax.axis_size("expert"), lax.axis_size("tensor")
    groups = [[e * parts + t for e in range(owners) for t in range(c, parts, 2)] for c in range(2)]
    full = lax.all_gather(own, BOTH, axis_index_groups=groups)
    return full.reshape(owners, parts // 2, *own.shape)


def gather_slots(own, tag, seen, first=()):
    if not is_cube():
        return [gather_all(own)] * (lax.axis_size("expert") // NB)
    slots = []
    far_own = after(own, *first) if first else own
    for k in range(4):
        block = send(far_own, dz=k) if k else own
        over_x = send(block, dx=1)
        over_y = send(block, dy=1)
        far = send(over_x, dy=1) if k in ODD else send(over_y, dx=1)
        for link, value in zip("zxyd", (block, over_x, over_y, far)):
            seen[tag + link + str(k)] = value
        slots.append([[block, over_y], [over_x, far]])
    return slots


def added(*terms):
    return sum(t.astype(F32) for t in terms)


def scatter_corner(parts, odd):
    return send(parts[1][1], dy=1) if odd else send(parts[1][1], dx=1)


def scatter_plane(parts, far, odd, hold=()):
    near, over_y, over_x = parts[0][0], parts[0][1], parts[1][0]
    if odd:
        over_x, over_y = added(over_x, far).astype(BF16), after(over_y, far)
    else:
        over_x, over_y = after(over_x, far), added(over_y, far).astype(BF16)
    if hold:
        over_y = after(over_y, *hold)
    from_x, from_y = send(over_x, dx=1), send(over_y, dy=1)
    return added(near, from_x, from_y), {"d": far, "x": from_x, "y": from_y}


def scatter_all(slots):
    full = jnp.stack(
        [jnp.stack([s[b][y] for s in slots for b in range(NB)]) for y in range(len(slots[0][0]))]
    )
    mine = lax.psum_scatter(full, "tensor", axis_index_groups=same_core(), scatter_dimension=0)
    return lax.psum_scatter(mine, "expert", scatter_dimension=0).astype(F32)


def scatter_corners(pairs, seen):
    if not is_cube():
        return []
    far = [scatter_corner(pair, i == 0) for i, pair in enumerate(pairs)]
    seen.update({"gd" + str(i): value for i, value in enumerate(far)})
    return far


def scatter_planes(pairs, far, hold, seen):
    if not is_cube():
        return pairs
    planes = []
    for i, pair in enumerate(pairs):
        plane, sent = scatter_plane(pair, far[i], i == 0, hold)
        planes.append(plane)
        seen.update({"g" + link + str(i): value for link, value in sent.items()})
    return planes


def scatter_ends(planes, hold):
    if not is_cube():
        return scatter_all(
            [[[a[i] for a in b] for b in pair] for pair in planes for i in range(pair[0][0].shape[0])]
        )
    low, high = planes
    total = low + send(after(high.astype(BF16), *hold), dz=2).astype(F32)
    return total[0] + send(total[1].astype(BF16), dz=1).astype(F32)


def tensor_order():
    part = lax.axis_index("tensor")
    if is_cube():
        return [part ^ i for i in (0, 2, 1, 3)]
    return [jnp.int32(i) for i in range(lax.axis_size("tensor"))]


def order_spots():
    if not is_cube():
        return lambda s: s
    part = lax.axis_index("tensor")
    return lambda s: (part ^ s) % 2 * 2 + (part ^ s) // 2


def tensor_gather(own, beside=()):
    if not is_cube():
        full = lax.all_gather(own, "tensor")
        return [full[i] for i in range(full.shape[0])]
    over_y = after(send(own, dy=1), *beside)
    return [own, over_y, core_swap(own), core_swap(over_y)]


def tensor_scatter(product, pieces, tag, seen, beside=()):
    if not is_cube():
        full = jnp.concatenate([product(p).astype(BF16) for p in pieces], axis=1)
        return lax.psum_scatter(full, "tensor", scatter_dimension=1, tiled=True).astype(F32)
    away_y = product(pieces[3]).astype(BF16)
    away = product(pieces[2]).astype(BF16)
    from_y, near = core_swap(away_y), core_swap(away)
    away = added(product(pieces[1]), from_y).astype(BF16)
    over_y = after(send(away, dy=1), *beside) if beside else send(away, dy=1)
    seen.update({tag + "0": from_y, tag + "1": near, tag + "y": over_y, tag + "s": away})
    return added(product(pieces[0]), near, over_y)


def tensor_sum(value):
    if not is_cube():
        return lax.psum(value, "tensor")
    value = value + core_swap(value)
    return value + send(value, dy=1)


def row_blocks():
    if not is_cube():
        return [jnp.int32(i) for i in range(8)]
    owner = lax.axis_index("expert")
    return [owner ^ (b | first << 1 | second << 2) for b in (0, 1) for first in (0, 1) for second in (0, 1)]


def expert_sum(value, tag, seen):
    half = value.shape[0] // 2
    if not is_cube():
        value = lax.psum(value, "expert")
        return value[:half], value[half:]
    for step in ({"dx": 1}, {"dz": 1}, {"dz": 2}):
        half = value.shape[0] // 2
        value = added(value[:half], send(value[half:], **step)).astype(BF16)
    for step in ({"dz": 2}, {"dz": 1}):
        seen[tag] = send(value, **step)
        value = jnp.concatenate([value, seen[tag]], axis=0)
        seen[tag + str(step["dz"])] = seen[tag]
    return value, send(value, dx=1)


def expert_total(sums, tops):
    if not is_cube():
        return lax.psum(sums, "expert"), lax.pmax(tops, "expert")
    count = sums.shape[0]
    both = jnp.concatenate([sums, tops], axis=0)
    for step in ({"dx": 1}, {"dz": 1}, {"dz": 2}):
        other = send(both, **step)
        both = jnp.concatenate([both[:count] + other[:count], jnp.maximum(both[count:], other[count:])])
    return both[:count], both[count:]


def one_hot(pos_row):
    rows = lax.broadcasted_iota(jnp.int32, (CAP, pos_row.shape[1]), 0)
    return rows == pos_row


def as_bf16(mask):
    return jnp.where(mask, 1.0, 0.0).astype(BF16)


def pick_kernel(group, slices, where_ref, *refs):
    pos_refs, x_refs = refs[:NB], refs[NB : NB + NB * slices]
    out_ref, hot_ref = refs[-2:]
    step = pl.program_id(0)
    for b in range(NB):
        for i in range(group):
            hot_ref[b, i * CAP : (i + 1) * CAP, :] = as_bf16(
                one_hot(pos_refs[b][0, pl.ds(step * group + i, 1), :])
            )
        for y in range(slices):
            out_ref[b, y] = matmul(hot_ref[b], x_refs[b * slices + y][...]).astype(BF16)


def pick_rows(where, pos, blocks):
    held = pos.shape[1]
    group = 2
    if isinstance(blocks, list):
        slices = len(blocks[0])
        flat = [a for b in blocks for a in b]
        tokens, width = flat[0].shape
        specs = [pl.BlockSpec((tokens, width), lambda i, where: (0, 0)) for _ in flat]
    else:
        slices, tokens, width = blocks.shape[1:]
        flat = [blocks] * (NB * slices)

        def part_spec(b, y):
            return pl.BlockSpec(
                (None, None, tokens, width),
                lambda i, where: (where[NB + b], where[2 * NB + 2 * slices + y], 0, 0),
            )

        specs = [part_spec(b, y) for b in range(NB) for y in range(slices)]

    def block_spec(b):
        return pl.BlockSpec((1, held, tokens), lambda i, where: (where[b], 0, 0))

    return pl.pallas_call(
        partial(pick_kernel, group, slices),
        grid_spec=pltpu.PrefetchScalarGridSpec(
            num_scalar_prefetch=1,
            grid=(held // group,),
            in_specs=[block_spec(b) for b in range(NB)]
            + specs,
            out_specs=pl.BlockSpec(
                (NB, slices, group * CAP, width), lambda i, where: (0, 0, i, 0)
            ),
            scratch_shapes=[pltpu.VMEM((NB, group * CAP, tokens), BF16)],
        ),
        out_shape=jax.ShapeDtypeStruct((NB, slices, held * CAP, width), BF16),
        compiler_params=pltpu.CompilerParams(vmem_limit_bytes=VMEM),
        cost_estimate=cost(
            flops=2 * NB * slices * held * CAP * tokens * width,
            bytes_accessed=2 * NB * slices * (held * CAP + tokens) * width,
            transcendentals=0,
        ),
        name="pick_rows",
    )(where, *([pos] * NB), *flat)


def expert_kernel(slices, where_ref, *refs):
    pos_refs, gate_refs = refs[:NB], refs[NB : 2 * NB]
    rows_mine, rows_theirs, cot_mine, cot_theirs, wg_ref, wu_ref, wd_ref = refs[2 * NB : 2 * NB + 7]
    scaled_ref, gate_grad_ref, up_grad_ref, prob_ref, keep_ref, give_ref = refs[2 * NB + 7 :]
    e = pl.program_id(0)
    width = rows_mine.shape[3]
    ff = wg_ref.shape[2]
    gate_pre = jnp.zeros((NB * CAP, ff), F32)
    up_pre = jnp.zeros((NB * CAP, ff), F32)
    grad_hidden = jnp.zeros((NB * CAP, ff), F32)

    def columns(j):
        return pl.ds(pl.multiple_of(where_ref[2 * NB + j] * width, width), width)

    for j in range(2 * slices):
        x_ref, c_ref = (rows_mine, cot_mine) if j < slices else (rows_theirs, cot_theirs)
        x = x_ref[:, j % slices].reshape(NB * CAP, width)
        c = c_ref[:, j % slices].reshape(NB * CAP, width)
        gate_pre = gate_pre + matmul(x, wg_ref[0, columns(j), :])
        up_pre = up_pre + matmul(x, wu_ref[0, columns(j), :])
        grad_hidden = grad_hidden + matmul_nt(c, wd_ref[0, :, columns(j)])
    masks = [one_hot(pos_refs[b][0, pl.ds(e, 1), :]) for b in range(NB)]
    gates = jnp.concatenate(
        [
            jnp.sum(jnp.where(masks[b], gate_refs[b][0, pl.ds(e, 1), :], 0.0), axis=1, keepdims=True)
            for b in range(NB)
        ],
        axis=0,
    )
    sigma = jax.nn.sigmoid(gate_pre)
    swish = gate_pre * sigma
    hidden = (swish * up_pre).astype(BF16).astype(F32)
    prob = jnp.sum(hidden * grad_hidden, axis=1, keepdims=True)
    for b in range(NB):
        prob_ref[0, b : b + 1, :] = jnp.sum(
            jnp.where(masks[b], prob[b * CAP : (b + 1) * CAP], 0.0), axis=0, keepdims=True
        )
    grad_hidden = grad_hidden * gates
    scaled_ref[0] = (hidden * gates).astype(BF16)
    gate_grad = (grad_hidden * up_pre * (sigma * (1.0 + gate_pre * (1.0 - sigma)))).astype(BF16)
    up_grad = (grad_hidden * swish).astype(BF16)
    gate_grad_ref[0] = gate_grad
    up_grad_ref[0] = up_grad
    for j in range(2 * slices):
        to = keep_ref if j < slices else give_ref
        back = matmul_nt(gate_grad, wg_ref[0, columns(j), :]) + matmul_nt(
            up_grad, wu_ref[0, columns(j), :]
        )
        to[:, j % slices] = back.astype(BF16).reshape(NB, CAP, width)


def expert_slot(where, pos, gate, rows, cots, w_gate, w_up, w_down):
    held, depth, ff = w_gate.shape
    tokens = pos.shape[2]
    slices, width = rows[0].shape[1], rows[0].shape[3]

    def block_spec(b):
        return pl.BlockSpec((1, held, tokens), lambda e, where: (where[b], 0, 0))

    rows_spec = pl.BlockSpec((NB, slices, CAP, width), lambda e, where: (0, 0, e, 0))
    rows_shape = jax.ShapeDtypeStruct((NB, slices, held * CAP, width), BF16)
    in_spec = pl.BlockSpec((1, depth, ff), lambda e, where: (e, 0, 0))
    hidden_spec = pl.BlockSpec((1, NB * CAP, ff), lambda e, where: (e, 0, 0))
    hidden_shape = jax.ShapeDtypeStruct((held, NB * CAP, ff), BF16)
    return pl.pallas_call(
        partial(expert_kernel, slices),
        grid_spec=pltpu.PrefetchScalarGridSpec(
            num_scalar_prefetch=1,
            grid=(held,),
            in_specs=[block_spec(b) for b in range(2 * NB)]
            + [rows_spec] * 4
            + [in_spec, in_spec, pl.BlockSpec((1, ff, depth), lambda e, where: (e, 0, 0))],
            out_specs=[hidden_spec] * 3
            + [pl.BlockSpec((1, NB, tokens), lambda e, where: (e, 0, 0)), rows_spec, rows_spec],
        ),
        out_shape=[hidden_shape] * 3
        + [jax.ShapeDtypeStruct((held, NB, tokens), F32), rows_shape, rows_shape],
        compiler_params=pltpu.CompilerParams(vmem_limit_bytes=VMEM),
        cost_estimate=cost(
            flops=10 * NB * held * CAP * depth * ff,
            bytes_accessed=6 * held * depth * ff + 6 * NB * held * CAP * depth,
            transcendentals=NB * held * CAP * ff,
        ),
        name="expert_slot",
    )(where, *([pos] * NB), *([gate] * NB), *rows, *cots, w_gate, w_up, w_down)


def down_kernel(slices, slots, where_ref, *refs):
    scaled_refs, wd_ref, keep_ref, give_ref = refs[:slots], refs[slots], refs[-2], refs[-1]
    width = keep_ref.shape[3]
    for j in range(2 * slices):
        to = keep_ref if j < slices else give_ref
        columns = pl.ds(pl.multiple_of(where_ref[2 * NB + j] * width, width), width)
        for k in range(slots):
            rows = matmul(scaled_refs[k][0], wd_ref[0, :, columns])
            to[k * NB : (k + 1) * NB, j % slices] = rows.astype(BF16).reshape(NB, CAP, width)


def down_slots(where, scaled, w_down, slices):
    held, ff, depth = w_down.shape
    width = depth // (2 * slices)
    slots = len(scaled)
    rows_spec = pl.BlockSpec((slots * NB, slices, CAP, width), lambda e, where: (0, 0, e, 0))
    rows_shape = jax.ShapeDtypeStruct((slots * NB, slices, held * CAP, width), BF16)
    return pl.pallas_call(
        partial(down_kernel, slices, slots),
        grid_spec=pltpu.PrefetchScalarGridSpec(
            num_scalar_prefetch=1,
            grid=(held,),
            in_specs=[pl.BlockSpec((1, NB * CAP, ff), lambda e, where: (e, 0, 0))] * slots
            + [pl.BlockSpec((1, ff, depth), lambda e, where: (e, 0, 0))],
            out_specs=[rows_spec, rows_spec],
        ),
        out_shape=[rows_shape, rows_shape],
        compiler_params=pltpu.CompilerParams(vmem_limit_bytes=VMEM),
        cost_estimate=cost(
            flops=2 * slots * NB * held * CAP * depth * ff,
            bytes_accessed=2 * held * depth * ff + 2 * slots * NB * held * CAP * depth,
            transcendentals=0,
        ),
        name="down_slots",
    )(where, *scaled, w_down)


def place_kernel(slices, held, slots, where_ref, *refs):
    count = NB * slots
    at_refs, mine_ref, theirs_ref = refs[:count], refs[count], refs[count + 1]
    out_refs, hot_ref = refs[count + 2 : -1], refs[-1]
    b, y = pl.program_id(0), pl.program_id(1)
    tokens = hot_ref.shape[0]
    for block in range(count):

        @pl.when((b == block) & (y == 0))
        def _():
            at = at_refs[block][0]
            for tile in range(held * CAP // 128):
                lanes = lax.broadcasted_iota(jnp.int32, (tokens, 128), 1) + tile * 128
                mask = None
                for e in range(tile * 128 // CAP, (tile * 128 + 127) // CAP + 1):
                    hit = at[:, e : e + 1] == lanes
                    mask = hit if mask is None else mask | hit
                hot_ref[:, tile * 128 : (tile + 1) * 128] = as_bf16(mask)

    rows = (mine_ref[0, 0].astype(F32) + theirs_ref[0, 0].astype(F32)).astype(BF16)
    placed = matmul(hot_ref[...], rows).astype(BF16)
    for block in range(count):
        for part in range(slices):

            @pl.when((b == block) & (y == part))
            def _():
                out_refs[block % NB * slices + part][block // NB] = placed


def place_rows(wheres, at, mine, theirs):
    _, slices, count, width = mine.shape
    _, tokens, held = at.shape
    slots = len(wheres)
    blocks = jnp.concatenate([w[:NB] for w in wheres])

    def block_spec(b):
        return pl.BlockSpec((1, tokens, held), lambda i, y, where: (where[b], 0, 0))

    rows_spec = pl.BlockSpec((1, 1, count, width), lambda i, y, where: (i, y, 0, 0))
    out = pl.pallas_call(
        partial(place_kernel, slices, held, slots),
        grid_spec=pltpu.PrefetchScalarGridSpec(
            num_scalar_prefetch=1,
            grid=(NB * slots, slices),
            in_specs=[block_spec(b) for b in range(NB * slots)] + [rows_spec, rows_spec],
            out_specs=[pl.BlockSpec((slots, tokens, width), lambda i, y, where: (0, 0, 0))]
            * (NB * slices),
            scratch_shapes=[pltpu.VMEM((tokens, count), BF16)],
        ),
        out_shape=[jax.ShapeDtypeStruct((slots, tokens, width), BF16)] * (NB * slices),
        compiler_params=pltpu.CompilerParams(vmem_limit_bytes=VMEM),
        cost_estimate=cost(
            flops=2 * NB * slots * slices * count * tokens * width,
            bytes_accessed=2 * NB * slots * slices * (2 * count + tokens) * width,
            transcendentals=0,
        ),
        name="place_rows",
    )(blocks, *([at] * (NB * slots)), mine, theirs)
    return [out[b * slices : (b + 1) * slices] for b in range(NB)]


def weight_kernel(slots, slices, where_ref, *refs):
    rows, gate_grads, up_grads = refs[: 2 * slots], refs[2 * slots : 3 * slots], refs[3 * slots : 4 * slots]
    gate_ref, up_ref = refs[4 * slots :]
    width = rows[0].shape[3]
    for j in range(2 * slices):
        columns = pl.ds(pl.multiple_of(where_ref[2 * NB + j] * width, width), width)
        gate = up = None
        for k in range(slots):
            x = rows[2 * k + j // slices][:, j % slices].reshape(NB * CAP, width)
            terms = matmul_tn(x, gate_grads[k][0]), matmul_tn(x, up_grads[k][0])
            gate, up = terms if gate is None else (gate + terms[0], up + terms[1])
        gate_ref[0, columns, :] = gate
        up_ref[0, columns, :] = up


def weight_down_kernel(slots, slices, where_ref, *refs):
    cots, scaled, down_ref = refs[: 2 * slots], refs[2 * slots : 3 * slots], refs[3 * slots]
    width = cots[0].shape[3]
    for j in range(2 * slices):
        columns = pl.ds(pl.multiple_of(where_ref[2 * NB + j] * width, width), width)
        down = None
        for k in range(slots):
            c = cots[2 * k + j // slices][:, j % slices].reshape(NB * CAP, width)
            term = matmul_tn(scaled[k][0], c)
            down = term if down is None else down + term
        down_ref[0, :, columns] = down


def weight_grads(kernel, where, rows, hiddens, outs, name):
    slots = len(rows)
    held, _, ff = hiddens[0].shape
    slices, width = rows[0][0].shape[1], rows[0][0].shape[3]
    depth = 2 * slices * width
    rows_spec = pl.BlockSpec((NB, slices, CAP, width), lambda e, where: (0, 0, e, 0))
    hidden_spec = pl.BlockSpec((1, NB * CAP, ff), lambda e, where: (e, 0, 0))
    return pl.pallas_call(
        partial(kernel, slots, slices),
        grid_spec=pltpu.PrefetchScalarGridSpec(
            num_scalar_prefetch=1,
            grid=(held,),
            in_specs=[rows_spec] * (2 * slots) + [hidden_spec] * len(hiddens),
            out_specs=[pl.BlockSpec((1, *o), lambda e, where: (e, 0, 0)) for o in outs],
        ),
        out_shape=[jax.ShapeDtypeStruct((held, *o), F32) for o in outs],
        compiler_params=pltpu.CompilerParams(vmem_limit_bytes=VMEM),
        cost_estimate=cost(flops=10**10, bytes_accessed=10**6, transcendentals=0),
        name=name,
    )(where, *[a for pair in rows for a in pair], *hiddens)


def settle_kernel(where_ref, *refs):
    halves, (output_ref, value_ref, query_ref, key_ref) = refs[:6], refs[6:]

    def settle(output, value, both):
        output_ref[...] = output[...].astype(F32).T
        value_ref[...] = value[...].astype(F32)
        width = query_ref.shape[1]
        query_ref[...] = both[:, :width].astype(F32)
        key_ref[...] = both[:, width:].astype(F32)

    @pl.when(pl.program_id(0) < 4)
    def _():
        settle(*halves[0::2])

    @pl.when(pl.program_id(0) >= 4)
    def _():
        settle(*halves[1::2])


def settle_rows(where, output, value, both):
    rows = 2 * value[0].shape[0]
    step = rows // 8
    width = value[0].shape[1]
    near = lambda n: pl.BlockSpec((step, n), lambda i, where: (jnp.minimum(i, 3), 0))
    far = lambda n: pl.BlockSpec((step, n), lambda i, where: (jnp.maximum(i, 4) - 4, 0))
    placed = pl.BlockSpec((step, width), lambda i, where: (where[i], 0))
    return pl.pallas_call(
        settle_kernel,
        grid_spec=pltpu.PrefetchScalarGridSpec(
            num_scalar_prefetch=1,
            grid=(8,),
            in_specs=[s(n) for n in (width, width, 2 * width) for s in (near, far)],
            out_specs=[pl.BlockSpec((width, step), lambda i, where: (0, where[i]))] + [placed] * 3,
        ),
        out_shape=[jax.ShapeDtypeStruct((width, rows), F32)]
        + [jax.ShapeDtypeStruct((rows, width), F32)] * 3,
        compiler_params=pltpu.CompilerParams(vmem_limit_bytes=VMEM),
        cost_estimate=cost(flops=0, bytes_accessed=24 * rows * width, transcendentals=0),
        name="settle_rows",
    )(where, *output, *value, *both)


def project_kernel(
    in_ref, ag_ref, wq_ref, wk_ref, wv_ref, qg_ref, kg_ref,
    x_ref, inv_ref, qr_ref, kr_ref, q_ref, k_ref, v_ref,
):
    @pl.when(pl.program_id(0) == 0)
    def _():
        for first in range(0, in_ref.shape[0], 256):
            rows = in_ref[first : first + 256, :].astype(F32)
            inverse = lax.rsqrt(jnp.mean(rows * rows, axis=1, keepdims=True) + 1e-05)
            inv_ref[first : first + 256, :] = inverse
            x_ref[first : first + 256, :] = (rows * inverse * ag_ref[...]).astype(BF16)

    x = x_ref[...]
    for w_ref, gain_ref, raw_ref, to_ref in ((wq_ref, qg_ref, qr_ref, q_ref), (wk_ref, kg_ref, kr_ref, k_ref)):
        raw = matmul(x, w_ref[...])
        raw_ref[...] = raw
        for h in range(raw.shape[1] // HD):
            part = raw[:, h * HD : (h + 1) * HD]
            inverse = lax.rsqrt(jnp.mean(part * part, axis=1, keepdims=True) + 1e-06)
            gain = gain_ref[:, h * HD : (h + 1) * HD]
            to_ref[:, h * HD : (h + 1) * HD] = (part * inverse * gain).astype(BF16)
    v_ref[...] = matmul(x, wv_ref[...]).astype(BF16)


def project(inputs, attn_gain, w_query, w_key, w_value, query_gain, key_gain):
    tokens, depth = inputs.shape
    columns = w_query.shape[1]
    step = min(256, columns)
    whole = pl.BlockSpec((tokens, depth), lambda i: (0, 0))
    weight = pl.BlockSpec((depth, step), lambda i: (0, i))
    gain = pl.BlockSpec((1, step), lambda i: (0, i))
    out = pl.BlockSpec((tokens, step), lambda i: (0, i))
    return pl.pallas_call(
        project_kernel,
        grid=(columns // step,),
        in_specs=[whole, pl.BlockSpec((1, depth), lambda i: (0, 0)), weight, weight, weight, gain, gain],
        out_specs=[whole, pl.BlockSpec((tokens, 1), lambda i: (0, 0))] + [out] * 5,
        out_shape=[
            jax.ShapeDtypeStruct((tokens, depth), BF16),
            jax.ShapeDtypeStruct((tokens, 1), F32),
        ]
        + [jax.ShapeDtypeStruct((tokens, columns), t) for t in (F32, F32, BF16, BF16, BF16)],
        compiler_params=pltpu.CompilerParams(vmem_limit_bytes=VMEM),
        cost_estimate=cost(
            flops=6 * tokens * depth * columns,
            bytes_accessed=4 * tokens * depth + 6 * depth * columns + 14 * tokens * columns,
            transcendentals=0,
        ),
        name="project",
    )(
        inputs, attn_gain.reshape(1, -1), w_query, w_key, w_value,
        query_gain.reshape(1, -1), key_gain.reshape(1, -1),
    )


def allowed_pairs(pieces_ref, base, first, rows, keys):
    query = first + lax.broadcasted_iota(jnp.int32, (rows, 1), 0)
    key = lax.broadcasted_iota(jnp.int32, (1, keys), 1)

    def piece_of(at, other):
        found = jnp.full(at.shape, other, jnp.int32)
        for j in range(2):
            start, length = pieces_ref[base + j], pieces_ref[base + 2 + j]
            found = jnp.where((at >= start) & (at < start + length), j, found)
        return found

    return (key <= query) | (piece_of(query, -1) == piece_of(key, -2))


def query_blocks():
    half = LENGTH // 2
    return ((0, half, half), (half, half, LENGTH))


def attend_kernel(scale, pieces_ref, q_ref, k_ref, v_ref, o_ref, log_ref, top_ref):
    base = pl.program_id(0) * 4
    best = None
    for first, rows, keys in query_blocks():
        allowed = allowed_pairs(pieces_ref, base, first, rows, keys)
        scores = matmul_nt(q_ref[first : first + rows, :], k_ref[:keys, :]) * scale
        masked = jnp.where(allowed, scores, -1e30)
        top = jnp.max(masked, axis=1, keepdims=True)
        weights = jnp.exp(masked - top)
        total = jnp.sum(weights, axis=1, keepdims=True)
        probs = (weights * (1.0 / total)).astype(BF16)
        o_ref[first : first + rows, :] = matmul(probs, v_ref[:keys, :]).astype(BF16)
        log_ref[0, first : first + rows, :] = top + jnp.log(total)
        most = jnp.max(top, axis=0, keepdims=True)
        best = most if best is None else jnp.maximum(best, most)
    top_ref[0] = jnp.broadcast_to(best, (8, HD))


def attend(pieces, queries, keys, values, scale):
    tokens, columns = queries.shape
    sequences, heads = tokens // LENGTH, columns // HD
    block = pl.BlockSpec((LENGTH, HD), lambda s, h, pieces: (s, h))
    return pl.pallas_call(
        partial(attend_kernel, scale),
        grid_spec=pltpu.PrefetchScalarGridSpec(
            num_scalar_prefetch=1,
            grid=(sequences, heads),
            in_specs=[block] * 3,
            out_specs=[
                block,
                pl.BlockSpec((1, LENGTH, 1), lambda s, h, pieces: (h, s, 0)),
                pl.BlockSpec((1, 8, HD), lambda s, h, pieces: (s * heads + h, 0, 0)),
            ],
        ),
        out_shape=[
            jax.ShapeDtypeStruct((tokens, columns), BF16),
            jax.ShapeDtypeStruct((heads, tokens, 1), F32),
            jax.ShapeDtypeStruct((sequences * heads, 8, HD), F32),
        ],
        compiler_params=pltpu.CompilerParams(vmem_limit_bytes=VMEM),
        cost_estimate=cost(
            flops=4 * tokens * LENGTH * columns,
            bytes_accessed=8 * tokens * columns,
            transcendentals=tokens * heads * LENGTH,
        ),
        name="attend",
    )(pieces, queries, keys, values)


def attend_back_kernel(
    scale, pieces_ref, q_ref, k_ref, v_ref, g_ref, log_ref, qr_ref, kr_ref, qg_ref, kg_ref,
    gq_ref, gk_ref, gv_ref, gqg_ref, gkg_ref, dq_ref, dk_ref, dv_ref,
):
    base = pl.program_id(0) * 4
    blocks = query_blocks()
    for first, rows, keys in blocks[::-1]:
        allowed = allowed_pairs(pieces_ref, base, first, rows, keys)
        q, g = q_ref[first : first + rows, :], g_ref[first : first + rows, :]
        k, v = k_ref[:keys, :], v_ref[:keys, :]
        scores = matmul_nt(q, k) * scale
        probs = jnp.exp(jnp.where(allowed, scores, -1e30) - log_ref[0, first : first + rows, :])
        grad_p = matmul_nt(g, v)
        delta = jnp.sum(probs * grad_p, axis=1, keepdims=True)
        grad_s = (probs * (grad_p - delta)).astype(BF16)
        dq_ref[first : first + rows, :] = matmul(grad_s, k) * scale
        dk = matmul_tn(grad_s, q) * scale
        dv = matmul_tn(probs.astype(BF16), g)
        if keys == LENGTH:
            dk_ref[...] = dk
            dv_ref[...] = dv
        else:
            dk_ref[:keys, :] += dk
            dv_ref[:keys, :] += dv
    gv_ref[...] = dv_ref[...].astype(BF16)
    for raw_ref, gain_ref, grad_ref, to_ref, sum_ref in (
        (qr_ref, qg_ref, dq_ref, gq_ref, gqg_ref),
        (kr_ref, kg_ref, dk_ref, gk_ref, gkg_ref),
    ):
        raw, grad = raw_ref[...], grad_ref[...]
        inverse = lax.rsqrt(jnp.mean(raw * raw, axis=1, keepdims=True) + 1e-06)
        hat = raw * inverse
        up = grad * gain_ref[...]
        mean = jnp.mean(up * hat, axis=1, keepdims=True)
        to_ref[...] = (inverse * (up - hat * mean)).astype(BF16)
        sum_ref[0] = jnp.sum(grad * hat, axis=0, keepdims=True)


def attend_back(pieces, queries, keys, values, grads, logs, query_raw, key_raw, query_gain, key_gain, scale):
    tokens, columns = queries.shape
    sequences, heads = tokens // LENGTH, columns // HD
    block = pl.BlockSpec((LENGTH, HD), lambda s, h, pieces: (s, h))
    gain = pl.BlockSpec((1, HD), lambda s, h, pieces: (0, h))
    sums = pl.BlockSpec((1, 1, HD), lambda s, h, pieces: (s, 0, h))
    return pl.pallas_call(
        partial(attend_back_kernel, scale),
        grid_spec=pltpu.PrefetchScalarGridSpec(
            num_scalar_prefetch=1,
            grid=(sequences, heads),
            in_specs=[block] * 4
            + [pl.BlockSpec((1, LENGTH, 1), lambda s, h, pieces: (h, s, 0)), block, block, gain, gain],
            out_specs=[block, block, block, sums, sums],
            scratch_shapes=[pltpu.VMEM((LENGTH, HD), F32)] * 3,
        ),
        out_shape=[jax.ShapeDtypeStruct((tokens, columns), BF16)] * 3
        + [jax.ShapeDtypeStruct((sequences, 1, columns), F32)] * 2,
        compiler_params=pltpu.CompilerParams(vmem_limit_bytes=VMEM),
        cost_estimate=cost(
            flops=10 * tokens * LENGTH * columns,
            bytes_accessed=22 * tokens * columns,
            transcendentals=tokens * heads * LENGTH,
        ),
        name="attend_back",
    )(
        pieces, queries, keys, values, grads, logs, query_raw, key_raw,
        query_gain.reshape(1, -1), key_gain.reshape(1, -1),
    )


def expert_steps(slots):
    order = list(ORDER) if is_cube() else list(range(slots))
    steps = [("cot", order[0]), ("row", order[0]), ("cot", order[1]), ("exp", order[0])]
    for i, k in enumerate(order):
        if i + 1 < slots:
            steps.append(("row", order[i + 1]))
        else:
            steps.append(("down", 0))
        if i + 2 < slots:
            steps.append(("cot", order[i + 2]))
        steps.append(("place", k))
        if i + 1 < slots:
            steps.append(("exp", order[i + 1]))
    return steps


def due(step, seen):
    return [seen[name] for name in DUE.get(step, ()) if name in seen]


def per_device(
    inputs,
    attn_gain,
    w_query,
    w_key,
    w_value,
    w_output,
    query_gain,
    key_gain,
    moe_gain,
    w_router,
    w_gate,
    w_up,
    w_down,
    routes,
    piece_start,
    piece_length,
    clip_threshold,
    cotangent,
):
    tokens_here, width = inputs.shape
    slice_width = cotangent.shape[1]
    owner = lax.axis_index("expert")
    column = lax.axis_index("tensor") * slice_width
    heads_here = query_gain.shape[0] // HD
    experts_here = w_gate.shape[0]
    owners = lax.axis_size("expert")
    sequences = tokens_here // LENGTH
    scale = 1.0 / math.sqrt(HD)
    where = slot_blocks()
    slots = len(where)
    slices = lax.axis_size("tensor") // 2

    def own_columns(value):
        return lax.dynamic_slice_in_dim(value, column, slice_width, value.ndim - 1)

    seen = {}
    all_routes = gather_routes(routes.T)
    cot_slots = gather_slots(cotangent.astype(BF16), "c", seen, [all_routes])
    order = tensor_order()

    held_ids = owner * experts_here + jnp.arange(experts_here, dtype=jnp.int32)
    chosen = jnp.any(all_routes[:, None] == held_ids[None, :, None, None], axis=2)
    places = jnp.arange(tokens_here, dtype=jnp.int32)
    before = (places[:, None] < places[None, :]).astype(BF16)
    earlier = jnp.einsum(
        "set,tu->seu", chosen.astype(BF16), before, preferred_element_type=F32
    ).astype(jnp.int32)
    pos = jnp.where(chosen, earlier, -1)
    at = jnp.where(
        chosen, earlier + jnp.arange(experts_here, dtype=jnp.int32)[None, :, None] * CAP, -1
    ).transpose(0, 2, 1)

    output_pieces = [lax.dynamic_slice_in_dim(w_output, o * slice_width, slice_width, 1) for o in order]
    normed_a, attn_inv, query_raw, key_raw, queries, keys, values = project(
        inputs, attn_gain, w_query, w_key, w_value, query_gain, key_gain
    )
    blocks = row_blocks()
    normed_rows = jnp.concatenate(
        [lax.dynamic_slice_in_dim(normed_a, r * (width // 8), width // 8, 1) for r in blocks], axis=1
    )
    pieces = jnp.concatenate([piece_start, piece_length], axis=1).reshape(-1)
    attended, logs, tops = attend(
        after(pieces, values, all_routes), queries, keys, values, scale
    )
    head_top = jnp.max(tops[:, 0, 0].reshape(sequences, heads_here), axis=0)
    attended = after(attended, *due("attended", seen))
    branch = tensor_scatter(partial(matmul, attended), output_pieces, "b", seen, [pos, at])
    residual = own_columns(inputs).astype(F32) + branch
    gain_slice = own_columns(moe_gain)
    router_slice = lax.dynamic_slice_in_dim(w_router, column, slice_width, 0)
    lifted = residual * gain_slice
    row_sums = tensor_sum(
        jnp.concatenate(
            [
                lax.dot_general(
                    router_slice,
                    lifted.astype(BF16),
                    (((0,), (1,)), ((), ())),
                    preferred_element_type=F32,
                ),
                jnp.sum(residual * residual, axis=1)[None],
            ],
            axis=0,
        )
    )
    moe_inv_row = lax.rsqrt(row_sums[E] / width + 1e-05)
    moe_inv = moe_inv_row[:, None]
    normed_m = (lifted * moe_inv).astype(BF16)
    normed_m = after(normed_m, *due("normed", seen))

    normed_slots = gather_slots(normed_m, "n", seen)
    router = jax.nn.softmax(row_sums[:E] * moe_inv_row[None], axis=0)
    gate = lax.all_to_all(
        router.reshape(owners, experts_here, tokens_here),
        "expert",
        split_axis=0,
        concat_axis=0,
        tiled=True,
    )

    rows, cots, back, sums = [None] * slots, [None] * slots, [None] * slots, [None] * slots
    scaled, gate_grads, up_grads, probs = [None] * slots, [None] * slots, [None] * slots, [None] * slots
    last = normed_m
    downs = {}

    def turn(name, k):
        return after(where[k], last, *due(name, seen))

    def lower(k):
        keep, give = down_slots(turn("down" + str(k), 0), scaled[2 * k : 2 * k + 2], w_down, slices)
        downs[k] = (keep, core_swap(give))
        seen["sd" + str(k)] = downs[k][1]
        return keep

    for kind, k in expert_steps(slots):
        now = turn(kind + str(k), k)
        if kind == "cot":
            last = pick_rows(now, pos, cot_slots[k])
            cots[k] = (last, core_swap(last))
            seen["sc" + str(k)] = cots[k][1]
        elif kind == "row":
            last = pick_rows(now, pos, normed_slots[k])
            rows[k] = (last, core_swap(last))
            seen["sr" + str(k)] = rows[k][1]
        elif kind == "exp":
            scaled[k], gate_grads[k], up_grads[k], probs[k], keep, give = expert_slot(
                now, pos, gate, rows[k], cots[k], w_gate, w_up, w_down
            )
            last = scaled[k]
            back[k] = (keep, core_swap(give))
            seen["sg" + str(k)] = back[k][1]
        elif kind == "down":
            last = lower(k)
        else:
            placed = place_rows([now], at, *back[k])
            last = placed[0][0]
            back[k] = [[a[0] for a in b] for b in placed]
            if is_cube():
                odd = k in ODD
                sums[k], sent = scatter_plane(back[k], scatter_corner(back[k], odd), odd)
                if k:
                    sums[k] = sent["z"] = send(sums[k].astype(BF16), dz=k)
                seen.update({"e" + link + str(k): value for link, value in sent.items()})
    for k in range(1, slots // 2):
        last = lower(k)
    pairs = []
    for k in range(slots // 2):
        pairs.append(place_rows([turn("pd" + str(k), 2 * k), where[2 * k + 1]], at, *downs[k]))
        last = pairs[k][0][0]
    far = scatter_corners(pairs, seen)
    grad_gate, grad_up = weight_grads(
        weight_kernel,
        turn("weight", 0),
        rows,
        gate_grads + up_grads,
        [w_gate.shape[1:]] * 2,
        "weight_grads",
    )
    if is_cube():
        expert_path = added(*[after(s, grad_gate) for s in sums])
    else:
        expert_path = scatter_all(back)

    prob_grads = jnp.stack([probs[k][:, b] for k in range(slots) for b in range(NB)])
    if is_cube():
        prob_grads = prob_grads[jnp.arange(owners, dtype=jnp.int32) ^ owner]
    prob_grads = lax.all_to_all(prob_grads, "expert", split_axis=0, concat_axis=0, tiled=True)
    prob_grads = tensor_sum(prob_grads.reshape(E, tokens_here))
    grad_logits = (
        router * (prob_grads - jnp.sum(router * prob_grads, axis=0, keepdims=True))
    ).astype(BF16)
    grad_router = lax.dot_general(
        normed_m, grad_logits, (((0,), (1,)), ((), ())), preferred_element_type=F32
    )
    router_path = lax.dot_general(
        grad_logits, router_slice, (((0,), (1,)), ((), ())), preferred_element_type=F32
    )
    grad_normed = expert_path + router_path
    moe_hat = residual * moe_inv
    grad_moe_gain = jnp.sum(grad_normed * moe_hat, axis=0)
    upstream = grad_normed * gain_slice
    mean_dot = tensor_sum(jnp.sum(upstream * moe_hat, axis=-1).reshape(8, -1)).reshape(-1, 1) / width
    grad_residual = cotangent + moe_inv * (upstream - moe_hat * mean_dot)
    grad_branch = after(grad_residual.astype(BF16), *due("residual_grad", seen))
    (grad_down,) = weight_grads(
        weight_down_kernel,
        after(where[0], grad_branch),
        cots,
        scaled,
        [w_down.shape[1:]],
        "weight_down_grads",
    )
    branch_pieces = tensor_gather(grad_branch, [grad_down])

    planes = scatter_planes(pairs, far, branch_pieces[1:2], seen)
    grad_branch = jnp.concatenate(branch_pieces, axis=1)

    grad_output = matmul_tn(grad_branch, attended).astype(BF16)
    spots = order_spots()
    eighth = width // 8
    wide = slice_width // eighth
    grad_output = jnp.concatenate(
        [
            lax.dynamic_slice_in_dim(
                grad_output, (spots(r // wide) * wide + r % wide) * eighth, eighth, 0
            )
            for r in blocks
        ],
        axis=0,
    )
    sum_output = expert_sum(grad_output, "o", seen)
    grad_attended = matmul_nt(grad_branch, jnp.concatenate(output_pieces, axis=1)).astype(BF16)
    grad_attended = after(grad_attended, grad_output)
    grad_query_raw, grad_key_raw, grad_v, grad_query_gain, grad_key_gain = attend_back(
        after(pieces, *due("back", seen)),
        queries,
        keys,
        values,
        grad_attended,
        logs,
        query_raw,
        key_raw,
        query_gain,
        key_gain,
        scale,
    )
    sum_value = expert_sum(matmul_tn(normed_rows, grad_v).astype(BF16), "v", seen)
    grad_raw = jnp.concatenate([grad_query_raw, grad_key_raw, grad_v], axis=1)
    grad_both = matmul_tn(normed_rows, grad_raw[:, : 2 * slice_width]).astype(BF16)
    sum_both = expert_sum(grad_both, "qk", seen)
    grad_raw = after(grad_raw, grad_both, *due("normed_grad", seen))
    weights = jnp.concatenate([w_query, w_key, w_value], axis=1)
    weight_pieces = [lax.dynamic_slice_in_dim(weights, o * slice_width, slice_width, 0) for o in order]
    grad_normed_a = tensor_scatter(partial(matmul_nt, grad_raw), weight_pieces, "h", seen)
    attn_hat = own_columns(inputs).astype(F32) * attn_inv
    upstream = grad_normed_a * own_columns(attn_gain)
    grad_attn_gain = jnp.sum(grad_normed_a * attn_hat, axis=0)
    mean_dot = tensor_sum(jnp.sum(upstream * attn_hat, axis=-1).reshape(8, -1)).reshape(-1, 1) / width
    grad_input = grad_residual + attn_inv * (upstream - attn_hat * mean_dot)

    small = jnp.concatenate(
        [
            grad_router.T,
            jnp.stack(
                [
                    grad_attn_gain,
                    grad_moe_gain,
                    jnp.sum(grad_query_gain, axis=(0, 1)),
                    jnp.sum(grad_key_gain, axis=(0, 1)),
                ]
            ),
        ],
        axis=0,
    )
    top_row = jnp.pad(head_top, (0, slice_width - heads_here), constant_values=-3e38)
    small, top_row = expert_total(small, top_row[None])
    head_top = top_row[0, :heads_here]
    mixture = scatter_ends(planes, [small, *due("ends", seen)])
    out = residual + mixture
    sum_moe_gain, sum_query_gain, sum_key_gain = small[E + 1], small[E + 2], small[E + 3]
    every = lax.all_gather(small[: E + 1], "tensor")
    sum_router = every[:, :E].transpose(0, 2, 1).reshape(width, E)
    sum_attn_gain = every[:, E].reshape(width)
    sum_output, sum_value, sum_query, sum_key = settle_rows(
        jnp.stack(blocks), sum_output, sum_value, sum_both
    )
    factor = clip_threshold / jnp.maximum(head_top, clip_threshold)
    spread = jnp.repeat(jnp.sqrt(factor), HD)
    query_clipped = (w_query.astype(F32) * spread[None, :]).astype(BF16)
    key_clipped = (w_key.astype(F32) * spread[None, :]).astype(BF16)
    return (
        out,
        grad_input,
        sum_attn_gain,
        sum_query,
        sum_key,
        sum_value,
        sum_output,
        sum_query_gain,
        sum_key_gain,
        sum_moe_gain,
        sum_router,
        grad_gate,
        grad_up,
        grad_down,
        head_top,
        query_clipped,
        key_clipped,
    )


def solution(mesh):
    return jax.shard_map(
        per_device,
        mesh=mesh,
        in_specs=(
            P("expert", None),
            P(),
            P(None, "tensor"),
            P(None, "tensor"),
            P(None, "tensor"),
            P("tensor", None),
            P("tensor"),
            P("tensor"),
            P(),
            P(),
            P("expert", None, "tensor"),
            P("expert", None, "tensor"),
            P("expert", "tensor", None),
            P("expert", None),
            P("expert", None),
            P("expert", None),
            P("tensor"),
            P("expert", "tensor"),
        ),
        out_specs=(
            P("expert", "tensor"),
            P("expert", "tensor"),
            P(),
            P(None, "tensor"),
            P(None, "tensor"),
            P(None, "tensor"),
            P("tensor", None),
            P("tensor"),
            P("tensor"),
            P("tensor"),
            P(),
            P("expert", None, "tensor"),
            P("expert", None, "tensor"),
            P("expert", "tensor", None),
            P("tensor"),
            P(None, "tensor"),
            P(None, "tensor"),
        ),
        check_vma=False,
    )
```

```python
from functools import partial
import math

import jax
import jax.numpy as jnp
from jax import lax
from jax.experimental import pallas as pl
from jax.experimental.pallas import tpu as pltpu
from jax.sharding import PartitionSpec as P

HD = 128
E = 64
TOP = 8
LENGTH = 1024
CAP = 160
NB = 2
BOTH = ("expert", "tensor")
F32 = jnp.float32
BF16 = jnp.bfloat16
VMEM = 60 * 1024 * 1024
WEIGHT = 16
ORDER = (0, 2, 3, 1)
ODD = (1, 2)
DUE = {
    "attended": ("cx0", "cy0"),
    "branch": ("cz2",),
    "normed": ("cd0",),
    "row0": ("cx2", "cz3", "cy2"),
    "exp0": ("cx3",),
    "row2": ("sc2", "cy3"),
    "cot3": ("sg0",),
    "place0": ("sr2",),
    "exp2": ("sc3",),
    "cot1": ("sg2",),
    "place2": ("sr3", "ed0"),
    "exp3": ("sc1",),
    "place3": ("ex0", "ey0", "ed2"),
    "down0": ("ex2", "ey2"),
    "place1": ("ed3",),
    "pd0": ("ed1", "sd0"),
    "pd1": ("ex3", "ey3", "ex1", "ey1"),
    "residual_grad": ("gd0",),
    "back": ("gd1",),
    "normed_grad": ("gx0", "gx1", "gy0"),
    "ends": ("qk2",),
}


def cost(flops, bytes_accessed, transcendentals):
    return pl.CostEstimate(
        flops=flops * WEIGHT, bytes_accessed=bytes_accessed * WEIGHT, transcendentals=transcendentals * WEIGHT
    )


def matmul(left, right):
    return jnp.dot(left, right, preferred_element_type=F32)


def matmul_nt(left, right):
    return lax.dot_general(left, right, (((1,), (1,)), ((), ())), preferred_element_type=F32)


def matmul_tn(left, right):
    return lax.dot_general(left, right, (((0,), (0,)), ((), ())), preferred_element_type=F32)


def after(value, *others):
    return lax.optimization_barrier((value, *others))[0]


def flip(dz, dx, dy, dc):
    pairs = []
    for z in range(4):
        for x in range(2):
            for y in range(2):
                for c in range(2):
                    pairs.append(
                        (
                            ((z * 2 + x) * 2 + y) * 2 + c,
                            (((z ^ dz) * 2 + (x ^ dx)) * 2 + (y ^ dy)) * 2 + (c ^ dc),
                        )
                    )
    return pairs


def send(value, dz=0, dx=0, dy=0, dc=0):
    return lax.ppermute(value, BOTH, flip(dz, dx, dy, dc))


def is_cube():
    return lax.axis_size("expert") == 8 and lax.axis_size("tensor") == 4


def core_swap(value):
    if is_cube():
        return send(value, dc=1)
    count = lax.axis_size("tensor")
    return lax.ppermute(value, "tensor", [(i, i ^ 1) for i in range(count)])


def slot_blocks():
    owner, part = lax.axis_index("expert"), lax.axis_index("tensor")
    core = part % 2
    found = []
    for k in range(lax.axis_size("expert") // NB):
        places = [k * NB + b for b in range(NB)]
        if is_cube():
            owners = [owner ^ p for p in places]
            mine = [part ^ (y * 2) for y in range(2)]
        else:
            owners = places
            mine = [y * 2 + core for y in range(lax.axis_size("tensor") // 2)]
        theirs = [m ^ 1 for m in mine]
        rows = [m // 2 for m in mine]
        found.append(
            jnp.stack([jnp.asarray(v, jnp.int32) for v in places + owners + mine + theirs + rows])
        )
    return found


def gather_routes(routes):
    if not is_cube():
        return lax.all_gather(routes, "expert")
    both = jnp.stack([routes, send(routes, dx=1)])
    both = jnp.concatenate([both, send(both, dz=1)])
    return jnp.concatenate([both, send(both, dz=2)])


def same_core():
    count = lax.axis_size("tensor")
    return [[y * 2 + c for y in range(count // 2)] for c in range(2)]


def gather_all(own):
    owners, parts = lax.axis_size("expert"), lax.axis_size("tensor")
    groups = [[e * parts + t for e in range(owners) for t in range(c, parts, 2)] for c in range(2)]
    full = lax.all_gather(own, BOTH, axis_index_groups=groups)
    return full.reshape(owners, parts // 2, *own.shape)


def gather_slots(own, tag, seen, first=()):
    if not is_cube():
        return [gather_all(own)] * (lax.axis_size("expert") // NB)
    slots = []
    far_own = after(own, *first) if first else own
    for k in range(4):
        block = send(far_own, dz=k) if k else own
        over_x = send(block, dx=1)
        over_y = send(block, dy=1)
        far = send(over_x, dy=1) if k in ODD else send(over_y, dx=1)
        for link, value in zip("zxyd", (block, over_x, over_y, far)):
            seen[tag + link + str(k)] = value
        slots.append([[block, over_y], [over_x, far]])
    return slots


def added(*terms):
    return sum(t.astype(F32) for t in terms)


def scatter_corner(parts, odd):
    return send(parts[1][1], dy=1) if odd else send(parts[1][1], dx=1)


def scatter_plane(parts, far, odd, hold=()):
    near, over_y, over_x = parts[0][0], parts[0][1], parts[1][0]
    if odd:
        over_x, over_y = added(over_x, far).astype(BF16), after(over_y, far)
    else:
        over_x, over_y = after(over_x, far), added(over_y, far).astype(BF16)
    if hold:
        over_y = after(over_y, *hold)
    from_x, from_y = send(over_x, dx=1), send(over_y, dy=1)
    return added(near, from_x, from_y), {"d": far, "x": from_x, "y": from_y}


def scatter_all(slots):
    full = jnp.stack(
        [jnp.stack([s[b][y] for s in slots for b in range(NB)]) for y in range(len(slots[0][0]))]
    )
    mine = lax.psum_scatter(full, "tensor", axis_index_groups=same_core(), scatter_dimension=0)
    return lax.psum_scatter(mine, "expert", scatter_dimension=0).astype(F32)


def scatter_corners(pairs, seen):
    if not is_cube():
        return []
    far = [scatter_corner(pair, i == 0) for i, pair in enumerate(pairs)]
    seen.update({"gd" + str(i): value for i, value in enumerate(far)})
    return far


def scatter_planes(pairs, far, hold, seen):
    if not is_cube():
        return pairs
    planes = []
    for i, pair in enumerate(pairs):
        plane, sent = scatter_plane(pair, far[i], i == 0, hold)
        planes.append(plane)
        seen.update({"g" + link + str(i): value for link, value in sent.items()})
    return planes


def scatter_ends(planes, hold):
    if not is_cube():
        return scatter_all(
            [[[a[i] for a in b] for b in pair] for pair in planes for i in range(pair[0][0].shape[0])]
        )
    low, high = planes
    total = low + send(after(high.astype(BF16), *hold), dz=2).astype(F32)
    return total[0] + send(total[1].astype(BF16), dz=1).astype(F32)


def tensor_order():
    part = lax.axis_index("tensor")
    if is_cube():
        return [part ^ i for i in (0, 2, 1, 3)]
    return [jnp.int32(i) for i in range(lax.axis_size("tensor"))]


def order_spots():
    if not is_cube():
        return lambda s: s
    part = lax.axis_index("tensor")
    return lambda s: (part ^ s) % 2 * 2 + (part ^ s) // 2


def tensor_gather(own, beside=()):
    if not is_cube():
        full = lax.all_gather(own, "tensor")
        return [full[i] for i in range(full.shape[0])]
    over_y = after(send(own, dy=1), *beside)
    return [own, over_y, core_swap(own), core_swap(over_y)]


def tensor_scatter(product, pieces, tag, seen, beside=()):
    if not is_cube():
        full = jnp.concatenate([product(p).astype(BF16) for p in pieces], axis=1)
        return lax.psum_scatter(full, "tensor", scatter_dimension=1, tiled=True).astype(F32)
    away_y = product(pieces[3]).astype(BF16)
    away = product(pieces[2]).astype(BF16)
    from_y, near = core_swap(away_y), core_swap(away)
    away = added(product(pieces[1]), from_y).astype(BF16)
    over_y = after(send(away, dy=1), *beside) if beside else send(away, dy=1)
    seen.update({tag + "0": from_y, tag + "1": near, tag + "y": over_y, tag + "s": away})
    return added(product(pieces[0]), near, over_y)


def tensor_sum(value):
    if not is_cube():
        return lax.psum(value, "tensor")
    value = value + core_swap(value)
    return value + send(value, dy=1)


def row_blocks():
    if not is_cube():
        return [jnp.int32(i) for i in range(8)]
    owner = lax.axis_index("expert")
    return [owner ^ (b | first << 1 | second << 2) for b in (0, 1) for first in (0, 1) for second in (0, 1)]


def expert_sum(value, tag, seen):
    half = value.shape[0] // 2
    if not is_cube():
        value = lax.psum(value, "expert")
        return value[:half], value[half:]
    for step in ({"dx": 1}, {"dz": 1}, {"dz": 2}):
        half = value.shape[0] // 2
        value = added(value[:half], send(value[half:], **step)).astype(BF16)
    for step in ({"dz": 2}, {"dz": 1}):
        seen[tag] = send(value, **step)
        value = jnp.concatenate([value, seen[tag]], axis=0)
        seen[tag + str(step["dz"])] = seen[tag]
    return value, send(value, dx=1)


def expert_total(sums, tops):
    if not is_cube():
        return lax.psum(sums, "expert"), lax.pmax(tops, "expert")
    count = sums.shape[0]
    both = jnp.concatenate([sums, tops], axis=0)
    for step in ({"dx": 1}, {"dz": 1}, {"dz": 2}):
        other = send(both, **step)
        both = jnp.concatenate([both[:count] + other[:count], jnp.maximum(both[count:], other[count:])])
    return both[:count], both[count:]


def one_hot(pos_row):
    rows = lax.broadcasted_iota(jnp.int32, (CAP, pos_row.shape[1]), 0)
    return rows == pos_row


def as_bf16(mask):
    return jnp.where(mask, 1.0, 0.0).astype(BF16)


def pick_kernel(group, slices, where_ref, *refs):
    pos_refs, x_refs = refs[:NB], refs[NB : NB + NB * slices]
    out_ref, hot_ref = refs[-2:]
    step = pl.program_id(0)
    for b in range(NB):
        for i in range(group):
            hot_ref[b, i * CAP : (i + 1) * CAP, :] = as_bf16(
                one_hot(pos_refs[b][0, pl.ds(step * group + i, 1), :])
            )
        for y in range(slices):
            out_ref[b, y] = matmul(hot_ref[b], x_refs[b * slices + y][...]).astype(BF16)


def pick_rows(where, pos, blocks):
    held = pos.shape[1]
    group = 2
    if isinstance(blocks, list):
        slices = len(blocks[0])
        flat = [a for b in blocks for a in b]
        tokens, width = flat[0].shape
        specs = [pl.BlockSpec((tokens, width), lambda i, where: (0, 0)) for _ in flat]
    else:
        slices, tokens, width = blocks.shape[1:]
        flat = [blocks] * (NB * slices)

        def part_spec(b, y):
            return pl.BlockSpec(
                (None, None, tokens, width),
                lambda i, where: (where[NB + b], where[2 * NB + 2 * slices + y], 0, 0),
            )

        specs = [part_spec(b, y) for b in range(NB) for y in range(slices)]

    def block_spec(b):
        return pl.BlockSpec((1, held, tokens), lambda i, where: (where[b], 0, 0))

    return pl.pallas_call(
        partial(pick_kernel, group, slices),
        grid_spec=pltpu.PrefetchScalarGridSpec(
            num_scalar_prefetch=1,
            grid=(held // group,),
            in_specs=[block_spec(b) for b in range(NB)]
            + specs,
            out_specs=pl.BlockSpec(
                (NB, slices, group * CAP, width), lambda i, where: (0, 0, i, 0)
            ),
            scratch_shapes=[pltpu.VMEM((NB, group * CAP, tokens), BF16)],
        ),
        out_shape=jax.ShapeDtypeStruct((NB, slices, held * CAP, width), BF16),
        compiler_params=pltpu.CompilerParams(vmem_limit_bytes=VMEM),
        cost_estimate=cost(
            flops=2 * NB * slices * held * CAP * tokens * width,
            bytes_accessed=2 * NB * slices * (held * CAP + tokens) * width,
            transcendentals=0,
        ),
        name="pick_rows",
    )(where, *([pos] * NB), *flat)


def expert_kernel(slices, where_ref, *refs):
    pos_refs, gate_refs = refs[:NB], refs[NB : 2 * NB]
    rows_mine, rows_theirs, cot_mine, cot_theirs, wg_ref, wu_ref, wd_ref = refs[2 * NB : 2 * NB + 7]
    scaled_ref, gate_grad_ref, up_grad_ref, prob_ref, keep_ref, give_ref = refs[2 * NB + 7 :]
    e = pl.program_id(0)
    width = rows_mine.shape[3]
    ff = wg_ref.shape[2]
    gate_pre = jnp.zeros((NB * CAP, ff), F32)
    up_pre = jnp.zeros((NB * CAP, ff), F32)
    grad_hidden = jnp.zeros((NB * CAP, ff), F32)

    def columns(j):
        return pl.ds(pl.multiple_of(where_ref[2 * NB + j] * width, width), width)

    for j in range(2 * slices):
        x_ref, c_ref = (rows_mine, cot_mine) if j < slices else (rows_theirs, cot_theirs)
        x = x_ref[:, j % slices].reshape(NB * CAP, width)
        c = c_ref[:, j % slices].reshape(NB * CAP, width)
        gate_pre = gate_pre + matmul(x, wg_ref[0, columns(j), :])
        up_pre = up_pre + matmul(x, wu_ref[0, columns(j), :])
        grad_hidden = grad_hidden + matmul_nt(c, wd_ref[0, :, columns(j)])
    masks = [one_hot(pos_refs[b][0, pl.ds(e, 1), :]) for b in range(NB)]
    gates = jnp.concatenate(
        [
            jnp.sum(jnp.where(masks[b], gate_refs[b][0, pl.ds(e, 1), :], 0.0), axis=1, keepdims=True)
            for b in range(NB)
        ],
        axis=0,
    )
    sigma = jax.nn.sigmoid(gate_pre)
    swish = gate_pre * sigma
    hidden = (swish * up_pre).astype(BF16).astype(F32)
    prob = jnp.sum(hidden * grad_hidden, axis=1, keepdims=True)
    for b in range(NB):
        prob_ref[0, b : b + 1, :] = jnp.sum(
            jnp.where(masks[b], prob[b * CAP : (b + 1) * CAP], 0.0), axis=0, keepdims=True
        )
    grad_hidden = grad_hidden * gates
    scaled_ref[0] = (hidden * gates).astype(BF16)
    gate_grad = (grad_hidden * up_pre * (sigma * (1.0 + gate_pre * (1.0 - sigma)))).astype(BF16)
    up_grad = (grad_hidden * swish).astype(BF16)
    gate_grad_ref[0] = gate_grad
    up_grad_ref[0] = up_grad
    for j in range(2 * slices):
        to = keep_ref if j < slices else give_ref
        back = matmul_nt(gate_grad, wg_ref[0, columns(j), :]) + matmul_nt(
            up_grad, wu_ref[0, columns(j), :]
        )
        to[:, j % slices] = back.astype(BF16).reshape(NB, CAP, width)


def expert_slot(where, pos, gate, rows, cots, w_gate, w_up, w_down):
    held, depth, ff = w_gate.shape
    tokens = pos.shape[2]
    slices, width = rows[0].shape[1], rows[0].shape[3]

    def block_spec(b):
        return pl.BlockSpec((1, held, tokens), lambda e, where: (where[b], 0, 0))

    rows_spec = pl.BlockSpec((NB, slices, CAP, width), lambda e, where: (0, 0, e, 0))
    rows_shape = jax.ShapeDtypeStruct((NB, slices, held * CAP, width), BF16)
    in_spec = pl.BlockSpec((1, depth, ff), lambda e, where: (e, 0, 0))
    hidden_spec = pl.BlockSpec((1, NB * CAP, ff), lambda e, where: (e, 0, 0))
    hidden_shape = jax.ShapeDtypeStruct((held, NB * CAP, ff), BF16)
    return pl.pallas_call(
        partial(expert_kernel, slices),
        grid_spec=pltpu.PrefetchScalarGridSpec(
            num_scalar_prefetch=1,
            grid=(held,),
            in_specs=[block_spec(b) for b in range(2 * NB)]
            + [rows_spec] * 4
            + [in_spec, in_spec, pl.BlockSpec((1, ff, depth), lambda e, where: (e, 0, 0))],
            out_specs=[hidden_spec] * 3
            + [pl.BlockSpec((1, NB, tokens), lambda e, where: (e, 0, 0)), rows_spec, rows_spec],
        ),
        out_shape=[hidden_shape] * 3
        + [jax.ShapeDtypeStruct((held, NB, tokens), F32), rows_shape, rows_shape],
        compiler_params=pltpu.CompilerParams(vmem_limit_bytes=VMEM),
        cost_estimate=cost(
            flops=10 * NB * held * CAP * depth * ff,
            bytes_accessed=6 * held * depth * ff + 6 * NB * held * CAP * depth,
            transcendentals=NB * held * CAP * ff,
        ),
        name="expert_slot",
    )(where, *([pos] * NB), *([gate] * NB), *rows, *cots, w_gate, w_up, w_down)


def down_kernel(slices, slots, where_ref, *refs):
    scaled_refs, wd_ref, keep_ref, give_ref = refs[:slots], refs[slots], refs[-2], refs[-1]
    width = keep_ref.shape[3]
    for j in range(2 * slices):
        to = keep_ref if j < slices else give_ref
        columns = pl.ds(pl.multiple_of(where_ref[2 * NB + j] * width, width), width)
        for k in range(slots):
            rows = matmul(scaled_refs[k][0], wd_ref[0, :, columns])
            to[k * NB : (k + 1) * NB, j % slices] = rows.astype(BF16).reshape(NB, CAP, width)


def down_slots(where, scaled, w_down, slices):
    held, ff, depth = w_down.shape
    width = depth // (2 * slices)
    slots = len(scaled)
    rows_spec = pl.BlockSpec((slots * NB, slices, CAP, width), lambda e, where: (0, 0, e, 0))
    rows_shape = jax.ShapeDtypeStruct((slots * NB, slices, held * CAP, width), BF16)
    return pl.pallas_call(
        partial(down_kernel, slices, slots),
        grid_spec=pltpu.PrefetchScalarGridSpec(
            num_scalar_prefetch=1,
            grid=(held,),
            in_specs=[pl.BlockSpec((1, NB * CAP, ff), lambda e, where: (e, 0, 0))] * slots
            + [pl.BlockSpec((1, ff, depth), lambda e, where: (e, 0, 0))],
            out_specs=[rows_spec, rows_spec],
        ),
        out_shape=[rows_shape, rows_shape],
        compiler_params=pltpu.CompilerParams(vmem_limit_bytes=VMEM),
        cost_estimate=cost(
            flops=2 * slots * NB * held * CAP * depth * ff,
            bytes_accessed=2 * held * depth * ff + 2 * slots * NB * held * CAP * depth,
            transcendentals=0,
        ),
        name="down_slots",
    )(where, *scaled, w_down)


def place_kernel(slices, held, slots, where_ref, *refs):
    count = NB * slots
    at_refs, mine_ref, theirs_ref = refs[:count], refs[count], refs[count + 1]
    out_refs, hot_ref = refs[count + 2 : -1], refs[-1]
    b, y = pl.program_id(0), pl.program_id(1)
    tokens = hot_ref.shape[0]
    for block in range(count):

        @pl.when((b == block) & (y == 0))
        def _():
            at = at_refs[block][0]
            for tile in range(held * CAP // 128):
                lanes = lax.broadcasted_iota(jnp.int32, (tokens, 128), 1) + tile * 128
                mask = None
                for e in range(tile * 128 // CAP, (tile * 128 + 127) // CAP + 1):
                    hit = at[:, e : e + 1] == lanes
                    mask = hit if mask is None else mask | hit
                hot_ref[:, tile * 128 : (tile + 1) * 128] = as_bf16(mask)

    rows = (mine_ref[0, 0].astype(F32) + theirs_ref[0, 0].astype(F32)).astype(BF16)
    placed = matmul(hot_ref[...], rows).astype(BF16)
    for block in range(count):
        for part in range(slices):

            @pl.when((b == block) & (y == part))
            def _():
                out_refs[block % NB * slices + part][block // NB] = placed


def place_rows(wheres, at, mine, theirs):
    _, slices, count, width = mine.shape
    _, tokens, held = at.shape
    slots = len(wheres)
    blocks = jnp.concatenate([w[:NB] for w in wheres])

    def block_spec(b):
        return pl.BlockSpec((1, tokens, held), lambda i, y, where: (where[b], 0, 0))

    rows_spec = pl.BlockSpec((1, 1, count, width), lambda i, y, where: (i, y, 0, 0))
    out = pl.pallas_call(
        partial(place_kernel, slices, held, slots),
        grid_spec=pltpu.PrefetchScalarGridSpec(
            num_scalar_prefetch=1,
            grid=(NB * slots, slices),
            in_specs=[block_spec(b) for b in range(NB * slots)] + [rows_spec, rows_spec],
            out_specs=[pl.BlockSpec((slots, tokens, width), lambda i, y, where: (0, 0, 0))]
            * (NB * slices),
            scratch_shapes=[pltpu.VMEM((tokens, count), BF16)],
        ),
        out_shape=[jax.ShapeDtypeStruct((slots, tokens, width), BF16)] * (NB * slices),
        compiler_params=pltpu.CompilerParams(vmem_limit_bytes=VMEM),
        cost_estimate=cost(
            flops=2 * NB * slots * slices * count * tokens * width,
            bytes_accessed=2 * NB * slots * slices * (2 * count + tokens) * width,
            transcendentals=0,
        ),
        name="place_rows",
    )(blocks, *([at] * (NB * slots)), mine, theirs)
    return [out[b * slices : (b + 1) * slices] for b in range(NB)]


def weight_kernel(slots, slices, where_ref, *refs):
    rows, gate_grads, up_grads = refs[: 2 * slots], refs[2 * slots : 3 * slots], refs[3 * slots : 4 * slots]
    gate_ref, up_ref = refs[4 * slots :]
    width = rows[0].shape[3]
    for j in range(2 * slices):
        columns = pl.ds(pl.multiple_of(where_ref[2 * NB + j] * width, width), width)
        gate = up = None
        for k in range(slots):
            x = rows[2 * k + j // slices][:, j % slices].reshape(NB * CAP, width)
            terms = matmul_tn(x, gate_grads[k][0]), matmul_tn(x, up_grads[k][0])
            gate, up = terms if gate is None else (gate + terms[0], up + terms[1])
        gate_ref[0, columns, :] = gate
        up_ref[0, columns, :] = up


def weight_down_kernel(slots, slices, where_ref, *refs):
    cots, scaled, down_ref = refs[: 2 * slots], refs[2 * slots : 3 * slots], refs[3 * slots]
    width = cots[0].shape[3]
    for j in range(2 * slices):
        columns = pl.ds(pl.multiple_of(where_ref[2 * NB + j] * width, width), width)
        down = None
        for k in range(slots):
            c = cots[2 * k + j // slices][:, j % slices].reshape(NB * CAP, width)
            term = matmul_tn(scaled[k][0], c)
            down = term if down is None else down + term
        down_ref[0, :, columns] = down


def weight_grads(kernel, where, rows, hiddens, outs, name):
    slots = len(rows)
    held, _, ff = hiddens[0].shape
    slices, width = rows[0][0].shape[1], rows[0][0].shape[3]
    depth = 2 * slices * width
    rows_spec = pl.BlockSpec((NB, slices, CAP, width), lambda e, where: (0, 0, e, 0))
    hidden_spec = pl.BlockSpec((1, NB * CAP, ff), lambda e, where: (e, 0, 0))
    return pl.pallas_call(
        partial(kernel, slots, slices),
        grid_spec=pltpu.PrefetchScalarGridSpec(
            num_scalar_prefetch=1,
            grid=(held,),
            in_specs=[rows_spec] * (2 * slots) + [hidden_spec] * len(hiddens),
            out_specs=[pl.BlockSpec((1, *o), lambda e, where: (e, 0, 0)) for o in outs],
        ),
        out_shape=[jax.ShapeDtypeStruct((held, *o), F32) for o in outs],
        compiler_params=pltpu.CompilerParams(vmem_limit_bytes=VMEM),
        cost_estimate=cost(flops=10**10, bytes_accessed=10**6, transcendentals=0),
        name=name,
    )(where, *[a for pair in rows for a in pair], *hiddens)


def settle_kernel(where_ref, *refs):
    halves, (output_ref, value_ref, query_ref, key_ref) = refs[:6], refs[6:]

    def settle(output, value, both):
        output_ref[...] = output[...].astype(F32).T
        value_ref[...] = value[...].astype(F32)
        width = query_ref.shape[1]
        query_ref[...] = both[:, :width].astype(F32)
        key_ref[...] = both[:, width:].astype(F32)

    @pl.when(pl.program_id(0) < 4)
    def _():
        settle(*halves[0::2])

    @pl.when(pl.program_id(0) >= 4)
    def _():
        settle(*halves[1::2])


def settle_rows(where, output, value, both):
    rows = 2 * value[0].shape[0]
    step = rows // 8
    width = value[0].shape[1]
    near = lambda n: pl.BlockSpec((step, n), lambda i, where: (jnp.minimum(i, 3), 0))
    far = lambda n: pl.BlockSpec((step, n), lambda i, where: (jnp.maximum(i, 4) - 4, 0))
    placed = pl.BlockSpec((step, width), lambda i, where: (where[i], 0))
    return pl.pallas_call(
        settle_kernel,
        grid_spec=pltpu.PrefetchScalarGridSpec(
            num_scalar_prefetch=1,
            grid=(8,),
            in_specs=[s(n) for n in (width, width, 2 * width) for s in (near, far)],
            out_specs=[pl.BlockSpec((width, step), lambda i, where: (0, where[i]))] + [placed] * 3,
        ),
        out_shape=[jax.ShapeDtypeStruct((width, rows), F32)]
        + [jax.ShapeDtypeStruct((rows, width), F32)] * 3,
        compiler_params=pltpu.CompilerParams(vmem_limit_bytes=VMEM),
        cost_estimate=cost(flops=0, bytes_accessed=24 * rows * width, transcendentals=0),
        name="settle_rows",
    )(where, *output, *value, *both)


def project_kernel(
    in_ref, ag_ref, wq_ref, wk_ref, wv_ref, qg_ref, kg_ref,
    x_ref, inv_ref, qr_ref, kr_ref, q_ref, k_ref, v_ref,
):
    @pl.when(pl.program_id(0) == 0)
    def _():
        for first in range(0, in_ref.shape[0], 256):
            rows = in_ref[first : first + 256, :].astype(F32)
            inverse = lax.rsqrt(jnp.mean(rows * rows, axis=1, keepdims=True) + 1e-05)
            inv_ref[first : first + 256, :] = inverse
            x_ref[first : first + 256, :] = (rows * inverse * ag_ref[...]).astype(BF16)

    x = x_ref[...]
    for w_ref, gain_ref, raw_ref, to_ref in ((wq_ref, qg_ref, qr_ref, q_ref), (wk_ref, kg_ref, kr_ref, k_ref)):
        raw = matmul(x, w_ref[...])
        raw_ref[...] = raw
        for h in range(raw.shape[1] // HD):
            part = raw[:, h * HD : (h + 1) * HD]
            inverse = lax.rsqrt(jnp.mean(part * part, axis=1, keepdims=True) + 1e-06)
            gain = gain_ref[:, h * HD : (h + 1) * HD]
            to_ref[:, h * HD : (h + 1) * HD] = (part * inverse * gain).astype(BF16)
    v_ref[...] = matmul(x, wv_ref[...]).astype(BF16)


def project(inputs, attn_gain, w_query, w_key, w_value, query_gain, key_gain):
    tokens, depth = inputs.shape
    columns = w_query.shape[1]
    step = min(256, columns)
    whole = pl.BlockSpec((tokens, depth), lambda i: (0, 0))
    weight = pl.BlockSpec((depth, step), lambda i: (0, i))
    gain = pl.BlockSpec((1, step), lambda i: (0, i))
    out = pl.BlockSpec((tokens, step), lambda i: (0, i))
    return pl.pallas_call(
        project_kernel,
        grid=(columns // step,),
        in_specs=[whole, pl.BlockSpec((1, depth), lambda i: (0, 0)), weight, weight, weight, gain, gain],
        out_specs=[whole, pl.BlockSpec((tokens, 1), lambda i: (0, 0))] + [out] * 5,
        out_shape=[
            jax.ShapeDtypeStruct((tokens, depth), BF16),
            jax.ShapeDtypeStruct((tokens, 1), F32),
        ]
        + [jax.ShapeDtypeStruct((tokens, columns), t) for t in (F32, F32, BF16, BF16, BF16)],
        compiler_params=pltpu.CompilerParams(vmem_limit_bytes=VMEM),
        cost_estimate=cost(
            flops=6 * tokens * depth * columns,
            bytes_accessed=4 * tokens * depth + 6 * depth * columns + 14 * tokens * columns,
            transcendentals=0,
        ),
        name="project",
    )(
        inputs, attn_gain.reshape(1, -1), w_query, w_key, w_value,
        query_gain.reshape(1, -1), key_gain.reshape(1, -1),
    )


def allowed_pairs(pieces_ref, base, first, rows, keys):
    query = first + lax.broadcasted_iota(jnp.int32, (rows, 1), 0)
    key = lax.broadcasted_iota(jnp.int32, (1, keys), 1)

    def piece_of(at, other):
        found = jnp.full(at.shape, other, jnp.int32)
        for j in range(2):
            start, length = pieces_ref[base + j], pieces_ref[base + 2 + j]
            found = jnp.where((at >= start) & (at < start + length), j, found)
        return found

    return (key <= query) | (piece_of(query, -1) == piece_of(key, -2))


def query_blocks():
    half = LENGTH // 2
    return ((0, half, half), (half, half, LENGTH))


def attend_kernel(scale, pieces_ref, q_ref, k_ref, v_ref, o_ref, log_ref, top_ref):
    base = pl.program_id(0) * 4
    best = None
    for first, rows, keys in query_blocks():
        allowed = allowed_pairs(pieces_ref, base, first, rows, keys)
        scores = matmul_nt(q_ref[first : first + rows, :], k_ref[:keys, :]) * scale
        masked = jnp.where(allowed, scores, -1e30)
        top = jnp.max(masked, axis=1, keepdims=True)
        weights = jnp.exp(masked - top)
        total = jnp.sum(weights, axis=1, keepdims=True)
        probs = (weights * (1.0 / total)).astype(BF16)
        o_ref[first : first + rows, :] = matmul(probs, v_ref[:keys, :]).astype(BF16)
        log_ref[0, first : first + rows, :] = top + jnp.log(total)
        most = jnp.max(top, axis=0, keepdims=True)
        best = most if best is None else jnp.maximum(best, most)
    top_ref[0] = jnp.broadcast_to(best, (8, HD))


def attend(pieces, queries, keys, values, scale):
    tokens, columns = queries.shape
    sequences, heads = tokens // LENGTH, columns // HD
    block = pl.BlockSpec((LENGTH, HD), lambda s, h, pieces: (s, h))
    return pl.pallas_call(
        partial(attend_kernel, scale),
        grid_spec=pltpu.PrefetchScalarGridSpec(
            num_scalar_prefetch=1,
            grid=(sequences, heads),
            in_specs=[block] * 3,
            out_specs=[
                block,
                pl.BlockSpec((1, LENGTH, 1), lambda s, h, pieces: (h, s, 0)),
                pl.BlockSpec((1, 8, HD), lambda s, h, pieces: (s * heads + h, 0, 0)),
            ],
        ),
        out_shape=[
            jax.ShapeDtypeStruct((tokens, columns), BF16),
            jax.ShapeDtypeStruct((heads, tokens, 1), F32),
            jax.ShapeDtypeStruct((sequences * heads, 8, HD), F32),
        ],
        compiler_params=pltpu.CompilerParams(vmem_limit_bytes=VMEM),
        cost_estimate=cost(
            flops=4 * tokens * LENGTH * columns,
            bytes_accessed=8 * tokens * columns,
            transcendentals=tokens * heads * LENGTH,
        ),
        name="attend",
    )(pieces, queries, keys, values)


def attend_back_kernel(
    scale, pieces_ref, q_ref, k_ref, v_ref, g_ref, log_ref, qr_ref, kr_ref, qg_ref, kg_ref,
    gq_ref, gk_ref, gv_ref, gqg_ref, gkg_ref, dq_ref, dk_ref, dv_ref,
):
    base = pl.program_id(0) * 4
    blocks = query_blocks()
    for first, rows, keys in blocks[::-1]:
        allowed = allowed_pairs(pieces_ref, base, first, rows, keys)
        q, g = q_ref[first : first + rows, :], g_ref[first : first + rows, :]
        k, v = k_ref[:keys, :], v_ref[:keys, :]
        scores = matmul_nt(q, k) * scale
        probs = jnp.exp(jnp.where(allowed, scores, -1e30) - log_ref[0, first : first + rows, :])
        grad_p = matmul_nt(g, v)
        delta = jnp.sum(probs * grad_p, axis=1, keepdims=True)
        grad_s = (probs * (grad_p - delta)).astype(BF16)
        dq_ref[first : first + rows, :] = matmul(grad_s, k) * scale
        dk = matmul_tn(grad_s, q) * scale
        dv = matmul_tn(probs.astype(BF16), g)
        if keys == LENGTH:
            dk_ref[...] = dk
            dv_ref[...] = dv
        else:
            dk_ref[:keys, :] += dk
            dv_ref[:keys, :] += dv
    gv_ref[...] = dv_ref[...].astype(BF16)
    for raw_ref, gain_ref, grad_ref, to_ref, sum_ref in (
        (qr_ref, qg_ref, dq_ref, gq_ref, gqg_ref),
        (kr_ref, kg_ref, dk_ref, gk_ref, gkg_ref),
    ):
        raw, grad = raw_ref[...], grad_ref[...]
        inverse = lax.rsqrt(jnp.mean(raw * raw, axis=1, keepdims=True) + 1e-06)
        hat = raw * inverse
        up = grad * gain_ref[...]
        mean = jnp.mean(up * hat, axis=1, keepdims=True)
        to_ref[...] = (inverse * (up - hat * mean)).astype(BF16)
        sum_ref[0] = jnp.sum(grad * hat, axis=0, keepdims=True)


def attend_back(pieces, queries, keys, values, grads, logs, query_raw, key_raw, query_gain, key_gain, scale):
    tokens, columns = queries.shape
    sequences, heads = tokens // LENGTH, columns // HD
    block = pl.BlockSpec((LENGTH, HD), lambda s, h, pieces: (s, h))
    gain = pl.BlockSpec((1, HD), lambda s, h, pieces: (0, h))
    sums = pl.BlockSpec((1, 1, HD), lambda s, h, pieces: (s, 0, h))
    return pl.pallas_call(
        partial(attend_back_kernel, scale),
        grid_spec=pltpu.PrefetchScalarGridSpec(
            num_scalar_prefetch=1,
            grid=(sequences, heads),
            in_specs=[block] * 4
            + [pl.BlockSpec((1, LENGTH, 1), lambda s, h, pieces: (h, s, 0)), block, block, gain, gain],
            out_specs=[block, block, block, sums, sums],
            scratch_shapes=[pltpu.VMEM((LENGTH, HD), F32)] * 3,
        ),
        out_shape=[jax.ShapeDtypeStruct((tokens, columns), BF16)] * 3
        + [jax.ShapeDtypeStruct((sequences, 1, columns), F32)] * 2,
        compiler_params=pltpu.CompilerParams(vmem_limit_bytes=VMEM),
        cost_estimate=cost(
            flops=10 * tokens * LENGTH * columns,
            bytes_accessed=22 * tokens * columns,
            transcendentals=tokens * heads * LENGTH,
        ),
        name="attend_back",
    )(
        pieces, queries, keys, values, grads, logs, query_raw, key_raw,
        query_gain.reshape(1, -1), key_gain.reshape(1, -1),
    )


def expert_steps(slots):
    order = list(ORDER) if is_cube() else list(range(slots))
    steps = [("cot", order[0]), ("row", order[0]), ("cot", order[1]), ("exp", order[0])]
    for i, k in enumerate(order):
        if i + 1 < slots:
            steps.append(("row", order[i + 1]))
        else:
            steps.append(("down", 0))
        if i + 2 < slots:
            steps.append(("cot", order[i + 2]))
        steps.append(("place", k))
        if i + 1 < slots:
            steps.append(("exp", order[i + 1]))
    return steps


def due(step, seen):
    return [seen[name] for name in DUE.get(step, ()) if name in seen]


def per_device(
    inputs,
    attn_gain,
    w_query,
    w_key,
    w_value,
    w_output,
    query_gain,
    key_gain,
    moe_gain,
    w_router,
    w_gate,
    w_up,
    w_down,
    routes,
    piece_start,
    piece_length,
    clip_threshold,
    cotangent,
):
    tokens_here, width = inputs.shape
    slice_width = cotangent.shape[1]
    owner = lax.axis_index("expert")
    column = lax.axis_index("tensor") * slice_width
    heads_here = query_gain.shape[0] // HD
    experts_here = w_gate.shape[0]
    owners = lax.axis_size("expert")
    sequences = tokens_here // LENGTH
    scale = 1.0 / math.sqrt(HD)
    where = slot_blocks()
    slots = len(where)
    slices = lax.axis_size("tensor") // 2

    def own_columns(value):
        return lax.dynamic_slice_in_dim(value, column, slice_width, value.ndim - 1)

    seen = {}
    all_routes = gather_routes(routes.T)
    cot_slots = gather_slots(cotangent.astype(BF16), "c", seen, [all_routes])
    order = tensor_order()

    held_ids = owner * experts_here + jnp.arange(experts_here, dtype=jnp.int32)
    chosen = jnp.any(all_routes[:, None] == held_ids[None, :, None, None], axis=2)
    places = jnp.arange(tokens_here, dtype=jnp.int32)
    before = (places[:, None] < places[None, :]).astype(BF16)
    earlier = jnp.einsum(
        "set,tu->seu", chosen.astype(BF16), before, preferred_element_type=F32
    ).astype(jnp.int32)
    pos = jnp.where(chosen, earlier, -1)
    at = jnp.where(
        chosen, earlier + jnp.arange(experts_here, dtype=jnp.int32)[None, :, None] * CAP, -1
    ).transpose(0, 2, 1)

    output_pieces = [lax.dynamic_slice_in_dim(w_output, o * slice_width, slice_width, 1) for o in order]
    normed_a, attn_inv, query_raw, key_raw, queries, keys, values = project(
        inputs, attn_gain, w_query, w_key, w_value, query_gain, key_gain
    )
    blocks = row_blocks()
    normed_rows = jnp.concatenate(
        [lax.dynamic_slice_in_dim(normed_a, r * (width // 8), width // 8, 1) for r in blocks], axis=1
    )
    pieces = jnp.concatenate([piece_start, piece_length], axis=1).reshape(-1)
    attended, logs, tops = attend(
        after(pieces, values, all_routes), queries, keys, values, scale
    )
    head_top = jnp.max(tops[:, 0, 0].reshape(sequences, heads_here), axis=0)
    attended = after(attended, *due("attended", seen))
    branch = tensor_scatter(partial(matmul, attended), output_pieces, "b", seen, [pos, at])
    branch = after(branch, *due("branch", seen))
    residual = own_columns(inputs).astype(F32) + branch
    gain_slice = own_columns(moe_gain)
    router_slice = lax.dynamic_slice_in_dim(w_router, column, slice_width, 0)
    lifted = residual * gain_slice
    row_sums = tensor_sum(
        jnp.concatenate(
            [
                lax.dot_general(
                    router_slice,
                    lifted.astype(BF16),
                    (((0,), (1,)), ((), ())),
                    preferred_element_type=F32,
                ),
                jnp.sum(residual * residual, axis=1)[None],
            ],
            axis=0,
        )
    )
    moe_inv_row = lax.rsqrt(row_sums[E] / width + 1e-05)
    moe_inv = moe_inv_row[:, None]
    normed_m = (lifted * moe_inv).astype(BF16)
    normed_m = after(normed_m, *due("normed", seen))

    normed_slots = gather_slots(normed_m, "n", seen)
    router = jax.nn.softmax(row_sums[:E] * moe_inv_row[None], axis=0)
    gate = lax.all_to_all(
        router.reshape(owners, experts_here, tokens_here),
        "expert",
        split_axis=0,
        concat_axis=0,
        tiled=True,
    )

    rows, cots, back, sums = [None] * slots, [None] * slots, [None] * slots, [None] * slots
    scaled, gate_grads, up_grads, probs = [None] * slots, [None] * slots, [None] * slots, [None] * slots
    last = normed_m
    downs = {}

    def turn(name, k):
        return after(where[k], last, *due(name, seen))

    def lower(k):
        keep, give = down_slots(turn("down" + str(k), 0), scaled[2 * k : 2 * k + 2], w_down, slices)
        downs[k] = (keep, core_swap(give))
        seen["sd" + str(k)] = downs[k][1]
        return keep

    for kind, k in expert_steps(slots):
        now = turn(kind + str(k), k)
        if kind == "cot":
            last = pick_rows(now, pos, cot_slots[k])
            cots[k] = (last, core_swap(last))
            seen["sc" + str(k)] = cots[k][1]
        elif kind == "row":
            last = pick_rows(now, pos, normed_slots[k])
            rows[k] = (last, core_swap(last))
            seen["sr" + str(k)] = rows[k][1]
        elif kind == "exp":
            scaled[k], gate_grads[k], up_grads[k], probs[k], keep, give = expert_slot(
                now, pos, gate, rows[k], cots[k], w_gate, w_up, w_down
            )
            last = scaled[k]
            back[k] = (keep, core_swap(give))
            seen["sg" + str(k)] = back[k][1]
        elif kind == "down":
            last = lower(k)
        else:
            placed = place_rows([now], at, *back[k])
            last = placed[0][0]
            back[k] = [[a[0] for a in b] for b in placed]
            if is_cube():
                odd = k in ODD
                sums[k], sent = scatter_plane(back[k], scatter_corner(back[k], odd), odd)
                if k:
                    sums[k] = sent["z"] = send(sums[k].astype(BF16), dz=k)
                seen.update({"e" + link + str(k): value for link, value in sent.items()})
    for k in range(1, slots // 2):
        last = lower(k)
    pairs = []
    for k in range(slots // 2):
        pairs.append(place_rows([turn("pd" + str(k), 2 * k), where[2 * k + 1]], at, *downs[k]))
        last = pairs[k][0][0]
    far = scatter_corners(pairs, seen)
    if is_cube():
        expert_path = added(*[after(s, last) for s in sums])
    else:
        expert_path = scatter_all(back)

    prob_grads = jnp.stack([probs[k][:, b] for k in range(slots) for b in range(NB)])
    if is_cube():
        prob_grads = prob_grads[jnp.arange(owners, dtype=jnp.int32) ^ owner]
    prob_grads = lax.all_to_all(prob_grads, "expert", split_axis=0, concat_axis=0, tiled=True)
    prob_grads = tensor_sum(prob_grads.reshape(E, tokens_here))
    grad_logits = (
        router * (prob_grads - jnp.sum(router * prob_grads, axis=0, keepdims=True))
    ).astype(BF16)
    grad_router = lax.dot_general(
        normed_m, grad_logits, (((0,), (1,)), ((), ())), preferred_element_type=F32
    )
    router_path = lax.dot_general(
        grad_logits, router_slice, (((0,), (1,)), ((), ())), preferred_element_type=F32
    )
    grad_normed = expert_path + router_path
    moe_hat = residual * moe_inv
    grad_moe_gain = jnp.sum(grad_normed * moe_hat, axis=0)
    upstream = grad_normed * gain_slice
    mean_dot = tensor_sum(jnp.sum(upstream * moe_hat, axis=-1).reshape(8, -1)).reshape(-1, 1) / width
    grad_residual = cotangent + moe_inv * (upstream - moe_hat * mean_dot)
    grad_branch = after(grad_residual.astype(BF16), *due("residual_grad", seen))
    (grad_down,) = weight_grads(
        weight_down_kernel,
        after(where[0], grad_branch),
        cots,
        scaled,
        [w_down.shape[1:]],
        "weight_down_grads",
    )
    branch_pieces = tensor_gather(grad_branch, [grad_down])

    planes = scatter_planes(pairs, far, branch_pieces[1:2], seen)
    grad_branch = jnp.concatenate(branch_pieces, axis=1)

    grad_output = matmul_tn(grad_branch, attended).astype(BF16)
    spots = order_spots()
    eighth = width // 8
    wide = slice_width // eighth
    grad_output = jnp.concatenate(
        [
            lax.dynamic_slice_in_dim(
                grad_output, (spots(r // wide) * wide + r % wide) * eighth, eighth, 0
            )
            for r in blocks
        ],
        axis=0,
    )
    sum_output = expert_sum(grad_output, "o", seen)
    grad_attended = matmul_nt(grad_branch, jnp.concatenate(output_pieces, axis=1)).astype(BF16)
    grad_attended = after(grad_attended, grad_output)
    grad_query_raw, grad_key_raw, grad_v, grad_query_gain, grad_key_gain = attend_back(
        after(pieces, *due("back", seen)),
        queries,
        keys,
        values,
        grad_attended,
        logs,
        query_raw,
        key_raw,
        query_gain,
        key_gain,
        scale,
    )
    sum_value = expert_sum(matmul_tn(normed_rows, grad_v).astype(BF16), "v", seen)
    grad_raw = jnp.concatenate([grad_query_raw, grad_key_raw, grad_v], axis=1)
    grad_both = matmul_tn(normed_rows, grad_raw[:, : 2 * slice_width]).astype(BF16)
    sum_both = expert_sum(grad_both, "qk", seen)
    grad_raw = after(grad_raw, grad_both, *due("normed_grad", seen))
    weights = jnp.concatenate([w_query, w_key, w_value], axis=1)
    weight_pieces = [lax.dynamic_slice_in_dim(weights, o * slice_width, slice_width, 0) for o in order]
    grad_normed_a = tensor_scatter(partial(matmul_nt, grad_raw), weight_pieces, "h", seen)
    attn_hat = own_columns(inputs).astype(F32) * attn_inv
    upstream = grad_normed_a * own_columns(attn_gain)
    grad_attn_gain = jnp.sum(grad_normed_a * attn_hat, axis=0)
    mean_dot = tensor_sum(jnp.sum(upstream * attn_hat, axis=-1).reshape(8, -1)).reshape(-1, 1) / width
    grad_input = grad_residual + attn_inv * (upstream - attn_hat * mean_dot)

    small = jnp.concatenate(
        [
            grad_router.T,
            jnp.stack(
                [
                    grad_attn_gain,
                    grad_moe_gain,
                    jnp.sum(grad_query_gain, axis=(0, 1)),
                    jnp.sum(grad_key_gain, axis=(0, 1)),
                ]
            ),
        ],
        axis=0,
    )
    top_row = jnp.pad(head_top, (0, slice_width - heads_here), constant_values=-3e38)
    small, top_row = expert_total(small, top_row[None])
    head_top = top_row[0, :heads_here]
    grad_gate, grad_up = weight_grads(
        weight_kernel,
        after(where[0], small, *due("ends", seen)),
        rows,
        gate_grads + up_grads,
        [w_gate.shape[1:]] * 2,
        "weight_grads",
    )
    mixture = scatter_ends(planes, [small, *due("ends", seen)])
    out = residual + mixture
    sum_moe_gain, sum_query_gain, sum_key_gain = small[E + 1], small[E + 2], small[E + 3]
    every = lax.all_gather(small[: E + 1], "tensor")
    sum_router = every[:, :E].transpose(0, 2, 1).reshape(width, E)
    sum_attn_gain = every[:, E].reshape(width)
    sum_output, sum_value, sum_query, sum_key = settle_rows(
        jnp.stack(blocks), sum_output, sum_value, sum_both
    )
    factor = clip_threshold / jnp.maximum(head_top, clip_threshold)
    spread = jnp.repeat(jnp.sqrt(factor), HD)
    query_clipped = (w_query.astype(F32) * spread[None, :]).astype(BF16)
    key_clipped = (w_key.astype(F32) * spread[None, :]).astype(BF16)
    return (
        out,
        grad_input,
        sum_attn_gain,
        sum_query,
        sum_key,
        sum_value,
        sum_output,
        sum_query_gain,
        sum_key_gain,
        sum_moe_gain,
        sum_router,
        grad_gate,
        grad_up,
        grad_down,
        head_top,
        query_clipped,
        key_clipped,
    )


def solution(mesh):
    return jax.shard_map(
        per_device,
        mesh=mesh,
        in_specs=(
            P("expert", None),
            P(),
            P(None, "tensor"),
            P(None, "tensor"),
            P(None, "tensor"),
            P("tensor", None),
            P("tensor"),
            P("tensor"),
            P(),
            P(),
            P("expert", None, "tensor"),
            P("expert", None, "tensor"),
            P("expert", "tensor", None),
            P("expert", None),
            P("expert", None),
            P("expert", None),
            P("tensor"),
            P("expert", "tensor"),
        ),
        out_specs=(
            P("expert", "tensor"),
            P("expert", "tensor"),
            P(),
            P(None, "tensor"),
            P(None, "tensor"),
            P(None, "tensor"),
            P("tensor", None),
            P("tensor"),
            P("tensor"),
            P("tensor"),
            P(),
            P("expert", None, "tensor"),
            P("expert", None, "tensor"),
            P("expert", "tensor", None),
            P("tensor"),
            P(None, "tensor"),
            P(None, "tensor"),
        ),
        check_vma=False,
    )
```

```python
from functools import partial
import math

import jax
import jax.numpy as jnp
from jax import lax
from jax.experimental import pallas as pl
from jax.experimental.pallas import tpu as pltpu
from jax.sharding import PartitionSpec as P

HD = 128
E = 64
TOP = 8
LENGTH = 1024
CAP = 160
NB = 2
BOTH = ("expert", "tensor")
F32 = jnp.float32
BF16 = jnp.bfloat16
VMEM = 60 * 1024 * 1024
WEIGHT = 16
ORDER = (0, 2, 3, 1)
ODD = (1, 2)
DUE = {
    "attended": ("cx0", "cy0"),
    "normed": ("cz2", "cd0"),
    "row0": ("cx2", "cz3", "cy2"),
    "exp0": ("cx3",),
    "row2": ("sc2", "cy3"),
    "cot3": ("sg0",),
    "place0": ("sr2",),
    "exp2": ("sc3",),
    "cot1": ("sg2",),
    "place2": ("sr3", "ed0"),
    "exp3": ("sc1",),
    "place3": ("ex0", "ey0", "ed2"),
    "down1": ("ex2", "ey2", "ed3"),
    "pd0": ("ed1", "sd0"),
    "weight": ("ex3", "ey3", "ex1", "ey1"),
    "residual_grad": ("gd0", "gd1"),
    "back": ("gx0",),
    "normed_grad": ("gy0",),
    "ends": ("qk2",),
}


def cost(flops, bytes_accessed, transcendentals):
    return pl.CostEstimate(
        flops=flops * WEIGHT, bytes_accessed=bytes_accessed * WEIGHT, transcendentals=transcendentals * WEIGHT
    )


def matmul(left, right):
    return jnp.dot(left, right, preferred_element_type=F32)


def matmul_nt(left, right):
    return lax.dot_general(left, right, (((1,), (1,)), ((), ())), preferred_element_type=F32)


def matmul_tn(left, right):
    return lax.dot_general(left, right, (((0,), (0,)), ((), ())), preferred_element_type=F32)


def after(value, *others):
    return lax.optimization_barrier((value, *others))[0]


def flip(dz, dx, dy, dc):
    pairs = []
    for z in range(4):
        for x in range(2):
            for y in range(2):
                for c in range(2):
                    pairs.append(
                        (
                            ((z * 2 + x) * 2 + y) * 2 + c,
                            (((z ^ dz) * 2 + (x ^ dx)) * 2 + (y ^ dy)) * 2 + (c ^ dc),
                        )
                    )
    return pairs


def send(value, dz=0, dx=0, dy=0, dc=0):
    return lax.ppermute(value, BOTH, flip(dz, dx, dy, dc))


def is_cube():
    return lax.axis_size("expert") == 8 and lax.axis_size("tensor") == 4


def core_swap(value):
    if is_cube():
        return send(value, dc=1)
    count = lax.axis_size("tensor")
    return lax.ppermute(value, "tensor", [(i, i ^ 1) for i in range(count)])


def slot_blocks():
    owner, part = lax.axis_index("expert"), lax.axis_index("tensor")
    core = part % 2
    found = []
    for k in range(lax.axis_size("expert") // NB):
        places = [k * NB + b for b in range(NB)]
        if is_cube():
            owners = [owner ^ p for p in places]
            mine = [part ^ (y * 2) for y in range(2)]
        else:
            owners = places
            mine = [y * 2 + core for y in range(lax.axis_size("tensor") // 2)]
        theirs = [m ^ 1 for m in mine]
        rows = [m // 2 for m in mine]
        found.append(
            jnp.stack([jnp.asarray(v, jnp.int32) for v in places + owners + mine + theirs + rows])
        )
    return found


def gather_routes(routes):
    if not is_cube():
        return lax.all_gather(routes, "expert")
    both = jnp.stack([routes, send(routes, dx=1)])
    both = jnp.concatenate([both, send(both, dz=1)])
    return jnp.concatenate([both, send(both, dz=2)])


def same_core():
    count = lax.axis_size("tensor")
    return [[y * 2 + c for y in range(count // 2)] for c in range(2)]


def gather_all(own):
    owners, parts = lax.axis_size("expert"), lax.axis_size("tensor")
    groups = [[e * parts + t for e in range(owners) for t in range(c, parts, 2)] for c in range(2)]
    full = lax.all_gather(own, BOTH, axis_index_groups=groups)
    return full.reshape(owners, parts // 2, *own.shape)


def gather_slots(own, tag, seen, first=()):
    if not is_cube():
        return [gather_all(own)] * (lax.axis_size("expert") // NB)
    slots = []
    far_own = after(own, *first) if first else own
    for k in range(4):
        block = send(far_own, dz=k) if k else own
        over_x = send(block, dx=1)
        over_y = send(block, dy=1)
        far = send(over_x, dy=1) if k in ODD else send(over_y, dx=1)
        for link, value in zip("zxyd", (block, over_x, over_y, far)):
            seen[tag + link + str(k)] = value
        slots.append([[block, over_y], [over_x, far]])
    return slots


def added(*terms):
    return sum(t.astype(F32) for t in terms)


def scatter_corner(parts, odd):
    return send(parts[1][1], dy=1) if odd else send(parts[1][1], dx=1)


def scatter_plane(parts, far, odd, hold=(), hold_x=()):
    near, over_y, over_x = parts[0][0], parts[0][1], parts[1][0]
    if odd:
        over_x, over_y = added(over_x, far).astype(BF16), after(over_y, far)
    else:
        over_x, over_y = after(over_x, far), added(over_y, far).astype(BF16)
    if hold:
        over_y = after(over_y, *hold)
    if hold_x:
        over_x = after(over_x, *hold_x)
    from_x, from_y = send(over_x, dx=1), send(over_y, dy=1)
    return added(near, from_x, from_y), {"d": far, "x": from_x, "y": from_y}


def scatter_all(slots):
    full = jnp.stack(
        [jnp.stack([s[b][y] for s in slots for b in range(NB)]) for y in range(len(slots[0][0]))]
    )
    mine = lax.psum_scatter(full, "tensor", axis_index_groups=same_core(), scatter_dimension=0)
    return lax.psum_scatter(mine, "expert", scatter_dimension=0).astype(F32)


def scatter_corners(pairs, seen):
    if not is_cube():
        return []
    far = [scatter_corner(pair, i == 0) for i, pair in enumerate(pairs)]
    seen.update({"gd" + str(i): value for i, value in enumerate(far)})
    return far


def scatter_ends(planes, hold):
    if not is_cube():
        return scatter_all(
            [[[a[i] for a in b] for b in pair] for pair in planes for i in range(pair[0][0].shape[0])]
        )
    low, high = planes
    total = low + send(after(high.astype(BF16), *hold), dz=2).astype(F32)
    return total[0] + send(total[1].astype(BF16), dz=1).astype(F32)


def tensor_order():
    part = lax.axis_index("tensor")
    if is_cube():
        return [part ^ i for i in (0, 2, 1, 3)]
    return [jnp.int32(i) for i in range(lax.axis_size("tensor"))]


def order_spots():
    if not is_cube():
        return lambda s: s
    part = lax.axis_index("tensor")
    return lambda s: (part ^ s) % 2 * 2 + (part ^ s) // 2


def tensor_gather(own, beside=()):
    if not is_cube():
        full = lax.all_gather(own, "tensor")
        return [full[i] for i in range(full.shape[0])]
    over_y = after(send(own, dy=1), *beside)
    return [own, over_y, core_swap(own), core_swap(over_y)]


def tensor_scatter(product, pieces, tag, seen, beside=()):
    if not is_cube():
        full = jnp.concatenate([product(p).astype(BF16) for p in pieces], axis=1)
        return lax.psum_scatter(full, "tensor", scatter_dimension=1, tiled=True).astype(F32)
    away_y = product(pieces[3]).astype(BF16)
    away = product(pieces[2]).astype(BF16)
    from_y, near = core_swap(away_y), core_swap(away)
    away = added(product(pieces[1]), from_y).astype(BF16)
    over_y = after(send(away, dy=1), *beside) if beside else send(away, dy=1)
    seen.update({tag + "0": from_y, tag + "1": near, tag + "y": over_y, tag + "s": away})
    return added(product(pieces[0]), near, over_y)


def tensor_sum(value):
    if not is_cube():
        return lax.psum(value, "tensor")
    value = value + core_swap(value)
    return value + send(value, dy=1)


def row_blocks():
    if not is_cube():
        return [jnp.int32(i) for i in range(8)]
    owner = lax.axis_index("expert")
    return [owner ^ (b | first << 1 | second << 2) for b in (0, 1) for first in (0, 1) for second in (0, 1)]


def expert_sum(value, tag, seen):
    half = value.shape[0] // 2
    if not is_cube():
        value = lax.psum(value, "expert")
        return value[:half], value[half:]
    for step in ({"dx": 1}, {"dz": 1}, {"dz": 2}):
        half = value.shape[0] // 2
        other = send(value[half:], **step)
        seen.setdefault(tag + "x", other)
        value = added(value[:half], other).astype(BF16)
    for step in ({"dz": 2}, {"dz": 1}):
        seen[tag] = send(value, **step)
        value = jnp.concatenate([value, seen[tag]], axis=0)
        seen[tag + str(step["dz"])] = seen[tag]
    return value, send(value, dx=1)


def expert_total(sums, tops, seen):
    if not is_cube():
        return lax.psum(sums, "expert"), lax.pmax(tops, "expert")
    count = sums.shape[0]
    both = jnp.concatenate([sums, tops], axis=0)
    for step in ({"dx": 1}, {"dz": 1}, {"dz": 2}):
        other = send(both, **step)
        seen.setdefault("t1", other)
        both = jnp.concatenate([both[:count] + other[:count], jnp.maximum(both[count:], other[count:])])
    return both[:count], both[count:]


def one_hot(pos_row):
    rows = lax.broadcasted_iota(jnp.int32, (CAP, pos_row.shape[1]), 0)
    return rows == pos_row


def as_bf16(mask):
    return jnp.where(mask, 1.0, 0.0).astype(BF16)


def pick_kernel(group, slices, where_ref, *refs):
    pos_refs, x_refs = refs[:NB], refs[NB : NB + NB * slices]
    out_ref, hot_ref = refs[-2:]
    step = pl.program_id(0)
    for b in range(NB):
        for i in range(group):
            hot_ref[b, i * CAP : (i + 1) * CAP, :] = as_bf16(
                one_hot(pos_refs[b][0, pl.ds(step * group + i, 1), :])
            )
        for y in range(slices):
            out_ref[b, y] = matmul(hot_ref[b], x_refs[b * slices + y][...]).astype(BF16)


def pick_rows(where, pos, blocks):
    held = pos.shape[1]
    group = 2
    if isinstance(blocks, list):
        slices = len(blocks[0])
        flat = [a for b in blocks for a in b]
        tokens, width = flat[0].shape
        specs = [pl.BlockSpec((tokens, width), lambda i, where: (0, 0)) for _ in flat]
    else:
        slices, tokens, width = blocks.shape[1:]
        flat = [blocks] * (NB * slices)

        def part_spec(b, y):
            return pl.BlockSpec(
                (None, None, tokens, width),
                lambda i, where: (where[NB + b], where[2 * NB + 2 * slices + y], 0, 0),
            )

        specs = [part_spec(b, y) for b in range(NB) for y in range(slices)]

    def block_spec(b):
        return pl.BlockSpec((1, held, tokens), lambda i, where: (where[b], 0, 0))

    return pl.pallas_call(
        partial(pick_kernel, group, slices),
        grid_spec=pltpu.PrefetchScalarGridSpec(
            num_scalar_prefetch=1,
            grid=(held // group,),
            in_specs=[block_spec(b) for b in range(NB)]
            + specs,
            out_specs=pl.BlockSpec(
                (NB, slices, group * CAP, width), lambda i, where: (0, 0, i, 0)
            ),
            scratch_shapes=[pltpu.VMEM((NB, group * CAP, tokens), BF16)],
        ),
        out_shape=jax.ShapeDtypeStruct((NB, slices, held * CAP, width), BF16),
        compiler_params=pltpu.CompilerParams(vmem_limit_bytes=VMEM),
        cost_estimate=cost(
            flops=2 * NB * slices * held * CAP * tokens * width,
            bytes_accessed=2 * NB * slices * (held * CAP + tokens) * width,
            transcendentals=0,
        ),
        name="pick_rows",
    )(where, *([pos] * NB), *flat)


def expert_kernel(slices, where_ref, *refs):
    pos_refs, gate_refs = refs[:NB], refs[NB : 2 * NB]
    rows_mine, rows_theirs, cot_mine, cot_theirs, wg_ref, wu_ref, wd_ref = refs[2 * NB : 2 * NB + 7]
    scaled_ref, gate_grad_ref, up_grad_ref, prob_ref, keep_ref, give_ref = refs[2 * NB + 7 :]
    e = pl.program_id(0)
    width = rows_mine.shape[3]
    ff = wg_ref.shape[2]
    gate_pre = jnp.zeros((NB * CAP, ff), F32)
    up_pre = jnp.zeros((NB * CAP, ff), F32)
    grad_hidden = jnp.zeros((NB * CAP, ff), F32)

    def columns(j):
        return pl.ds(pl.multiple_of(where_ref[2 * NB + j] * width, width), width)

    for j in range(2 * slices):
        x_ref, c_ref = (rows_mine, cot_mine) if j < slices else (rows_theirs, cot_theirs)
        x = x_ref[:, j % slices].reshape(NB * CAP, width)
        c = c_ref[:, j % slices].reshape(NB * CAP, width)
        gate_pre = gate_pre + matmul(x, wg_ref[0, columns(j), :])
        up_pre = up_pre + matmul(x, wu_ref[0, columns(j), :])
        grad_hidden = grad_hidden + matmul_nt(c, wd_ref[0, :, columns(j)])
    masks = [one_hot(pos_refs[b][0, pl.ds(e, 1), :]) for b in range(NB)]
    gates = jnp.concatenate(
        [
            jnp.sum(jnp.where(masks[b], gate_refs[b][0, pl.ds(e, 1), :], 0.0), axis=1, keepdims=True)
            for b in range(NB)
        ],
        axis=0,
    )
    sigma = jax.nn.sigmoid(gate_pre)
    swish = gate_pre * sigma
    hidden = (swish * up_pre).astype(BF16).astype(F32)
    prob = jnp.sum(hidden * grad_hidden, axis=1, keepdims=True)
    for b in range(NB):
        prob_ref[0, b : b + 1, :] = jnp.sum(
            jnp.where(masks[b], prob[b * CAP : (b + 1) * CAP], 0.0), axis=0, keepdims=True
        )
    grad_hidden = grad_hidden * gates
    scaled_ref[0] = (hidden * gates).astype(BF16)
    gate_grad = (grad_hidden * up_pre * (sigma * (1.0 + gate_pre * (1.0 - sigma)))).astype(BF16)
    up_grad = (grad_hidden * swish).astype(BF16)
    gate_grad_ref[0] = gate_grad
    up_grad_ref[0] = up_grad
    for j in range(2 * slices):
        to = keep_ref if j < slices else give_ref
        back = matmul_nt(gate_grad, wg_ref[0, columns(j), :]) + matmul_nt(
            up_grad, wu_ref[0, columns(j), :]
        )
        to[:, j % slices] = back.astype(BF16).reshape(NB, CAP, width)


def expert_slot(where, pos, gate, rows, cots, w_gate, w_up, w_down):
    held, depth, ff = w_gate.shape
    tokens = pos.shape[2]
    slices, width = rows[0].shape[1], rows[0].shape[3]

    def block_spec(b):
        return pl.BlockSpec((1, held, tokens), lambda e, where: (where[b], 0, 0))

    rows_spec = pl.BlockSpec((NB, slices, CAP, width), lambda e, where: (0, 0, e, 0))
    rows_shape = jax.ShapeDtypeStruct((NB, slices, held * CAP, width), BF16)
    in_spec = pl.BlockSpec((1, depth, ff), lambda e, where: (e, 0, 0))
    hidden_spec = pl.BlockSpec((1, NB * CAP, ff), lambda e, where: (e, 0, 0))
    hidden_shape = jax.ShapeDtypeStruct((held, NB * CAP, ff), BF16)
    return pl.pallas_call(
        partial(expert_kernel, slices),
        grid_spec=pltpu.PrefetchScalarGridSpec(
            num_scalar_prefetch=1,
            grid=(held,),
            in_specs=[block_spec(b) for b in range(2 * NB)]
            + [rows_spec] * 4
            + [in_spec, in_spec, pl.BlockSpec((1, ff, depth), lambda e, where: (e, 0, 0))],
            out_specs=[hidden_spec] * 3
            + [pl.BlockSpec((1, NB, tokens), lambda e, where: (e, 0, 0)), rows_spec, rows_spec],
        ),
        out_shape=[hidden_shape] * 3
        + [jax.ShapeDtypeStruct((held, NB, tokens), F32), rows_shape, rows_shape],
        compiler_params=pltpu.CompilerParams(vmem_limit_bytes=VMEM),
        cost_estimate=cost(
            flops=10 * NB * held * CAP * depth * ff,
            bytes_accessed=6 * held * depth * ff + 6 * NB * held * CAP * depth,
            transcendentals=NB * held * CAP * ff,
        ),
        name="expert_slot",
    )(where, *([pos] * NB), *([gate] * NB), *rows, *cots, w_gate, w_up, w_down)


def down_kernel(slices, slots, where_ref, *refs):
    scaled_refs, wd_ref, keep_ref, give_ref = refs[:slots], refs[slots], refs[-2], refs[-1]
    width = keep_ref.shape[3]
    for j in range(2 * slices):
        to = keep_ref if j < slices else give_ref
        columns = pl.ds(pl.multiple_of(where_ref[2 * NB + j] * width, width), width)
        for k in range(slots):
            rows = matmul(scaled_refs[k][0], wd_ref[0, :, columns])
            to[k * NB : (k + 1) * NB, j % slices] = rows.astype(BF16).reshape(NB, CAP, width)


def down_slots(where, scaled, w_down, slices):
    held, ff, depth = w_down.shape
    width = depth // (2 * slices)
    slots = len(scaled)
    rows_spec = pl.BlockSpec((slots * NB, slices, CAP, width), lambda e, where: (0, 0, e, 0))
    rows_shape = jax.ShapeDtypeStruct((slots * NB, slices, held * CAP, width), BF16)
    return pl.pallas_call(
        partial(down_kernel, slices, slots),
        grid_spec=pltpu.PrefetchScalarGridSpec(
            num_scalar_prefetch=1,
            grid=(held,),
            in_specs=[pl.BlockSpec((1, NB * CAP, ff), lambda e, where: (e, 0, 0))] * slots
            + [pl.BlockSpec((1, ff, depth), lambda e, where: (e, 0, 0))],
            out_specs=[rows_spec, rows_spec],
        ),
        out_shape=[rows_shape, rows_shape],
        compiler_params=pltpu.CompilerParams(vmem_limit_bytes=VMEM),
        cost_estimate=cost(
            flops=2 * slots * NB * held * CAP * depth * ff,
            bytes_accessed=2 * held * depth * ff + 2 * slots * NB * held * CAP * depth,
            transcendentals=0,
        ),
        name="down_slots",
    )(where, *scaled, w_down)


def place_kernel(slices, held, slots, where_ref, *refs):
    count = NB * slots
    at_refs, mine_ref, theirs_ref = refs[:count], refs[count], refs[count + 1]
    out_refs, hot_ref = refs[count + 2 : -1], refs[-1]
    b, y = pl.program_id(0), pl.program_id(1)
    tokens = hot_ref.shape[0]
    for block in range(count):

        @pl.when((b == block) & (y == 0))
        def _():
            at = at_refs[block][0]
            for tile in range(held * CAP // 128):
                lanes = lax.broadcasted_iota(jnp.int32, (tokens, 128), 1) + tile * 128
                mask = None
                for e in range(tile * 128 // CAP, (tile * 128 + 127) // CAP + 1):
                    hit = at[:, e : e + 1] == lanes
                    mask = hit if mask is None else mask | hit
                hot_ref[:, tile * 128 : (tile + 1) * 128] = as_bf16(mask)

    rows = (mine_ref[0, 0].astype(F32) + theirs_ref[0, 0].astype(F32)).astype(BF16)
    placed = matmul(hot_ref[...], rows).astype(BF16)
    for block in range(count):
        for part in range(slices):

            @pl.when((b == block) & (y == part))
            def _():
                out_refs[block % NB * slices + part][block // NB] = placed


def place_rows(wheres, at, mine, theirs):
    _, slices, count, width = mine.shape
    _, tokens, held = at.shape
    slots = len(wheres)
    blocks = jnp.concatenate([w[:NB] for w in wheres])

    def block_spec(b):
        return pl.BlockSpec((1, tokens, held), lambda i, y, where: (where[b], 0, 0))

    rows_spec = pl.BlockSpec((1, 1, count, width), lambda i, y, where: (i, y, 0, 0))
    out = pl.pallas_call(
        partial(place_kernel, slices, held, slots),
        grid_spec=pltpu.PrefetchScalarGridSpec(
            num_scalar_prefetch=1,
            grid=(NB * slots, slices),
            in_specs=[block_spec(b) for b in range(NB * slots)] + [rows_spec, rows_spec],
            out_specs=[pl.BlockSpec((slots, tokens, width), lambda i, y, where: (0, 0, 0))]
            * (NB * slices),
            scratch_shapes=[pltpu.VMEM((tokens, count), BF16)],
        ),
        out_shape=[jax.ShapeDtypeStruct((slots, tokens, width), BF16)] * (NB * slices),
        compiler_params=pltpu.CompilerParams(vmem_limit_bytes=VMEM),
        cost_estimate=cost(
            flops=2 * NB * slots * slices * count * tokens * width,
            bytes_accessed=2 * NB * slots * slices * (2 * count + tokens) * width,
            transcendentals=0,
        ),
        name="place_rows",
    )(blocks, *([at] * (NB * slots)), mine, theirs)
    return [out[b * slices : (b + 1) * slices] for b in range(NB)]


def weight_kernel(slots, slices, where_ref, *refs):
    rows, gate_grads, up_grads = refs[: 2 * slots], refs[2 * slots : 3 * slots], refs[3 * slots : 4 * slots]
    gate_ref, up_ref = refs[4 * slots :]
    width = rows[0].shape[3]
    for j in range(2 * slices):
        columns = pl.ds(pl.multiple_of(where_ref[2 * NB + j] * width, width), width)
        gate = up = None
        for k in range(slots):
            x = rows[2 * k + j // slices][:, j % slices].reshape(NB * CAP, width)
            terms = matmul_tn(x, gate_grads[k][0]), matmul_tn(x, up_grads[k][0])
            gate, up = terms if gate is None else (gate + terms[0], up + terms[1])
        gate_ref[0, columns, :] = gate
        up_ref[0, columns, :] = up


def weight_down_kernel(slots, slices, where_ref, *refs):
    cots, scaled, down_ref = refs[: 2 * slots], refs[2 * slots : 3 * slots], refs[3 * slots]
    width = cots[0].shape[3]
    for j in range(2 * slices):
        columns = pl.ds(pl.multiple_of(where_ref[2 * NB + j] * width, width), width)
        down = None
        for k in range(slots):
            c = cots[2 * k + j // slices][:, j % slices].reshape(NB * CAP, width)
            term = matmul_tn(scaled[k][0], c)
            down = term if down is None else down + term
        down_ref[0, :, columns] = down


def weight_grads(kernel, where, rows, hiddens, outs, name):
    slots = len(rows)
    held, _, ff = hiddens[0].shape
    slices, width = rows[0][0].shape[1], rows[0][0].shape[3]
    depth = 2 * slices * width
    rows_spec = pl.BlockSpec((NB, slices, CAP, width), lambda e, where: (0, 0, e, 0))
    hidden_spec = pl.BlockSpec((1, NB * CAP, ff), lambda e, where: (e, 0, 0))
    return pl.pallas_call(
        partial(kernel, slots, slices),
        grid_spec=pltpu.PrefetchScalarGridSpec(
            num_scalar_prefetch=1,
            grid=(held,),
            in_specs=[rows_spec] * (2 * slots) + [hidden_spec] * len(hiddens),
            out_specs=[pl.BlockSpec((1, *o), lambda e, where: (e, 0, 0)) for o in outs],
        ),
        out_shape=[jax.ShapeDtypeStruct((held, *o), F32) for o in outs],
        compiler_params=pltpu.CompilerParams(vmem_limit_bytes=VMEM),
        cost_estimate=cost(flops=10**10, bytes_accessed=10**6, transcendentals=0),
        name=name,
    )(where, *[a for pair in rows for a in pair], *hiddens)


def settle_kernel(where_ref, *refs):
    halves, (output_ref, value_ref, query_ref, key_ref) = refs[:6], refs[6:]

    def settle(output, value, both):
        output_ref[...] = output[...].astype(F32).T
        value_ref[...] = value[...].astype(F32)
        width = query_ref.shape[1]
        query_ref[...] = both[:, :width].astype(F32)
        key_ref[...] = both[:, width:].astype(F32)

    @pl.when(pl.program_id(0) < 4)
    def _():
        settle(*halves[0::2])

    @pl.when(pl.program_id(0) >= 4)
    def _():
        settle(*halves[1::2])


def settle_rows(where, output, value, both):
    rows = 2 * value[0].shape[0]
    step = rows // 8
    width = value[0].shape[1]
    near = lambda n: pl.BlockSpec((step, n), lambda i, where: (jnp.minimum(i, 3), 0))
    far = lambda n: pl.BlockSpec((step, n), lambda i, where: (jnp.maximum(i, 4) - 4, 0))
    placed = pl.BlockSpec((step, width), lambda i, where: (where[i], 0))
    return pl.pallas_call(
        settle_kernel,
        grid_spec=pltpu.PrefetchScalarGridSpec(
            num_scalar_prefetch=1,
            grid=(8,),
            in_specs=[s(n) for n in (width, width, 2 * width) for s in (near, far)],
            out_specs=[pl.BlockSpec((width, step), lambda i, where: (0, where[i]))] + [placed] * 3,
        ),
        out_shape=[jax.ShapeDtypeStruct((width, rows), F32)]
        + [jax.ShapeDtypeStruct((rows, width), F32)] * 3,
        compiler_params=pltpu.CompilerParams(vmem_limit_bytes=VMEM),
        cost_estimate=cost(flops=0, bytes_accessed=24 * rows * width, transcendentals=0),
        name="settle_rows",
    )(where, *output, *value, *both)


def project_kernel(
    in_ref, ag_ref, wq_ref, wk_ref, wv_ref, qg_ref, kg_ref,
    x_ref, inv_ref, qr_ref, kr_ref, q_ref, k_ref, v_ref,
):
    @pl.when(pl.program_id(0) == 0)
    def _():
        for first in range(0, in_ref.shape[0], 256):
            rows = in_ref[first : first + 256, :].astype(F32)
            inverse = lax.rsqrt(jnp.mean(rows * rows, axis=1, keepdims=True) + 1e-05)
            inv_ref[first : first + 256, :] = inverse
            x_ref[first : first + 256, :] = (rows * inverse * ag_ref[...]).astype(BF16)

    x = x_ref[...]
    for w_ref, gain_ref, raw_ref, to_ref in ((wq_ref, qg_ref, qr_ref, q_ref), (wk_ref, kg_ref, kr_ref, k_ref)):
        raw = matmul(x, w_ref[...])
        raw_ref[...] = raw
        for h in range(raw.shape[1] // HD):
            part = raw[:, h * HD : (h + 1) * HD]
            inverse = lax.rsqrt(jnp.mean(part * part, axis=1, keepdims=True) + 1e-06)
            gain = gain_ref[:, h * HD : (h + 1) * HD]
            to_ref[:, h * HD : (h + 1) * HD] = (part * inverse * gain).astype(BF16)
    v_ref[...] = matmul(x, wv_ref[...]).astype(BF16)


def project(inputs, attn_gain, w_query, w_key, w_value, query_gain, key_gain):
    tokens, depth = inputs.shape
    columns = w_query.shape[1]
    step = min(256, columns)
    whole = pl.BlockSpec((tokens, depth), lambda i: (0, 0))
    weight = pl.BlockSpec((depth, step), lambda i: (0, i))
    gain = pl.BlockSpec((1, step), lambda i: (0, i))
    out = pl.BlockSpec((tokens, step), lambda i: (0, i))
    return pl.pallas_call(
        project_kernel,
        grid=(columns // step,),
        in_specs=[whole, pl.BlockSpec((1, depth), lambda i: (0, 0)), weight, weight, weight, gain, gain],
        out_specs=[whole, pl.BlockSpec((tokens, 1), lambda i: (0, 0))] + [out] * 5,
        out_shape=[
            jax.ShapeDtypeStruct((tokens, depth), BF16),
            jax.ShapeDtypeStruct((tokens, 1), F32),
        ]
        + [jax.ShapeDtypeStruct((tokens, columns), t) for t in (F32, F32, BF16, BF16, BF16)],
        compiler_params=pltpu.CompilerParams(vmem_limit_bytes=VMEM),
        cost_estimate=cost(
            flops=6 * tokens * depth * columns,
            bytes_accessed=4 * tokens * depth + 6 * depth * columns + 14 * tokens * columns,
            transcendentals=0,
        ),
        name="project",
    )(
        inputs, attn_gain.reshape(1, -1), w_query, w_key, w_value,
        query_gain.reshape(1, -1), key_gain.reshape(1, -1),
    )


def allowed_pairs(pieces_ref, base, first, rows, keys):
    query = first + lax.broadcasted_iota(jnp.int32, (rows, 1), 0)
    key = lax.broadcasted_iota(jnp.int32, (1, keys), 1)

    def piece_of(at, other):
        found = jnp.full(at.shape, other, jnp.int32)
        for j in range(2):
            start, length = pieces_ref[base + j], pieces_ref[base + 2 + j]
            found = jnp.where((at >= start) & (at < start + length), j, found)
        return found

    return (key <= query) | (piece_of(query, -1) == piece_of(key, -2))


def query_blocks():
    half = LENGTH // 2
    return ((0, half, half), (half, half, LENGTH))


def attend_kernel(scale, pieces_ref, q_ref, k_ref, v_ref, o_ref, log_ref, top_ref):
    base = pl.program_id(0) * 4
    best = None
    for first, rows, keys in query_blocks():
        allowed = allowed_pairs(pieces_ref, base, first, rows, keys)
        scores = matmul_nt(q_ref[first : first + rows, :], k_ref[:keys, :]) * scale
        masked = jnp.where(allowed, scores, -1e30)
        top = jnp.max(masked, axis=1, keepdims=True)
        weights = jnp.exp(masked - top)
        total = jnp.sum(weights, axis=1, keepdims=True)
        probs = (weights * (1.0 / total)).astype(BF16)
        o_ref[first : first + rows, :] = matmul(probs, v_ref[:keys, :]).astype(BF16)
        log_ref[0, first : first + rows, :] = top + jnp.log(total)
        most = jnp.max(top, axis=0, keepdims=True)
        best = most if best is None else jnp.maximum(best, most)
    top_ref[0] = jnp.broadcast_to(best, (8, HD))


def attend(pieces, queries, keys, values, scale):
    tokens, columns = queries.shape
    sequences, heads = tokens // LENGTH, columns // HD
    block = pl.BlockSpec((LENGTH, HD), lambda s, h, pieces: (s, h))
    return pl.pallas_call(
        partial(attend_kernel, scale),
        grid_spec=pltpu.PrefetchScalarGridSpec(
            num_scalar_prefetch=1,
            grid=(sequences, heads),
            in_specs=[block] * 3,
            out_specs=[
                block,
                pl.BlockSpec((1, LENGTH, 1), lambda s, h, pieces: (h, s, 0)),
                pl.BlockSpec((1, 8, HD), lambda s, h, pieces: (s * heads + h, 0, 0)),
            ],
        ),
        out_shape=[
            jax.ShapeDtypeStruct((tokens, columns), BF16),
            jax.ShapeDtypeStruct((heads, tokens, 1), F32),
            jax.ShapeDtypeStruct((sequences * heads, 8, HD), F32),
        ],
        compiler_params=pltpu.CompilerParams(vmem_limit_bytes=VMEM),
        cost_estimate=cost(
            flops=4 * tokens * LENGTH * columns,
            bytes_accessed=8 * tokens * columns,
            transcendentals=tokens * heads * LENGTH,
        ),
        name="attend",
    )(pieces, queries, keys, values)


def attend_back_kernel(
    scale, pieces_ref, q_ref, k_ref, v_ref, g_ref, log_ref, qr_ref, kr_ref, qg_ref, kg_ref,
    gq_ref, gk_ref, gv_ref, gqg_ref, gkg_ref, dq_ref, dk_ref, dv_ref,
):
    base = pl.program_id(0) * 4
    blocks = query_blocks()
    for first, rows, keys in blocks[::-1]:
        allowed = allowed_pairs(pieces_ref, base, first, rows, keys)
        q, g = q_ref[first : first + rows, :], g_ref[first : first + rows, :]
        k, v = k_ref[:keys, :], v_ref[:keys, :]
        scores = matmul_nt(q, k) * scale
        probs = jnp.exp(jnp.where(allowed, scores, -1e30) - log_ref[0, first : first + rows, :])
        grad_p = matmul_nt(g, v)
        delta = jnp.sum(probs * grad_p, axis=1, keepdims=True)
        grad_s = (probs * (grad_p - delta)).astype(BF16)
        dq_ref[first : first + rows, :] = matmul(grad_s, k) * scale
        dk = matmul_tn(grad_s, q) * scale
        dv = matmul_tn(probs.astype(BF16), g)
        if keys == LENGTH:
            dk_ref[...] = dk
            dv_ref[...] = dv
        else:
            dk_ref[:keys, :] += dk
            dv_ref[:keys, :] += dv
    gv_ref[...] = dv_ref[...].astype(BF16)
    for raw_ref, gain_ref, grad_ref, to_ref, sum_ref in (
        (qr_ref, qg_ref, dq_ref, gq_ref, gqg_ref),
        (kr_ref, kg_ref, dk_ref, gk_ref, gkg_ref),
    ):
        raw, grad = raw_ref[...], grad_ref[...]
        inverse = lax.rsqrt(jnp.mean(raw * raw, axis=1, keepdims=True) + 1e-06)
        hat = raw * inverse
        up = grad * gain_ref[...]
        mean = jnp.mean(up * hat, axis=1, keepdims=True)
        to_ref[...] = (inverse * (up - hat * mean)).astype(BF16)
        sum_ref[0] = jnp.sum(grad * hat, axis=0, keepdims=True)


def attend_back(pieces, queries, keys, values, grads, logs, query_raw, key_raw, query_gain, key_gain, scale):
    tokens, columns = queries.shape
    sequences, heads = tokens // LENGTH, columns // HD
    block = pl.BlockSpec((LENGTH, HD), lambda s, h, pieces: (s, h))
    gain = pl.BlockSpec((1, HD), lambda s, h, pieces: (0, h))
    sums = pl.BlockSpec((1, 1, HD), lambda s, h, pieces: (s, 0, h))
    return pl.pallas_call(
        partial(attend_back_kernel, scale),
        grid_spec=pltpu.PrefetchScalarGridSpec(
            num_scalar_prefetch=1,
            grid=(sequences, heads),
            in_specs=[block] * 4
            + [pl.BlockSpec((1, LENGTH, 1), lambda s, h, pieces: (h, s, 0)), block, block, gain, gain],
            out_specs=[block, block, block, sums, sums],
            scratch_shapes=[pltpu.VMEM((LENGTH, HD), F32)] * 3,
        ),
        out_shape=[jax.ShapeDtypeStruct((tokens, columns), BF16)] * 3
        + [jax.ShapeDtypeStruct((sequences, 1, columns), F32)] * 2,
        compiler_params=pltpu.CompilerParams(vmem_limit_bytes=VMEM),
        cost_estimate=cost(
            flops=10 * tokens * LENGTH * columns,
            bytes_accessed=22 * tokens * columns,
            transcendentals=tokens * heads * LENGTH,
        ),
        name="attend_back",
    )(
        pieces, queries, keys, values, grads, logs, query_raw, key_raw,
        query_gain.reshape(1, -1), key_gain.reshape(1, -1),
    )


def expert_steps(slots):
    order = list(ORDER) if is_cube() else list(range(slots))
    steps = [("cot", order[0]), ("row", order[0]), ("cot", order[1]), ("exp", order[0])]
    for i, k in enumerate(order):
        if i + 1 < slots:
            steps.append(("row", order[i + 1]))
        else:
            steps.append(("down", 0))
        if i + 2 < slots:
            steps.append(("cot", order[i + 2]))
        steps.append(("place", k))
        if i + 1 < slots:
            steps.append(("exp", order[i + 1]))
    return steps


def due(step, seen):
    return [seen[name] for name in DUE.get(step, ()) if name in seen]


def per_device(
    inputs,
    attn_gain,
    w_query,
    w_key,
    w_value,
    w_output,
    query_gain,
    key_gain,
    moe_gain,
    w_router,
    w_gate,
    w_up,
    w_down,
    routes,
    piece_start,
    piece_length,
    clip_threshold,
    cotangent,
):
    tokens_here, width = inputs.shape
    slice_width = cotangent.shape[1]
    owner = lax.axis_index("expert")
    column = lax.axis_index("tensor") * slice_width
    heads_here = query_gain.shape[0] // HD
    experts_here = w_gate.shape[0]
    owners = lax.axis_size("expert")
    sequences = tokens_here // LENGTH
    scale = 1.0 / math.sqrt(HD)
    where = slot_blocks()
    slots = len(where)
    slices = lax.axis_size("tensor") // 2

    def own_columns(value):
        return lax.dynamic_slice_in_dim(value, column, slice_width, value.ndim - 1)

    seen = {}
    all_routes = gather_routes(routes.T)
    cot_slots = gather_slots(cotangent.astype(BF16), "c", seen, [all_routes])
    order = tensor_order()

    held_ids = owner * experts_here + jnp.arange(experts_here, dtype=jnp.int32)
    chosen = jnp.any(all_routes[:, None] == held_ids[None, :, None, None], axis=2)
    places = jnp.arange(tokens_here, dtype=jnp.int32)
    before = (places[:, None] < places[None, :]).astype(BF16)
    earlier = jnp.einsum(
        "set,tu->seu", chosen.astype(BF16), before, preferred_element_type=F32
    ).astype(jnp.int32)
    pos = jnp.where(chosen, earlier, -1)
    at = jnp.where(
        chosen, earlier + jnp.arange(experts_here, dtype=jnp.int32)[None, :, None] * CAP, -1
    ).transpose(0, 2, 1)

    output_pieces = [lax.dynamic_slice_in_dim(w_output, o * slice_width, slice_width, 1) for o in order]
    normed_a, attn_inv, query_raw, key_raw, queries, keys, values = project(
        inputs, attn_gain, w_query, w_key, w_value, query_gain, key_gain
    )
    blocks = row_blocks()
    normed_rows = jnp.concatenate(
        [lax.dynamic_slice_in_dim(normed_a, r * (width // 8), width // 8, 1) for r in blocks], axis=1
    )
    pieces = jnp.concatenate([piece_start, piece_length], axis=1).reshape(-1)
    attended, logs, tops = attend(
        after(pieces, values, all_routes), queries, keys, values, scale
    )
    head_top = jnp.max(tops[:, 0, 0].reshape(sequences, heads_here), axis=0)
    attended = after(attended, *due("attended", seen))
    branch = tensor_scatter(partial(matmul, attended), output_pieces, "b", seen, [pos, at])
    residual = own_columns(inputs).astype(F32) + branch
    gain_slice = own_columns(moe_gain)
    router_slice = lax.dynamic_slice_in_dim(w_router, column, slice_width, 0)
    lifted = residual * gain_slice
    row_sums = tensor_sum(
        jnp.concatenate(
            [
                lax.dot_general(
                    router_slice,
                    lifted.astype(BF16),
                    (((0,), (1,)), ((), ())),
                    preferred_element_type=F32,
                ),
                jnp.sum(residual * residual, axis=1)[None],
            ],
            axis=0,
        )
    )
    moe_inv_row = lax.rsqrt(row_sums[E] / width + 1e-05)
    moe_inv = moe_inv_row[:, None]
    normed_m = (lifted * moe_inv).astype(BF16)
    normed_m = after(normed_m, *due("normed", seen))

    normed_slots = gather_slots(normed_m, "n", seen)
    router = jax.nn.softmax(row_sums[:E] * moe_inv_row[None], axis=0)
    gate = lax.all_to_all(
        router.reshape(owners, experts_here, tokens_here),
        "expert",
        split_axis=0,
        concat_axis=0,
        tiled=True,
    )

    rows, cots, back, sums = [None] * slots, [None] * slots, [None] * slots, [None] * slots
    scaled, gate_grads, up_grads, probs = [None] * slots, [None] * slots, [None] * slots, [None] * slots
    last = normed_m
    downs = {}

    def turn(name, k):
        return after(where[k], last, *due(name, seen))

    def lower(k):
        keep, give = down_slots(turn("down" + str(k), 0), scaled[2 * k : 2 * k + 2], w_down, slices)
        downs[k] = (keep, core_swap(give))
        seen["sd" + str(k)] = downs[k][1]
        return keep

    for kind, k in expert_steps(slots):
        now = turn(kind + str(k), k)
        if kind == "cot":
            last = pick_rows(now, pos, cot_slots[k])
            cots[k] = (last, core_swap(last))
            seen["sc" + str(k)] = cots[k][1]
        elif kind == "row":
            last = pick_rows(now, pos, normed_slots[k])
            rows[k] = (last, core_swap(last))
            seen["sr" + str(k)] = rows[k][1]
        elif kind == "exp":
            scaled[k], gate_grads[k], up_grads[k], probs[k], keep, give = expert_slot(
                now, pos, gate, rows[k], cots[k], w_gate, w_up, w_down
            )
            last = scaled[k]
            back[k] = (keep, core_swap(give))
            seen["sg" + str(k)] = back[k][1]
        elif kind == "down":
            last = lower(k)
        else:
            placed = place_rows([now], at, *back[k])
            last = placed[0][0]
            back[k] = [[a[0] for a in b] for b in placed]
            if is_cube():
                odd = k in ODD
                sums[k], sent = scatter_plane(back[k], scatter_corner(back[k], odd), odd)
                if k:
                    sums[k] = sent["z"] = send(sums[k].astype(BF16), dz=k)
                seen.update({"e" + link + str(k): value for link, value in sent.items()})
    for k in range(1, slots // 2):
        last = lower(k)
    pairs = []
    for k in range(slots // 2):
        pairs.append(place_rows([turn("pd" + str(k), 2 * k), where[2 * k + 1]], at, *downs[k]))
        last = pairs[k][0][0]
    far = scatter_corners(pairs, seen)
    grad_gate, grad_up = weight_grads(
        weight_kernel,
        turn("weight", 0),
        rows,
        gate_grads + up_grads,
        [w_gate.shape[1:]] * 2,
        "weight_grads",
    )
    if is_cube():
        expert_path = added(*[after(s, grad_gate) for s in sums])
    else:
        expert_path = scatter_all(back)

    prob_grads = jnp.stack([probs[k][:, b] for k in range(slots) for b in range(NB)])
    if is_cube():
        prob_grads = prob_grads[jnp.arange(owners, dtype=jnp.int32) ^ owner]
    prob_grads = lax.all_to_all(prob_grads, "expert", split_axis=0, concat_axis=0, tiled=True)
    prob_grads = tensor_sum(prob_grads.reshape(E, tokens_here))
    grad_logits = (
        router * (prob_grads - jnp.sum(router * prob_grads, axis=0, keepdims=True))
    ).astype(BF16)
    grad_router = lax.dot_general(
        normed_m, grad_logits, (((0,), (1,)), ((), ())), preferred_element_type=F32
    )
    router_path = lax.dot_general(
        grad_logits, router_slice, (((0,), (1,)), ((), ())), preferred_element_type=F32
    )
    grad_normed = expert_path + router_path
    moe_hat = residual * moe_inv
    grad_moe_gain = jnp.sum(grad_normed * moe_hat, axis=0)
    upstream = grad_normed * gain_slice
    mean_dot = tensor_sum(jnp.sum(upstream * moe_hat, axis=-1).reshape(8, -1)).reshape(-1, 1) / width
    grad_residual = cotangent + moe_inv * (upstream - moe_hat * mean_dot)
    grad_branch = after(grad_residual.astype(BF16), *due("residual_grad", seen))
    (grad_down,) = weight_grads(
        weight_down_kernel,
        after(where[0], grad_branch),
        cots,
        scaled,
        [w_down.shape[1:]],
        "weight_down_grads",
    )
    branch_pieces = tensor_gather(grad_branch, [grad_down])

    planes = pairs
    if is_cube():
        plane, sent = scatter_plane(pairs[0], far[0], True, branch_pieces[1:2])
        planes = [plane]
        seen.update({"g" + link + "0": value for link, value in sent.items()})
    grad_branch = jnp.concatenate(branch_pieces, axis=1)

    grad_output = matmul_tn(grad_branch, attended).astype(BF16)
    spots = order_spots()
    eighth = width // 8
    wide = slice_width // eighth
    grad_output = jnp.concatenate(
        [
            lax.dynamic_slice_in_dim(
                grad_output, (spots(r // wide) * wide + r % wide) * eighth, eighth, 0
            )
            for r in blocks
        ],
        axis=0,
    )
    sum_output = expert_sum(grad_output, "o", seen)
    grad_attended = matmul_nt(grad_branch, jnp.concatenate(output_pieces, axis=1)).astype(BF16)
    grad_attended = after(grad_attended, grad_output)
    grad_query_raw, grad_key_raw, grad_v, grad_query_gain, grad_key_gain = attend_back(
        after(pieces, *due("back", seen)),
        queries,
        keys,
        values,
        grad_attended,
        logs,
        query_raw,
        key_raw,
        query_gain,
        key_gain,
        scale,
    )
    sum_value = expert_sum(matmul_tn(normed_rows, grad_v).astype(BF16), "v", seen)
    grad_raw = jnp.concatenate([grad_query_raw, grad_key_raw, grad_v], axis=1)
    grad_both = matmul_tn(normed_rows, grad_raw[:, : 2 * slice_width]).astype(BF16)
    sum_both = expert_sum(grad_both, "qk", seen)
    grad_raw = after(grad_raw, grad_both, *due("normed_grad", seen))
    weights = jnp.concatenate([w_query, w_key, w_value], axis=1)
    weight_pieces = [lax.dynamic_slice_in_dim(weights, o * slice_width, slice_width, 0) for o in order]
    grad_normed_a = tensor_scatter(partial(matmul_nt, grad_raw), weight_pieces, "h", seen)
    attn_hat = own_columns(inputs).astype(F32) * attn_inv
    upstream = grad_normed_a * own_columns(attn_gain)
    grad_attn_gain = jnp.sum(grad_normed_a * attn_hat, axis=0)
    mean_dot = tensor_sum(jnp.sum(upstream * attn_hat, axis=-1).reshape(8, -1)).reshape(-1, 1) / width
    grad_input = grad_residual + attn_inv * (upstream - attn_hat * mean_dot)

    small = jnp.concatenate(
        [
            grad_router.T,
            jnp.stack(
                [
                    grad_attn_gain,
                    grad_moe_gain,
                    jnp.sum(grad_query_gain, axis=(0, 1)),
                    jnp.sum(grad_key_gain, axis=(0, 1)),
                ]
            ),
        ],
        axis=0,
    )
    top_row = jnp.pad(head_top, (0, slice_width - heads_here), constant_values=-3e38)
    small, top_row = expert_total(small, top_row[None], seen)
    head_top = top_row[0, :heads_here]
    if is_cube():
        free = [seen["qkx"], seen["t1"]]
        planes.append(scatter_plane(pairs[1], far[1], False, branch_pieces[1:2], free)[0])
    mixture = scatter_ends(planes, [small, *due("ends", seen)])
    out = residual + mixture
    sum_moe_gain, sum_query_gain, sum_key_gain = small[E + 1], small[E + 2], small[E + 3]
    every = lax.all_gather(small[: E + 1], "tensor")
    sum_router = every[:, :E].transpose(0, 2, 1).reshape(width, E)
    sum_attn_gain = every[:, E].reshape(width)
    sum_output, sum_value, sum_query, sum_key = settle_rows(
        jnp.stack(blocks), sum_output, sum_value, sum_both
    )
    factor = clip_threshold / jnp.maximum(head_top, clip_threshold)
    spread = jnp.repeat(jnp.sqrt(factor), HD)
    query_clipped = (w_query.astype(F32) * spread[None, :]).astype(BF16)
    key_clipped = (w_key.astype(F32) * spread[None, :]).astype(BF16)
    return (
        out,
        grad_input,
        sum_attn_gain,
        sum_query,
        sum_key,
        sum_value,
        sum_output,
        sum_query_gain,
        sum_key_gain,
        sum_moe_gain,
        sum_router,
        grad_gate,
        grad_up,
        grad_down,
        head_top,
        query_clipped,
        key_clipped,
    )


def solution(mesh):
    return jax.shard_map(
        per_device,
        mesh=mesh,
        in_specs=(
            P("expert", None),
            P(),
            P(None, "tensor"),
            P(None, "tensor"),
            P(None, "tensor"),
            P("tensor", None),
            P("tensor"),
            P("tensor"),
            P(),
            P(),
            P("expert", None, "tensor"),
            P("expert", None, "tensor"),
            P("expert", "tensor", None),
            P("expert", None),
            P("expert", None),
            P("expert", None),
            P("tensor"),
            P("expert", "tensor"),
        ),
        out_specs=(
            P("expert", "tensor"),
            P("expert", "tensor"),
            P(),
            P(None, "tensor"),
            P(None, "tensor"),
            P(None, "tensor"),
            P("tensor", None),
            P("tensor"),
            P("tensor"),
            P("tensor"),
            P(),
            P("expert", None, "tensor"),
            P("expert", None, "tensor"),
            P("expert", "tensor", None),
            P("tensor"),
            P(None, "tensor"),
            P(None, "tensor"),
        ),
        check_vma=False,
    )
```

```python
from functools import partial
import math

import jax
import jax.numpy as jnp
from jax import lax
from jax.experimental import pallas as pl
from jax.experimental.pallas import tpu as pltpu
from jax.sharding import PartitionSpec as P

HD = 128
E = 64
TOP = 8
LENGTH = 1024
CAP = 160
NB = 2
BOTH = ("expert", "tensor")
F32 = jnp.float32
BF16 = jnp.bfloat16
VMEM = 60 * 1024 * 1024
WEIGHT = 16
ORDER = (0, 2, 3, 1)
ODD = (1, 2)
DUE = {
    "attended": ("cx0", "cy0"),
    "normed": ("cz2", "cd0"),
    "row0": ("cx2", "cz3", "cy2"),
    "exp0": ("cx3",),
    "row2": ("sc2", "cy3"),
    "cot3": ("sg0",),
    "place0": ("sr2",),
    "exp2": ("sc3",),
    "cot1": ("sg2",),
    "place2": ("sr3", "ed0"),
    "exp3": ("sc1",),
    "place3": ("ex0", "ey0", "ed2"),
    "down1": ("ex2", "ey2", "ed3"),
    "pd0": ("ed1", "sd0"),
    "weight": ("ex3", "ey3", "ex1", "ey1"),
    "residual_grad": ("gd0", "gd1"),
    "back": ("gx0",),
    "normed_grad": ("gy0",),
    "ends": ("qk2",),
}


def cost(flops, bytes_accessed, transcendentals):
    return pl.CostEstimate(
        flops=flops * WEIGHT, bytes_accessed=bytes_accessed * WEIGHT, transcendentals=transcendentals * WEIGHT
    )


def matmul(left, right):
    return jnp.dot(left, right, preferred_element_type=F32)


def matmul_nt(left, right):
    return lax.dot_general(left, right, (((1,), (1,)), ((), ())), preferred_element_type=F32)


def matmul_tn(left, right):
    return lax.dot_general(left, right, (((0,), (0,)), ((), ())), preferred_element_type=F32)


def after(value, *others):
    return lax.optimization_barrier((value, *others))[0]


def flip(dz, dx, dy, dc):
    pairs = []
    for z in range(4):
        for x in range(2):
            for y in range(2):
                for c in range(2):
                    pairs.append(
                        (
                            ((z * 2 + x) * 2 + y) * 2 + c,
                            (((z ^ dz) * 2 + (x ^ dx)) * 2 + (y ^ dy)) * 2 + (c ^ dc),
                        )
                    )
    return pairs


def send(value, dz=0, dx=0, dy=0, dc=0):
    return lax.ppermute(value, BOTH, flip(dz, dx, dy, dc))


def is_cube():
    return lax.axis_size("expert") == 8 and lax.axis_size("tensor") == 4


def core_swap(value):
    if is_cube():
        return send(value, dc=1)
    count = lax.axis_size("tensor")
    return lax.ppermute(value, "tensor", [(i, i ^ 1) for i in range(count)])


def slot_blocks():
    owner, part = lax.axis_index("expert"), lax.axis_index("tensor")
    core = part % 2
    found = []
    for k in range(lax.axis_size("expert") // NB):
        places = [k * NB + b for b in range(NB)]
        if is_cube():
            owners = [owner ^ p for p in places]
            mine = [part ^ (y * 2) for y in range(2)]
        else:
            owners = places
            mine = [y * 2 + core for y in range(lax.axis_size("tensor") // 2)]
        theirs = [m ^ 1 for m in mine]
        rows = [m // 2 for m in mine]
        found.append(
            jnp.stack([jnp.asarray(v, jnp.int32) for v in places + owners + mine + theirs + rows])
        )
    return found


def gather_routes(routes):
    if not is_cube():
        return lax.all_gather(routes, "expert")
    both = jnp.stack([routes, send(routes, dx=1)])
    both = jnp.concatenate([both, send(both, dz=1)])
    return jnp.concatenate([both, send(both, dz=2)])


def same_core():
    count = lax.axis_size("tensor")
    return [[y * 2 + c for y in range(count // 2)] for c in range(2)]


def gather_all(own):
    owners, parts = lax.axis_size("expert"), lax.axis_size("tensor")
    groups = [[e * parts + t for e in range(owners) for t in range(c, parts, 2)] for c in range(2)]
    full = lax.all_gather(own, BOTH, axis_index_groups=groups)
    return full.reshape(owners, parts // 2, *own.shape)


def gather_slots(own, tag, seen, first=()):
    if not is_cube():
        return [gather_all(own)] * (lax.axis_size("expert") // NB)
    slots = []
    far_own = after(own, *first) if first else own
    for k in range(4):
        block = send(far_own, dz=k) if k else own
        over_x = send(block, dx=1)
        over_y = send(block, dy=1)
        far = send(over_x, dy=1) if k in ODD else send(over_y, dx=1)
        for link, value in zip("zxyd", (block, over_x, over_y, far)):
            seen[tag + link + str(k)] = value
        slots.append([[block, over_y], [over_x, far]])
    return slots


def added(*terms):
    return sum(t.astype(F32) for t in terms)


def scatter_corner(parts, odd):
    return send(parts[1][1], dy=1) if odd else send(parts[1][1], dx=1)


def scatter_plane(parts, far, odd, hold=(), hold_x=()):
    near, over_y, over_x = parts[0][0], parts[0][1], parts[1][0]
    if odd:
        over_x, over_y = added(over_x, far).astype(BF16), after(over_y, far)
    else:
        over_x, over_y = after(over_x, far), added(over_y, far).astype(BF16)
    if hold:
        over_y = after(over_y, *hold)
    if hold_x:
        over_x = after(over_x, *hold_x)
    from_x, from_y = send(over_x, dx=1), send(over_y, dy=1)
    return added(near, from_x, from_y), {"d": far, "x": from_x, "y": from_y}


def scatter_all(slots):
    full = jnp.stack(
        [jnp.stack([s[b][y] for s in slots for b in range(NB)]) for y in range(len(slots[0][0]))]
    )
    mine = lax.psum_scatter(full, "tensor", axis_index_groups=same_core(), scatter_dimension=0)
    return lax.psum_scatter(mine, "expert", scatter_dimension=0).astype(F32)


def scatter_corners(pairs, seen):
    if not is_cube():
        return []
    far = [scatter_corner(pair, i == 0) for i, pair in enumerate(pairs)]
    seen.update({"gd" + str(i): value for i, value in enumerate(far)})
    return far


def tensor_order():
    part = lax.axis_index("tensor")
    if is_cube():
        return [part ^ i for i in (0, 2, 1, 3)]
    return [jnp.int32(i) for i in range(lax.axis_size("tensor"))]


def order_spots():
    if not is_cube():
        return lambda s: s
    part = lax.axis_index("tensor")
    return lambda s: (part ^ s) % 2 * 2 + (part ^ s) // 2


def tensor_gather(own, beside=()):
    if not is_cube():
        full = lax.all_gather(own, "tensor")
        return [full[i] for i in range(full.shape[0])]
    over_y = after(send(own, dy=1), *beside)
    return [own, over_y, core_swap(own), core_swap(over_y)]


def tensor_scatter(product, pieces, tag, seen, beside=()):
    if not is_cube():
        full = jnp.concatenate([product(p).astype(BF16) for p in pieces], axis=1)
        return lax.psum_scatter(full, "tensor", scatter_dimension=1, tiled=True).astype(F32)
    away_y = product(pieces[3]).astype(BF16)
    away = product(pieces[2]).astype(BF16)
    from_y, near = core_swap(away_y), core_swap(away)
    away = added(product(pieces[1]), from_y).astype(BF16)
    over_y = after(send(away, dy=1), *beside) if beside else send(away, dy=1)
    seen.update({tag + "0": from_y, tag + "1": near, tag + "y": over_y, tag + "s": away})
    return added(product(pieces[0]), near, over_y)


def tensor_sum(value):
    if not is_cube():
        return lax.psum(value, "tensor")
    value = value + core_swap(value)
    return value + send(value, dy=1)


def row_blocks():
    if not is_cube():
        return [jnp.int32(i) for i in range(8)]
    owner = lax.axis_index("expert")
    return [owner ^ (b | first << 1 | second << 2) for b in (0, 1) for first in (0, 1) for second in (0, 1)]


def expert_sum(value, tag, seen):
    half = value.shape[0] // 2
    if not is_cube():
        value = lax.psum(value, "expert")
        return value[:half], value[half:]
    for step in ({"dx": 1}, {"dz": 1}, {"dz": 2}):
        half = value.shape[0] // 2
        other = send(value[half:], **step)
        seen.setdefault(tag + "x", other)
        value = added(value[:half], other).astype(BF16)
    for step in ({"dz": 2}, {"dz": 1}):
        seen[tag] = send(value, **step)
        value = jnp.concatenate([value, seen[tag]], axis=0)
        seen[tag + str(step["dz"])] = seen[tag]
    return value, send(value, dx=1)


def expert_total(sums, tops, seen):
    if not is_cube():
        return lax.psum(sums, "expert"), lax.pmax(tops, "expert")
    count = sums.shape[0]
    both = jnp.concatenate([sums, tops], axis=0)
    for step in ({"dx": 1}, {"dz": 1}, {"dz": 2}):
        other = send(both, **step)
        seen.setdefault("t1", other)
        both = jnp.concatenate([both[:count] + other[:count], jnp.maximum(both[count:], other[count:])])
    return both[:count], both[count:]


def one_hot(pos_row):
    rows = lax.broadcasted_iota(jnp.int32, (CAP, pos_row.shape[1]), 0)
    return rows == pos_row


def as_bf16(mask):
    return jnp.where(mask, 1.0, 0.0).astype(BF16)


def pick_kernel(group, slices, where_ref, *refs):
    pos_refs, x_refs = refs[:NB], refs[NB : NB + NB * slices]
    out_ref, hot_ref = refs[-2:]
    step = pl.program_id(0)
    for b in range(NB):
        for i in range(group):
            hot_ref[b, i * CAP : (i + 1) * CAP, :] = as_bf16(
                one_hot(pos_refs[b][0, pl.ds(step * group + i, 1), :])
            )
        for y in range(slices):
            out_ref[b, y] = matmul(hot_ref[b], x_refs[b * slices + y][...]).astype(BF16)


def pick_rows(where, pos, blocks):
    held = pos.shape[1]
    group = 2
    if isinstance(blocks, list):
        slices = len(blocks[0])
        flat = [a for b in blocks for a in b]
        tokens, width = flat[0].shape
        specs = [pl.BlockSpec((tokens, width), lambda i, where: (0, 0)) for _ in flat]
    else:
        slices, tokens, width = blocks.shape[1:]
        flat = [blocks] * (NB * slices)

        def part_spec(b, y):
            return pl.BlockSpec(
                (None, None, tokens, width),
                lambda i, where: (where[NB + b], where[2 * NB + 2 * slices + y], 0, 0),
            )

        specs = [part_spec(b, y) for b in range(NB) for y in range(slices)]

    def block_spec(b):
        return pl.BlockSpec((1, held, tokens), lambda i, where: (where[b], 0, 0))

    return pl.pallas_call(
        partial(pick_kernel, group, slices),
        grid_spec=pltpu.PrefetchScalarGridSpec(
            num_scalar_prefetch=1,
            grid=(held // group,),
            in_specs=[block_spec(b) for b in range(NB)]
            + specs,
            out_specs=pl.BlockSpec(
                (NB, slices, group * CAP, width), lambda i, where: (0, 0, i, 0)
            ),
            scratch_shapes=[pltpu.VMEM((NB, group * CAP, tokens), BF16)],
        ),
        out_shape=jax.ShapeDtypeStruct((NB, slices, held * CAP, width), BF16),
        compiler_params=pltpu.CompilerParams(vmem_limit_bytes=VMEM),
        cost_estimate=cost(
            flops=2 * NB * slices * held * CAP * tokens * width,
            bytes_accessed=2 * NB * slices * (held * CAP + tokens) * width,
            transcendentals=0,
        ),
        name="pick_rows",
    )(where, *([pos] * NB), *flat)


def expert_kernel(slices, where_ref, *refs):
    pos_refs, gate_refs = refs[:NB], refs[NB : 2 * NB]
    rows_mine, rows_theirs, cot_mine, cot_theirs, wg_ref, wu_ref, wd_ref = refs[2 * NB : 2 * NB + 7]
    scaled_ref, gate_grad_ref, up_grad_ref, prob_ref, keep_ref, give_ref = refs[2 * NB + 7 :]
    e = pl.program_id(0)
    width = rows_mine.shape[3]
    ff = wg_ref.shape[2]
    gate_pre = jnp.zeros((NB * CAP, ff), F32)
    up_pre = jnp.zeros((NB * CAP, ff), F32)
    grad_hidden = jnp.zeros((NB * CAP, ff), F32)

    def columns(j):
        return pl.ds(pl.multiple_of(where_ref[2 * NB + j] * width, width), width)

    for j in range(2 * slices):
        x_ref, c_ref = (rows_mine, cot_mine) if j < slices else (rows_theirs, cot_theirs)
        x = x_ref[:, j % slices].reshape(NB * CAP, width)
        c = c_ref[:, j % slices].reshape(NB * CAP, width)
        gate_pre = gate_pre + matmul(x, wg_ref[0, columns(j), :])
        up_pre = up_pre + matmul(x, wu_ref[0, columns(j), :])
        grad_hidden = grad_hidden + matmul_nt(c, wd_ref[0, :, columns(j)])
    masks = [one_hot(pos_refs[b][0, pl.ds(e, 1), :]) for b in range(NB)]
    gates = jnp.concatenate(
        [
            jnp.sum(jnp.where(masks[b], gate_refs[b][0, pl.ds(e, 1), :], 0.0), axis=1, keepdims=True)
            for b in range(NB)
        ],
        axis=0,
    )
    sigma = jax.nn.sigmoid(gate_pre)
    swish = gate_pre * sigma
    hidden = (swish * up_pre).astype(BF16).astype(F32)
    prob = jnp.sum(hidden * grad_hidden, axis=1, keepdims=True)
    for b in range(NB):
        prob_ref[0, b : b + 1, :] = jnp.sum(
            jnp.where(masks[b], prob[b * CAP : (b + 1) * CAP], 0.0), axis=0, keepdims=True
        )
    grad_hidden = grad_hidden * gates
    scaled_ref[0] = (hidden * gates).astype(BF16)
    gate_grad = (grad_hidden * up_pre * (sigma * (1.0 + gate_pre * (1.0 - sigma)))).astype(BF16)
    up_grad = (grad_hidden * swish).astype(BF16)
    gate_grad_ref[0] = gate_grad
    up_grad_ref[0] = up_grad
    for j in range(2 * slices):
        to = keep_ref if j < slices else give_ref
        back = matmul_nt(gate_grad, wg_ref[0, columns(j), :]) + matmul_nt(
            up_grad, wu_ref[0, columns(j), :]
        )
        to[:, j % slices] = back.astype(BF16).reshape(NB, CAP, width)


def expert_slot(where, pos, gate, rows, cots, w_gate, w_up, w_down):
    held, depth, ff = w_gate.shape
    tokens = pos.shape[2]
    slices, width = rows[0].shape[1], rows[0].shape[3]

    def block_spec(b):
        return pl.BlockSpec((1, held, tokens), lambda e, where: (where[b], 0, 0))

    rows_spec = pl.BlockSpec((NB, slices, CAP, width), lambda e, where: (0, 0, e, 0))
    rows_shape = jax.ShapeDtypeStruct((NB, slices, held * CAP, width), BF16)
    in_spec = pl.BlockSpec((1, depth, ff), lambda e, where: (e, 0, 0))
    hidden_spec = pl.BlockSpec((1, NB * CAP, ff), lambda e, where: (e, 0, 0))
    hidden_shape = jax.ShapeDtypeStruct((held, NB * CAP, ff), BF16)
    return pl.pallas_call(
        partial(expert_kernel, slices),
        grid_spec=pltpu.PrefetchScalarGridSpec(
            num_scalar_prefetch=1,
            grid=(held,),
            in_specs=[block_spec(b) for b in range(2 * NB)]
            + [rows_spec] * 4
            + [in_spec, in_spec, pl.BlockSpec((1, ff, depth), lambda e, where: (e, 0, 0))],
            out_specs=[hidden_spec] * 3
            + [pl.BlockSpec((1, NB, tokens), lambda e, where: (e, 0, 0)), rows_spec, rows_spec],
        ),
        out_shape=[hidden_shape] * 3
        + [jax.ShapeDtypeStruct((held, NB, tokens), F32), rows_shape, rows_shape],
        compiler_params=pltpu.CompilerParams(vmem_limit_bytes=VMEM),
        cost_estimate=cost(
            flops=10 * NB * held * CAP * depth * ff,
            bytes_accessed=6 * held * depth * ff + 6 * NB * held * CAP * depth,
            transcendentals=NB * held * CAP * ff,
        ),
        name="expert_slot",
    )(where, *([pos] * NB), *([gate] * NB), *rows, *cots, w_gate, w_up, w_down)


def down_kernel(slices, slots, where_ref, *refs):
    scaled_refs, wd_ref, keep_ref, give_ref = refs[:slots], refs[slots], refs[-2], refs[-1]
    width = keep_ref.shape[3]
    for j in range(2 * slices):
        to = keep_ref if j < slices else give_ref
        columns = pl.ds(pl.multiple_of(where_ref[2 * NB + j] * width, width), width)
        for k in range(slots):
            rows = matmul(scaled_refs[k][0], wd_ref[0, :, columns])
            to[k * NB : (k + 1) * NB, j % slices] = rows.astype(BF16).reshape(NB, CAP, width)


def down_slots(where, scaled, w_down, slices):
    held, ff, depth = w_down.shape
    width = depth // (2 * slices)
    slots = len(scaled)
    rows_spec = pl.BlockSpec((slots * NB, slices, CAP, width), lambda e, where: (0, 0, e, 0))
    rows_shape = jax.ShapeDtypeStruct((slots * NB, slices, held * CAP, width), BF16)
    return pl.pallas_call(
        partial(down_kernel, slices, slots),
        grid_spec=pltpu.PrefetchScalarGridSpec(
            num_scalar_prefetch=1,
            grid=(held,),
            in_specs=[pl.BlockSpec((1, NB * CAP, ff), lambda e, where: (e, 0, 0))] * slots
            + [pl.BlockSpec((1, ff, depth), lambda e, where: (e, 0, 0))],
            out_specs=[rows_spec, rows_spec],
        ),
        out_shape=[rows_shape, rows_shape],
        compiler_params=pltpu.CompilerParams(vmem_limit_bytes=VMEM),
        cost_estimate=cost(
            flops=2 * slots * NB * held * CAP * depth * ff,
            bytes_accessed=2 * held * depth * ff + 2 * slots * NB * held * CAP * depth,
            transcendentals=0,
        ),
        name="down_slots",
    )(where, *scaled, w_down)


def place_kernel(slices, held, slots, where_ref, *refs):
    count = NB * slots
    at_refs, mine_ref, theirs_ref = refs[:count], refs[count], refs[count + 1]
    out_refs, hot_ref = refs[count + 2 : -1], refs[-1]
    b, y = pl.program_id(0), pl.program_id(1)
    tokens = hot_ref.shape[0]
    for block in range(count):

        @pl.when((b == block) & (y == 0))
        def _():
            at = at_refs[block][0]
            for tile in range(held * CAP // 128):
                lanes = lax.broadcasted_iota(jnp.int32, (tokens, 128), 1) + tile * 128
                mask = None
                for e in range(tile * 128 // CAP, (tile * 128 + 127) // CAP + 1):
                    hit = at[:, e : e + 1] == lanes
                    mask = hit if mask is None else mask | hit
                hot_ref[:, tile * 128 : (tile + 1) * 128] = as_bf16(mask)

    rows = (mine_ref[0, 0].astype(F32) + theirs_ref[0, 0].astype(F32)).astype(BF16)
    placed = matmul(hot_ref[...], rows).astype(BF16)
    for block in range(count):
        for part in range(slices):

            @pl.when((b == block) & (y == part))
            def _():
                out_refs[block % NB * slices + part][block // NB] = placed


def place_rows(wheres, at, mine, theirs):
    _, slices, count, width = mine.shape
    _, tokens, held = at.shape
    slots = len(wheres)
    blocks = jnp.concatenate([w[:NB] for w in wheres])

    def block_spec(b):
        return pl.BlockSpec((1, tokens, held), lambda i, y, where: (where[b], 0, 0))

    rows_spec = pl.BlockSpec((1, 1, count, width), lambda i, y, where: (i, y, 0, 0))
    out = pl.pallas_call(
        partial(place_kernel, slices, held, slots),
        grid_spec=pltpu.PrefetchScalarGridSpec(
            num_scalar_prefetch=1,
            grid=(NB * slots, slices),
            in_specs=[block_spec(b) for b in range(NB * slots)] + [rows_spec, rows_spec],
            out_specs=[pl.BlockSpec((slots, tokens, width), lambda i, y, where: (0, 0, 0))]
            * (NB * slices),
            scratch_shapes=[pltpu.VMEM((tokens, count), BF16)],
        ),
        out_shape=[jax.ShapeDtypeStruct((slots, tokens, width), BF16)] * (NB * slices),
        compiler_params=pltpu.CompilerParams(vmem_limit_bytes=VMEM),
        cost_estimate=cost(
            flops=2 * NB * slots * slices * count * tokens * width,
            bytes_accessed=2 * NB * slots * slices * (2 * count + tokens) * width,
            transcendentals=0,
        ),
        name="place_rows",
    )(blocks, *([at] * (NB * slots)), mine, theirs)
    return [out[b * slices : (b + 1) * slices] for b in range(NB)]


def weight_kernel(slots, slices, where_ref, *refs):
    rows, gate_grads, up_grads = refs[: 2 * slots], refs[2 * slots : 3 * slots], refs[3 * slots : 4 * slots]
    gate_ref, up_ref = refs[4 * slots :]
    width = rows[0].shape[3]
    for j in range(2 * slices):
        columns = pl.ds(pl.multiple_of(where_ref[2 * NB + j] * width, width), width)
        gate = up = None
        for k in range(slots):
            x = rows[2 * k + j // slices][:, j % slices].reshape(NB * CAP, width)
            terms = matmul_tn(x, gate_grads[k][0]), matmul_tn(x, up_grads[k][0])
            gate, up = terms if gate is None else (gate + terms[0], up + terms[1])
        gate_ref[0, columns, :] = gate
        up_ref[0, columns, :] = up


def weight_down_kernel(slots, slices, where_ref, *refs):
    cots, scaled, down_ref = refs[: 2 * slots], refs[2 * slots : 3 * slots], refs[3 * slots]
    width = cots[0].shape[3]
    for j in range(2 * slices):
        columns = pl.ds(pl.multiple_of(where_ref[2 * NB + j] * width, width), width)
        down = None
        for k in range(slots):
            c = cots[2 * k + j // slices][:, j % slices].reshape(NB * CAP, width)
            term = matmul_tn(scaled[k][0], c)
            down = term if down is None else down + term
        down_ref[0, :, columns] = down


def weight_grads(kernel, where, rows, hiddens, outs, name):
    slots = len(rows)
    held, _, ff = hiddens[0].shape
    slices, width = rows[0][0].shape[1], rows[0][0].shape[3]
    depth = 2 * slices * width
    rows_spec = pl.BlockSpec((NB, slices, CAP, width), lambda e, where: (0, 0, e, 0))
    hidden_spec = pl.BlockSpec((1, NB * CAP, ff), lambda e, where: (e, 0, 0))
    return pl.pallas_call(
        partial(kernel, slots, slices),
        grid_spec=pltpu.PrefetchScalarGridSpec(
            num_scalar_prefetch=1,
            grid=(held,),
            in_specs=[rows_spec] * (2 * slots) + [hidden_spec] * len(hiddens),
            out_specs=[pl.BlockSpec((1, *o), lambda e, where: (e, 0, 0)) for o in outs],
        ),
        out_shape=[jax.ShapeDtypeStruct((held, *o), F32) for o in outs],
        compiler_params=pltpu.CompilerParams(vmem_limit_bytes=VMEM),
        cost_estimate=cost(flops=10**10, bytes_accessed=10**6, transcendentals=0),
        name=name,
    )(where, *[a for pair in rows for a in pair], *hiddens)


def settle_kernel(where_ref, *refs):
    halves, (output_ref, value_ref, query_ref, key_ref) = refs[:6], refs[6:]

    def settle(output, value, both):
        output_ref[...] = output[...].astype(F32).T
        value_ref[...] = value[...].astype(F32)
        width = query_ref.shape[1]
        query_ref[...] = both[:, :width].astype(F32)
        key_ref[...] = both[:, width:].astype(F32)

    @pl.when(pl.program_id(0) < 4)
    def _():
        settle(*halves[0::2])

    @pl.when(pl.program_id(0) >= 4)
    def _():
        settle(*halves[1::2])


def settle_rows(where, output, value, both):
    rows = 2 * value[0].shape[0]
    step = rows // 8
    width = value[0].shape[1]
    near = lambda n: pl.BlockSpec((step, n), lambda i, where: (jnp.minimum(i, 3), 0))
    far = lambda n: pl.BlockSpec((step, n), lambda i, where: (jnp.maximum(i, 4) - 4, 0))
    placed = pl.BlockSpec((step, width), lambda i, where: (where[i], 0))
    return pl.pallas_call(
        settle_kernel,
        grid_spec=pltpu.PrefetchScalarGridSpec(
            num_scalar_prefetch=1,
            grid=(8,),
            in_specs=[s(n) for n in (width, width, 2 * width) for s in (near, far)],
            out_specs=[pl.BlockSpec((width, step), lambda i, where: (0, where[i]))] + [placed] * 3,
        ),
        out_shape=[jax.ShapeDtypeStruct((width, rows), F32)]
        + [jax.ShapeDtypeStruct((rows, width), F32)] * 3,
        compiler_params=pltpu.CompilerParams(vmem_limit_bytes=VMEM),
        cost_estimate=cost(flops=0, bytes_accessed=24 * rows * width, transcendentals=0),
        name="settle_rows",
    )(where, *output, *value, *both)


def project_kernel(
    in_ref, ag_ref, wq_ref, wk_ref, wv_ref, qg_ref, kg_ref,
    x_ref, inv_ref, qr_ref, kr_ref, q_ref, k_ref, v_ref,
):
    @pl.when(pl.program_id(0) == 0)
    def _():
        for first in range(0, in_ref.shape[0], 256):
            rows = in_ref[first : first + 256, :].astype(F32)
            inverse = lax.rsqrt(jnp.mean(rows * rows, axis=1, keepdims=True) + 1e-05)
            inv_ref[first : first + 256, :] = inverse
            x_ref[first : first + 256, :] = (rows * inverse * ag_ref[...]).astype(BF16)

    x = x_ref[...]
    for w_ref, gain_ref, raw_ref, to_ref in ((wq_ref, qg_ref, qr_ref, q_ref), (wk_ref, kg_ref, kr_ref, k_ref)):
        raw = matmul(x, w_ref[...])
        raw_ref[...] = raw
        for h in range(raw.shape[1] // HD):
            part = raw[:, h * HD : (h + 1) * HD]
            inverse = lax.rsqrt(jnp.mean(part * part, axis=1, keepdims=True) + 1e-06)
            gain = gain_ref[:, h * HD : (h + 1) * HD]
            to_ref[:, h * HD : (h + 1) * HD] = (part * inverse * gain).astype(BF16)
    v_ref[...] = matmul(x, wv_ref[...]).astype(BF16)


def project(inputs, attn_gain, w_query, w_key, w_value, query_gain, key_gain):
    tokens, depth = inputs.shape
    columns = w_query.shape[1]
    step = min(256, columns)
    whole = pl.BlockSpec((tokens, depth), lambda i: (0, 0))
    weight = pl.BlockSpec((depth, step), lambda i: (0, i))
    gain = pl.BlockSpec((1, step), lambda i: (0, i))
    out = pl.BlockSpec((tokens, step), lambda i: (0, i))
    return pl.pallas_call(
        project_kernel,
        grid=(columns // step,),
        in_specs=[whole, pl.BlockSpec((1, depth), lambda i: (0, 0)), weight, weight, weight, gain, gain],
        out_specs=[whole, pl.BlockSpec((tokens, 1), lambda i: (0, 0))] + [out] * 5,
        out_shape=[
            jax.ShapeDtypeStruct((tokens, depth), BF16),
            jax.ShapeDtypeStruct((tokens, 1), F32),
        ]
        + [jax.ShapeDtypeStruct((tokens, columns), t) for t in (F32, F32, BF16, BF16, BF16)],
        compiler_params=pltpu.CompilerParams(vmem_limit_bytes=VMEM),
        cost_estimate=cost(
            flops=6 * tokens * depth * columns,
            bytes_accessed=4 * tokens * depth + 6 * depth * columns + 14 * tokens * columns,
            transcendentals=0,
        ),
        name="project",
    )(
        inputs, attn_gain.reshape(1, -1), w_query, w_key, w_value,
        query_gain.reshape(1, -1), key_gain.reshape(1, -1),
    )


def allowed_pairs(pieces_ref, base, first, rows, keys):
    query = first + lax.broadcasted_iota(jnp.int32, (rows, 1), 0)
    key = lax.broadcasted_iota(jnp.int32, (1, keys), 1)

    def piece_of(at, other):
        found = jnp.full(at.shape, other, jnp.int32)
        for j in range(2):
            start, length = pieces_ref[base + j], pieces_ref[base + 2 + j]
            found = jnp.where((at >= start) & (at < start + length), j, found)
        return found

    return (key <= query) | (piece_of(query, -1) == piece_of(key, -2))


def query_blocks():
    half = LENGTH // 2
    return ((0, half, half), (half, half, LENGTH))


def attend_kernel(scale, pieces_ref, q_ref, k_ref, v_ref, o_ref, log_ref, top_ref):
    base = pl.program_id(0) * 4
    best = None
    for first, rows, keys in query_blocks():
        allowed = allowed_pairs(pieces_ref, base, first, rows, keys)
        scores = matmul_nt(q_ref[first : first + rows, :], k_ref[:keys, :]) * scale
        masked = jnp.where(allowed, scores, -1e30)
        top = jnp.max(masked, axis=1, keepdims=True)
        weights = jnp.exp(masked - top)
        total = jnp.sum(weights, axis=1, keepdims=True)
        probs = (weights * (1.0 / total)).astype(BF16)
        o_ref[first : first + rows, :] = matmul(probs, v_ref[:keys, :]).astype(BF16)
        log_ref[0, first : first + rows, :] = top + jnp.log(total)
        most = jnp.max(top, axis=0, keepdims=True)
        best = most if best is None else jnp.maximum(best, most)
    top_ref[0] = jnp.broadcast_to(best, (8, HD))


def attend(pieces, queries, keys, values, scale):
    tokens, columns = queries.shape
    sequences, heads = tokens // LENGTH, columns // HD
    block = pl.BlockSpec((LENGTH, HD), lambda s, h, pieces: (s, h))
    return pl.pallas_call(
        partial(attend_kernel, scale),
        grid_spec=pltpu.PrefetchScalarGridSpec(
            num_scalar_prefetch=1,
            grid=(sequences, heads),
            in_specs=[block] * 3,
            out_specs=[
                block,
                pl.BlockSpec((1, LENGTH, 1), lambda s, h, pieces: (h, s, 0)),
                pl.BlockSpec((1, 8, HD), lambda s, h, pieces: (s * heads + h, 0, 0)),
            ],
        ),
        out_shape=[
            jax.ShapeDtypeStruct((tokens, columns), BF16),
            jax.ShapeDtypeStruct((heads, tokens, 1), F32),
            jax.ShapeDtypeStruct((sequences * heads, 8, HD), F32),
        ],
        compiler_params=pltpu.CompilerParams(vmem_limit_bytes=VMEM),
        cost_estimate=cost(
            flops=4 * tokens * LENGTH * columns,
            bytes_accessed=8 * tokens * columns,
            transcendentals=tokens * heads * LENGTH,
        ),
        name="attend",
    )(pieces, queries, keys, values)


def attend_back_kernel(
    scale, pieces_ref, q_ref, k_ref, v_ref, g_ref, log_ref, qr_ref, kr_ref, qg_ref, kg_ref,
    gq_ref, gk_ref, gv_ref, gqg_ref, gkg_ref, dq_ref, dk_ref, dv_ref,
):
    base = pl.program_id(0) * 4
    blocks = query_blocks()
    for first, rows, keys in blocks[::-1]:
        allowed = allowed_pairs(pieces_ref, base, first, rows, keys)
        q, g = q_ref[first : first + rows, :], g_ref[first : first + rows, :]
        k, v = k_ref[:keys, :], v_ref[:keys, :]
        scores = matmul_nt(q, k) * scale
        probs = jnp.exp(jnp.where(allowed, scores, -1e30) - log_ref[0, first : first + rows, :])
        grad_p = matmul_nt(g, v)
        delta = jnp.sum(probs * grad_p, axis=1, keepdims=True)
        grad_s = (probs * (grad_p - delta)).astype(BF16)
        dq_ref[first : first + rows, :] = matmul(grad_s, k) * scale
        dk = matmul_tn(grad_s, q) * scale
        dv = matmul_tn(probs.astype(BF16), g)
        if keys == LENGTH:
            dk_ref[...] = dk
            dv_ref[...] = dv
        else:
            dk_ref[:keys, :] += dk
            dv_ref[:keys, :] += dv
    gv_ref[...] = dv_ref[...].astype(BF16)
    for raw_ref, gain_ref, grad_ref, to_ref, sum_ref in (
        (qr_ref, qg_ref, dq_ref, gq_ref, gqg_ref),
        (kr_ref, kg_ref, dk_ref, gk_ref, gkg_ref),
    ):
        raw, grad = raw_ref[...], grad_ref[...]
        inverse = lax.rsqrt(jnp.mean(raw * raw, axis=1, keepdims=True) + 1e-06)
        hat = raw * inverse
        up = grad * gain_ref[...]
        mean = jnp.mean(up * hat, axis=1, keepdims=True)
        to_ref[...] = (inverse * (up - hat * mean)).astype(BF16)
        sum_ref[0] = jnp.sum(grad * hat, axis=0, keepdims=True)


def attend_back(pieces, queries, keys, values, grads, logs, query_raw, key_raw, query_gain, key_gain, scale):
    tokens, columns = queries.shape
    sequences, heads = tokens // LENGTH, columns // HD
    block = pl.BlockSpec((LENGTH, HD), lambda s, h, pieces: (s, h))
    gain = pl.BlockSpec((1, HD), lambda s, h, pieces: (0, h))
    sums = pl.BlockSpec((1, 1, HD), lambda s, h, pieces: (s, 0, h))
    return pl.pallas_call(
        partial(attend_back_kernel, scale),
        grid_spec=pltpu.PrefetchScalarGridSpec(
            num_scalar_prefetch=1,
            grid=(sequences, heads),
            in_specs=[block] * 4
            + [pl.BlockSpec((1, LENGTH, 1), lambda s, h, pieces: (h, s, 0)), block, block, gain, gain],
            out_specs=[block, block, block, sums, sums],
            scratch_shapes=[pltpu.VMEM((LENGTH, HD), F32)] * 3,
        ),
        out_shape=[jax.ShapeDtypeStruct((tokens, columns), BF16)] * 3
        + [jax.ShapeDtypeStruct((sequences, 1, columns), F32)] * 2,
        compiler_params=pltpu.CompilerParams(vmem_limit_bytes=VMEM),
        cost_estimate=cost(
            flops=10 * tokens * LENGTH * columns,
            bytes_accessed=22 * tokens * columns,
            transcendentals=tokens * heads * LENGTH,
        ),
        name="attend_back",
    )(
        pieces, queries, keys, values, grads, logs, query_raw, key_raw,
        query_gain.reshape(1, -1), key_gain.reshape(1, -1),
    )


def expert_steps(slots):
    order = list(ORDER) if is_cube() else list(range(slots))
    steps = [("cot", order[0]), ("row", order[0]), ("cot", order[1]), ("exp", order[0])]
    for i, k in enumerate(order):
        if i + 1 < slots:
            steps.append(("row", order[i + 1]))
        else:
            steps.append(("down", 0))
        if i + 2 < slots:
            steps.append(("cot", order[i + 2]))
        steps.append(("place", k))
        if i + 1 < slots:
            steps.append(("exp", order[i + 1]))
    return steps


def due(step, seen):
    return [seen[name] for name in DUE.get(step, ()) if name in seen]


def per_device(
    inputs,
    attn_gain,
    w_query,
    w_key,
    w_value,
    w_output,
    query_gain,
    key_gain,
    moe_gain,
    w_router,
    w_gate,
    w_up,
    w_down,
    routes,
    piece_start,
    piece_length,
    clip_threshold,
    cotangent,
):
    tokens_here, width = inputs.shape
    slice_width = cotangent.shape[1]
    owner = lax.axis_index("expert")
    column = lax.axis_index("tensor") * slice_width
    heads_here = query_gain.shape[0] // HD
    experts_here = w_gate.shape[0]
    owners = lax.axis_size("expert")
    sequences = tokens_here // LENGTH
    scale = 1.0 / math.sqrt(HD)
    where = slot_blocks()
    slots = len(where)
    slices = lax.axis_size("tensor") // 2

    def own_columns(value):
        return lax.dynamic_slice_in_dim(value, column, slice_width, value.ndim - 1)

    seen = {}
    all_routes = gather_routes(routes.T)
    cot_slots = gather_slots(cotangent.astype(BF16), "c", seen, [all_routes])
    order = tensor_order()

    held_ids = owner * experts_here + jnp.arange(experts_here, dtype=jnp.int32)
    chosen = jnp.any(all_routes[:, None] == held_ids[None, :, None, None], axis=2)
    places = jnp.arange(tokens_here, dtype=jnp.int32)
    before = (places[:, None] < places[None, :]).astype(BF16)
    earlier = jnp.einsum(
        "set,tu->seu", chosen.astype(BF16), before, preferred_element_type=F32
    ).astype(jnp.int32)
    pos = jnp.where(chosen, earlier, -1)
    at = jnp.where(
        chosen, earlier + jnp.arange(experts_here, dtype=jnp.int32)[None, :, None] * CAP, -1
    ).transpose(0, 2, 1)

    output_pieces = [lax.dynamic_slice_in_dim(w_output, o * slice_width, slice_width, 1) for o in order]
    normed_a, attn_inv, query_raw, key_raw, queries, keys, values = project(
        inputs, attn_gain, w_query, w_key, w_value, query_gain, key_gain
    )
    blocks = row_blocks()
    normed_rows = jnp.concatenate(
        [lax.dynamic_slice_in_dim(normed_a, r * (width // 8), width // 8, 1) for r in blocks], axis=1
    )
    pieces = jnp.concatenate([piece_start, piece_length], axis=1).reshape(-1)
    attended, logs, tops = attend(
        after(pieces, values, all_routes), queries, keys, values, scale
    )
    head_top = jnp.max(tops[:, 0, 0].reshape(sequences, heads_here), axis=0)
    attended = after(attended, *due("attended", seen))
    branch = tensor_scatter(partial(matmul, attended), output_pieces, "b", seen, [pos, at])
    residual = own_columns(inputs).astype(F32) + branch
    gain_slice = own_columns(moe_gain)
    router_slice = lax.dynamic_slice_in_dim(w_router, column, slice_width, 0)
    lifted = residual * gain_slice
    row_sums = tensor_sum(
        jnp.concatenate(
            [
                lax.dot_general(
                    router_slice,
                    lifted.astype(BF16),
                    (((0,), (1,)), ((), ())),
                    preferred_element_type=F32,
                ),
                jnp.sum(residual * residual, axis=1)[None],
            ],
            axis=0,
        )
    )
    moe_inv_row = lax.rsqrt(row_sums[E] / width + 1e-05)
    moe_inv = moe_inv_row[:, None]
    normed_m = (lifted * moe_inv).astype(BF16)
    normed_m = after(normed_m, *due("normed", seen))

    normed_slots = gather_slots(normed_m, "n", seen)
    router = jax.nn.softmax(row_sums[:E] * moe_inv_row[None], axis=0)
    gate = lax.all_to_all(
        router.reshape(owners, experts_here, tokens_here),
        "expert",
        split_axis=0,
        concat_axis=0,
        tiled=True,
    )

    rows, cots, back, sums = [None] * slots, [None] * slots, [None] * slots, [None] * slots
    scaled, gate_grads, up_grads, probs = [None] * slots, [None] * slots, [None] * slots, [None] * slots
    last = normed_m
    downs = {}

    def turn(name, k):
        return after(where[k], last, *due(name, seen))

    def lower(k):
        first = slots - 2 - 2 * k
        keep, give = down_slots(
            turn("down" + str(k), 0), scaled[first : first + 2], w_down, slices
        )
        downs[k] = (keep, core_swap(give))
        seen["sd" + str(k)] = downs[k][1]
        return keep

    for kind, k in expert_steps(slots):
        now = turn(kind + str(k), k)
        if kind == "cot":
            last = pick_rows(now, pos, cot_slots[k])
            cots[k] = (last, core_swap(last))
            seen["sc" + str(k)] = cots[k][1]
        elif kind == "row":
            last = pick_rows(now, pos, normed_slots[k])
            rows[k] = (last, core_swap(last))
            seen["sr" + str(k)] = rows[k][1]
        elif kind == "exp":
            scaled[k], gate_grads[k], up_grads[k], probs[k], keep, give = expert_slot(
                now, pos, gate, rows[k], cots[k], w_gate, w_up, w_down
            )
            last = scaled[k]
            back[k] = (keep, core_swap(give))
            seen["sg" + str(k)] = back[k][1]
        elif kind == "down":
            last = lower(k)
        else:
            placed = place_rows([now], at, *back[k])
            last = placed[0][0]
            back[k] = [[a[0] for a in b] for b in placed]
            if is_cube():
                odd = k in ODD
                sums[k], sent = scatter_plane(back[k], scatter_corner(back[k], odd), odd)
                if k:
                    sums[k] = sent["z"] = send(sums[k].astype(BF16), dz=k)
                seen.update({"e" + link + str(k): value for link, value in sent.items()})
    for k in range(1, slots // 2):
        last = lower(k)
    pairs = []
    for k in range(slots // 2):
        first = slots - 2 - 2 * k
        pairs.append(place_rows([turn("pd" + str(k), first), where[first + 1]], at, *downs[k]))
        last = pairs[k][0][0]
    far = scatter_corners(pairs, seen)
    grad_gate, grad_up = weight_grads(
        weight_kernel,
        turn("weight", 0),
        rows,
        gate_grads + up_grads,
        [w_gate.shape[1:]] * 2,
        "weight_grads",
    )
    if is_cube():
        expert_path = added(*[after(s, grad_gate) for s in sums])
    else:
        expert_path = scatter_all(back)

    prob_grads = jnp.stack([probs[k][:, b] for k in range(slots) for b in range(NB)])
    if is_cube():
        prob_grads = prob_grads[jnp.arange(owners, dtype=jnp.int32) ^ owner]
    prob_grads = lax.all_to_all(prob_grads, "expert", split_axis=0, concat_axis=0, tiled=True)
    prob_grads = tensor_sum(prob_grads.reshape(E, tokens_here))
    grad_logits = (
        router * (prob_grads - jnp.sum(router * prob_grads, axis=0, keepdims=True))
    ).astype(BF16)
    grad_router = lax.dot_general(
        normed_m, grad_logits, (((0,), (1,)), ((), ())), preferred_element_type=F32
    )
    router_path = lax.dot_general(
        grad_logits, router_slice, (((0,), (1,)), ((), ())), preferred_element_type=F32
    )
    grad_normed = expert_path + router_path
    moe_hat = residual * moe_inv
    grad_moe_gain = jnp.sum(grad_normed * moe_hat, axis=0)
    upstream = grad_normed * gain_slice
    mean_dot = tensor_sum(jnp.sum(upstream * moe_hat, axis=-1).reshape(8, -1)).reshape(-1, 1) / width
    grad_residual = cotangent + moe_inv * (upstream - moe_hat * mean_dot)
    grad_branch = after(grad_residual.astype(BF16), *due("residual_grad", seen))
    (grad_down,) = weight_grads(
        weight_down_kernel,
        after(where[0], grad_branch),
        cots,
        scaled,
        [w_down.shape[1:]],
        "weight_down_grads",
    )
    branch_pieces = tensor_gather(grad_branch, [grad_down])

    if is_cube():
        high, sent = scatter_plane(pairs[0], far[0], True, branch_pieces[1:2])
        high = seen["gz"] = send(high.astype(BF16), dz=2)
        seen.update({"g" + link + "0": value for link, value in sent.items()})
    grad_branch = jnp.concatenate(branch_pieces, axis=1)

    grad_output = matmul_tn(grad_branch, attended).astype(BF16)
    spots = order_spots()
    eighth = width // 8
    wide = slice_width // eighth
    grad_output = jnp.concatenate(
        [
            lax.dynamic_slice_in_dim(
                grad_output, (spots(r // wide) * wide + r % wide) * eighth, eighth, 0
            )
            for r in blocks
        ],
        axis=0,
    )
    sum_output = expert_sum(grad_output, "o", seen)
    grad_attended = matmul_nt(grad_branch, jnp.concatenate(output_pieces, axis=1)).astype(BF16)
    grad_attended = after(grad_attended, grad_output)
    grad_query_raw, grad_key_raw, grad_v, grad_query_gain, grad_key_gain = attend_back(
        after(pieces, *due("back", seen)),
        queries,
        keys,
        values,
        grad_attended,
        logs,
        query_raw,
        key_raw,
        query_gain,
        key_gain,
        scale,
    )
    sum_value = expert_sum(matmul_tn(normed_rows, grad_v).astype(BF16), "v", seen)
    grad_raw = jnp.concatenate([grad_query_raw, grad_key_raw, grad_v], axis=1)
    grad_both = matmul_tn(normed_rows, grad_raw[:, : 2 * slice_width]).astype(BF16)
    sum_both = expert_sum(grad_both, "qk", seen)
    grad_raw = after(grad_raw, grad_both, *due("normed_grad", seen))
    weights = jnp.concatenate([w_query, w_key, w_value], axis=1)
    weight_pieces = [lax.dynamic_slice_in_dim(weights, o * slice_width, slice_width, 0) for o in order]
    grad_normed_a = tensor_scatter(partial(matmul_nt, grad_raw), weight_pieces, "h", seen)
    attn_hat = own_columns(inputs).astype(F32) * attn_inv
    upstream = grad_normed_a * own_columns(attn_gain)
    grad_attn_gain = jnp.sum(grad_normed_a * attn_hat, axis=0)
    mean_dot = tensor_sum(jnp.sum(upstream * attn_hat, axis=-1).reshape(8, -1)).reshape(-1, 1) / width
    grad_input = grad_residual + attn_inv * (upstream - attn_hat * mean_dot)

    small = jnp.concatenate(
        [
            grad_router.T,
            jnp.stack(
                [
                    grad_attn_gain,
                    grad_moe_gain,
                    jnp.sum(grad_query_gain, axis=(0, 1)),
                    jnp.sum(grad_key_gain, axis=(0, 1)),
                ]
            ),
        ],
        axis=0,
    )
    top_row = jnp.pad(head_top, (0, slice_width - heads_here), constant_values=-3e38)
    small, top_row = expert_total(small, top_row[None], seen)
    head_top = top_row[0, :heads_here]
    if is_cube():
        free = [seen["qkx"], seen["t1"], high]
        total = added(scatter_plane(pairs[1], far[1], False, branch_pieces[1:2], free)[0], high)
        mixture = total[0] + send(total[1].astype(BF16), dz=1).astype(F32)
    else:
        mixture = scatter_all(
            [[[a[i] for a in b] for b in pair] for pair in pairs[::-1] for i in range(2)]
        )
    out = residual + mixture
    sum_moe_gain, sum_query_gain, sum_key_gain = small[E + 1], small[E + 2], small[E + 3]
    every = lax.all_gather(small[: E + 1], "tensor")
    sum_router = every[:, :E].transpose(0, 2, 1).reshape(width, E)
    sum_attn_gain = every[:, E].reshape(width)
    sum_output, sum_value, sum_query, sum_key = settle_rows(
        jnp.stack(blocks), sum_output, sum_value, sum_both
    )
    factor = clip_threshold / jnp.maximum(head_top, clip_threshold)
    spread = jnp.repeat(jnp.sqrt(factor), HD)
    query_clipped = (w_query.astype(F32) * spread[None, :]).astype(BF16)
    key_clipped = (w_key.astype(F32) * spread[None, :]).astype(BF16)
    return (
        out,
        grad_input,
        sum_attn_gain,
        sum_query,
        sum_key,
        sum_value,
        sum_output,
        sum_query_gain,
        sum_key_gain,
        sum_moe_gain,
        sum_router,
        grad_gate,
        grad_up,
        grad_down,
        head_top,
        query_clipped,
        key_clipped,
    )


def solution(mesh):
    return jax.shard_map(
        per_device,
        mesh=mesh,
        in_specs=(
            P("expert", None),
            P(),
            P(None, "tensor"),
            P(None, "tensor"),
            P(None, "tensor"),
            P("tensor", None),
            P("tensor"),
            P("tensor"),
            P(),
            P(),
            P("expert", None, "tensor"),
            P("expert", None, "tensor"),
            P("expert", "tensor", None),
            P("expert", None),
            P("expert", None),
            P("expert", None),
            P("tensor"),
            P("expert", "tensor"),
        ),
        out_specs=(
            P("expert", "tensor"),
            P("expert", "tensor"),
            P(),
            P(None, "tensor"),
            P(None, "tensor"),
            P(None, "tensor"),
            P("tensor", None),
            P("tensor"),
            P("tensor"),
            P("tensor"),
            P(),
            P("expert", None, "tensor"),
            P("expert", None, "tensor"),
            P("expert", "tensor", None),
            P("tensor"),
            P(None, "tensor"),
            P(None, "tensor"),
        ),
        check_vma=False,
    )
```
